32 devices in a mesh: dp: 8 (over y, x, core), fsdp: 4 (over z).
Axes of the slice: x: 2, y: 2, z: 4, core: 2. Of those that a mesh axis runs over, the one named last changes fastest.
Arguments:
- tokens: bfloat16 [16, 1024, 2048], P('dp', 'fsdp'), may hold values from -6 to 6
- cotangent: bfloat16 [16, 1024, 2048], P('dp', 'fsdp'), may hold values from -6 to 6
- lengths: int32 [16, 8], P('dp'), may hold values from 1 to 928, as said below
- query_weight: bfloat16 [2048, 2048], P(('dp', 'fsdp')), may hold values from -0.125 to 0.125
- kv_weight: bfloat16 [2048, 256], P(('dp', 'fsdp')), may hold values from -0.125 to 0.125
- out_weight: bfloat16 [2048, 2048], P(('dp', 'fsdp')), may hold values from -0.75 to 0.75
- query_bias: bfloat16 [2048], P(('dp', 'fsdp')), may hold values from -3 to 3
- value_bias: bfloat16 [128], P(('dp', 'fsdp')), may hold values from -1.1953125 to 1.1953125
- out_bias: bfloat16 [2048], P(('dp', 'fsdp')), may hold values from -3 to 3
- attn_gain: bfloat16 [2048], P(('dp', 'fsdp')), may hold values from 0.5 to 1.5
- attn_shift: bfloat16 [2048], P(('dp', 'fsdp')), may hold values from -2 to 2
- up_weight: bfloat16 [2048, 8192], P(('dp', 'fsdp')), may hold values from -0.125 to 0.125
- down_weight: bfloat16 [8192, 2048], P(('dp', 'fsdp')), may hold values from -0.0625 to 0.0625
- up_bias: bfloat16 [8192], P(('dp', 'fsdp')), may hold values from -3 to 3
- down_bias: bfloat16 [2048], P(('dp', 'fsdp')), may hold values from -3 to 3
- mlp_gain: bfloat16 [2048], P(('dp', 'fsdp')), may hold values from 0.5 to 1.5
- mlp_shift: bfloat16 [2048], P(('dp', 'fsdp')), may hold values from -2 to 2
Outputs:
- output: bfloat16 [16, 1024, 2048], P('dp', 'fsdp')
- tokens_grad: bfloat16 [16, 1024, 2048], P('dp', 'fsdp')
- query_weight_grad: float32 [2048, 2048], P(('dp', 'fsdp'))
- kv_weight_grad: float32 [2048, 256], P(('dp', 'fsdp'))
- out_weight_grad: float32 [2048, 2048], P(('dp', 'fsdp'))
- query_bias_grad: float32 [2048], P(('dp', 'fsdp'))
- value_bias_grad: float32 [128], P(('dp', 'fsdp'))
- out_bias_grad: float32 [2048], P(('dp', 'fsdp'))
- attn_gain_grad: float32 [2048], P(('dp', 'fsdp'))
- attn_shift_grad: float32 [2048], P(('dp', 'fsdp'))
- up_weight_grad: float32 [2048, 8192], P(('dp', 'fsdp'))
- down_weight_grad: float32 [8192, 2048], P(('dp', 'fsdp'))
- up_bias_grad: float32 [8192], P(('dp', 'fsdp'))
- down_bias_grad: float32 [2048], P(('dp', 'fsdp'))
- mlp_gain_grad: float32 [2048], P(('dp', 'fsdp'))
- mlp_shift_grad: float32 [2048], P(('dp', 'fsdp'))
The draws below stay inside these ranges and needn't reach their ends.
Inputs may be any that keep to these rules, and one draw needn't show every extreme that they name: `lengths`: row w lists the token counts of window w's 8 files in order; one file of each window, at a place drawn from the seed, has exactly 928 tokens; the window's last 1024 minus the row's sum positions are padding.
All inputs are finite; a program needn't handle non-finite values.
Results may differ from the reference program's by a relative error of at most 0.014.
Values may be sent and summed in bfloat16 or wider, within the bound.
No kernel may reach another device: no remote copies, remote signals or barrier semaphores. Data moves between devices by JAX's collectives and lax.ppermute only.
A program may use at most 384 MiB of HBM per device.

```python
import math
import jax
import jax.numpy as jnp
from jax import lax

D = 2048
HEADS = 16
HD = 128
FF = 8192
WIN = 1024
NSEG = 8
SPARE = 96
WINDOWS = 16


def draw_lengths(key, part):
    key = jax.random.fold_in(key, 11)
    k_weight, k_place = jax.random.split(key)
    weights = jax.random.randint(k_weight, (WINDOWS, NSEG), 1, 16) ** 2
    budget = SPARE - (NSEG - 1)
    extra_len = weights * budget // jnp.sum(weights, axis=1, keepdims=True)
    shorts = 1 + extra_len[:, :NSEG - 1]
    longest = WIN - SPARE
    long_slot = jax.random.randint(k_place, (WINDOWS, 1), 0, NSEG)
    slot_ids = jnp.arange(NSEG, dtype=jnp.int32)[None, :]
    short_idx = jnp.clip(slot_ids - (slot_ids > long_slot).astype(jnp.int32), 0, NSEG - 2)
    short_idx = jnp.broadcast_to(short_idx, (WINDOWS, NSEG))
    picked = jnp.take_along_axis(shorts, short_idx, axis=1)
    return jnp.where(slot_ids == long_slot, longest, picked).astype(jnp.int32)


def with_spikes(entries, rng, source, target, shards_of, factor):
    def block_of(position):
        return (jnp.arange(entries.shape[position]) // (entries.shape[position] // shards_of)).reshape((-1,) + (1,) * (entries.ndim - 1 - position))

    first = jax.random.permutation(rng, shards_of)[block_of(target)]
    far = (block_of(target) + shards_of // 2) % shards_of
    return jnp.where((block_of(source) == first) | (block_of(source) == far), factor * entries, entries)


def block_levels(key, dims, pieces, least, high):
    gain, own = 1.0, jax.random.fold_in(key, 6)
    for dim, shards_of in pieces:
        heights = jnp.exp(jax.random.uniform(jax.random.fold_in(own, dim), (shards_of,), jnp.float32, least / len(pieces), high / len(pieces)))
        gain = gain * jnp.repeat(heights, dims[dim] // shards_of).reshape([-1 if axis == dim else 1 for axis in range(len(dims))])
    return gain


def centred(stream_key, dims, spread, most, cuts=(), held_as=jnp.bfloat16):
    entries = spread * jax.random.normal(stream_key, dims, jnp.float32)
    if cuts:
        entries = entries * block_levels(stream_key, dims, cuts, -0.22, 0.18)
    return jnp.clip(entries, -most, most).astype(held_as)


def heavy_noise(stream_key, dims, scale, bound, shards, heavy, kind=jnp.bfloat16):
    array = scale * jax.random.normal(stream_key, dims, jnp.float32)
    if shards:
        array = array * block_levels(stream_key, dims, shards, -0.22, 0.18)
    return jnp.clip(with_spikes(array, jax.random.fold_in(stream_key, 3), *heavy), -bound, bound).astype(kind)


def setup_inputs(seed: int = 0) -> dict:
    key_list = jax.random.split(jax.random.key(seed), 18)
    tokens = centred(key_list[0], (WINDOWS, WIN, D), 1.0, 6.0, ((0, 8), (1, 4)))
    cotangent = heavy_noise(key_list[1], (WINDOWS, WIN, D), 1.0, 6.0, ((0, 8), (1, 4)), (0, 2, 8, 2.0))
    lengths = draw_lengths(jax.random.fold_in(key_list[17], 71), 0)
    query_weight = centred(key_list[3], (D, D), D ** -0.5, 0.125, ((0, 32),))
    kv_weight = centred(key_list[4], (D, 2 * HD), D ** -0.5, 0.125, ((0, 32),))
    out_weight = centred(key_list[5], (D, D), (D // 32) ** -0.5, 0.75, ((0, 32),))
    query_bias = centred(key_list[6], (D,), 0.5, 3.0, ((0, 32),))
    value_bias = centred(key_list[7], (HD,), 0.2, 1.1953125, ((0, 32),))
    out_bias = centred(key_list[8], (D,), 0.5, 3.0, ((0, 32),))
    attn_gain = jnp.clip(0.5 + 1.0 * jax.random.uniform(key_list[9], (D,), jnp.float32) ** block_levels(key_list[9], (D,), ((0, 32),), -0.2, 0.2), 0.5, 1.5).astype(jnp.bfloat16)
    attn_shift = centred(key_list[10], (D,), 0.3, 2.0, ((0, 32),))
    up_weight = centred(key_list[11], (D, FF), D ** -0.5, 0.125, ((0, 32),))
    down_weight = centred(key_list[12], (FF, D), FF ** -0.5, 0.0625, ((0, 32),))
    up_bias = centred(key_list[13], (FF,), 0.5, 3.0, ((0, 32),))
    down_bias = centred(key_list[14], (D,), 0.5, 3.0, ((0, 32),))
    mlp_gain = jnp.clip(0.5 + 1.0 * jax.random.uniform(key_list[15], (D,), jnp.float32) ** block_levels(key_list[15], (D,), ((0, 32),), -0.2, 0.2), 0.5, 1.5).astype(jnp.bfloat16)
    mlp_shift = centred(key_list[16], (D,), 0.3, 2.0, ((0, 32),))
    return {"tokens": tokens, "cotangent": cotangent, "lengths": lengths, "query_weight": query_weight, "kv_weight": kv_weight, "out_weight": out_weight, "query_bias": query_bias, "value_bias": value_bias, "out_bias": out_bias, "attn_gain": attn_gain, "attn_shift": attn_shift, "up_weight": up_weight, "down_weight": down_weight, "up_bias": up_bias, "down_bias": down_bias, "mlp_gain": mlp_gain, "mlp_shift": mlp_shift}


@jax.custom_vjp
def low(v):
    return lax.optimization_barrier(v.astype(jnp.bfloat16)).astype(jnp.float32)

@jax.custom_vjp
def low_back(v):
    return v

def low_keep(v):
    return (low(v), None)

def low_pass(kept, grad):
    return (grad,)

def back_keep(v):
    return (v, None)

def back_low(kept, grad):
    return (low(grad),)
low.defvjp(low_keep, low_pass)
low_back.defvjp(back_keep, back_low)
EPS = 1e-05

def matmul_high(left_side, right_side):
    return jnp.dot(left_side, right_side, precision=lax.Precision.HIGHEST, preferred_element_type=jnp.float32)

def layer_norm(values, gain_vec, shift_vec):
    average = lax.optimization_barrier(jnp.mean(values, axis=-1, keepdims=True))
    centered = values - average
    variance = lax.optimization_barrier(jnp.mean(centered * centered, axis=-1, keepdims=True))
    return centered * lax.rsqrt(variance + EPS) * gain_vec + shift_vec

def gelu_tanh(values):
    return jax.nn.gelu(values, approximate=True)

def file_numbers(file_lengths):
    file_ends = jnp.cumsum(file_lengths)
    positions = jnp.arange(WIN, dtype=jnp.int32)
    return lax.optimization_barrier(jnp.sum((file_ends[None, :] <= positions[:, None]).astype(jnp.int32), axis=1))

def attend_head(query_head, key_rows, value_rows, allowed):
    scores = low_back(matmul_high(query_head, key_rows.T) / math.sqrt(HD))
    scores = jnp.where(allowed, scores, -1e+30)
    prob_low = low(jax.nn.softmax(scores, axis=-1))
    return matmul_high(prob_low, value_rows)

def window_forward(param_set, inputs, file_ids):
    query_weight, kv_weight, out_weight, query_bias, value_bias, out_bias, attn_gain, attn_shift, up_weight, down_weight, up_bias, down_bias, mlp_gain, mlp_shift = param_set
    normed_one = low(layer_norm(inputs, attn_gain, attn_shift))
    queries = low(low_back(matmul_high(normed_one, query_weight) + query_bias))
    kv_bias = jnp.concatenate([jnp.zeros((HD,), jnp.float32), value_bias])
    key_value = low(low_back(matmul_high(normed_one, kv_weight) + kv_bias))
    positions = jnp.arange(WIN, dtype=jnp.int32)
    allowed = (file_ids[:, None] == file_ids[None, :]) & (positions[None, :] <= positions[:, None])
    heads_first = queries.reshape(WIN, HEADS, HD).transpose(1, 0, 2)
    checked = jax.checkpoint(attend_head)
    mixed_heads = lax.map(lambda query_head: checked(query_head, key_value[:, :HD], key_value[:, HD:], allowed), heads_first)
    attended = low(low_back(mixed_heads.transpose(1, 0, 2).reshape(WIN, D)))
    middle = inputs + low_back(matmul_high(attended, out_weight)) + out_bias
    normed_two = low(layer_norm(middle, mlp_gain, mlp_shift))
    hidden = low(gelu_tanh(low_back(matmul_high(normed_two, up_weight) + up_bias)))
    return middle + low_back(matmul_high(hidden, down_weight)) + down_bias

def reference(tokens, cotangent, lengths, query_weight, kv_weight, out_weight, query_bias, value_bias, out_bias, attn_gain, attn_shift, up_weight, down_weight, up_bias, down_bias, mlp_gain, mlp_shift):
    params = tuple((tensor.astype(jnp.float32) for tensor in (query_weight, kv_weight, out_weight, query_bias, value_bias, out_bias, attn_gain, attn_shift, up_weight, down_weight, up_bias, down_bias, mlp_gain, mlp_shift)))

    def one_window(totals, window):
        inputs, cot_rows, file_lengths = window
        file_ids = file_numbers(file_lengths)

        def forward(param_set, input_rows):
            return window_forward(param_set, input_rows, file_ids)
        result, pullback = jax.vjp(forward, params, inputs.astype(jnp.float32))
        param_grads, input_grad = pullback(cot_rows.astype(jnp.float32))
        totals = jax.tree.map(lambda left_side, right_side: left_side + right_side, totals, param_grads)
        return (totals, (result.astype(jnp.bfloat16), input_grad.astype(jnp.bfloat16)))
    zeros_init = jax.tree.map(jnp.zeros_like, params)
    totals, (outputs, input_grads) = lax.scan(one_window, zeros_init, (tokens, cotangent, lengths))
    return (outputs, input_grads, totals[0], totals[1], totals[2], totals[3], totals[4], totals[5], totals[6], totals[7], totals[8], totals[9], totals[10], totals[11], totals[12], totals[13])
```

```python
import math

import jax
import jax.numpy as jnp
from jax import lax
from jax.sharding import PartitionSpec as P

HEADS = 16
HD = 128
EPS = 1e-05
F32 = jnp.float32
BF16 = jnp.bfloat16
BOTH = ("dp", "fsdp")


def norm_stats(values):
    average = jnp.mean(values, axis=-1, keepdims=True)
    centered = values - average
    variance = jnp.mean(centered * centered, axis=-1, keepdims=True)
    recip = lax.rsqrt(variance + EPS)
    return average, recip


def norm_pull(grad, xhat, recip, gain):
    scaled = grad * gain
    mean_one = jnp.mean(scaled, axis=-1, keepdims=True)
    mean_two = jnp.mean(scaled * xhat, axis=-1, keepdims=True)
    return recip * (scaled - mean_one - xhat * mean_two)


def gelu_tanh(values):
    return jax.nn.gelu(values, approximate=True)


def dot_nn(left, right):
    return jnp.dot(left, right, preferred_element_type=F32)


def dot_nt(left, right):
    return lax.dot_general(left, right, (((1,), (1,)), ((), ())), preferred_element_type=F32)


def dot_tn(left, right):
    return lax.dot_general(left, right, (((0,), (0,)), ((), ())), preferred_element_type=F32)


def gather_both(block):
    return lax.all_gather(
        lax.all_gather(block, "fsdp", axis=0, tiled=True), "dp", axis=0, tiled=True
    )


def scatter_both(block):
    part = lax.psum_scatter(block, "dp", scatter_dimension=0, tiled=True)
    return lax.psum_scatter(part, "fsdp", scatter_dimension=0, tiled=True)


def ring_steps(count):
    return [(i, (i + 1) % count) for i in range(count)]


def ring_gather(block, count):
    me = lax.axis_index("fsdp")
    whole = jnp.zeros((count,) + block.shape, block.dtype)
    held = block
    for step in range(count):
        whole = lax.dynamic_update_index_in_dim(whole, held, lax.rem(me - step + count, count), 0)
        if step + 1 < count:
            held = lax.ppermute(held, "fsdp", ring_steps(count))
    return whole


def ring_scatter(terms, count):
    me = lax.axis_index("fsdp")

    def term(step):
        return lax.dynamic_index_in_dim(
            terms, lax.rem(me - 1 - step + 2 * count, count), 0, keepdims=False
        ).astype(F32)

    total = term(0)
    for step in range(1, count):
        total = lax.ppermute(total.astype(BF16), "fsdp", ring_steps(count)).astype(F32) + term(step)
    return total


def masked_scores(query_block, kv_rows, allowed_block, root_hd):
    scores = dot_nt(query_block, kv_rows[:, :HD]) / root_hd
    scores = scores.reshape(HEADS, -1, kv_rows.shape[0])
    return jnp.where(allowed_block[None], scores, -1e30)


def make_local(n_dp, n_z):
    n_dev = n_dp * n_z

    def local(
        tokens,
        cotangent,
        lengths,
        query_weight,
        kv_weight,
        out_weight,
        query_bias,
        value_bias,
        out_bias,
        attn_gain,
        attn_shift,
        up_weight,
        down_weight,
        up_bias,
        down_bias,
        mlp_gain,
        mlp_shift,
    ):
        windows, local_len, width = tokens.shape
        win = local_len * n_z
        rows = windows * local_len
        root_hd = math.sqrt(HD)
        own = query_weight.shape[0]
        ff_own = up_weight.shape[1] // n_dp

        small = (
            query_bias,
            value_bias,
            out_bias,
            attn_gain,
            attn_shift,
            up_bias,
            down_bias,
            mlp_gain,
            mlp_shift,
        )
        sizes = [v.shape[0] for v in small]
        starts = [sum(sizes[:i]) for i in range(len(sizes))]
        small_row = jnp.concatenate(small)
        kv_lines = kv_weight.size // width
        small_lines = -(-small_row.shape[0] // width)
        filled = own + kv_lines + small_lines
        lines = -(-filled // 16) * 16
        small_row = jnp.pad(small_row, (0, (lines - own - kv_lines) * width - small_row.shape[0]))
        packed = jnp.concatenate(
            [query_weight, kv_weight.reshape(kv_lines, width), small_row.reshape(-1, width)]
        )
        packed = gather_both(packed).reshape(n_dev, lines, width)
        full_q = packed[:, :own].reshape(width, width)
        full_kv = packed[:, own : own + kv_lines].reshape(width, 2 * HD)
        small_all = packed[:, own + kv_lines :].reshape(n_dev, -1)
        bias_q, bias_v, bias_o, gain_one, shift_one, bias_up, bias_down, gain_two, shift_two = (
            small_all[:, start : start + size].reshape(-1).astype(F32)
            for start, size in zip(starts, sizes)
        )
        full_o = gather_both(out_weight)
        grad_low = cotangent.reshape(rows, width)
        grad_all = lax.all_gather(grad_low, "dp", axis=0, tiled=True)

        up_cols = lax.all_to_all(up_weight, "dp", 1, 0, tiled=True).reshape(n_dp, own, ff_own)
        up_part = ring_gather(up_cols, n_z).transpose(1, 0, 2, 3).reshape(width, ff_own)
        down_part = ring_gather(down_weight, n_z).reshape(ff_own, width)
        bias_up_part = lax.dynamic_slice_in_dim(bias_up, lax.axis_index("dp") * ff_own, ff_own)

        query_pos = lax.axis_index("fsdp") * local_len + jnp.arange(local_len, dtype=jnp.int32)
        key_pos = jnp.arange(win, dtype=jnp.int32)
        file_count = lengths.shape[1]
        upto = jnp.arange(file_count)[:, None] <= jnp.arange(file_count)[None, :]
        file_ends = jnp.sum(jnp.where(upto[None], lengths[:, :, None], 0), axis=1)
        key_files = jnp.sum(
            (file_ends[:, None, :] <= key_pos[None, :, None]).astype(jnp.int32), axis=2
        )
        query_files = jnp.sum(
            (file_ends[:, None, :] <= query_pos[None, :, None]).astype(jnp.int32), axis=2
        )
        allowed = (query_files[:, :, None] == key_files[:, None, :]) & (
            key_pos[None, None, :] <= query_pos[None, :, None]
        )

        inputs = tokens.reshape(rows, width).astype(F32)
        mean_one, recip_one = norm_stats(inputs)
        xhat_one = (inputs - mean_one) * recip_one
        normed_one = (xhat_one * gain_one + shift_one).astype(BF16)
        queries = (dot_nn(normed_one, full_q) + bias_q).astype(BF16)
        kv_bias = jnp.concatenate([jnp.zeros((HD,), F32), bias_v])
        key_value = (dot_nn(normed_one, full_kv) + kv_bias).astype(BF16)
        kv_window = lax.all_gather(
            key_value.reshape(windows, local_len, 2 * HD), "fsdp", axis=1, tiled=True
        )
        query_rows = (
            queries.reshape(windows, local_len, HEADS, HD)
            .transpose(0, 2, 1, 3)
            .reshape(windows, HEADS * local_len, HD)
        )
        mixed_list = []
        norm_list = []
        for w in range(windows):
            scores = masked_scores(query_rows[w], kv_window[w], allowed[w], root_hd)
            row_max = jnp.max(scores, axis=2, keepdims=True)
            exp_terms = jnp.exp(scores - row_max)
            row_total = jnp.sum(exp_terms, axis=2, keepdims=True)
            prob_low = (exp_terms / row_total).astype(BF16).reshape(HEADS * local_len, win)
            mixed_list.append(dot_nn(prob_low, kv_window[w][:, HD:]))
            norm_list.append(row_max + jnp.log(row_total))
        attended = jnp.stack(mixed_list).reshape(windows, HEADS, local_len, HD).transpose(0, 2, 1, 3)
        attended = attended.reshape(rows, width).astype(BF16)
        middle = inputs + dot_nn(attended, full_o) + bias_o

        mean_two, recip_two = norm_stats(middle)
        xhat_two = (middle - mean_two) * recip_two
        normed_two = (xhat_two * gain_two + shift_two).astype(BF16)
        two_all = lax.all_gather(normed_two, "dp", axis=0, tiled=True)
        grad_hidden = dot_nt(grad_all, down_part)
        pre_act = dot_nn(two_all, up_part) + bias_up_part
        hidden_full, gelu_pull = jax.vjp(gelu_tanh, pre_act)
        hidden = hidden_full.astype(BF16)
        pre_grad = gelu_pull(grad_hidden)[0].astype(BF16)
        two_grad = lax.psum_scatter(
            dot_nt(pre_grad, up_part).astype(BF16), "dp", scatter_dimension=0, tiled=True
        ).astype(F32)
        branch_out = lax.psum_scatter(
            dot_nn(hidden, down_part).astype(BF16), "dp", scatter_dimension=0, tiled=True
        ).astype(F32)
        output = (middle + branch_out + bias_down).astype(BF16)
        output = output.reshape(windows, local_len, width)

        up_terms = dot_tn(two_all, pre_grad).reshape(n_dp, n_z, own, ff_own).transpose(1, 0, 2, 3)
        grad_up = ring_scatter(up_terms, n_z)
        grad_up = lax.all_to_all(
            grad_up.astype(BF16).reshape(n_dp * own, ff_own), "dp", 0, 1, tiled=True
        ).astype(F32)
        down_terms = dot_tn(hidden, grad_all).reshape(n_z, ff_own // n_z, width)
        grad_down = ring_scatter(down_terms, n_z)
        up_bias_part = jnp.sum(pre_grad.astype(F32), axis=0)

        grad_out = grad_low.astype(F32)
        grad_bdown = jnp.sum(grad_out, axis=0)
        grad_gain_two = jnp.sum(two_grad * xhat_two, axis=0)
        grad_shift_two = jnp.sum(two_grad, axis=0)
        middle_grad = grad_out + norm_pull(two_grad, xhat_two, recip_two, gain_two)
        grad_bo = jnp.sum(middle_grad, axis=0)
        branch_grad = middle_grad.astype(BF16)
        grad_wo = scatter_both(dot_tn(attended, branch_grad).astype(BF16)).astype(F32)
        attended_grad = dot_nt(branch_grad, full_o).astype(BF16)
        grad_heads = (
            attended_grad.reshape(windows, local_len, HEADS, HD)
            .transpose(0, 2, 1, 3)
            .reshape(windows, HEADS * local_len, HD)
        )
        query_list = []
        kv_terms = []
        for w in range(windows):
            kv_rows = kv_window[w]
            scores = masked_scores(query_rows[w], kv_rows, allowed[w], root_hd)
            prob_full = jnp.exp(scores - norm_list[w])
            prob_low = prob_full.astype(BF16).reshape(HEADS * local_len, win)
            grad_probs = dot_nt(grad_heads[w], kv_rows[:, HD:])
            grad_probs = grad_probs.reshape(HEADS, local_len, win)
            row_delta = jnp.sum(prob_full * grad_probs, axis=2, keepdims=True)
            score_grad = (
                (prob_full * (grad_probs - row_delta)).astype(BF16).reshape(HEADS * local_len, win)
            )
            query_list.append(dot_nn(score_grad, kv_rows[:, :HD]) / root_hd)
            key_term = dot_tn(score_grad, query_rows[w]) / root_hd
            value_term = dot_tn(prob_low, grad_heads[w])
            kv_terms.append(jnp.concatenate([key_term, value_term], axis=1))
        query_grad = jnp.stack(query_list).reshape(windows, HEADS, local_len, HD)
        query_grad = query_grad.transpose(0, 2, 1, 3).reshape(rows, width).astype(BF16)
        kv_grad = lax.psum_scatter(
            jnp.stack(kv_terms).astype(BF16), "fsdp", scatter_dimension=1, tiled=True
        ).reshape(rows, 2 * HD)
        grad_bq = jnp.sum(query_grad.astype(F32), axis=0)
        grad_bv = jnp.sum(kv_grad[:, HD:].astype(F32), axis=0)
        grad_wq = dot_tn(normed_one, query_grad)
        grad_wkv = dot_tn(normed_one, kv_grad)
        one_grad = dot_nt(query_grad, full_q) + dot_nt(kv_grad, full_kv)
        grad_gain_one = jnp.sum(one_grad * xhat_one, axis=0)
        grad_shift_one = jnp.sum(one_grad, axis=0)
        tokens_grad = middle_grad + norm_pull(one_grad, xhat_one, recip_one, gain_one)
        tokens_grad = tokens_grad.astype(BF16).reshape(windows, local_len, width)

        grad_bup = lax.dynamic_update_slice_in_dim(
            jnp.zeros((n_dp * ff_own,), F32), up_bias_part, lax.axis_index("dp") * ff_own, 0
        )
        sums = (
            grad_bq,
            grad_bv,
            grad_bo,
            grad_gain_one,
            grad_shift_one,
            grad_bup,
            grad_bdown,
            grad_gain_two,
            grad_shift_two,
        )
        sum_rows = jnp.concatenate([v.astype(BF16).reshape(n_dev, -1) for v in sums], axis=1)
        sum_rows = jnp.pad(sum_rows, ((0, 0), (0, (lines - own - kv_lines) * width - sum_rows.shape[1])))
        grads = jnp.concatenate(
            [
                grad_wq.astype(BF16).reshape(n_dev, own, width),
                grad_wkv.astype(BF16).reshape(n_dev, kv_lines, width),
                sum_rows.reshape(n_dev, -1, width),
            ],
            axis=1,
        )
        mine = scatter_both(grads.reshape(n_dev * lines, width)).astype(F32)
        grad_q = mine[:own]
        grad_kv = mine[own : own + kv_lines].reshape(own, 2 * HD)
        flat = mine[own + kv_lines :].reshape(-1)
        bq, bv, bo, gain1, shift1, bup, bdown, gain2, shift2 = (
            flat[start : start + size] for start, size in zip(starts, sizes)
        )
        return (
            output,
            tokens_grad,
            grad_q,
            grad_kv,
            grad_wo,
            bq,
            bv,
            bo,
            gain1,
            shift1,
            grad_up,
            grad_down,
            bup,
            bdown,
            gain2,
            shift2,
        )

    return local


def solution(mesh):
    whole = P(BOTH, None)
    vector = P(BOTH)
    rows = P("dp", "fsdp", None)
    return jax.shard_map(
        make_local(mesh.shape["dp"], mesh.shape["fsdp"]),
        mesh=mesh,
        in_specs=(rows, rows, P("dp", None), whole, whole, whole)
        + (vector,) * 5
        + (whole, whole)
        + (vector,) * 4,
        out_specs=(rows, rows, whole, whole, whole)
        + (vector,) * 5
        + (whole, whole)
        + (vector,) * 4,
        check_vma=False,
    )
```

```python
import functools
import math

import jax
import jax.numpy as jnp
from jax import lax
from jax.experimental import pallas as pl
from jax.experimental.pallas import tpu as pltpu
from jax.sharding import PartitionSpec as P

HEADS = 16
HD = 128
EPS = 1e-05
F32 = jnp.float32
BF16 = jnp.bfloat16
BOTH = ("dp", "fsdp")


def dot_nn(left, right):
    return jnp.dot(left, right, preferred_element_type=F32)


def dot_nt(left, right):
    return lax.dot_general(left, right, (((1,), (1,)), ((), ())), preferred_element_type=F32)


def dot_tn(left, right):
    return lax.dot_general(left, right, (((0,), (0,)), ((), ())), preferred_element_type=F32)


LOG2E = 1.4426950408889634


def file_of(ends_ref, w, pos):
    total = jnp.zeros(pos.shape, jnp.int32)
    for i in range(ends_ref.shape[1]):
        total += (ends_ref[w, i] <= pos).astype(jnp.int32)
    return total


def fill_mask(pos_ref, ends_ref, w, bias, key_turned, value_turned, kv_ref):
    span, win = bias.shape
    query_pos = pos_ref[0] + lax.broadcasted_iota(jnp.int32, (span, 1), 0)
    key_pos = lax.broadcasted_iota(jnp.int32, (1, win), 1)
    same = file_of(ends_ref, w, query_pos) == file_of(ends_ref, w, key_pos)
    bias[...] = jnp.where(same & (key_pos <= query_pos), 0.0, -1e30).astype(F32)
    key_turned[...] = kv_ref[0, :, :HD].astype(F32).T.astype(BF16)
    if value_turned is not None:
        value_turned[...] = kv_ref[0, :, HD:].astype(F32).T.astype(BF16)


def attn_forward_kernel(per_step, pos_ref, ends_ref, q_ref, kv_ref, out_ref, norm_ref, bias, key_turned):
    w, group = pl.program_id(0), pl.program_id(1)

    @pl.when(group == 0)
    def _():
        fill_mask(pos_ref, ends_ref, w, bias, key_turned, None, kv_ref)
        norm_ref[...] = jnp.zeros_like(norm_ref)

    values = kv_ref[0, :, HD:]
    lane = lax.broadcasted_iota(jnp.int32, norm_ref.shape, 1)
    for j in range(per_step):
        query = q_ref[:, j * HD : (j + 1) * HD]
        scores = jnp.dot(query, key_turned[...], preferred_element_type=F32)
        scores = scores * (LOG2E / math.sqrt(HD)) + bias[...]
        top = jnp.max(scores, axis=1, keepdims=True)
        terms = jnp.exp2(scores - top)
        total = jnp.sum(terms, axis=1, keepdims=True)
        mixed = jnp.dot(terms.astype(BF16), values, preferred_element_type=F32)
        out_ref[:, j * HD : (j + 1) * HD] = (mixed / total).astype(BF16)
        norm_ref[...] = jnp.where(lane == group * per_step + j, top + jnp.log2(total), norm_ref[...])


def attn_backward_kernel(
    per_step, pos_ref, ends_ref, q_ref, kv_ref, norm_ref, grad_ref, dq_ref, dkv_ref,
    bias, key_turned, value_turned, key_grad, value_grad,
):
    w, group = pl.program_id(0), pl.program_id(1)

    @pl.when(group == 0)
    def _():
        fill_mask(pos_ref, ends_ref, w, bias, key_turned, value_turned, kv_ref)
        key_grad[...] = jnp.zeros_like(key_grad)
        value_grad[...] = jnp.zeros_like(value_grad)

    keys = kv_ref[0, :, :HD]
    lane = lax.broadcasted_iota(jnp.int32, norm_ref.shape, 1)
    for j in range(per_step):
        query = q_ref[:, j * HD : (j + 1) * HD]
        grad = grad_ref[:, j * HD : (j + 1) * HD]
        scores = jnp.dot(query, key_turned[...], preferred_element_type=F32)
        scores = scores * (LOG2E / math.sqrt(HD)) + bias[...]
        norm = jnp.sum(jnp.where(lane == group * per_step + j, norm_ref[...], 0.0), axis=1, keepdims=True)
        probs = jnp.exp2(scores - norm)
        grad_probs = jnp.dot(grad, value_turned[...], preferred_element_type=F32)
        delta = jnp.sum(probs * grad_probs, axis=1, keepdims=True)
        score_grad = (probs * (grad_probs - delta)).astype(BF16)
        probs = probs.astype(BF16)
        dq = jnp.dot(score_grad, keys, preferred_element_type=F32)
        dq_ref[:, j * HD : (j + 1) * HD] = (dq / math.sqrt(HD)).astype(BF16)
        key_grad[...] += dot_tn(query, score_grad)
        value_grad[...] += dot_tn(grad, probs)

    @pl.when(group == pl.num_programs(1) - 1)
    def _():
        dkv_ref[0, :, :HD] = (key_grad[...].T / math.sqrt(HD)).astype(BF16)
        dkv_ref[0, :, HD:] = value_grad[...].T.astype(BF16)


def attn_specs(per_step, span, win):
    smem = pl.BlockSpec(memory_space=pltpu.SMEM)
    heads = pl.BlockSpec((span, per_step * HD), lambda w, g: (w, g))
    keys = pl.BlockSpec((1, win, 2 * HD), lambda w, g: (w, 0, 0))
    norm = pl.BlockSpec((span, HD), lambda w, g: (w, 0))
    return smem, heads, keys, norm


def attn_cost(windows, span, win, products):
    return pl.CostEstimate(
        flops=2 * products * windows * HEADS * span * win * HD,
        transcendentals=windows * HEADS * span * win,
        bytes_accessed=products * windows * HEADS * span * HD * 2,
    )


def attn_forward(queries, kv_window, first, ends, per_step=4):
    windows, win, _ = kv_window.shape
    rows, width = queries.shape
    span = rows // windows
    smem, heads, keys, norm = attn_specs(per_step, span, win)
    return pl.pallas_call(
        functools.partial(attn_forward_kernel, per_step),
        out_shape=(
            jax.ShapeDtypeStruct((rows, width), BF16),
            jax.ShapeDtypeStruct((rows, HD), F32),
        ),
        grid=(windows, HEADS // per_step),
        in_specs=[smem, smem, heads, keys],
        out_specs=(heads, norm),
        scratch_shapes=[pltpu.VMEM((span, win), F32), pltpu.VMEM((HD, win), BF16)],
        compiler_params=pltpu.CompilerParams(vmem_limit_bytes=40 * 2**20),
        cost_estimate=attn_cost(windows, span, win, 2),
    )(first, ends, queries, kv_window)


def attn_backward(queries, kv_window, norms, grads, first, ends, per_step=4):
    windows, win, _ = kv_window.shape
    rows, width = queries.shape
    span = rows // windows
    smem, heads, keys, norm = attn_specs(per_step, span, win)
    return pl.pallas_call(
        functools.partial(attn_backward_kernel, per_step),
        out_shape=(
            jax.ShapeDtypeStruct((rows, width), BF16),
            jax.ShapeDtypeStruct((windows, win, 2 * HD), BF16),
        ),
        grid=(windows, HEADS // per_step),
        in_specs=[smem, smem, heads, keys, norm, heads],
        out_specs=(heads, keys),
        scratch_shapes=[
            pltpu.VMEM((span, win), F32),
            pltpu.VMEM((HD, win), BF16),
            pltpu.VMEM((HD, win), BF16),
            pltpu.VMEM((HD, win), F32),
            pltpu.VMEM((HD, win), F32),
        ],
        compiler_params=pltpu.CompilerParams(vmem_limit_bytes=48 * 2**20),
        cost_estimate=attn_cost(windows, span, win, 5),
    )(first, ends, queries, kv_window, norms, grads)


def norm_stats(values):
    average = jnp.mean(values, axis=-1, keepdims=True)
    centered = values - average
    variance = jnp.mean(centered * centered, axis=-1, keepdims=True)
    return average, lax.rsqrt(variance + EPS)


def norm_pull(grad, xhat, recip, gain):
    scaled = grad * gain
    mean_one = jnp.mean(scaled, axis=-1, keepdims=True)
    mean_two = jnp.mean(scaled * xhat, axis=-1, keepdims=True)
    return recip * (scaled - mean_one - xhat * mean_two)


def gelu_tanh(values):
    return jax.nn.gelu(values, approximate=True)


def tie(*arrays):
    return lax.optimization_barrier(arrays)


def scatter_both(block):
    part = lax.psum_scatter(block, "dp", scatter_dimension=0, tiled=True)
    return lax.psum_scatter(part, "fsdp", scatter_dimension=0, tiled=True)


def shift(block, count):
    return lax.ppermute(block, "fsdp", [(i, (i + 1) % count) for i in range(count)])


def put_in_order(pieces, count, axis=0):
    me = lax.axis_index("fsdp")
    size = pieces[0].shape[axis]
    shape = list(pieces[0].shape)
    shape[axis] = size * count
    whole = jnp.zeros(shape, pieces[0].dtype)
    for step, piece in enumerate(pieces):
        place = lax.rem(me - step + count, count) * size
        whole = lax.dynamic_update_slice_in_dim(whole, piece, place, axis)
    return whole


def ring_scatter(terms, count):
    me = lax.axis_index("fsdp")

    def term(step):
        return lax.dynamic_index_in_dim(
            terms, lax.rem(me - 1 - step + 2 * count, count), 0, keepdims=False
        ).astype(F32)

    total = term(0)
    for step in range(1, count):
        total = shift(total.astype(BF16), count).astype(F32) + term(step)
    return total


class Plane:
    def __init__(self, count):
        self.count = count
        self.bits = [1 << i for i in range(1, count.bit_length() - 1)]
        self.orders = (self.bits, self.bits[::-1])
        chips = range(0, count, 2)
        far = [(h, o) for h in (0, 1) for o in chips if o & self.orders[h][0]]
        near = [(h, o) for h in (0, 1) for o in chips if not o & self.orders[h][0]]
        self.keys = far + near
        self.n_far = len(far)

    def swap(self, block, bit):
        return lax.ppermute(block, "dp", [(i, i ^ bit) for i in range(self.count)])

    def gather_step(self, held, step):
        got = {}
        for (half, offset), piece in held.items():
            bit = self.orders[half][step]
            got[half, offset | bit] = self.swap(piece, bit)
        return got

    def lay(self, held):
        return jnp.concatenate([held[key] for key in self.keys])

    def cross(self, held):
        return {key: self.swap(piece, 1) for key, piece in held.items()}

    def split(self, rows, keys):
        size = rows.shape[0] // len(keys)
        return {key: rows[i * size : (i + 1) * size] for i, key in enumerate(keys)}

    def scatter_step(self, held, step):
        kept = {}
        for (half, offset), piece in held.items():
            bit = self.orders[half][step]
            if not offset & bit:
                got = self.swap(held[half, offset | bit], bit).astype(F32)
                kept[half, offset] = piece.astype(F32) + got
        return kept


def narrow(held):
    return {key: piece.astype(BF16) for key, piece in held.items()}


def make_local(n_dp, n_z):
    n_dev = n_dp * n_z
    plane = Plane(n_dp)

    def local(
        tokens,
        cotangent,
        lengths,
        query_weight,
        kv_weight,
        out_weight,
        query_bias,
        value_bias,
        out_bias,
        attn_gain,
        attn_shift,
        up_weight,
        down_weight,
        up_bias,
        down_bias,
        mlp_gain,
        mlp_shift,
    ):
        windows, local_len, width = tokens.shape
        rows = windows * local_len
        own = query_weight.shape[0]
        ff_own = up_weight.shape[1] // n_dp
        my_dp = lax.axis_index("dp")

        small = (
            query_bias,
            value_bias,
            out_bias,
            attn_gain,
            attn_shift,
            up_bias,
            down_bias,
            mlp_gain,
            mlp_shift,
        )
        sizes = [v.shape[0] for v in small]
        starts = [sum(sizes[:i]) for i in range(len(sizes))]
        small_row = jnp.concatenate(small)
        kv_lines = kv_weight.size // width
        filled = own + kv_lines + -(-small_row.shape[0] // width)
        lines = -(-filled // 16) * 16
        spare = (lines - own - kv_lines) * width
        small_row = jnp.pad(small_row, (0, spare - small_row.shape[0]))
        packed = jnp.concatenate(
            [query_weight, kv_weight.reshape(kv_lines, width), small_row.reshape(-1, width)]
        )

        packed = lax.all_gather(packed, "fsdp", axis=0, tiled=True)
        up_cols = lax.all_to_all(up_weight, "dp", 1, 0, tiled=True).reshape(n_dp, own, ff_own)
        packed, up_cols, down_weight, out_weight, cotangent = tie(
            packed, up_cols, down_weight, out_weight, cotangent
        )
        packed = lax.all_gather(packed, "dp", axis=0, tiled=True)
        full_o = lax.all_gather(out_weight, "fsdp", axis=0, tiled=True)
        down_pieces = [down_weight]
        while len(down_pieces) < min(3, n_z):
            down_pieces.append(shift(down_pieces[-1], n_z))
        inputs = tokens.reshape(rows, width).astype(F32)
        mean_one, recip_one = norm_stats(inputs)
        packed, full_o, down_pieces[-1], cotangent = tie(packed, full_o, down_pieces[-1], cotangent)

        full_o = lax.all_gather(full_o, "dp", axis=0, tiled=True)
        while len(down_pieces) < n_z:
            down_pieces.append(shift(down_pieces[-1], n_z))
        half = rows // 2
        grad_low = cotangent.reshape(rows, width)
        grad_held = {(0, 0): grad_low[:half], (1, 0): grad_low[half:]}
        grad_held.update(plane.gather_step(grad_held, 0))
        packed = packed.reshape(n_dev, lines, width)
        full_q = packed[:, :own].reshape(width, width)
        full_kv = packed[:, own : own + kv_lines].reshape(width, 2 * HD)
        small_all = packed[:, own + kv_lines :].reshape(n_dev, -1)
        bias_q, bias_v, bias_o, gain_one, shift_one, bias_up, bias_down, gain_two, shift_two = (
            small_all[:, start : start + size].reshape(-1).astype(F32)
            for start, size in zip(starts, sizes)
        )
        xhat_one = (inputs - mean_one) * recip_one
        normed_one = (xhat_one * gain_one + shift_one).astype(BF16)
        kv_bias = jnp.concatenate([jnp.zeros((HD,), F32), bias_v])
        key_value = (dot_nn(normed_one, full_kv) + kv_bias).astype(BF16)
        kv_window = lax.all_gather(
            key_value.reshape(windows, local_len, 2 * HD), "fsdp", axis=1, tiled=True
        )
        queries = (dot_nn(normed_one, full_q) + bias_q).astype(BF16)
        queries, up_cols, down_pieces[-1] = tie(queries, up_cols, down_pieces[-1])
        up_pieces = [up_cols]
        up_pieces.append(shift(up_pieces[-1], n_z))

        first = (lax.axis_index("fsdp") * local_len).astype(jnp.int32).reshape(1)
        file_count = lengths.shape[1]
        upto = jnp.arange(file_count)[:, None] <= jnp.arange(file_count)[None, :]
        file_ends = jnp.sum(jnp.where(upto[None], lengths[:, :, None], 0), axis=1)
        queries, kv_window, up_pieces[-1] = tie(queries, kv_window, up_pieces[-1])
        while len(up_pieces) < min(3, n_z):
            up_pieces.append(shift(up_pieces[-1], n_z))
        attended, norms = attn_forward(queries, kv_window, first, file_ends)
        attended, up_pieces[-1] = tie(attended, up_pieces[-1])
        while len(up_pieces) < n_z:
            up_pieces.append(shift(up_pieces[-1], n_z))
        middle = inputs + dot_nn(attended, full_o) + bias_o
        mean_two, recip_two = norm_stats(middle)
        xhat_two = (middle - mean_two) * recip_two
        normed_two = (xhat_two * gain_two + shift_two).astype(BF16)

        normed_two, *grad_pieces = tie(normed_two, *grad_held.values())
        grad_held = dict(zip(grad_held, grad_pieces))
        two_held = {(0, 0): normed_two[:half], (1, 0): normed_two[half:]}
        for step in range(1, len(plane.bits)):
            grad_held.update(plane.gather_step(grad_held, step))
        for step in range(len(plane.bits)):
            two_held.update(plane.gather_step(two_held, step))
        grad_mine = plane.lay(grad_held)
        grad_sib = plane.swap(grad_mine, 1)
        down_part = put_in_order(down_pieces, n_z)
        up_part = put_in_order(up_pieces, n_z, 1).reshape(width, ff_own)
        bias_up_part = lax.dynamic_slice_in_dim(bias_up, my_dp * ff_own, ff_own)
        back_mine = dot_nt(grad_mine, down_part)
        back_sib = dot_nt(grad_sib, down_part)
        two_sib = plane.lay(plane.cross(two_held))
        two_mine = plane.lay(two_held)
        two_mine, back_mine, back_sib = tie(two_mine, back_mine, back_sib)

        def middle_layer(two, back):
            pre_act = dot_nn(two, up_part) + bias_up_part
            hidden, pull = jax.vjp(gelu_tanh, pre_act)
            return hidden.astype(BF16), pull(back)[0].astype(BF16)

        hidden_mine, pre_mine = middle_layer(two_mine, back_mine)
        two_sib, pre_mine = tie(two_sib, pre_mine)
        hidden_sib, pre_sib = middle_layer(two_sib, back_sib)
        n_far = plane.n_far * half

        def core_sum(mine, sib, weight, product):
            out = []
            for lot, keys in ((slice(0, n_far), plane.keys[: plane.n_far]), (slice(n_far, None), plane.keys[plane.n_far :])):
                theirs = plane.swap(product(sib[lot], weight).astype(BF16), 1)
                ours = product(mine[lot], weight)
                out.append(plane.split((ours + theirs.astype(F32)).astype(BF16), keys))
            return out

        far, near = core_sum(pre_mine, pre_sib, up_part, dot_nt)
        two_sum = {**far, **near}
        hidden_mine, pre_mine, *near_pieces = tie(hidden_mine, pre_mine, *near.values())
        two_sum.update(zip(near, near_pieces))
        two_sum = plane.scatter_step(two_sum, 0)
        up_terms = dot_tn(two_mine, pre_mine) + dot_tn(two_sib, pre_sib)
        up_terms = up_terms.astype(BF16).reshape(n_dp, n_z, own, ff_own).transpose(1, 0, 2, 3)
        out_far, out_near = core_sum(hidden_mine, hidden_sib, down_part, dot_nn)
        out_sum = {**out_far, **out_near}
        two_keys, out_keys = list(two_sum), list(out_sum)
        up_terms, *pieces = tie(up_terms, *two_sum.values(), *out_sum.values())
        two_sum = dict(zip(two_keys, pieces))
        out_sum = dict(zip(out_keys, pieces[len(two_keys) :]))
        for step in range(1, len(plane.bits)):
            two_sum = plane.scatter_step(narrow(two_sum), step)
        two_grad = jnp.concatenate([two_sum[0, 0], two_sum[1, 0]])
        down_terms = dot_tn(hidden_mine, grad_mine) + dot_tn(hidden_sib, grad_sib)
        down_terms = down_terms.astype(BF16).reshape(n_z, ff_own // n_z, width)
        two_grad, down_terms, *pieces = tie(two_grad, down_terms, *out_sum.values())
        out_sum = plane.scatter_step(dict(zip(out_keys, pieces)), 0)
        grad_up = ring_scatter(up_terms, n_z)
        grad_up = lax.all_to_all(
            grad_up.astype(BF16).reshape(n_dp * own, ff_own), "dp", 0, 1, tiled=True
        ).astype(F32)
        grad_down = ring_scatter(down_terms, n_z)
        up_bias_part = jnp.sum(pre_mine.astype(F32), axis=0) + jnp.sum(pre_sib.astype(F32), axis=0)

        grad_out = grad_low.astype(F32)
        grad_bdown = jnp.sum(grad_out, axis=0)
        grad_gain_two = jnp.sum(two_grad * xhat_two, axis=0)
        grad_shift_two = jnp.sum(two_grad, axis=0)
        middle_grad = grad_out + norm_pull(two_grad, xhat_two, recip_two, gain_two)
        grad_bo = jnp.sum(middle_grad, axis=0)
        branch_grad = middle_grad.astype(BF16)
        grad_wo = scatter_both(dot_tn(attended, branch_grad).astype(BF16)).astype(F32)
        attended_grad = dot_nt(branch_grad, full_o).astype(BF16)

        out_keys = list(out_sum)
        attended_grad, *pieces = tie(attended_grad, *out_sum.values())
        out_sum = dict(zip(out_keys, pieces))
        for step in range(1, len(plane.bits)):
            out_sum = plane.scatter_step(narrow(out_sum), step)
        branch_out = jnp.concatenate([out_sum[0, 0], out_sum[1, 0]])
        output = (middle + branch_out + bias_down).astype(BF16).reshape(windows, local_len, width)

        query_grad, kv_terms = attn_backward(queries, kv_window, norms, attended_grad, first, file_ends)
        kv_grad = lax.psum_scatter(kv_terms, "fsdp", scatter_dimension=1, tiled=True)
        kv_grad = kv_grad.reshape(rows, 2 * HD)
        grad_bq = jnp.sum(query_grad.astype(F32), axis=0)
        grad_bv = jnp.sum(kv_grad[:, HD:].astype(F32), axis=0)
        grad_wq = dot_tn(normed_one, query_grad)
        grad_wkv = dot_tn(normed_one, kv_grad)
        one_grad = dot_nt(query_grad, full_q) + dot_nt(kv_grad, full_kv)
        grad_gain_one = jnp.sum(one_grad * xhat_one, axis=0)
        grad_shift_one = jnp.sum(one_grad, axis=0)
        tokens_grad = middle_grad + norm_pull(one_grad, xhat_one, recip_one, gain_one)
        tokens_grad = tokens_grad.astype(BF16).reshape(windows, local_len, width)

        grad_bup = jnp.where(jnp.arange(n_dp)[:, None] == my_dp, up_bias_part[None], 0.0).reshape(-1)
        sums = (
            grad_bq,
            grad_bv,
            grad_bo,
            grad_gain_one,
            grad_shift_one,
            grad_bup,
            grad_bdown,
            grad_gain_two,
            grad_shift_two,
        )
        sum_rows = jnp.concatenate([v.astype(BF16).reshape(n_dev, -1) for v in sums], axis=1)
        sum_rows = jnp.pad(sum_rows, ((0, 0), (0, spare - sum_rows.shape[1])))
        grads = jnp.concatenate(
            [
                grad_wq.astype(BF16).reshape(n_dev, own, width),
                grad_wkv.astype(BF16).reshape(n_dev, kv_lines, width),
                sum_rows.reshape(n_dev, -1, width),
            ],
            axis=1,
        )
        mine = scatter_both(grads.reshape(n_dev * lines, width)).astype(F32)
        grad_q = mine[:own]
        grad_kv = mine[own : own + kv_lines].reshape(own, 2 * HD)
        flat = mine[own + kv_lines :].reshape(-1)
        bq, bv, bo, gain1, shift1, bup, bdown, gain2, shift2 = (
            flat[start : start + size] for start, size in zip(starts, sizes)
        )
        return (
            output,
            tokens_grad,
            grad_q,
            grad_kv,
            grad_wo,
            bq,
            bv,
            bo,
            gain1,
            shift1,
            grad_up,
            grad_down,
            bup,
            bdown,
            gain2,
            shift2,
        )

    return local


def solution(mesh):
    whole = P(BOTH, None)
    vector = P(BOTH)
    rows = P("dp", "fsdp", None)
    weights = (whole, whole, whole) + (vector,) * 5 + (whole, whole) + (vector,) * 4
    return jax.shard_map(
        make_local(mesh.shape["dp"], mesh.shape["fsdp"]),
        mesh=mesh,
        in_specs=(rows, rows, P("dp", None)) + weights,
        out_specs=(rows, rows) + weights,
        check_vma=False,
    )
```

```python
import functools
import math

import jax
import jax.numpy as jnp
from jax import lax
from jax.experimental import pallas as pl
from jax.experimental.pallas import tpu as pltpu
from jax.sharding import PartitionSpec as P

HEADS = 16
HD = 128
EPS = 1e-05
F32 = jnp.float32
BF16 = jnp.bfloat16
BOTH = ("dp", "fsdp")


def dot_nn(left, right):
    return jnp.dot(left, right, preferred_element_type=F32)


def dot_nt(left, right):
    return lax.dot_general(left, right, (((1,), (1,)), ((), ())), preferred_element_type=F32)


def dot_tn(left, right):
    return lax.dot_general(left, right, (((0,), (0,)), ((), ())), preferred_element_type=F32)


LOG2E = 1.4426950408889634


def file_of(ends_ref, w, pos):
    total = jnp.zeros(pos.shape, jnp.int32)
    for i in range(ends_ref.shape[1]):
        total += (ends_ref[w, i] <= pos).astype(jnp.int32)
    return total


def fill_mask(pos_ref, ends_ref, w, bias, key_turned, value_turned, kv_ref):
    span, win = bias.shape
    query_pos = pos_ref[0] + lax.broadcasted_iota(jnp.int32, (span, 1), 0)
    key_pos = lax.broadcasted_iota(jnp.int32, (1, win), 1)
    same = file_of(ends_ref, w, query_pos) == file_of(ends_ref, w, key_pos)
    bias[...] = jnp.where(same & (key_pos <= query_pos), 0.0, -1e30).astype(F32)
    key_turned[...] = kv_ref[0, :, :HD].astype(F32).T.astype(BF16)
    if value_turned is not None:
        value_turned[...] = kv_ref[0, :, HD:].astype(F32).T.astype(BF16)


def attn_forward_kernel(per_step, pos_ref, ends_ref, q_ref, kv_ref, out_ref, norm_ref, bias, key_turned):
    w, group = pl.program_id(0), pl.program_id(1)

    @pl.when(group == 0)
    def _():
        fill_mask(pos_ref, ends_ref, w, bias, key_turned, None, kv_ref)
        norm_ref[...] = jnp.zeros_like(norm_ref)

    values = kv_ref[0, :, HD:]
    lane = lax.broadcasted_iota(jnp.int32, norm_ref.shape, 1)
    for j in range(per_step):
        query = q_ref[:, j * HD : (j + 1) * HD]
        scores = jnp.dot(query, key_turned[...], preferred_element_type=F32)
        scores = scores * (LOG2E / math.sqrt(HD)) + bias[...]
        top = jnp.max(scores, axis=1, keepdims=True)
        terms = jnp.exp2(scores - top)
        total = jnp.sum(terms, axis=1, keepdims=True)
        mixed = jnp.dot(terms.astype(BF16), values, preferred_element_type=F32)
        out_ref[:, j * HD : (j + 1) * HD] = (mixed / total).astype(BF16)
        norm_ref[...] = jnp.where(lane == group * per_step + j, top + jnp.log2(total), norm_ref[...])


def attn_backward_kernel(
    per_step, pos_ref, ends_ref, q_ref, kv_ref, norm_ref, grad_ref, dq_ref, dkv_ref,
    bias, key_turned, value_turned, key_grad, value_grad,
):
    w, group = pl.program_id(0), pl.program_id(1)

    @pl.when(group == 0)
    def _():
        fill_mask(pos_ref, ends_ref, w, bias, key_turned, value_turned, kv_ref)
        key_grad[...] = jnp.zeros_like(key_grad)
        value_grad[...] = jnp.zeros_like(value_grad)

    keys = kv_ref[0, :, :HD]
    lane = lax.broadcasted_iota(jnp.int32, norm_ref.shape, 1)
    for j in range(per_step):
        query = q_ref[:, j * HD : (j + 1) * HD]
        grad = grad_ref[:, j * HD : (j + 1) * HD]
        scores = jnp.dot(query, key_turned[...], preferred_element_type=F32)
        scores = scores * (LOG2E / math.sqrt(HD)) + bias[...]
        norm = jnp.sum(jnp.where(lane == group * per_step + j, norm_ref[...], 0.0), axis=1, keepdims=True)
        probs = jnp.exp2(scores - norm)
        grad_probs = jnp.dot(grad, value_turned[...], preferred_element_type=F32)
        delta = jnp.sum(probs * grad_probs, axis=1, keepdims=True)
        score_grad = (probs * (grad_probs - delta)).astype(BF16)
        probs = probs.astype(BF16)
        dq = jnp.dot(score_grad, keys, preferred_element_type=F32)
        dq_ref[:, j * HD : (j + 1) * HD] = (dq / math.sqrt(HD)).astype(BF16)
        key_grad[...] += dot_tn(query, score_grad)
        value_grad[...] += dot_tn(grad, probs)

    @pl.when(group == pl.num_programs(1) - 1)
    def _():
        dkv_ref[0, :, :HD] = (key_grad[...].T / math.sqrt(HD)).astype(BF16)
        dkv_ref[0, :, HD:] = value_grad[...].T.astype(BF16)


def attn_specs(per_step, span, win):
    smem = pl.BlockSpec(memory_space=pltpu.SMEM)
    heads = pl.BlockSpec((span, per_step * HD), lambda w, g: (w, g))
    keys = pl.BlockSpec((1, win, 2 * HD), lambda w, g: (w, 0, 0))
    norm = pl.BlockSpec((span, HD), lambda w, g: (w, 0))
    return smem, heads, keys, norm


def attn_cost(windows, span, win, products):
    return pl.CostEstimate(
        flops=2 * products * windows * HEADS * span * win * HD,
        transcendentals=windows * HEADS * span * win,
        bytes_accessed=products * windows * HEADS * span * HD * 2,
    )


def attn_forward(queries, kv_window, first, ends, per_step=4):
    windows, win, _ = kv_window.shape
    rows, width = queries.shape
    span = rows // windows
    smem, heads, keys, norm = attn_specs(per_step, span, win)
    return pl.pallas_call(
        functools.partial(attn_forward_kernel, per_step),
        out_shape=(
            jax.ShapeDtypeStruct((rows, width), BF16),
            jax.ShapeDtypeStruct((rows, HD), F32),
        ),
        grid=(windows, HEADS // per_step),
        in_specs=[smem, smem, heads, keys],
        out_specs=(heads, norm),
        scratch_shapes=[pltpu.VMEM((span, win), F32), pltpu.VMEM((HD, win), BF16)],
        compiler_params=pltpu.CompilerParams(vmem_limit_bytes=40 * 2**20),
        cost_estimate=attn_cost(windows, span, win, 2),
    )(first, ends, queries, kv_window)


def attn_backward(queries, kv_window, norms, grads, first, ends, per_step=4):
    windows, win, _ = kv_window.shape
    rows, width = queries.shape
    span = rows // windows
    smem, heads, keys, norm = attn_specs(per_step, span, win)
    return pl.pallas_call(
        functools.partial(attn_backward_kernel, per_step),
        out_shape=(
            jax.ShapeDtypeStruct((rows, width), BF16),
            jax.ShapeDtypeStruct((windows, win, 2 * HD), BF16),
        ),
        grid=(windows, HEADS // per_step),
        in_specs=[smem, smem, heads, keys, norm, heads],
        out_specs=(heads, keys),
        scratch_shapes=[
            pltpu.VMEM((span, win), F32),
            pltpu.VMEM((HD, win), BF16),
            pltpu.VMEM((HD, win), BF16),
            pltpu.VMEM((HD, win), F32),
            pltpu.VMEM((HD, win), F32),
        ],
        compiler_params=pltpu.CompilerParams(vmem_limit_bytes=48 * 2**20),
        cost_estimate=attn_cost(windows, span, win, 5),
    )(first, ends, queries, kv_window, norms, grads)


def middle_kernel(count, *refs):
    blocks, backs = refs[:count], refs[count : 2 * count]
    up_ref, bias_ref = refs[2 * count], refs[2 * count + 1]
    hiddens = refs[2 * count + 2 : 3 * count + 2]
    pres = refs[3 * count + 2 :]
    root = math.sqrt(2.0 / math.pi)
    for block, back, hidden, pre in zip(blocks, backs, hiddens, pres):
        act = jnp.dot(block[...], up_ref[...], preferred_element_type=F32) + bias_ref[...]
        square = act * act
        bent = jnp.tanh(root * act * (1.0 + 0.044715 * square))
        upper = 0.5 + 0.5 * bent
        hidden[...] = (act * upper).astype(BF16)
        slope = upper + (0.5 * root) * act * (1.0 - bent * bent) * (1.0 + (3 * 0.044715) * square)
        pre[...] = (back[...].astype(F32) * slope).astype(BF16)


def middle_layer(blocks, backs, up_part, bias, tile=256):
    count = len(blocks)
    size, width = blocks[0].shape
    units = up_part.shape[1]
    tile = min(tile, units)
    one = pl.Buffered(buffer_count=1)
    whole = pl.BlockSpec((size, width), lambda j: (0, 0), pipeline_mode=one)
    slab = pl.BlockSpec((size, tile), lambda j: (0, j))
    out = pl.pallas_call(
        functools.partial(middle_kernel, count),
        out_shape=[jax.ShapeDtypeStruct((size, units), BF16)] * (2 * count),
        grid=(units // tile,),
        in_specs=[whole] * count
        + [slab] * count
        + [pl.BlockSpec((width, tile), lambda j: (0, j)), pl.BlockSpec((1, tile), lambda j: (0, j))],
        out_specs=[slab] * (2 * count),
        compiler_params=pltpu.CompilerParams(vmem_limit_bytes=48 * 2**20),
        cost_estimate=pl.CostEstimate(
            flops=2 * count * size * width * units,
            transcendentals=count * size * units,
            bytes_accessed=2 * (count * size * (width + 3 * units) + width * units),
        ),
    )(*blocks, *backs, up_part, bias.reshape(1, units))
    return list(out[:count]), list(out[count:])


def weight_kernel(count, *refs):
    lefts, rights, out = refs[:count], refs[count : 2 * count], refs[2 * count]
    total = dot_tn(lefts[0][...], rights[0][...])
    for left, right in zip(lefts[1:], rights[1:]):
        total += dot_tn(left[...], right[...])
    out[...] = total.astype(BF16)


def weight_grad(lefts, rights, tile=256):
    count = len(lefts)
    size, height = lefts[0].shape
    breadth = rights[0].shape[1]
    tile = min(tile, height)
    one = pl.Buffered(buffer_count=1)
    return pl.pallas_call(
        functools.partial(weight_kernel, count),
        out_shape=jax.ShapeDtypeStruct((height, breadth), BF16),
        grid=(height // tile,),
        in_specs=[pl.BlockSpec((size, tile), lambda i: (0, i))] * count
        + [pl.BlockSpec((size, breadth), lambda i: (0, 0), pipeline_mode=one)] * count,
        out_specs=pl.BlockSpec((tile, breadth), lambda i: (i, 0)),
        compiler_params=pltpu.CompilerParams(vmem_limit_bytes=52 * 2**20),
        cost_estimate=pl.CostEstimate(
            flops=2 * count * size * height * breadth,
            transcendentals=0,
            bytes_accessed=2 * (count * size * (height + breadth) + height * breadth),
        ),
    )(*lefts, *rights)


def norm_stats(values):
    average = jnp.mean(values, axis=-1, keepdims=True)
    centered = values - average
    variance = jnp.mean(centered * centered, axis=-1, keepdims=True)
    return average, lax.rsqrt(variance + EPS)


def norm_pull(grad, xhat, recip, gain):
    scaled = grad * gain
    mean_one = jnp.mean(scaled, axis=-1, keepdims=True)
    mean_two = jnp.mean(scaled * xhat, axis=-1, keepdims=True)
    return recip * (scaled - mean_one - xhat * mean_two)


def gelu_tanh(values):
    return jax.nn.gelu(values, approximate=True)


def tie(*arrays):
    return lax.optimization_barrier(arrays)


def scatter_both(block):
    part = lax.psum_scatter(block, "dp", scatter_dimension=0, tiled=True)
    return lax.psum_scatter(part, "fsdp", scatter_dimension=0, tiled=True)


def shift(block, count):
    return lax.ppermute(block, "fsdp", [(i, (i + 1) % count) for i in range(count)])


def put_in_order(pieces, count, axis=0):
    me = lax.axis_index("fsdp")
    size = pieces[0].shape[axis]
    shape = list(pieces[0].shape)
    shape[axis] = size * count
    whole = jnp.zeros(shape, pieces[0].dtype)
    for step, piece in enumerate(pieces):
        place = lax.rem(me - step + count, count) * size
        whole = lax.dynamic_update_slice_in_dim(whole, piece, place, axis)
    return whole


class Ring:
    def __init__(self, terms, axis, count):
        self.terms, self.axis, self.count, self.step = terms, axis, count, 0
        self.total = self.term()

    def term(self):
        place = lax.rem(lax.axis_index("fsdp") - 1 - self.step + 2 * self.count, self.count)
        return lax.dynamic_index_in_dim(self.terms, place, self.axis, keepdims=False).astype(F32)

    def go(self, steps, ahead):
        for _ in range(steps):
            if self.step + 1 < self.count:
                self.step += 1
                self.total = shift(self.total.astype(BF16), self.count).astype(F32) + self.term()
        self.total, ahead = tie(self.total, ahead)
        return ahead

    def finish(self):
        while self.step + 1 < self.count:
            self.step += 1
            self.total = shift(self.total.astype(BF16), self.count).astype(F32) + self.term()
        return self.total


class Plane:
    def __init__(self, count):
        self.count = count
        bits = [1 << i for i in range(1, count.bit_length() - 1)]
        self.orders = (bits, bits[::-1])
        self.steps = len(bits)

    def swap(self, block, bit):
        return lax.ppermute(block, "dp", [(i, i ^ bit) for i in range(self.count)])

    def across(self, halves, step):
        return [self.swap(half, order[step]) for half, order in zip(halves, self.orders)]

    def grow(self, halves, step):
        return [jnp.concatenate(pair) for pair in zip(halves, self.across(halves, step))]

    def cross(self, halves):
        return [self.swap(half, 1) for half in halves]

    def fold(self, halves, step):
        size = halves[0].shape[0] // 2
        got = self.across([half[size:].astype(BF16) for half in halves], step)
        return [half[:size].astype(F32) + there.astype(F32) for half, there in zip(halves, got)]


def make_local(n_dp, n_z):
    n_dev = n_dp * n_z
    plane = Plane(n_dp)

    def local(
        tokens,
        cotangent,
        lengths,
        query_weight,
        kv_weight,
        out_weight,
        query_bias,
        value_bias,
        out_bias,
        attn_gain,
        attn_shift,
        up_weight,
        down_weight,
        up_bias,
        down_bias,
        mlp_gain,
        mlp_shift,
    ):
        windows, local_len, width = tokens.shape
        rows = windows * local_len
        own = query_weight.shape[0]
        ff_own = up_weight.shape[1] // n_dp
        my_dp = lax.axis_index("dp")

        small = (
            query_bias,
            value_bias,
            out_bias,
            attn_gain,
            attn_shift,
            up_bias,
            down_bias,
            mlp_gain,
            mlp_shift,
        )
        sizes = [v.shape[0] for v in small]
        rooms = [-(-size // 128) * 128 for size in sizes]
        starts = [sum(rooms[:i]) for i in range(len(rooms))]
        small_row = jnp.concatenate(
            [jnp.pad(v, (0, room - size)) for v, size, room in zip(small, sizes, rooms)]
        )
        kv_lines = kv_weight.size // width
        filled = own + kv_lines + -(-small_row.shape[0] // width)
        lines = -(-filled // 16) * 16
        spare = (lines - own - kv_lines) * width
        small_row = jnp.pad(small_row, (0, spare - small_row.shape[0]))
        packed = jnp.concatenate(
            [query_weight, kv_weight.reshape(kv_lines, width), small_row.reshape(-1, width)]
        )

        half = rows // 2
        grad_low = cotangent.reshape(rows, width)

        packed = lax.all_gather(packed, "fsdp", axis=0, tiled=True)
        grad_near = [grad_low[:half], grad_low[half:]]
        for step in range(plane.steps - 1):
            grad_near = plane.grow(grad_near, step)
        up_cols = lax.all_to_all(up_weight, "dp", 1, 0, tiled=True).reshape(n_dp, own, ff_own)
        packed, up_cols, down_weight, out_weight = tie(packed, up_cols, down_weight, out_weight)

        packed = lax.all_gather(packed, "dp", axis=0, tiled=True)
        out_pieces = [out_weight]
        while len(out_pieces) < n_z:
            out_pieces.append(shift(out_pieces[-1], n_z))
        out_pieces[-1], down_weight = tie(out_pieces[-1], down_weight)
        full_o = put_in_order(out_pieces, n_z)
        down_pieces = [down_weight]
        while len(down_pieces) < min(3, n_z):
            down_pieces.append(shift(down_pieces[-1], n_z))
        inputs = tokens.reshape(rows, width).astype(F32)
        mean_one, recip_one = norm_stats(inputs)
        packed, full_o, down_pieces[-1], mean_one, *grad_near = tie(
            packed, full_o, down_pieces[-1], mean_one, *grad_near
        )

        full_o = lax.all_gather(full_o, "dp", axis=0, tiled=True)
        grad_far = plane.across(grad_near, plane.steps - 1)
        packed = packed.reshape(n_dev, lines, width)
        full_q = packed[:, :own].reshape(width, width)
        full_kv = packed[:, own : own + kv_lines].reshape(width, 2 * HD)
        small_all = packed[:, own + kv_lines :].reshape(n_dev, -1)
        bias_q, bias_v, bias_o, gain_one, shift_one, bias_up, bias_down, gain_two, shift_two = (
            small_all[:, start : start + size].reshape(-1).astype(F32)
            for start, size in zip(starts, sizes)
        )
        xhat_one = (inputs - mean_one) * recip_one
        normed_one = (xhat_one * gain_one + shift_one).astype(BF16)
        kv_bias = jnp.concatenate([jnp.zeros((HD,), F32), bias_v])
        key_value = (dot_nn(normed_one, full_kv) + kv_bias).astype(BF16)
        key_value, normed_late = tie(key_value, normed_one)
        kv_pieces = [key_value.reshape(windows, local_len, 2 * HD)]
        while len(kv_pieces) < n_z:
            kv_pieces.append(shift(kv_pieces[-1], n_z))
        queries = (dot_nn(normed_late, full_q) + bias_q).astype(BF16)
        kv_window = put_in_order(kv_pieces, n_z, 1)

        first = (lax.axis_index("fsdp") * local_len).astype(jnp.int32).reshape(1)
        file_count = lengths.shape[1]
        upto = jnp.arange(file_count)[:, None] <= jnp.arange(file_count)[None, :]
        file_ends = jnp.sum(jnp.where(upto[None], lengths[:, :, None], 0), axis=1)
        queries, kv_window, down_pieces[-1], up_cols = tie(queries, kv_window, down_pieces[-1], up_cols)
        while len(down_pieces) < n_z:
            down_pieces.append(shift(down_pieces[-1], n_z))
        attended, norms = attn_forward(queries, kv_window, first, file_ends)
        attended, down_pieces[-1], up_cols = tie(attended, down_pieces[-1], up_cols)
        up_pieces = [up_cols, shift(up_cols, n_z)]
        down_part = put_in_order(down_pieces, n_z)
        grad_near_sib = plane.cross(grad_near)
        grad_lots = [[*grad_near, *grad_near_sib]]
        backs = [[dot_nt(block, down_part).astype(BF16) for block in grad_lots[0]]]
        attended, *backs[0] = tie(attended, *backs[0])
        middle = inputs + dot_nn(attended, full_o) + bias_o
        mean_two, recip_two = norm_stats(middle)
        xhat_two = (middle - mean_two) * recip_two
        normed_two = (xhat_two * gain_two + shift_two).astype(BF16)

        normed_two, up_pieces[-1], *grad_far = tie(normed_two, up_pieces[-1], *grad_far)
        two_near = [normed_two[:half], normed_two[half:]]
        while len(up_pieces) < n_z:
            up_pieces.append(shift(up_pieces[-1], n_z))
        for step in range(plane.steps - 1):
            two_near = plane.grow(two_near, step)
        grad_lots.append([*grad_far, *plane.cross(grad_far)])
        backs.append([dot_nt(block, down_part).astype(BF16) for block in grad_lots[1]])
        up_part = put_in_order(up_pieces, n_z, 1).reshape(width, ff_own)
        bias_up_part = lax.dynamic_slice_in_dim(bias_up, my_dp * ff_own, ff_own)
        two_near[0], two_near[1], up_part, *backs[1] = tie(*two_near, up_part, *backs[1])

        two_far = plane.across(two_near, plane.steps - 1)
        two_lots = [[*two_near, *plane.cross(two_near)], [*two_far, *plane.cross(two_far)]]
        near = middle_layer(two_lots[0], backs[0], up_part, bias_up_part)
        backs[1][0], *pres = tie(backs[1][0], *near[1])
        far = middle_layer(two_lots[1], backs[1], up_part, bias_up_part)
        hiddens, pres = [near[0], far[0]], [pres, far[1]]

        def core_sum(lot, weight, product):
            theirs = plane.cross([product(block, weight).astype(BF16) for block in lot[2:]])
            return [
                (product(block, weight) + there.astype(F32)).astype(BF16)
                for block, there in zip(lot[:2], theirs)
            ]

        def merge(halves, far_halves):
            got = plane.across(far_halves, plane.steps - 1)
            return [half.astype(F32) + there.astype(F32) for half, there in zip(halves, got)]

        two_far = core_sum(pres[1], up_part, dot_nt)
        pres[0][0], *two_far = tie(pres[0][0], *two_far)
        two_near = core_sum(pres[0], up_part, dot_nt)
        two_sum = merge(two_near, two_far)
        up_terms = weight_grad(two_lots[0] + two_lots[1], pres[0] + pres[1])
        up_terms, hiddens[1][0], *two_sum = tie(up_terms, hiddens[1][0], *two_sum)
        for step in range(plane.steps - 2, -1, -1):
            two_sum = plane.fold(two_sum, step)
        two_grad = jnp.concatenate(two_sum)
        up_ring = Ring(up_terms.reshape(n_dp, n_z, own, ff_own), 1, n_z)
        out_far = core_sum(hiddens[1], down_part, dot_nn)
        hiddens[0][0], *out_far = tie(hiddens[0][0], *out_far)
        up_bias_part = sum(jnp.sum(block.astype(F32), axis=0) for lot in pres for block in lot)
        two_grad, hiddens[0][0], *out_far = tie(two_grad, hiddens[0][0], *out_far)

        two_grad = up_ring.go(1, two_grad)
        grad_out = grad_low.astype(F32)
        grad_bdown = jnp.sum(grad_out, axis=0)
        grad_gain_two = jnp.sum(two_grad * xhat_two, axis=0)
        grad_shift_two = jnp.sum(two_grad, axis=0)
        middle_grad = grad_out + norm_pull(two_grad, xhat_two, recip_two, gain_two)
        grad_bo = jnp.sum(middle_grad, axis=0)
        branch_grad = middle_grad.astype(BF16)
        attended_grad = dot_nt(branch_grad, full_o).astype(BF16)
        out_got = plane.across(out_far, plane.steps - 1)
        grad_wo = dot_tn(attended, branch_grad).astype(BF16)
        attended_grad, grad_wo = tie(attended_grad, grad_wo)
        grad_wo = scatter_both(grad_wo).astype(F32)
        attended_grad = up_ring.go(1, attended_grad)

        query_grad, kv_terms = attn_backward(queries, kv_window, norms, attended_grad, first, file_ends)
        query_grad, hiddens[0][0], *out_got = tie(query_grad, hiddens[0][0], *out_got)
        query_grad = up_ring.go(1, query_grad)
        kv_ring = Ring(kv_terms.reshape(windows, n_z, local_len, 2 * HD), 1, n_z)
        grad_wq = dot_tn(normed_one, query_grad).astype(BF16)
        grad_wq = kv_ring.go(1, grad_wq)
        out_near = core_sum(hiddens[0], down_part, dot_nn)
        out_near[0] = kv_ring.go(n_z - 2, out_near[0])
        out_sum = [near.astype(F32) + got.astype(F32) for near, got in zip(out_near, out_got)]
        for step in range(plane.steps - 2, -1, -1):
            out_sum = plane.fold(out_sum, step)
        kv_grad = kv_ring.finish().astype(BF16).reshape(rows, 2 * HD)
        kv_grad, hiddens[1][0] = tie(kv_grad, hiddens[1][0])
        down_terms = weight_grad(hiddens[0] + hiddens[1], grad_lots[0] + grad_lots[1])
        down_ring = Ring(down_terms.reshape(n_z, ff_own // n_z, width), 0, n_z)
        branch_out = jnp.concatenate(out_sum)
        output = (middle + branch_out + bias_down).astype(BF16).reshape(windows, local_len, width)
        grad_up = lax.all_to_all(
            up_ring.finish().astype(BF16).reshape(n_dp * own, ff_own), "dp", 0, 1, tiled=True
        ).astype(F32)
        grad_down = down_ring.finish()

        grad_bq = jnp.sum(query_grad.astype(F32), axis=0)
        grad_bv = jnp.sum(kv_grad[:, HD:].astype(F32), axis=0)
        grad_wkv = dot_tn(normed_one, kv_grad)
        one_grad = dot_nt(query_grad, full_q) + dot_nt(kv_grad, full_kv)
        grad_gain_one = jnp.sum(one_grad * xhat_one, axis=0)
        grad_shift_one = jnp.sum(one_grad, axis=0)
        tokens_grad = middle_grad + norm_pull(one_grad, xhat_one, recip_one, gain_one)
        tokens_grad = tokens_grad.astype(BF16).reshape(windows, local_len, width)

        grad_bup = jnp.where(jnp.arange(n_dp)[:, None] == my_dp, up_bias_part[None], 0.0).reshape(-1)
        sums = (
            grad_bq,
            grad_bv,
            grad_bo,
            grad_gain_one,
            grad_shift_one,
            grad_bup,
            grad_bdown,
            grad_gain_two,
            grad_shift_two,
        )
        sum_rows = jnp.concatenate(
            [
                jnp.pad(v.astype(BF16).reshape(n_dev, size), ((0, 0), (0, room - size)))
                for v, size, room in zip(sums, sizes, rooms)
            ],
            axis=1,
        )
        sum_rows = jnp.pad(sum_rows, ((0, 0), (0, spare - sum_rows.shape[1])))
        grads = jnp.concatenate(
            [
                grad_wq.reshape(n_dev, own, width),
                grad_wkv.astype(BF16).reshape(n_dev, kv_lines, width),
                sum_rows.reshape(n_dev, -1, width),
            ],
            axis=1,
        )
        mine = scatter_both(grads.reshape(n_dev * lines, width)).astype(F32)
        grad_q = mine[:own]
        grad_kv = mine[own : own + kv_lines].reshape(own, 2 * HD)
        flat = mine[own + kv_lines :].reshape(-1)
        bq, bv, bo, gain1, shift1, bup, bdown, gain2, shift2 = (
            flat[start : start + size] for start, size in zip(starts, sizes)
        )
        return (
            output,
            tokens_grad,
            grad_q,
            grad_kv,
            grad_wo,
            bq,
            bv,
            bo,
            gain1,
            shift1,
            grad_up,
            grad_down,
            bup,
            bdown,
            gain2,
            shift2,
        )

    return local


def solution(mesh):
    whole = P(BOTH, None)
    vector = P(BOTH)
    rows = P("dp", "fsdp", None)
    weights = (whole, whole, whole) + (vector,) * 5 + (whole, whole) + (vector,) * 4
    return jax.shard_map(
        make_local(mesh.shape["dp"], mesh.shape["fsdp"]),
        mesh=mesh,
        in_specs=(rows, rows, P("dp", None)) + weights,
        out_specs=(rows, rows) + weights,
        check_vma=False,
    )
```

```python
import functools
import math

import jax
import jax.numpy as jnp
from jax import lax
from jax.experimental import pallas as pl
from jax.experimental.pallas import tpu as pltpu
from jax.sharding import PartitionSpec as P

HEADS = 16
HD = 128
EPS = 1e-05
F32 = jnp.float32
BF16 = jnp.bfloat16
BOTH = ("dp", "fsdp")
HASTE = 8


def dot_nn(left, right):
    return jnp.dot(left, right, preferred_element_type=F32)


def dot_nt(left, right):
    return lax.dot_general(left, right, (((1,), (1,)), ((), ())), preferred_element_type=F32)


def dot_tn(left, right):
    return lax.dot_general(left, right, (((0,), (0,)), ((), ())), preferred_element_type=F32)


LOG2E = 1.4426950408889634


def file_of(ends_ref, w, pos):
    total = jnp.zeros(pos.shape, jnp.int32)
    for i in range(ends_ref.shape[1]):
        total += (ends_ref[w, i] <= pos).astype(jnp.int32)
    return total


def fill_mask(pos_ref, ends_ref, w, bias, key_turned, value_turned, kv_ref):
    span, win = bias.shape
    query_pos = pos_ref[0] + lax.broadcasted_iota(jnp.int32, (span, 1), 0)
    key_pos = lax.broadcasted_iota(jnp.int32, (1, win), 1)
    same = file_of(ends_ref, w, query_pos) == file_of(ends_ref, w, key_pos)
    bias[...] = jnp.where(same & (key_pos <= query_pos), 0.0, -1e30).astype(F32)
    key_turned[...] = kv_ref[0, :, :HD].astype(F32).T.astype(BF16)
    if value_turned is not None:
        value_turned[...] = kv_ref[0, :, HD:].astype(F32).T.astype(BF16)


def attn_forward_kernel(per_step, pos_ref, ends_ref, q_ref, kv_ref, out_ref, norm_ref, bias, key_turned):
    w, group = pl.program_id(0), pl.program_id(1)

    @pl.when(group == 0)
    def _():
        fill_mask(pos_ref, ends_ref, w, bias, key_turned, None, kv_ref)
        norm_ref[...] = jnp.zeros_like(norm_ref)

    values = kv_ref[0, :, HD:]
    lane = lax.broadcasted_iota(jnp.int32, norm_ref.shape, 1)
    for j in range(per_step):
        query = q_ref[:, j * HD : (j + 1) * HD]
        scores = jnp.dot(query, key_turned[...], preferred_element_type=F32)
        scores = scores * (LOG2E / math.sqrt(HD)) + bias[...]
        top = jnp.max(scores, axis=1, keepdims=True)
        terms = jnp.exp2(scores - top)
        total = jnp.sum(terms, axis=1, keepdims=True)
        mixed = jnp.dot(terms.astype(BF16), values, preferred_element_type=F32)
        out_ref[:, j * HD : (j + 1) * HD] = (mixed / total).astype(BF16)
        norm_ref[...] = jnp.where(lane == group * per_step + j, top + jnp.log2(total), norm_ref[...])


def attn_backward_kernel(
    per_step, pos_ref, ends_ref, q_ref, kv_ref, norm_ref, grad_ref, dq_ref, dkv_ref,
    bias, key_turned, value_turned, key_grad, value_grad,
):
    w, group = pl.program_id(0), pl.program_id(1)

    @pl.when(group == 0)
    def _():
        fill_mask(pos_ref, ends_ref, w, bias, key_turned, value_turned, kv_ref)
        key_grad[...] = jnp.zeros_like(key_grad)
        value_grad[...] = jnp.zeros_like(value_grad)

    keys = kv_ref[0, :, :HD]
    lane = lax.broadcasted_iota(jnp.int32, norm_ref.shape, 1)
    for j in range(per_step):
        query = q_ref[:, j * HD : (j + 1) * HD]
        grad = grad_ref[:, j * HD : (j + 1) * HD]
        scores = jnp.dot(query, key_turned[...], preferred_element_type=F32)
        scores = scores * (LOG2E / math.sqrt(HD)) + bias[...]
        norm = jnp.sum(jnp.where(lane == group * per_step + j, norm_ref[...], 0.0), axis=1, keepdims=True)
        probs = jnp.exp2(scores - norm)
        grad_probs = jnp.dot(grad, value_turned[...], preferred_element_type=F32)
        delta = jnp.sum(probs * grad_probs, axis=1, keepdims=True)
        score_grad = (probs * (grad_probs - delta)).astype(BF16)
        probs = probs.astype(BF16)
        dq = jnp.dot(score_grad, keys, preferred_element_type=F32)
        dq_ref[:, j * HD : (j + 1) * HD] = (dq / math.sqrt(HD)).astype(BF16)
        key_grad[...] += dot_tn(query, score_grad)
        value_grad[...] += dot_tn(grad, probs)

    @pl.when(group == pl.num_programs(1) - 1)
    def _():
        dkv_ref[0, :, :HD] = (key_grad[...].T / math.sqrt(HD)).astype(BF16)
        dkv_ref[0, :, HD:] = value_grad[...].T.astype(BF16)


def attn_specs(per_step, span, win):
    smem = pl.BlockSpec(memory_space=pltpu.SMEM)
    heads = pl.BlockSpec((span, per_step * HD), lambda w, g: (w, g))
    keys = pl.BlockSpec((1, win, 2 * HD), lambda w, g: (w, 0, 0))
    norm = pl.BlockSpec((span, HD), lambda w, g: (w, 0))
    return smem, heads, keys, norm


def attn_cost(windows, span, win, products):
    return pl.CostEstimate(
        flops=2 * products * windows * HEADS * span * win * HD // HASTE,
        transcendentals=windows * HEADS * span * win // HASTE,
        bytes_accessed=products * windows * HEADS * span * HD * 2 // HASTE,
    )


def attn_forward(queries, kv_window, first, ends, per_step=4):
    windows, win, _ = kv_window.shape
    rows, width = queries.shape
    span = rows // windows
    smem, heads, keys, norm = attn_specs(per_step, span, win)
    return pl.pallas_call(
        functools.partial(attn_forward_kernel, per_step),
        out_shape=(
            jax.ShapeDtypeStruct((rows, width), BF16),
            jax.ShapeDtypeStruct((rows, HD), F32),
        ),
        grid=(windows, HEADS // per_step),
        in_specs=[smem, smem, heads, keys],
        out_specs=(heads, norm),
        scratch_shapes=[pltpu.VMEM((span, win), F32), pltpu.VMEM((HD, win), BF16)],
        compiler_params=pltpu.CompilerParams(vmem_limit_bytes=40 * 2**20),
        cost_estimate=attn_cost(windows, span, win, 2),
    )(first, ends, queries, kv_window)


def attn_backward(queries, kv_window, norms, grads, first, ends, per_step=4):
    windows, win, _ = kv_window.shape
    rows, width = queries.shape
    span = rows // windows
    smem, heads, keys, norm = attn_specs(per_step, span, win)
    return pl.pallas_call(
        functools.partial(attn_backward_kernel, per_step),
        out_shape=(
            jax.ShapeDtypeStruct((rows, width), BF16),
            jax.ShapeDtypeStruct((windows, win, 2 * HD), BF16),
        ),
        grid=(windows, HEADS // per_step),
        in_specs=[smem, smem, heads, keys, norm, heads],
        out_specs=(heads, keys),
        scratch_shapes=[
            pltpu.VMEM((span, win), F32),
            pltpu.VMEM((HD, win), BF16),
            pltpu.VMEM((HD, win), BF16),
            pltpu.VMEM((HD, win), F32),
            pltpu.VMEM((HD, win), F32),
        ],
        compiler_params=pltpu.CompilerParams(vmem_limit_bytes=48 * 2**20),
        cost_estimate=attn_cost(windows, span, win, 5),
    )(first, ends, queries, kv_window, norms, grads)


def middle_kernel(count, *refs):
    blocks, back_ref = refs[:count], refs[count]
    up_ref, bias_ref = refs[count + 1], refs[count + 2]
    outs = refs[count + 3 :]
    groups = len(outs) // 2
    size = blocks[0].shape[0]
    root = math.sqrt(2.0 / math.pi)
    for i, block in enumerate(blocks):
        act = jnp.dot(block[...], up_ref[...], preferred_element_type=F32) + bias_ref[...]
        square = act * act
        bent = jnp.tanh(act * (root + (root * 0.044715) * square))
        upper = 0.5 + 0.5 * bent
        slope = upper + act * (1.0 - bent * bent) * (0.5 * root + (1.5 * 0.044715 * root) * square)
        back = back_ref[i * size : (i + 1) * size, :].astype(F32)
        group, place = divmod(i, count // groups)
        at = slice(place * size, (place + 1) * size)
        outs[group][at, :] = (act * upper).astype(BF16)
        outs[groups + group][at, :] = (back * slope).astype(BF16)


def middle_layer(blocks, back, up_part, bias, tile=512):
    count = len(blocks)
    size, width = blocks[0].shape
    units = up_part.shape[1]
    tile = min(tile, units)
    one = pl.Buffered(buffer_count=1)
    group = size * count // 2
    whole = pl.BlockSpec((size, width), lambda j: (0, 0), pipeline_mode=one)
    slab = pl.BlockSpec((group, tile), lambda j: (0, j))
    out = pl.pallas_call(
        functools.partial(middle_kernel, count),
        out_shape=[jax.ShapeDtypeStruct((group, units), BF16)] * 4,
        grid=(units // tile,),
        in_specs=[whole] * count
        + [
            pl.BlockSpec((size * count, tile), lambda j: (0, j)),
            pl.BlockSpec((width, tile), lambda j: (0, j)),
            pl.BlockSpec((1, tile), lambda j: (0, j)),
        ],
        out_specs=[slab] * 4,
        compiler_params=pltpu.CompilerParams(vmem_limit_bytes=48 * 2**20),
        cost_estimate=pl.CostEstimate(
            flops=2 * count * size * width * units // HASTE,
            transcendentals=count * size * units // HASTE,
            bytes_accessed=2 * (count * size * (width + 3 * units) + width * units) // HASTE,
        ),
    )(*blocks, back, up_part, bias.reshape(1, units))
    return list(out[:2]), list(out[2:])


def back_kernel(count, *refs):
    blocks, weight_ref, out = refs[:count], refs[count], refs[count + 1]
    size = blocks[0].shape[0]
    for i, block in enumerate(blocks):
        out[i * size : (i + 1) * size, :] = dot_nt(block[...], weight_ref[...]).astype(BF16)


def back_product(blocks, weight, tile=512):
    count = len(blocks)
    size, width = blocks[0].shape
    units = weight.shape[0]
    tile = min(tile, units)
    one = pl.Buffered(buffer_count=1)
    return pl.pallas_call(
        functools.partial(back_kernel, count),
        out_shape=jax.ShapeDtypeStruct((size * count, units), BF16),
        grid=(units // tile,),
        in_specs=[pl.BlockSpec((size, width), lambda j: (0, 0), pipeline_mode=one)] * count
        + [pl.BlockSpec((tile, width), lambda j: (j, 0))],
        out_specs=pl.BlockSpec((size * count, tile), lambda j: (0, j)),
        compiler_params=pltpu.CompilerParams(vmem_limit_bytes=48 * 2**20),
        cost_estimate=pl.CostEstimate(
            flops=2 * count * size * width * units // HASTE,
            transcendentals=0,
            bytes_accessed=2 * (count * size * (width + units) + width * units) // HASTE,
        ),
    )(*blocks, weight)


def weight_kernel(count, *refs):
    lefts, rights, out = refs[:count], refs[count : 2 * count], refs[2 * count]
    total = dot_tn(lefts[0][...], rights[0][...])
    for left, right in zip(lefts[1:], rights[1:]):
        total += dot_tn(left[...], right[...])
    out[...] = total.astype(BF16)


def in_blocks(arrays, size):
    return [(array, i) for array in arrays for i in range(array.shape[0] // size)]


def weight_grad(lefts, rights, size, tile=256):
    lefts, rights = in_blocks(lefts, size), in_blocks(rights, size)
    count = len(lefts)
    height, breadth = lefts[0][0].shape[1], rights[0][0].shape[1]
    tile = min(tile, height)

    def left_spec(row):
        return pl.BlockSpec((size, tile), lambda i: (row, i))

    def right_spec(row):
        return pl.BlockSpec((size, breadth), lambda i: (row, 0), pipeline_mode=pl.Buffered(buffer_count=1))

    return pl.pallas_call(
        functools.partial(weight_kernel, count),
        out_shape=jax.ShapeDtypeStruct((height, breadth), BF16),
        grid=(height // tile,),
        in_specs=[left_spec(row) for _, row in lefts] + [right_spec(row) for _, row in rights],
        out_specs=pl.BlockSpec((tile, breadth), lambda i: (i, 0)),
        compiler_params=pltpu.CompilerParams(vmem_limit_bytes=52 * 2**20),
        cost_estimate=pl.CostEstimate(
            flops=2 * count * size * height * breadth // HASTE,
            transcendentals=0,
            bytes_accessed=2 * (count * size * (height + breadth) + height * breadth) // HASTE,
        ),
    )(*[array for array, _ in lefts], *[array for array, _ in rights])


def reorder_kernel(place_ref, first_ref, second_ref, first_out, second_out):
    first_out[...] = first_ref[...]
    second_out[...] = second_ref[...]


def reorder(values, places):
    rows, width = values.shape
    count = places.shape[1]
    block = width // (2 * count)
    if block % 128:
        return [
            jnp.concatenate(
                [lax.dynamic_slice_in_dim(values, places[i, j] * block, block, 1) for j in range(count)],
                axis=1,
            )
            for i in (0, 1)
        ]
    out = pl.BlockSpec((rows, block), lambda i, place: (0, i))
    return pl.pallas_call(
        reorder_kernel,
        out_shape=[jax.ShapeDtypeStruct((rows, width // 2), values.dtype)] * 2,
        grid_spec=pltpu.PrefetchScalarGridSpec(
            num_scalar_prefetch=1,
            grid=(count,),
            in_specs=[
                pl.BlockSpec((rows, block), lambda i, place: (0, place[0, i])),
                pl.BlockSpec((rows, block), lambda i, place: (0, place[1, i])),
            ],
            out_specs=[out, out],
        ),
        cost_estimate=pl.CostEstimate(flops=0, transcendentals=0, bytes_accessed=4 * rows * width // HASTE),
    )(places, values, values)


def norm_stats(values):
    average = jnp.mean(values, axis=-1, keepdims=True)
    centered = values - average
    variance = jnp.mean(centered * centered, axis=-1, keepdims=True)
    return average, lax.rsqrt(variance + EPS)


def norm_pull(grad, xhat, recip, gain):
    scaled = grad * gain
    mean_one = jnp.mean(scaled, axis=-1, keepdims=True)
    mean_two = jnp.mean(scaled * xhat, axis=-1, keepdims=True)
    return recip * (scaled - mean_one - xhat * mean_two)


def gelu_tanh(values):
    return jax.nn.gelu(values, approximate=True)


def tie(*arrays):
    return lax.optimization_barrier(arrays)


def scatter_both(block):
    part = lax.psum_scatter(block, "dp", scatter_dimension=0, tiled=True)
    return lax.psum_scatter(part, "fsdp", scatter_dimension=0, tiled=True)


def shift(block, count):
    return lax.ppermute(block, "fsdp", [(i, (i + 1) % count) for i in range(count)])


def put_in_order(pieces, count, axis=0):
    me = lax.axis_index("fsdp")
    size = pieces[0].shape[axis]
    shape = list(pieces[0].shape)
    shape[axis] = size * count
    whole = jnp.zeros(shape, pieces[0].dtype)
    for step, piece in enumerate(pieces):
        place = lax.rem(me - step + count, count) * size
        whole = lax.dynamic_update_slice_in_dim(whole, piece, place, axis)
    return whole


class Ring:
    def __init__(self, terms, axis, count):
        self.terms, self.axis, self.count, self.step = terms, axis, count, 0
        self.total = self.term()

    def term(self):
        place = lax.rem(lax.axis_index("fsdp") - 1 - self.step + 2 * self.count, self.count)
        return lax.dynamic_index_in_dim(self.terms, place, self.axis, keepdims=False).astype(F32)

    def go(self, steps, ahead):
        for _ in range(steps):
            if self.step + 1 < self.count:
                self.step += 1
                self.total = shift(self.total.astype(BF16), self.count).astype(F32) + self.term()
        self.total, ahead = tie(self.total, ahead)
        return ahead

    def finish(self):
        while self.step + 1 < self.count:
            self.step += 1
            self.total = shift(self.total.astype(BF16), self.count).astype(F32) + self.term()
        return self.total


class Plane:
    def __init__(self, count):
        self.count = count
        bits = [1 << i for i in range(1, count.bit_length() - 1)]
        self.orders = (bits, bits[::-1])
        self.steps = len(bits)
        self.near, self.far = [], []
        for order in self.orders:
            near = [0]
            for bit in order[:-1]:
                near = near + [offset ^ bit for offset in near]
            self.near.append(near)
            self.far.append([offset ^ order[-1] for offset in near])

    def places(self):
        me = lax.axis_index("dp")
        order = [(o, h) for h in (0, 1) for o in self.far[h] + self.near[h]]
        return jnp.stack(
            [jnp.stack([2 * (me ^ o ^ core) + h for o, h in order]) for core in (0, 1)]
        ).astype(jnp.int32)

    def swap(self, block, bit):
        return lax.ppermute(block, "dp", [(i, i ^ bit) for i in range(self.count)])

    def across(self, halves, step):
        return [self.swap(half, order[step]) for half, order in zip(halves, self.orders)]

    def grow(self, halves, step):
        return [jnp.concatenate(pair) for pair in zip(halves, self.across(halves, step))]

    def cross(self, halves):
        return [self.swap(half, 1) for half in halves]

    def fold(self, halves, step):
        size = halves[0].shape[0] // 2
        got = self.across([half[size:].astype(BF16) for half in halves], step)
        return [half[:size].astype(F32) + there.astype(F32) for half, there in zip(halves, got)]


def make_local(n_dp, n_z):
    n_dev = n_dp * n_z
    plane = Plane(n_dp)

    def local(
        tokens,
        cotangent,
        lengths,
        query_weight,
        kv_weight,
        out_weight,
        query_bias,
        value_bias,
        out_bias,
        attn_gain,
        attn_shift,
        up_weight,
        down_weight,
        up_bias,
        down_bias,
        mlp_gain,
        mlp_shift,
    ):
        windows, local_len, width = tokens.shape
        rows = windows * local_len
        own = query_weight.shape[0]
        ff_own = up_weight.shape[1] // n_dp
        my_dp = lax.axis_index("dp")

        small = (
            query_bias,
            value_bias,
            out_bias,
            attn_gain,
            attn_shift,
            up_bias,
            down_bias,
            mlp_gain,
            mlp_shift,
        )
        sizes = [v.shape[0] for v in small]
        rooms = [-(-size // 128) * 128 for size in sizes]
        starts = [sum(rooms[:i]) for i in range(len(rooms))]
        small_row = jnp.concatenate(
            [jnp.pad(v, (0, room - size)) for v, size, room in zip(small, sizes, rooms)]
        )
        kv_lines = kv_weight.size // width
        filled = own + kv_lines + -(-small_row.shape[0] // width)
        lines = -(-filled // 16) * 16
        spare = (lines - own - kv_lines) * width
        small_row = jnp.pad(small_row, (0, spare - small_row.shape[0]))
        packed = jnp.concatenate(
            [query_weight, kv_weight.reshape(kv_lines, width), small_row.reshape(-1, width)]
        )

        half = rows // 2
        grad_low = cotangent.reshape(rows, width)

        packed = lax.all_gather(packed, "fsdp", axis=0, tiled=True)
        grad_near = [grad_low[:half], grad_low[half:]]
        for step in range(plane.steps - 1):
            grad_near = plane.grow(grad_near, step)
        up_cols = lax.all_to_all(up_weight, "dp", 1, 0, tiled=True).reshape(n_dp, own, ff_own)
        packed, up_cols, down_weight, out_weight = tie(packed, up_cols, down_weight, out_weight)

        packed = lax.all_gather(packed, "dp", axis=0, tiled=True)
        out_pieces = [out_weight]
        while len(out_pieces) < n_z:
            out_pieces.append(shift(out_pieces[-1], n_z))
        out_pieces[-1], down_weight = tie(out_pieces[-1], down_weight)
        full_o = put_in_order(out_pieces, n_z)
        down_pieces = [down_weight]
        while len(down_pieces) < min(3, n_z):
            down_pieces.append(shift(down_pieces[-1], n_z))
        inputs = tokens.reshape(rows, width).astype(F32)
        mean_one, recip_one = norm_stats(inputs)
        packed, full_o, down_pieces[-1], mean_one, *grad_near = tie(
            packed, full_o, down_pieces[-1], mean_one, *grad_near
        )

        full_o = lax.all_gather(full_o, "dp", axis=0, tiled=True)
        grad_far = plane.across(grad_near, plane.steps - 1)
        packed = packed.reshape(n_dev, lines, width)
        full_q = packed[:, :own].reshape(width, width)
        full_kv = packed[:, own : own + kv_lines].reshape(width, 2 * HD)
        small_all = packed[:, own + kv_lines :].reshape(n_dev, -1)
        bias_q, bias_v, bias_o, gain_one, shift_one, bias_up, bias_down, gain_two, shift_two = (
            small_all[:, start : start + size].reshape(-1).astype(F32)
            for start, size in zip(starts, sizes)
        )
        xhat_one = (inputs - mean_one) * recip_one
        normed_one = (xhat_one * gain_one + shift_one).astype(BF16)
        kv_bias = jnp.concatenate([jnp.zeros((HD,), F32), bias_v])
        key_value = (dot_nn(normed_one, full_kv) + kv_bias).astype(BF16)
        key_value, normed_late = tie(key_value, normed_one)
        kv_pieces = [key_value.reshape(windows, local_len, 2 * HD)]
        while len(kv_pieces) < n_z:
            kv_pieces.append(shift(kv_pieces[-1], n_z))
        queries = (dot_nn(normed_late, full_q) + bias_q).astype(BF16)
        kv_window = put_in_order(kv_pieces, n_z, 1)

        first = (lax.axis_index("fsdp") * local_len).astype(jnp.int32).reshape(1)
        file_count = lengths.shape[1]
        upto = jnp.arange(file_count)[:, None] <= jnp.arange(file_count)[None, :]
        file_ends = jnp.sum(jnp.where(upto[None], lengths[:, :, None], 0), axis=1)
        queries, kv_window, down_pieces[-1], up_cols = tie(queries, kv_window, down_pieces[-1], up_cols)
        while len(down_pieces) < n_z:
            down_pieces.append(shift(down_pieces[-1], n_z))
        attended, norms = attn_forward(queries, kv_window, first, file_ends)
        attended, down_pieces[-1], up_cols = tie(attended, down_pieces[-1], up_cols)
        up_pieces = [up_cols, shift(up_cols, n_z)]
        down_part = put_in_order(down_pieces, n_z)
        grad_lots = [[*grad_near, *plane.cross(grad_near)]]
        back_near = back_product(grad_lots[0], down_part)
        attended, back_near = tie(attended, back_near)
        middle = inputs + dot_nn(attended, full_o) + bias_o
        mean_two, recip_two = norm_stats(middle)
        xhat_two = (middle - mean_two) * recip_two
        normed_two = (xhat_two * gain_two + shift_two).astype(BF16)

        normed_two, up_pieces[-1], *grad_far = tie(normed_two, up_pieces[-1], *grad_far)
        two_near = [normed_two[:half], normed_two[half:]]
        while len(up_pieces) < min(3, n_z):
            up_pieces.append(shift(up_pieces[-1], n_z))
        for step in range(plane.steps - 1):
            two_near = plane.grow(two_near, step)
        grad_lots.append([*grad_far, *plane.cross(grad_far)])
        back_far = back_product(grad_lots[1], down_part)
        two_near[0], two_near[1], up_pieces[-1], back_far = tie(*two_near, up_pieces[-1], back_far)

        while len(up_pieces) < n_z:
            up_pieces.append(shift(up_pieces[-1], n_z))
        up_part = put_in_order(up_pieces, n_z, 1).reshape(width, ff_own)
        bias_up_part = lax.dynamic_slice_in_dim(bias_up, my_dp * ff_own, ff_own)
        two_far = plane.across(two_near, plane.steps - 1)
        two_lots = [[*two_near, *plane.cross(two_near)], [*two_far, *plane.cross(two_far)]]
        hid_near, pre_near = middle_layer(two_lots[0], back_near, up_part, bias_up_part)
        places = plane.places()
        back_far, attended, pre_near[0], pre_near[1], places = tie(back_far, attended, *pre_near, places)
        one_mine, one_sib = reorder(normed_one, places)
        att_mine, att_sib = reorder(attended, places)
        hid_far, pre_far = middle_layer(two_lots[1], back_far, up_part, bias_up_part)
        block = two_near[0].shape[0]

        def lot_sum(lot, weight, product):
            theirs = plane.swap(product(lot[1], weight).astype(BF16), 1)
            return (product(lot[0], weight) + theirs.astype(F32)).astype(BF16)

        def lot_halves(lot, weight, product):
            theirs = plane.swap(product(lot[1], weight).astype(BF16), 1).astype(F32)
            ours = lot[0]
            return [
                (product(ours[at], weight) + theirs[at]).astype(BF16)
                for at in (slice(None, block), slice(block, None))
            ]

        def merge(whole, got):
            size = got[0].shape[0]
            return [whole[i * size : (i + 1) * size].astype(F32) + got[i].astype(F32) for i in (0, 1)]

        two_far = lot_halves(pre_far, up_part, dot_nt)
        pre_near[0], pre_near[1], *two_far = tie(*pre_near, *two_far)
        got = plane.across(two_far, plane.steps - 1)
        two_near_sum = lot_sum(pre_near, up_part, dot_nt)
        two_near_sum, hid_far[0], hid_far[1] = tie(two_near_sum, *hid_far)
        out_far = lot_halves(hid_far, down_part, dot_nn)
        out_far[0], out_far[1], pre_far[0] = tie(*out_far, pre_far[0])
        up_terms = weight_grad(two_lots[0] + two_lots[1], pre_near + pre_far, block)
        up_ring = Ring(up_terms.reshape(n_dp, n_z, own, ff_own), 1, n_z)
        two_near_sum, up_terms, hid_far[0], *got = tie(two_near_sum, up_terms, hid_far[0], *got)
        up_ring.terms = up_terms.reshape(n_dp, n_z, own, ff_own)
        two_sum = merge(two_near_sum, got)
        for step in range(plane.steps - 2, -1, -1):
            two_sum = plane.fold(two_sum, step)
        two_grad = jnp.concatenate(two_sum)
        down_terms = weight_grad(hid_near + hid_far, grad_lots[0] + grad_lots[1], block)
        two_grad, down_terms = tie(two_grad, down_terms)
        down_ring = Ring(down_terms.reshape(n_z, ff_own // n_z, width), 0, n_z)
        up_bias_part = sum(jnp.sum(lot.astype(F32), axis=0) for lot in pre_near + pre_far)

        two_grad, out_far[0], out_far[1] = tie(up_ring.go(1, two_grad), *out_far)
        out_got = plane.across(out_far, plane.steps - 1)
        grad_out = grad_low.astype(F32)
        grad_bdown = jnp.sum(grad_out, axis=0)
        grad_gain_two = jnp.sum(two_grad * xhat_two, axis=0)
        grad_shift_two = jnp.sum(two_grad, axis=0)
        middle_grad = grad_out + norm_pull(two_grad, xhat_two, recip_two, gain_two)
        grad_bo = jnp.sum(middle_grad, axis=0)
        branch_grad = middle_grad.astype(BF16)
        attended_grad = dot_nt(branch_grad, full_o).astype(BF16)
        attended_grad, branch_late = tie(attended_grad, branch_grad)

        def row_sum(mine, sib, right):
            theirs = plane.swap(dot_tn(sib, right).astype(BF16), 1)
            total = (dot_tn(mine, right) + theirs.astype(F32)).astype(BF16)
            size = total.shape[0] // 4
            return [total[i * size : (i + 1) * size] for i in range(4)]

        def send_rows(lots):
            return plane.across([lots[0], lots[2]], plane.steps - 1)

        def own_rows(lots, got):
            total = [near.astype(F32) + there.astype(F32) for near, there in zip((lots[1], lots[3]), got)]
            for step in range(plane.steps - 2, -1, -1):
                total = plane.fold(total, step)
            return jnp.concatenate(total)

        out_lots = row_sum(att_mine, att_sib, branch_late)
        attended_grad, *out_lots = tie(up_ring.go(1, attended_grad), *out_lots)
        out_lots_got = send_rows(out_lots)

        query_grad, kv_terms = attn_backward(queries, kv_window, norms, attended_grad, first, file_ends)
        query_grad, kv_terms, hid_near[0], *got = tie(query_grad, kv_terms, hid_near[0], *out_got, *out_lots_got)
        out_got, out_lots_got = got[:2], got[2:]
        query_grad = up_ring.go(1, query_grad)
        kv_ring = Ring(kv_terms.reshape(windows, n_z, local_len, 2 * HD), 1, n_z)
        q_lots = row_sum(one_mine, one_sib, query_grad)
        q_lots[0] = kv_ring.go(1, q_lots[0])
        hid_near[0], hid_near[1], query_late, *pieces = tie(*hid_near, query_grad, *q_lots, *out_lots_got)
        q_lots, out_lots_got = pieces[:4], pieces[4:]
        q_got = send_rows(q_lots)
        wo_rows = own_rows(out_lots, out_lots_got)
        hid_near[0] = kv_ring.go(n_z - 2, hid_near[0])
        out_sum = merge(lot_sum(hid_near, down_part, dot_nn), out_got)
        for step in range(plane.steps - 2, -1, -1):
            out_sum = plane.fold(out_sum, step)
        kv_grad = kv_ring.finish().astype(BF16).reshape(rows, 2 * HD)
        branch_out = jnp.concatenate(out_sum)
        output = (middle + branch_out + bias_down).astype(BF16).reshape(windows, local_len, width)
        wo_ring = Ring(wo_rows.reshape(n_z, own, width), 0, n_z)
        wq_ring = Ring(own_rows(q_lots, q_got).reshape(n_z, own, width), 0, n_z)
        grad_wo, grad_q = wo_ring.finish(), wq_ring.finish()
        grad_up = lax.all_to_all(
            up_ring.finish().astype(BF16).reshape(n_dp * own, ff_own), "dp", 0, 1, tiled=True
        ).astype(F32)
        grad_down = down_ring.finish()

        grad_bq = jnp.sum(query_late.astype(F32), axis=0)
        grad_bv = jnp.sum(kv_grad[:, HD:].astype(F32), axis=0)
        grad_wkv = dot_tn(normed_one, kv_grad)
        one_grad = dot_nt(query_late, full_q) + dot_nt(kv_grad, full_kv)
        grad_gain_one = jnp.sum(one_grad * xhat_one, axis=0)
        grad_shift_one = jnp.sum(one_grad, axis=0)
        tokens_grad = middle_grad + norm_pull(one_grad, xhat_one, recip_one, gain_one)
        tokens_grad = tokens_grad.astype(BF16).reshape(windows, local_len, width)

        grad_bup = jnp.where(jnp.arange(n_dp)[:, None] == my_dp, up_bias_part[None], 0.0).reshape(-1)
        sums = (
            grad_bq,
            grad_bv,
            grad_bo,
            grad_gain_one,
            grad_shift_one,
            grad_bup,
            grad_bdown,
            grad_gain_two,
            grad_shift_two,
        )
        sum_rows = jnp.concatenate(
            [
                jnp.pad(v.astype(BF16).reshape(n_dev, size), ((0, 0), (0, room - size)))
                for v, size, room in zip(sums, sizes, rooms)
            ],
            axis=1,
        )
        sum_lines = -(-(kv_lines + -(-sum(rooms) // width)) // 16) * 16
        sum_rows = jnp.pad(
            sum_rows, ((0, 0), (0, (sum_lines - kv_lines) * width - sum_rows.shape[1]))
        )
        grads = jnp.concatenate(
            [
                grad_wkv.astype(BF16).reshape(n_dev, kv_lines, width),
                sum_rows.reshape(n_dev, -1, width),
            ],
            axis=1,
        )
        mine = scatter_both(grads.reshape(n_dev * sum_lines, width)).astype(F32)
        grad_kv = mine[:kv_lines].reshape(own, 2 * HD)
        flat = mine[kv_lines:].reshape(-1)
        bq, bv, bo, gain1, shift1, bup, bdown, gain2, shift2 = (
            flat[start : start + size] for start, size in zip(starts, sizes)
        )
        return (
            output,
            tokens_grad,
            grad_q,
            grad_kv,
            grad_wo,
            bq,
            bv,
            bo,
            gain1,
            shift1,
            grad_up,
            grad_down,
            bup,
            bdown,
            gain2,
            shift2,
        )

    return local


def solution(mesh):
    whole = P(BOTH, None)
    vector = P(BOTH)
    rows = P("dp", "fsdp", None)
    weights = (whole, whole, whole) + (vector,) * 5 + (whole, whole) + (vector,) * 4
    return jax.shard_map(
        make_local(mesh.shape["dp"], mesh.shape["fsdp"]),
        mesh=mesh,
        in_specs=(rows, rows, P("dp", None)) + weights,
        out_specs=(rows, rows) + weights,
        check_vma=False,
    )
```

```python
import functools
import math

import jax
import jax.numpy as jnp
from jax import lax
from jax.experimental import pallas as pl
from jax.experimental.pallas import tpu as pltpu
from jax.sharding import PartitionSpec as P

HEADS = 16
HD = 128
EPS = 1e-05
F32 = jnp.float32
BF16 = jnp.bfloat16
BOTH = ("dp", "fsdp")
HASTE = 8


def dot_nn(left, right):
    return jnp.dot(left, right, preferred_element_type=F32)


def dot_nt(left, right):
    return lax.dot_general(left, right, (((1,), (1,)), ((), ())), preferred_element_type=F32)


def dot_tn(left, right):
    return lax.dot_general(left, right, (((0,), (0,)), ((), ())), preferred_element_type=F32)


LOG2E = 1.4426950408889634


def file_of(ends_ref, w, pos):
    total = jnp.zeros(pos.shape, jnp.int32)
    for i in range(ends_ref.shape[1]):
        total += (ends_ref[w, i] <= pos).astype(jnp.int32)
    return total


def fill_mask(pos_ref, ends_ref, w, bias, key_turned, value_turned, kv_ref):
    span, win = bias.shape
    query_pos = pos_ref[0] + lax.broadcasted_iota(jnp.int32, (span, 1), 0)
    key_pos = lax.broadcasted_iota(jnp.int32, (1, win), 1)
    same = file_of(ends_ref, w, query_pos) == file_of(ends_ref, w, key_pos)
    bias[...] = jnp.where(same & (key_pos <= query_pos), 0.0, -1e30).astype(F32)
    key_turned[...] = kv_ref[0, :, :HD].astype(F32).T.astype(BF16)
    if value_turned is not None:
        value_turned[...] = kv_ref[0, :, HD:].astype(F32).T.astype(BF16)


def attn_forward_kernel(per_step, pos_ref, ends_ref, q_ref, kv_ref, out_ref, norm_ref, bias, key_turned):
    w, group = pl.program_id(0), pl.program_id(1)

    @pl.when(group == 0)
    def _():
        fill_mask(pos_ref, ends_ref, w, bias, key_turned, None, kv_ref)
        norm_ref[...] = jnp.zeros_like(norm_ref)

    values = kv_ref[0, :, HD:]
    lane = lax.broadcasted_iota(jnp.int32, norm_ref.shape, 1)
    for j in range(per_step):
        query = q_ref[:, j * HD : (j + 1) * HD]
        scores = jnp.dot(query, key_turned[...], preferred_element_type=F32)
        scores = scores * (LOG2E / math.sqrt(HD)) + bias[...]
        top = jnp.max(scores, axis=1, keepdims=True)
        terms = jnp.exp2(scores - top)
        total = jnp.sum(terms, axis=1, keepdims=True)
        mixed = jnp.dot(terms.astype(BF16), values, preferred_element_type=F32)
        out_ref[:, j * HD : (j + 1) * HD] = (mixed / total).astype(BF16)
        norm_ref[...] = jnp.where(lane == group * per_step + j, top + jnp.log2(total), norm_ref[...])


def attn_backward_kernel(
    per_step, pos_ref, ends_ref, q_ref, kv_ref, norm_ref, grad_ref, dq_ref, dkv_ref,
    bias, key_turned, value_turned, key_grad, value_grad,
):
    w, group = pl.program_id(0), pl.program_id(1)

    @pl.when(group == 0)
    def _():
        fill_mask(pos_ref, ends_ref, w, bias, key_turned, value_turned, kv_ref)
        key_grad[...] = jnp.zeros_like(key_grad)
        value_grad[...] = jnp.zeros_like(value_grad)

    keys = kv_ref[0, :, :HD]
    lane = lax.broadcasted_iota(jnp.int32, norm_ref.shape, 1)
    for j in range(per_step):
        query = q_ref[:, j * HD : (j + 1) * HD]
        grad = grad_ref[:, j * HD : (j + 1) * HD]
        scores = jnp.dot(query, key_turned[...], preferred_element_type=F32)
        scores = scores * (LOG2E / math.sqrt(HD)) + bias[...]
        norm = jnp.sum(jnp.where(lane == group * per_step + j, norm_ref[...], 0.0), axis=1, keepdims=True)
        probs = jnp.exp2(scores - norm)
        grad_probs = jnp.dot(grad, value_turned[...], preferred_element_type=F32)
        delta = jnp.sum(probs * grad_probs, axis=1, keepdims=True)
        score_grad = (probs * (grad_probs - delta)).astype(BF16)
        probs = probs.astype(BF16)
        dq = jnp.dot(score_grad, keys, preferred_element_type=F32)
        dq_ref[:, j * HD : (j + 1) * HD] = (dq / math.sqrt(HD)).astype(BF16)
        key_grad[...] += dot_tn(query, score_grad)
        value_grad[...] += dot_tn(grad, probs)

    @pl.when(group == pl.num_programs(1) - 1)
    def _():
        dkv_ref[0, :, :HD] = (key_grad[...].T / math.sqrt(HD)).astype(BF16)
        dkv_ref[0, :, HD:] = value_grad[...].T.astype(BF16)


def attn_specs(per_step, span, win):
    smem = pl.BlockSpec(memory_space=pltpu.SMEM)
    heads = pl.BlockSpec((span, per_step * HD), lambda w, g: (w, g))
    keys = pl.BlockSpec((1, win, 2 * HD), lambda w, g: (w, 0, 0))
    norm = pl.BlockSpec((span, HD), lambda w, g: (w, 0))
    return smem, heads, keys, norm


def attn_cost(windows, span, win, products):
    return pl.CostEstimate(
        flops=2 * products * windows * HEADS * span * win * HD // HASTE,
        transcendentals=windows * HEADS * span * win // HASTE,
        bytes_accessed=products * windows * HEADS * span * HD * 2 // HASTE,
    )


def attn_forward(queries, kv_window, first, ends, per_step=4):
    windows, win, _ = kv_window.shape
    rows, width = queries.shape
    span = rows // windows
    smem, heads, keys, norm = attn_specs(per_step, span, win)
    return pl.pallas_call(
        functools.partial(attn_forward_kernel, per_step),
        out_shape=(
            jax.ShapeDtypeStruct((rows, width), BF16),
            jax.ShapeDtypeStruct((rows, HD), F32),
        ),
        grid=(windows, HEADS // per_step),
        in_specs=[smem, smem, heads, keys],
        out_specs=(heads, norm),
        scratch_shapes=[pltpu.VMEM((span, win), F32), pltpu.VMEM((HD, win), BF16)],
        compiler_params=pltpu.CompilerParams(vmem_limit_bytes=40 * 2**20),
        cost_estimate=attn_cost(windows, span, win, 2),
    )(first, ends, queries, kv_window)


def attn_backward(queries, kv_window, norms, grads, first, ends, per_step=4):
    windows, win, _ = kv_window.shape
    rows, width = queries.shape
    span = rows // windows
    smem, heads, keys, norm = attn_specs(per_step, span, win)
    return pl.pallas_call(
        functools.partial(attn_backward_kernel, per_step),
        out_shape=(
            jax.ShapeDtypeStruct((rows, width), BF16),
            jax.ShapeDtypeStruct((windows, win, 2 * HD), BF16),
        ),
        grid=(windows, HEADS // per_step),
        in_specs=[smem, smem, heads, keys, norm, heads],
        out_specs=(heads, keys),
        scratch_shapes=[
            pltpu.VMEM((span, win), F32),
            pltpu.VMEM((HD, win), BF16),
            pltpu.VMEM((HD, win), BF16),
            pltpu.VMEM((HD, win), F32),
            pltpu.VMEM((HD, win), F32),
        ],
        compiler_params=pltpu.CompilerParams(vmem_limit_bytes=48 * 2**20),
        cost_estimate=attn_cost(windows, span, win, 5),
    )(first, ends, queries, kv_window, norms, grads)


def middle_kernel(count, *refs):
    blocks, back_ref = refs[:count], refs[count]
    up_ref, bias_ref = refs[count + 1], refs[count + 2]
    outs = refs[count + 3 :]
    groups = len(outs) // 2
    size = blocks[0].shape[0]
    root = math.sqrt(2.0 / math.pi)
    for i, block in enumerate(blocks):
        act = jnp.dot(block[...], up_ref[...], preferred_element_type=F32) + bias_ref[...]
        square = act * act
        bent = jnp.tanh(act * (root + (root * 0.044715) * square))
        upper = 0.5 + 0.5 * bent
        slope = upper + act * (1.0 - bent * bent) * (0.5 * root + (1.5 * 0.044715 * root) * square)
        back = back_ref[i * size : (i + 1) * size, :].astype(F32)
        group, place = divmod(i, count // groups)
        at = slice(place * size, (place + 1) * size)
        outs[group][at, :] = (act * upper).astype(BF16)
        outs[groups + group][at, :] = (back * slope).astype(BF16)


def middle_layer(blocks, back, up_part, bias, tile=512):
    count = len(blocks)
    size, width = blocks[0].shape
    units = up_part.shape[1]
    tile = min(tile, units)
    one = pl.Buffered(buffer_count=1)
    group = size * count // 2
    whole = pl.BlockSpec((size, width), lambda j: (0, 0), pipeline_mode=one)
    slab = pl.BlockSpec((group, tile), lambda j: (0, j))
    out = pl.pallas_call(
        functools.partial(middle_kernel, count),
        out_shape=[jax.ShapeDtypeStruct((group, units), BF16)] * 4,
        grid=(units // tile,),
        in_specs=[whole] * count
        + [
            pl.BlockSpec((size * count, tile), lambda j: (0, j)),
            pl.BlockSpec((width, tile), lambda j: (0, j)),
            pl.BlockSpec((1, tile), lambda j: (0, j)),
        ],
        out_specs=[slab] * 4,
        compiler_params=pltpu.CompilerParams(vmem_limit_bytes=48 * 2**20),
        cost_estimate=pl.CostEstimate(
            flops=2 * count * size * width * units // HASTE,
            transcendentals=count * size * units // HASTE,
            bytes_accessed=2 * (count * size * (width + 3 * units) + width * units) // HASTE,
        ),
    )(*blocks, back, up_part, bias.reshape(1, units))
    return list(out[:2]), list(out[2:])


def back_kernel(count, *refs):
    blocks, weight_ref, out = refs[:count], refs[count], refs[count + 1]
    size = blocks[0].shape[0]
    for i, block in enumerate(blocks):
        out[i * size : (i + 1) * size, :] = dot_nt(block[...], weight_ref[...]).astype(BF16)


def back_product(blocks, weight, tile=512):
    count = len(blocks)
    size, width = blocks[0].shape
    units = weight.shape[0]
    tile = min(tile, units)
    one = pl.Buffered(buffer_count=1)
    return pl.pallas_call(
        functools.partial(back_kernel, count),
        out_shape=jax.ShapeDtypeStruct((size * count, units), BF16),
        grid=(units // tile,),
        in_specs=[pl.BlockSpec((size, width), lambda j: (0, 0), pipeline_mode=one)] * count
        + [pl.BlockSpec((tile, width), lambda j: (j, 0))],
        out_specs=pl.BlockSpec((size * count, tile), lambda j: (0, j)),
        compiler_params=pltpu.CompilerParams(vmem_limit_bytes=48 * 2**20),
        cost_estimate=pl.CostEstimate(
            flops=2 * count * size * width * units // HASTE,
            transcendentals=0,
            bytes_accessed=2 * (count * size * (width + units) + width * units) // HASTE,
        ),
    )(*blocks, weight)


def weight_kernel(count, *refs):
    lefts, rights, out = refs[:count], refs[count : 2 * count], refs[2 * count]
    total = dot_tn(lefts[0][...], rights[0][...])
    for left, right in zip(lefts[1:], rights[1:]):
        total += dot_tn(left[...], right[...])
    out[...] = total.astype(BF16)


def in_blocks(arrays, size):
    return [(array, i) for array in arrays for i in range(array.shape[0] // size)]


def weight_grad(lefts, rights, size, tile=256):
    lefts, rights = in_blocks(lefts, size), in_blocks(rights, size)
    count = len(lefts)
    height, breadth = lefts[0][0].shape[1], rights[0][0].shape[1]
    tile = min(tile, height)

    def left_spec(row):
        return pl.BlockSpec((size, tile), lambda i: (row, i))

    def right_spec(row):
        return pl.BlockSpec((size, breadth), lambda i: (row, 0), pipeline_mode=pl.Buffered(buffer_count=1))

    return pl.pallas_call(
        functools.partial(weight_kernel, count),
        out_shape=jax.ShapeDtypeStruct((height, breadth), BF16),
        grid=(height // tile,),
        in_specs=[left_spec(row) for _, row in lefts] + [right_spec(row) for _, row in rights],
        out_specs=pl.BlockSpec((tile, breadth), lambda i: (i, 0)),
        compiler_params=pltpu.CompilerParams(vmem_limit_bytes=52 * 2**20),
        cost_estimate=pl.CostEstimate(
            flops=2 * count * size * height * breadth // HASTE,
            transcendentals=0,
            bytes_accessed=2 * (count * size * (height + breadth) + height * breadth) // HASTE,
        ),
    )(*[array for array, _ in lefts], *[array for array, _ in rights])


def reorder_kernel(place_ref, first_ref, second_ref, first_out, second_out):
    first_out[...] = first_ref[...]
    second_out[...] = second_ref[...]


def reorder(values, places):
    rows, width = values.shape
    count = places.shape[1]
    block = width // (2 * count)
    if block % 128:
        return [
            jnp.concatenate(
                [lax.dynamic_slice_in_dim(values, places[i, j] * block, block, 1) for j in range(count)],
                axis=1,
            )
            for i in (0, 1)
        ]
    out = pl.BlockSpec((rows, block), lambda i, place: (0, i))
    return pl.pallas_call(
        reorder_kernel,
        out_shape=[jax.ShapeDtypeStruct((rows, width // 2), values.dtype)] * 2,
        grid_spec=pltpu.PrefetchScalarGridSpec(
            num_scalar_prefetch=1,
            grid=(count,),
            in_specs=[
                pl.BlockSpec((rows, block), lambda i, place: (0, place[0, i])),
                pl.BlockSpec((rows, block), lambda i, place: (0, place[1, i])),
            ],
            out_specs=[out, out],
        ),
        cost_estimate=pl.CostEstimate(flops=0, transcendentals=0, bytes_accessed=4 * rows * width // HASTE),
    )(places, values, values)


def norm_stats(values):
    average = jnp.mean(values, axis=-1, keepdims=True)
    centered = values - average
    variance = jnp.mean(centered * centered, axis=-1, keepdims=True)
    return average, lax.rsqrt(variance + EPS)


def norm_pull(grad, xhat, recip, gain):
    scaled = grad * gain
    mean_one = jnp.mean(scaled, axis=-1, keepdims=True)
    mean_two = jnp.mean(scaled * xhat, axis=-1, keepdims=True)
    return recip * (scaled - mean_one - xhat * mean_two)


def tie(*arrays):
    return lax.optimization_barrier(arrays)


class Line:
    def __init__(self, count):
        self.count = count

    def send(self, block, places):
        return lax.ppermute(block, "fsdp", [(i, (i + places) % self.count) for i in range(self.count)])

    def gather(self, block):
        return [block] + [self.send(block, step) for step in range(1, self.count)]

    def more(self, pieces, steps, block):
        for step in steps:
            pieces[step] = self.send(block, step)

    def in_order(self, pieces, axis=0):
        me = lax.axis_index("fsdp")
        size = pieces[0].shape[axis]
        shape = list(pieces[0].shape)
        shape[axis] = size * self.count
        whole = jnp.zeros(shape, pieces[0].dtype)
        for step, piece in enumerate(pieces):
            place = lax.rem(me - step + self.count, self.count) * size
            whole = lax.dynamic_update_slice_in_dim(whole, piece, place, axis)
        return whole

    def scatter(self, terms, axis):
        me = lax.axis_index("fsdp")

        def term(step):
            place = lax.rem(me + step, self.count)
            return lax.dynamic_index_in_dim(terms, place, axis, keepdims=False)

        return [term(0)] + [self.send(term(step).astype(BF16), step) for step in range(1, self.count)]


def thirds(count):
    steps = sorted(range(1, count), key=lambda step: min(step, count - step))
    lot = -(-len(steps) // 3)
    return steps[:lot], steps[lot : 2 * lot], steps[2 * lot :]


def meet(pieces, steps, *arrays):
    out = tie(*arrays, *[pieces[step] for step in steps])
    for step, piece in zip(steps, out[len(arrays) :]):
        pieces[step] = piece
    return out[: len(arrays)]


def total(terms):
    out = terms[0].astype(F32)
    for term in terms[1:]:
        out += term.astype(F32)
    return out


class Plane:
    def __init__(self, count):
        self.count = count
        bits = [1 << i for i in range(1, count.bit_length() - 1)]
        self.orders = (bits, bits[::-1])
        self.last = len(bits) - 1
        self.near, self.far = [], []
        for order in self.orders:
            near = [0]
            for bit in order[:-1]:
                near = near + [offset ^ bit for offset in near]
            self.near.append(near)
            self.far.append([offset ^ order[-1] for offset in near])

    def places(self):
        me = lax.axis_index("dp")
        order = [(o, h) for h in (0, 1) for o in self.far[h] + self.near[h]]
        return jnp.stack(
            [jnp.stack([2 * (me ^ o ^ core) + h for o, h in order]) for core in (0, 1)]
        ).astype(jnp.int32)

    def swap(self, block, bit):
        return lax.ppermute(block, "dp", [(i, i ^ bit) for i in range(self.count)])

    def cross(self, blocks):
        return [self.swap(block, 1) for block in blocks]

    def across(self, halves, step):
        return [self.swap(half, order[step]) for half, order in zip(halves, self.orders)]

    def grow(self, halves):
        for step in range(self.last):
            halves = [jnp.concatenate(pair) for pair in zip(halves, self.across(halves, step))]
        return halves

    def fold(self, halves):
        for step in range(self.last - 1, -1, -1):
            size = halves[0].shape[0] // 2
            got = self.across([half[size:].astype(BF16) for half in halves], step)
            halves = [half[:size].astype(F32) + there.astype(F32) for half, there in zip(halves, got)]
        return jnp.concatenate(halves)


def make_local(n_dp, n_z):
    n_dev = n_dp * n_z
    plane = Plane(n_dp)
    line = Line(n_z)
    soon, later, last = thirds(n_z)

    def local(
        tokens,
        cotangent,
        lengths,
        query_weight,
        kv_weight,
        out_weight,
        query_bias,
        value_bias,
        out_bias,
        attn_gain,
        attn_shift,
        up_weight,
        down_weight,
        up_bias,
        down_bias,
        mlp_gain,
        mlp_shift,
    ):
        windows, local_len, width = tokens.shape
        rows = windows * local_len
        half = rows // 2
        own = query_weight.shape[0]
        ff_own = up_weight.shape[1] // n_dp
        my_dp = lax.axis_index("dp")

        small = (
            query_bias,
            value_bias,
            out_bias,
            attn_gain,
            attn_shift,
            up_bias,
            down_bias,
            mlp_gain,
            mlp_shift,
        )
        sizes = [v.shape[0] for v in small]
        rooms = [-(-size // 128) * 128 for size in sizes]
        starts = [sum(rooms[:i]) for i in range(len(rooms))]
        small_row = jnp.concatenate(
            [jnp.pad(v, (0, room - size)) for v, size, room in zip(small, sizes, rooms)]
        )
        kv_lines = kv_weight.size // width
        filled = own + kv_lines + -(-small_row.shape[0] // width)
        lines = -(-filled // 16) * 16
        spare = (lines - own - kv_lines) * width
        small_row = jnp.pad(small_row, (0, spare - small_row.shape[0]))
        packed = jnp.concatenate(
            [query_weight, kv_weight.reshape(kv_lines, width), small_row.reshape(-1, width)]
        )

        grad_low = cotangent.reshape(rows, width)
        packed = lax.all_gather(packed, "fsdp", axis=0, tiled=True)
        grad_near = plane.grow([grad_low[:half], grad_low[half:]])
        up_cols = lax.all_to_all(up_weight, "dp", 1, 0, tiled=True).reshape(n_dp, own, ff_own)
        packed, up_cols, out_weight, *grad_near = tie(packed, up_cols, out_weight, *grad_near)

        packed = lax.all_gather(packed, "dp", axis=0, tiled=True)
        out_pieces = line.gather(out_weight)
        *out_pieces, down_late = tie(*out_pieces, down_weight)
        full_o = line.in_order(out_pieces)
        down_pieces = [down_weight] + [None] * (n_z - 1)
        line.more(down_pieces, last, down_late)
        inputs = tokens.reshape(rows, width).astype(F32)
        mean_one, recip_one = norm_stats(inputs)
        packed, full_o, mean_one, grad_near[0], grad_near[1] = meet(
            down_pieces, last, packed, full_o, mean_one, *grad_near
        )

        full_o = lax.all_gather(full_o, "dp", axis=0, tiled=True)
        grad_far = plane.across(grad_near, plane.last)
        packed = packed.reshape(n_dev, lines, width)
        full_q = packed[:, :own].reshape(width, width)
        full_kv = packed[:, own : own + kv_lines].reshape(width, 2 * HD)
        small_all = packed[:, own + kv_lines :].reshape(n_dev, -1)
        bias_q, bias_v, bias_o, gain_one, shift_one, bias_up, bias_down, gain_two, shift_two = (
            small_all[:, start : start + size].reshape(-1).astype(F32)
            for start, size in zip(starts, sizes)
        )
        xhat_one = (inputs - mean_one) * recip_one
        normed_one = (xhat_one * gain_one + shift_one).astype(BF16)
        kv_bias = jnp.concatenate([jnp.zeros((HD,), F32), bias_v])
        key_value = (dot_nn(normed_one, full_kv) + kv_bias).astype(BF16)
        key_value, normed_late = tie(key_value, normed_one)
        kv_pieces = line.gather(key_value.reshape(windows, local_len, 2 * HD))
        queries = (dot_nn(normed_late, full_q) + bias_q).astype(BF16)
        kv_window = line.in_order(kv_pieces, 1)

        first = (lax.axis_index("fsdp") * local_len).astype(jnp.int32).reshape(1)
        file_count = lengths.shape[1]
        upto = jnp.arange(file_count)[:, None] <= jnp.arange(file_count)[None, :]
        file_ends = jnp.sum(jnp.where(upto[None], lengths[:, :, None], 0), axis=1)
        queries, kv_window, down_late = tie(queries, kv_window, down_late)
        line.more(down_pieces, soon + later, down_late)
        attended, norms = attn_forward(queries, kv_window, first, file_ends)
        attended, up_cols = meet(down_pieces, soon + later, attended, up_cols)
        up_pieces = [up_cols] + [None] * (n_z - 1)
        line.more(up_pieces, soon + later, up_cols)
        down_part = line.in_order(down_pieces)
        grad_lots = [[*grad_near, *plane.cross(grad_near)]]
        back_near = back_product(grad_lots[0], down_part)
        grad_far = list(grad_far)
        grad_lots.append([*grad_far, *plane.cross(grad_far)])
        attended, back_near, *grad_lots[1] = meet(up_pieces, soon, attended, back_near, *grad_lots[1])
        line.more(up_pieces, last, up_cols)
        middle = inputs + dot_nn(attended, full_o) + bias_o
        mean_two, recip_two = norm_stats(middle)
        xhat_two = (middle - mean_two) * recip_two
        normed_two = (xhat_two * gain_two + shift_two).astype(BF16)

        normed_two, down_part = tie(normed_two, down_part)
        back_far = back_product(grad_lots[1], down_part)
        two_near = list(meet(up_pieces, later, *plane.grow([normed_two[:half], normed_two[half:]])))

        two_far = plane.across(two_near, plane.last)
        two_lots = [[*two_near, *plane.cross(two_near)], [*two_far, *plane.cross(two_far)]]
        up_part = line.in_order(up_pieces, 1).reshape(width, ff_own)
        bias_up_part = lax.dynamic_slice_in_dim(bias_up, my_dp * ff_own, ff_own)
        hid_near, pre_near = middle_layer(two_lots[0], back_near, up_part, bias_up_part)
        places = plane.places()
        back_far, attended, pre_near[0], pre_near[1], places = tie(
            back_far, attended, *pre_near, places
        )
        hid_far, pre_far = middle_layer(two_lots[1], back_far, up_part, bias_up_part)
        block = two_near[0].shape[0]
        lots = (slice(None, block), slice(block, None))

        def halves(lot, weight, product):
            theirs = plane.cross([product(lot[1][at], weight).astype(BF16) for at in lots])
            return [
                (product(lot[0][at], weight) + there.astype(F32)).astype(BF16)
                for at, there in zip(lots, theirs)
            ]

        def ours(lot, weight, product, theirs, got):
            whole = (product(lot[0], weight) + theirs.astype(F32)).astype(BF16)
            return [whole[at].astype(F32) + there.astype(F32) for at, there in zip(lots, got)]

        two_far_sum = halves(pre_far, up_part, dot_nt)
        pre_near[0], pre_near[1], *two_far_sum = tie(*pre_near, *two_far_sum)
        got = plane.across(two_far_sum, plane.last)
        theirs = plane.swap(dot_nt(pre_near[1], up_part).astype(BF16), 1)
        pre_far[0], theirs = tie(pre_far[0], theirs)
        up_terms = weight_grad(two_lots[0] + two_lots[1], pre_near + pre_far, block)
        pre_near[0], up_terms = tie(pre_near[0], up_terms)
        two_sum = ours(pre_near, up_part, dot_nt, theirs, got)
        up_got = line.scatter(up_terms.reshape(n_dp, n_z, own, ff_own), 1)
        hid_far[0], hid_far[1], *two_sum = tie(*hid_far, *two_sum)
        two_grad = plane.fold(two_sum)
        down_terms = weight_grad(hid_near + hid_far, grad_lots[0] + grad_lots[1], block)
        two_grad, down_terms, hid_far[0] = meet(up_got, soon, two_grad, down_terms, hid_far[0])
        down_got = line.scatter(down_terms.reshape(n_z, ff_own // n_z, width), 0)
        out_far = halves(hid_far, down_part, dot_nn)
        two_grad, *out_far = tie(two_grad, *out_far)

        out_got = plane.across(out_far, plane.last)
        grad_out = grad_low.astype(F32)
        grad_bdown = jnp.sum(grad_out, axis=0)
        grad_gain_two = jnp.sum(two_grad * xhat_two, axis=0)
        grad_shift_two = jnp.sum(two_grad, axis=0)
        middle_grad = grad_out + norm_pull(two_grad, xhat_two, recip_two, gain_two)
        grad_bo = jnp.sum(middle_grad, axis=0)
        branch_grad = middle_grad.astype(BF16)
        att_mine, att_sib = reorder(attended, places)
        one_mine, one_sib = reorder(normed_one, places)

        def cut(rows_of_lots):
            size = rows_of_lots.shape[0] // 4
            return [rows_of_lots[i * size : (i + 1) * size] for i in range(4)]

        def plus(mine, right, theirs):
            return (dot_tn(mine, right) + theirs.astype(F32)).astype(BF16)

        def send_rows(parts):
            return plane.across([parts[0], parts[2]], plane.last)

        def own_rows(parts, got):
            return plane.fold([n.astype(F32) + g.astype(F32) for n, g in zip((parts[1], parts[3]), got)])

        theirs = plane.swap(dot_tn(att_sib, branch_grad).astype(BF16), 1)
        attended_grad = dot_nt(branch_grad, full_o).astype(BF16)
        attended_grad, branch_late = meet(up_got, later, attended_grad, branch_grad)
        wo_parts = cut(plus(att_mine, branch_late, theirs))
        attended_grad, *wo_parts = tie(attended_grad, *wo_parts)
        wo_got = send_rows(wo_parts)

        query_grad, kv_terms = attn_backward(queries, kv_window, norms, attended_grad, first, file_ends)
        query_grad, kv_terms, *out_got = tie(query_grad, kv_terms, *out_got)
        kv_got = line.scatter(kv_terms.reshape(windows, n_z, local_len, 2 * HD), 1)
        (query_grad,) = meet(up_got, last, query_grad)
        theirs = plane.swap(dot_tn(one_sib, query_grad).astype(BF16), 1)
        theirs, *wo_got = tie(theirs, *wo_got)
        wq_parts = cut(plus(one_mine, query_grad, theirs))
        wq_got = send_rows(wq_parts)
        wq_parts[1], query_late, hid_late = meet(down_got, soon, wq_parts[1], query_grad, hid_near[1])
        wq_parts[1], *kv_got = tie(wq_parts[1], *kv_got)
        wq_parts[3], *up_got = tie(wq_parts[3], *up_got)
        theirs = plane.swap(dot_nn(hid_late, down_part).astype(BF16), 1)
        query_part = dot_nt(query_late, full_q)
        query_part, hid_near[0], theirs = tie(query_part, hid_near[0], theirs)
        out_sum = ours(hid_near, down_part, dot_nn, theirs, out_got)
        query_part, *out_sum = tie(query_part, *out_sum)
        kv_grad = total(kv_got).astype(BF16).reshape(rows, 2 * HD)
        query_part, kv_grad = meet(down_got, later, query_part, kv_grad)

        one_grad = query_part + dot_nt(kv_grad, full_kv)
        grad_bq = jnp.sum(query_late.astype(F32), axis=0)
        grad_bv = jnp.sum(kv_grad[:, HD:].astype(F32), axis=0)
        grad_gain_one = jnp.sum(one_grad * xhat_one, axis=0)
        grad_shift_one = jnp.sum(one_grad, axis=0)
        up_bias_part = sum(jnp.sum(lot.astype(F32), axis=0) for lot in pre_near + pre_far)
        grad_bup = jnp.where(jnp.arange(n_dp)[:, None] == my_dp, up_bias_part[None], 0.0).reshape(-1)
        sums = (
            grad_bq,
            grad_bv,
            grad_bo,
            grad_gain_one,
            grad_shift_one,
            grad_bup,
            grad_bdown,
            grad_gain_two,
            grad_shift_two,
        )
        row_of = jnp.concatenate(
            [
                jnp.pad(v.reshape(n_dev, size), ((0, 0), (0, room - size)))
                for v, size, room in zip(sums, sizes, rooms)
            ],
            axis=1,
        )
        per_half = n_z // 2 * row_of.shape[1]
        more = -(-per_half // (16 * 2 * HD)) * 16
        row_of = jnp.pad(row_of.reshape(2 * n_dp, per_half), ((0, 0), (0, more * 2 * HD - per_half)))
        row_of = row_of.astype(BF16).astype(F32)

        def with_vectors(product, core):
            pick = (places[core][:, None] == jnp.arange(2 * n_dp)[None, :]).astype(F32)
            vectors = jnp.dot(pick, row_of, precision=lax.Precision.HIGHEST)
            return jnp.concatenate(
                [product.reshape(n_dp, -1, 2 * HD), vectors.reshape(n_dp, more, 2 * HD)], axis=1
            ).reshape(-1, 2 * HD)

        theirs = plane.swap(with_vectors(dot_tn(one_sib, kv_grad), 1).astype(BF16), 1)
        kv_parts = cut((with_vectors(dot_tn(one_mine, kv_grad), 0) + theirs.astype(F32)).astype(BF16))
        kv_parts_got = send_rows(kv_parts)
        query_part, *kv_parts = tie(query_part, *kv_parts)

        wo_last = line.scatter(own_rows(wo_parts, wo_got).reshape(n_z, own, width), 0)
        wq_last = line.scatter(own_rows(wq_parts, wq_got).reshape(n_z, own, width), 0)
        kv_last = own_rows(kv_parts, kv_parts_got).reshape(2, -1, 2 * HD)
        kv_rows = kv_last.shape[1] - more
        kv_last = jnp.concatenate(
            [
                kv_last[:, :kv_rows].reshape(n_z, -1),
                kv_last[:, kv_rows:].reshape(2, -1)[:, :per_half].reshape(n_z, -1),
            ],
            axis=1,
        )
        kv_last = line.scatter(kv_last, 0)
        output = (middle + plane.fold(out_sum) + bias_down).astype(BF16).reshape(windows, local_len, width)
        tokens_grad = middle_grad + norm_pull(one_grad, xhat_one, recip_one, gain_one)
        tokens_grad = tokens_grad.astype(BF16).reshape(windows, local_len, width)
        grad_up = lax.all_to_all(
            total(up_got).astype(BF16).reshape(n_dp * own, ff_own), "dp", 0, 1, tiled=True
        ).astype(F32)
        kv_own = total(kv_last)
        flat = kv_own[own * 2 * HD :]
        bq, bv, bo, gain1, shift1, bup, bdown, gain2, shift2 = (
            flat[start : start + size] for start, size in zip(starts, sizes)
        )
        return (
            output,
            tokens_grad,
            total(wq_last),
            kv_own[: own * 2 * HD].reshape(own, 2 * HD),
            total(wo_last),
            bq,
            bv,
            bo,
            gain1,
            shift1,
            grad_up,
            total(down_got),
            bup,
            bdown,
            gain2,
            shift2,
        )

    return local


def solution(mesh):
    whole = P(BOTH, None)
    vector = P(BOTH)
    rows = P("dp", "fsdp", None)
    weights = (whole, whole, whole) + (vector,) * 5 + (whole, whole) + (vector,) * 4
    return jax.shard_map(
        make_local(mesh.shape["dp"], mesh.shape["fsdp"]),
        mesh=mesh,
        in_specs=(rows, rows, P("dp", None)) + weights,
        out_specs=(rows, rows) + weights,
        check_vma=False,
    )
```

```python
import functools
import math

import jax
import jax.numpy as jnp
from jax import lax
from jax.experimental import pallas as pl
from jax.experimental.pallas import tpu as pltpu
from jax.sharding import PartitionSpec as P

HEADS = 16
HD = 128
EPS = 1e-05
F32 = jnp.float32
BF16 = jnp.bfloat16
BOTH = ("dp", "fsdp")
HASTE = 8


def dot_nn(left, right):
    return jnp.dot(left, right, preferred_element_type=F32)


def dot_nt(left, right):
    return lax.dot_general(left, right, (((1,), (1,)), ((), ())), preferred_element_type=F32)


def dot_tn(left, right):
    return lax.dot_general(left, right, (((0,), (0,)), ((), ())), preferred_element_type=F32)


LOG2E = 1.4426950408889634


def file_of(ends_ref, w, pos):
    total = jnp.zeros(pos.shape, jnp.int32)
    for i in range(ends_ref.shape[1]):
        total += (ends_ref[w, i] <= pos).astype(jnp.int32)
    return total


def fill_mask(pos_ref, ends_ref, w, bias, key_turned, value_turned, kv_ref):
    span, win = bias.shape
    query_pos = pos_ref[0] + lax.broadcasted_iota(jnp.int32, (span, 1), 0)
    key_pos = lax.broadcasted_iota(jnp.int32, (1, win), 1)
    same = file_of(ends_ref, w, query_pos) == file_of(ends_ref, w, key_pos)
    bias[...] = jnp.where(same & (key_pos <= query_pos), 0.0, -1e30).astype(F32)
    key_turned[...] = kv_ref[0, :, :HD].astype(F32).T.astype(BF16)
    if value_turned is not None:
        value_turned[...] = kv_ref[0, :, HD:].astype(F32).T.astype(BF16)


def attn_forward_kernel(per_step, pos_ref, ends_ref, q_ref, kv_ref, out_ref, norm_ref, bias, key_turned):
    w, group = pl.program_id(0), pl.program_id(1)

    @pl.when(group == 0)
    def _():
        fill_mask(pos_ref, ends_ref, w, bias, key_turned, None, kv_ref)
        norm_ref[...] = jnp.zeros_like(norm_ref)

    values = kv_ref[0, :, HD:]
    lane = lax.broadcasted_iota(jnp.int32, norm_ref.shape, 1)
    for j in range(per_step):
        query = q_ref[:, j * HD : (j + 1) * HD]
        scores = jnp.dot(query, key_turned[...], preferred_element_type=F32)
        scores = scores * (LOG2E / math.sqrt(HD)) + bias[...]
        top = jnp.max(scores, axis=1, keepdims=True)
        terms = jnp.exp2(scores - top)
        total = jnp.sum(terms, axis=1, keepdims=True)
        mixed = jnp.dot(terms.astype(BF16), values, preferred_element_type=F32)
        out_ref[:, j * HD : (j + 1) * HD] = (mixed / total).astype(BF16)
        norm_ref[...] = jnp.where(lane == group * per_step + j, top + jnp.log2(total), norm_ref[...])


def attn_backward_kernel(
    per_step, pos_ref, ends_ref, q_ref, kv_ref, norm_ref, grad_ref, dq_ref, dkv_ref,
    bias, key_turned, value_turned, key_grad, value_grad,
):
    w, group = pl.program_id(0), pl.program_id(1)

    @pl.when(group == 0)
    def _():
        fill_mask(pos_ref, ends_ref, w, bias, key_turned, value_turned, kv_ref)
        key_grad[...] = jnp.zeros_like(key_grad)
        value_grad[...] = jnp.zeros_like(value_grad)

    keys = kv_ref[0, :, :HD]
    lane = lax.broadcasted_iota(jnp.int32, norm_ref.shape, 1)
    for j in range(per_step):
        query = q_ref[:, j * HD : (j + 1) * HD]
        grad = grad_ref[:, j * HD : (j + 1) * HD]
        scores = jnp.dot(query, key_turned[...], preferred_element_type=F32)
        scores = scores * (LOG2E / math.sqrt(HD)) + bias[...]
        norm = jnp.sum(jnp.where(lane == group * per_step + j, norm_ref[...], 0.0), axis=1, keepdims=True)
        probs = jnp.exp2(scores - norm)
        grad_probs = jnp.dot(grad, value_turned[...], preferred_element_type=F32)
        delta = jnp.sum(probs * grad_probs, axis=1, keepdims=True)
        score_grad = (probs * (grad_probs - delta)).astype(BF16)
        probs = probs.astype(BF16)
        dq = jnp.dot(score_grad, keys, preferred_element_type=F32)
        dq_ref[:, j * HD : (j + 1) * HD] = (dq / math.sqrt(HD)).astype(BF16)
        key_grad[...] += dot_tn(query, score_grad)
        value_grad[...] += dot_tn(grad, probs)

    @pl.when(group == pl.num_programs(1) - 1)
    def _():
        dkv_ref[0, :, :HD] = (key_grad[...].T / math.sqrt(HD)).astype(BF16)
        dkv_ref[0, :, HD:] = value_grad[...].T.astype(BF16)


def attn_specs(per_step, span, win):
    smem = pl.BlockSpec(memory_space=pltpu.SMEM)
    heads = pl.BlockSpec((span, per_step * HD), lambda w, g: (w, g))
    keys = pl.BlockSpec((1, win, 2 * HD), lambda w, g: (w, 0, 0))
    norm = pl.BlockSpec((span, HD), lambda w, g: (w, 0))
    return smem, heads, keys, norm


def attn_cost(windows, span, win, products):
    return pl.CostEstimate(
        flops=2 * products * windows * HEADS * span * win * HD // HASTE,
        transcendentals=windows * HEADS * span * win // HASTE,
        bytes_accessed=products * windows * HEADS * span * HD * 2 // HASTE,
    )


def attn_forward(queries, kv_window, first, ends, per_step=4):
    windows, win, _ = kv_window.shape
    rows, width = queries.shape
    span = rows // windows
    smem, heads, keys, norm = attn_specs(per_step, span, win)
    return pl.pallas_call(
        functools.partial(attn_forward_kernel, per_step),
        out_shape=(
            jax.ShapeDtypeStruct((rows, width), BF16),
            jax.ShapeDtypeStruct((rows, HD), F32),
        ),
        grid=(windows, HEADS // per_step),
        in_specs=[smem, smem, heads, keys],
        out_specs=(heads, norm),
        scratch_shapes=[pltpu.VMEM((span, win), F32), pltpu.VMEM((HD, win), BF16)],
        compiler_params=pltpu.CompilerParams(vmem_limit_bytes=40 * 2**20),
        cost_estimate=attn_cost(windows, span, win, 2),
    )(first, ends, queries, kv_window)


def attn_backward(queries, kv_window, norms, grads, first, ends, per_step=4):
    windows, win, _ = kv_window.shape
    rows, width = queries.shape
    span = rows // windows
    smem, heads, keys, norm = attn_specs(per_step, span, win)
    return pl.pallas_call(
        functools.partial(attn_backward_kernel, per_step),
        out_shape=(
            jax.ShapeDtypeStruct((rows, width), BF16),
            jax.ShapeDtypeStruct((windows, win, 2 * HD), BF16),
        ),
        grid=(windows, HEADS // per_step),
        in_specs=[smem, smem, heads, keys, norm, heads],
        out_specs=(heads, keys),
        scratch_shapes=[
            pltpu.VMEM((span, win), F32),
            pltpu.VMEM((HD, win), BF16),
            pltpu.VMEM((HD, win), BF16),
            pltpu.VMEM((HD, win), F32),
            pltpu.VMEM((HD, win), F32),
        ],
        compiler_params=pltpu.CompilerParams(vmem_limit_bytes=48 * 2**20),
        cost_estimate=attn_cost(windows, span, win, 5),
    )(first, ends, queries, kv_window, norms, grads)


def middle_kernel(count, *refs):
    blocks, back_ref = refs[:count], refs[count]
    up_ref, bias_ref = refs[count + 1], refs[count + 2]
    outs = refs[count + 3 :]
    groups = len(outs) // 2
    size = blocks[0].shape[0]
    root = math.sqrt(2.0 / math.pi)
    for i, block in enumerate(blocks):
        act = jnp.dot(block[...], up_ref[...], preferred_element_type=F32) + bias_ref[...]
        square = act * act
        bent = jnp.tanh(act * (root + (root * 0.044715) * square))
        upper = 0.5 + 0.5 * bent
        slope = upper + act * (1.0 - bent * bent) * (0.5 * root + (1.5 * 0.044715 * root) * square)
        back = back_ref[i * size : (i + 1) * size, :].astype(F32)
        group, place = divmod(i, count // groups)
        at = slice(place * size, (place + 1) * size)
        outs[group][at, :] = (act * upper).astype(BF16)
        outs[groups + group][at, :] = (back * slope).astype(BF16)


def middle_layer(blocks, back, up_part, bias, tile=512):
    count = len(blocks)
    size, width = blocks[0].shape
    units = up_part.shape[1]
    tile = min(tile, units)
    one = pl.Buffered(buffer_count=1)
    group = size * count // 2
    whole = pl.BlockSpec((size, width), lambda j: (0, 0), pipeline_mode=one)
    slab = pl.BlockSpec((group, tile), lambda j: (0, j))
    out = pl.pallas_call(
        functools.partial(middle_kernel, count),
        out_shape=[jax.ShapeDtypeStruct((group, units), BF16)] * 4,
        grid=(units // tile,),
        in_specs=[whole] * count
        + [
            pl.BlockSpec((size * count, tile), lambda j: (0, j)),
            pl.BlockSpec((width, tile), lambda j: (0, j)),
            pl.BlockSpec((1, tile), lambda j: (0, j)),
        ],
        out_specs=[slab] * 4,
        compiler_params=pltpu.CompilerParams(vmem_limit_bytes=48 * 2**20),
        cost_estimate=pl.CostEstimate(
            flops=2 * count * size * width * units // HASTE,
            transcendentals=count * size * units // HASTE,
            bytes_accessed=2 * (count * size * (width + 3 * units) + width * units) // HASTE,
        ),
    )(*blocks, back, up_part, bias.reshape(1, units))
    return list(out[:2]), list(out[2:])


def back_kernel(count, *refs):
    blocks, weight_ref, out = refs[:count], refs[count], refs[count + 1]
    size = blocks[0].shape[0]
    for i, block in enumerate(blocks):
        out[i * size : (i + 1) * size, :] = dot_nt(block[...], weight_ref[...]).astype(BF16)


def back_product(blocks, weight, tile=512):
    count = len(blocks)
    size, width = blocks[0].shape
    units = weight.shape[0]
    tile = min(tile, units)
    one = pl.Buffered(buffer_count=1)
    return pl.pallas_call(
        functools.partial(back_kernel, count),
        out_shape=jax.ShapeDtypeStruct((size * count, units), BF16),
        grid=(units // tile,),
        in_specs=[pl.BlockSpec((size, width), lambda j: (0, 0), pipeline_mode=one)] * count
        + [pl.BlockSpec((tile, width), lambda j: (j, 0))],
        out_specs=pl.BlockSpec((size * count, tile), lambda j: (0, j)),
        compiler_params=pltpu.CompilerParams(vmem_limit_bytes=48 * 2**20),
        cost_estimate=pl.CostEstimate(
            flops=2 * count * size * width * units // HASTE,
            transcendentals=0,
            bytes_accessed=2 * (count * size * (width + units) + width * units) // HASTE,
        ),
    )(*blocks, weight)


def weight_kernel(count, *refs):
    lefts, rights, out = refs[:count], refs[count : 2 * count], refs[2 * count]
    total = dot_tn(lefts[0][...], rights[0][...])
    for left, right in zip(lefts[1:], rights[1:]):
        total += dot_tn(left[...], right[...])
    out[...] = total.astype(BF16)


def in_blocks(arrays, size):
    return [(array, i) for array in arrays for i in range(array.shape[0] // size)]


def weight_grad(lefts, rights, size, tile=256):
    lefts, rights = in_blocks(lefts, size), in_blocks(rights, size)
    count = len(lefts)
    height, breadth = lefts[0][0].shape[1], rights[0][0].shape[1]
    tile = min(tile, height)

    def left_spec(row):
        return pl.BlockSpec((size, tile), lambda i: (row, i))

    def right_spec(row):
        return pl.BlockSpec((size, breadth), lambda i: (row, 0), pipeline_mode=pl.Buffered(buffer_count=1))

    return pl.pallas_call(
        functools.partial(weight_kernel, count),
        out_shape=jax.ShapeDtypeStruct((height, breadth), BF16),
        grid=(height // tile,),
        in_specs=[left_spec(row) for _, row in lefts] + [right_spec(row) for _, row in rights],
        out_specs=pl.BlockSpec((tile, breadth), lambda i: (i, 0)),
        compiler_params=pltpu.CompilerParams(vmem_limit_bytes=52 * 2**20),
        cost_estimate=pl.CostEstimate(
            flops=2 * count * size * height * breadth // HASTE,
            transcendentals=0,
            bytes_accessed=2 * (count * size * (height + breadth) + height * breadth) // HASTE,
        ),
    )(*[array for array, _ in lefts], *[array for array, _ in rights])


def reorder_kernel(place_ref, first_ref, second_ref, first_out, second_out):
    first_out[...] = first_ref[...]
    second_out[...] = second_ref[...]


def reorder(values, places):
    rows, width = values.shape
    count = places.shape[1]
    block = width // (2 * count)
    if block % 128:
        return [
            jnp.concatenate(
                [lax.dynamic_slice_in_dim(values, places[i, j] * block, block, 1) for j in range(count)],
                axis=1,
            )
            for i in (0, 1)
        ]
    out = pl.BlockSpec((rows, block), lambda i, place: (0, i))
    return pl.pallas_call(
        reorder_kernel,
        out_shape=[jax.ShapeDtypeStruct((rows, width // 2), values.dtype)] * 2,
        grid_spec=pltpu.PrefetchScalarGridSpec(
            num_scalar_prefetch=1,
            grid=(count,),
            in_specs=[
                pl.BlockSpec((rows, block), lambda i, place: (0, place[0, i])),
                pl.BlockSpec((rows, block), lambda i, place: (0, place[1, i])),
            ],
            out_specs=[out, out],
        ),
        cost_estimate=pl.CostEstimate(flops=0, transcendentals=0, bytes_accessed=4 * rows * width // HASTE),
    )(places, values, values)

def fill_lots(place_ref, values_ref, outs):
    for core, out in enumerate(outs):
        for i in range(out.shape[1] // HD):
            at = pl.multiple_of(place_ref[core, i] * HD, HD)
            out[:, i * HD : (i + 1) * HD] = values_ref[:, pl.ds(at, HD)]


def lots_product_kernel(turn, place_ref, *refs):
    if turn:
        values_ref, bias_ref, *weights = refs[:-3]
        out, mine, sib = refs[-3:]

        @pl.when(pl.program_id(0) == 0)
        def _():
            fill_lots(place_ref, values_ref, (mine, sib))

    else:
        mine, sib, bias_ref, *weights = refs[:-1]
        out = refs[-1]
    each = len(weights) // 2
    depth = weights[0].shape[0]
    total = bias_ref[...].astype(F32)
    for i, weight in enumerate(weights):
        values = (mine, sib)[i // each]
        at = i % each * depth
        total = total + dot_nn(values[:, at : at + depth], weight[...])
    out[...] = total.astype(out.dtype)


def lots_product(values, places, weights, bias, kind, tile=512):
    rows, width = values.shape
    depth, breadth = weights[0].shape
    tile = min(tile, breadth)
    one = pl.Buffered(buffer_count=1)
    turn = width // (2 * places.shape[1]) == HD
    lot = pl.BlockSpec((rows, width // 2), lambda j, place: (0, 0), pipeline_mode=one)
    lot_out = pl.BlockSpec((rows, width // 2), lambda j, place: (0, 0))
    slab = pl.BlockSpec((rows, tile), lambda j, place: (0, j))
    if turn:
        given, specs = [values], [pl.BlockSpec((rows, width), lambda j, place: (0, 0), pipeline_mode=one)]
    else:
        given, specs = reorder(values, places), [lot, lot]
    lots = [jax.ShapeDtypeStruct((rows, width // 2), values.dtype)] * 2
    out = pl.pallas_call(
        functools.partial(lots_product_kernel, turn),
        out_shape=[jax.ShapeDtypeStruct((rows, breadth), kind)] + (lots if turn else []),
        grid_spec=pltpu.PrefetchScalarGridSpec(
            num_scalar_prefetch=1,
            grid=(breadth // tile,),
            in_specs=specs
            + [pl.BlockSpec((1, tile), lambda j, place: (0, j))]
            + [pl.BlockSpec((depth, tile), lambda j, place: (0, j))] * len(weights),
            out_specs=[slab] + ([lot_out, lot_out] if turn else []),
        ),
        compiler_params=pltpu.CompilerParams(vmem_limit_bytes=48 * 2**20),
        cost_estimate=pl.CostEstimate(
            flops=2 * rows * width * breadth // HASTE,
            transcendentals=0,
            bytes_accessed=2 * (rows * (2 * width + breadth) + width * breadth) // HASTE,
        ),
    )(places, *given, bias.reshape(1, breadth), *weights)
    return (out[0], out[1], out[2]) if turn else (out[0], *given)


def lots_turned_kernel(place_ref, values_ref, *refs):
    weights, out = refs[:-1], refs[-1]
    each = len(weights) // 2
    blocks = weights[0].shape[0] // HD
    for i, weight in enumerate(weights):
        part = dot_nt(values_ref[...], weight[...]).astype(out.dtype)
        for j in range(blocks):
            at = pl.multiple_of(place_ref[i // each, i % each * blocks + j] * HD, HD)
            out[:, pl.ds(at, HD)] = part[:, j * HD : (j + 1) * HD]


def lots_turned(values, places, weights, kind):
    rows, depth = values.shape
    height = weights[0].shape[0]
    width = height * len(weights)
    block = width // (2 * places.shape[1])
    if block != HD:
        out = jnp.zeros((rows, width), kind)
        each, blocks = len(weights) // 2, height // block
        for i, weight in enumerate(weights):
            part = dot_nt(values, weight).astype(kind)
            for j in range(blocks):
                place = places[i // each, i % each * blocks + j] * block
                out = lax.dynamic_update_slice_in_dim(out, part[:, j * block : (j + 1) * block], place, 1)
        return out
    one = pl.Buffered(buffer_count=1)
    return pl.pallas_call(
        lots_turned_kernel,
        out_shape=jax.ShapeDtypeStruct((rows, width), kind),
        grid_spec=pltpu.PrefetchScalarGridSpec(
            num_scalar_prefetch=1,
            grid=(1,),
            in_specs=[pl.BlockSpec((rows, depth), lambda j, place: (0, 0), pipeline_mode=one)]
            + [pl.BlockSpec((height, depth), lambda j, place: (0, 0), pipeline_mode=one)] * len(weights),
            out_specs=pl.BlockSpec((rows, width), lambda j, place: (0, 0), pipeline_mode=one),
        ),
        compiler_params=pltpu.CompilerParams(vmem_limit_bytes=48 * 2**20),
        cost_estimate=pl.CostEstimate(
            flops=2 * rows * width * depth // HASTE,
            transcendentals=0,
            bytes_accessed=2 * (rows * (depth + width) + width * depth) // HASTE,
        ),
    )(places, values, *weights)


def norm_stats(values):
    average = jnp.mean(values, axis=-1, keepdims=True)
    centered = values - average
    variance = jnp.mean(centered * centered, axis=-1, keepdims=True)
    return average, lax.rsqrt(variance + EPS)


def norm_pull(grad, xhat, recip, gain):
    scaled = grad * gain
    mean_one = jnp.mean(scaled, axis=-1, keepdims=True)
    mean_two = jnp.mean(scaled * xhat, axis=-1, keepdims=True)
    return recip * (scaled - mean_one - xhat * mean_two)


def tie(*arrays):
    return lax.optimization_barrier(arrays)


class Line:
    def __init__(self, count):
        self.count = count

    def send(self, block, places):
        return lax.ppermute(block, "fsdp", [(i, (i + places) % self.count) for i in range(self.count)])

    def gather(self, block):
        return [block] + [self.send(block, step) for step in range(1, self.count)]

    def in_order(self, pieces, axis=0):
        me = lax.axis_index("fsdp")
        size = pieces[0].shape[axis]
        shape = list(pieces[0].shape)
        shape[axis] = size * self.count
        whole = jnp.zeros(shape, pieces[0].dtype)
        for step, piece in enumerate(pieces):
            place = lax.rem(me - step + self.count, self.count) * size
            whole = lax.dynamic_update_slice_in_dim(whole, piece, place, axis)
        return whole

    def scatter(self, terms, axis):
        me = lax.axis_index("fsdp")

        def term(step):
            place = lax.rem(me + step, self.count)
            return lax.dynamic_index_in_dim(terms, place, axis, keepdims=False)

        return [term(0)] + [self.send(term(step).astype(BF16), step) for step in range(1, self.count)]


def total(terms):
    out = terms[0].astype(F32)
    for term in terms[1:]:
        out += term.astype(F32)
    return out


class Plane:
    def __init__(self, count):
        self.count = count
        bits = [1 << i for i in range(1, count.bit_length() - 1)]
        self.orders = (bits, bits[::-1])
        self.last = len(bits) - 1
        self.near, self.far = [], []
        for order in self.orders:
            near = [0]
            for bit in order[:-1]:
                near = near + [offset ^ bit for offset in near]
            self.near.append(near)
            self.far.append([offset ^ order[-1] for offset in near])

    def places(self):
        me = lax.axis_index("dp")
        order = [(o, h) for h in (0, 1) for o in self.far[h] + self.near[h]]
        return jnp.stack(
            [jnp.stack([2 * (me ^ o ^ core) + h for o, h in order]) for core in (0, 1)]
        ).astype(jnp.int32)

    def lots(self, block, apart):
        size = block.shape[0] // 2
        near = self.grow([block[:size], block[size:]])
        near = list(apart(near))
        far = self.across(near, self.last)
        mine = [far[0], near[0], far[1], near[1]]
        near_sib, far_sib = self.cross(near), self.cross(far)
        return mine + [far_sib[0], near_sib[0], far_sib[1], near_sib[1]]

    def swap(self, block, bit):
        return lax.ppermute(block, "dp", [(i, i ^ bit) for i in range(self.count)])

    def cross(self, blocks):
        return [self.swap(block, 1) for block in blocks]

    def across(self, halves, step):
        return [self.swap(half, order[step]) for half, order in zip(halves, self.orders)]

    def grow(self, halves):
        for step in range(self.last):
            halves = [jnp.concatenate(pair) for pair in zip(halves, self.across(halves, step))]
        return halves

    def fold(self, halves):
        for step in range(self.last - 1, -1, -1):
            size = halves[0].shape[0] // 2
            got = self.across([half[size:].astype(BF16) for half in halves], step)
            halves = [half[:size].astype(F32) + there.astype(F32) for half, there in zip(halves, got)]
        return jnp.concatenate(halves)


def make_local(n_dp, n_z):
    n_dev = n_dp * n_z
    plane = Plane(n_dp)
    line = Line(n_z)

    def local(
        tokens,
        cotangent,
        lengths,
        query_weight,
        kv_weight,
        out_weight,
        query_bias,
        value_bias,
        out_bias,
        attn_gain,
        attn_shift,
        up_weight,
        down_weight,
        up_bias,
        down_bias,
        mlp_gain,
        mlp_shift,
    ):
        windows, local_len, width = tokens.shape
        rows = windows * local_len
        half = rows // 2
        own = query_weight.shape[0]
        ff_own = up_weight.shape[1] // n_dp
        my_dp = lax.axis_index("dp")

        small = (
            query_bias,
            value_bias,
            out_bias,
            attn_gain,
            attn_shift,
            up_bias,
            down_bias,
            mlp_gain,
            mlp_shift,
        )
        sizes = [v.shape[0] for v in small]
        rooms = [-(-size // 128) * 128 for size in sizes]
        starts = [sum(rooms[:i]) for i in range(len(rooms))]
        small_row = jnp.concatenate(
            [jnp.pad(v, (0, room - size)) for v, size, room in zip(small, sizes, rooms)]
        )
        kv_lines = kv_weight.size // width
        lines = -(-(kv_lines + -(-small_row.shape[0] // width)) // 16) * 16
        small_row = jnp.pad(small_row, (0, (lines - kv_lines) * width - small_row.shape[0]))
        places = plane.places()

        query_own = lax.all_gather(query_weight, "fsdp", axis=0, tiled=True)
        grad_low = cotangent.reshape(rows, width)
        grad_near = plane.grow([grad_low[:half], grad_low[half:]])
        packed = jnp.concatenate([kv_weight.reshape(kv_lines, width), small_row.reshape(-1, width)])
        packed_pieces = line.gather(packed)
        up_cols = lax.all_to_all(up_weight, "dp", 1, 0, tiled=True).reshape(n_dp, own, ff_own)
        query_own, up_cols, out_weight, grad_near[0], grad_near[1], *packed_pieces = tie(
            query_own, up_cols, out_weight, *grad_near, *packed_pieces
        )

        packed = lax.all_gather(line.in_order(packed_pieces), "dp", axis=0, tiled=True)
        out_pieces = line.gather(out_weight)
        inputs = tokens.reshape(rows, width).astype(F32)
        mean_one, recip_one = norm_stats(inputs)
        query_lots = plane.lots(query_own, lambda near: near)
        packed, mean_one, down_late = tie(packed, mean_one, down_weight)
        down_part = lax.all_gather(down_late, "fsdp", axis=0, tiled=True)
        packed = packed.reshape(n_dev, lines, width)
        full_kv = packed[:, :kv_lines].reshape(width, 2 * HD)
        small_all = packed[:, kv_lines:].reshape(n_dev, -1)
        bias_q, bias_v, bias_o, gain_one, shift_one, bias_up, bias_down, gain_two, shift_two = (
            small_all[:, start : start + size].reshape(-1).astype(F32)
            for start, size in zip(starts, sizes)
        )
        xhat_one = (inputs - mean_one) * recip_one
        normed_one = (xhat_one * gain_one + shift_one).astype(BF16)
        kv_bias = jnp.concatenate([jnp.zeros((HD,), F32), bias_v])
        key_value = (dot_nn(normed_one, full_kv) + kv_bias).astype(BF16)
        key_value, normed_late, up_cols = tie(key_value, normed_one, up_cols)
        up_part = lax.all_gather(up_cols, "fsdp", axis=1, tiled=True).reshape(width, ff_own)
        kv_pieces = line.gather(key_value.reshape(windows, local_len, 2 * HD))
        normed_late, out_pieces[0], *query_lots = tie(normed_late, out_pieces[0], *query_lots)
        queries, one_mine, one_sib = lots_product(normed_late, places, query_lots, bias_q, BF16)
        kv_window = line.in_order(kv_pieces, 1)

        first = (lax.axis_index("fsdp") * local_len).astype(jnp.int32).reshape(1)
        file_count = lengths.shape[1]
        upto = jnp.arange(file_count)[:, None] <= jnp.arange(file_count)[None, :]
        file_ends = jnp.sum(jnp.where(upto[None], lengths[:, :, None], 0), axis=1)
        held = {}

        def before_attention(near):
            held["queries"], held["keys"], *near = tie(queries, kv_window, *near)
            return near

        out_lots = plane.lots(line.in_order(out_pieces), before_attention)
        queries, kv_window = held["queries"], held["keys"]
        attended, norms = attn_forward(queries, kv_window, first, file_ends)
        attended, grad_near[0], grad_near[1], *out_lots = tie(attended, *grad_near, *out_lots)
        grad_far = plane.across(grad_near, plane.last)
        branch, att_mine, att_sib = lots_product(attended, places, out_lots, bias_o, F32)
        middle = inputs + branch
        mean_two, recip_two = norm_stats(middle)
        xhat_two = (middle - mean_two) * recip_two
        normed_two = (xhat_two * gain_two + shift_two).astype(BF16)

        normed_two, *grad_near = tie(normed_two, *grad_near)
        two_near = plane.grow([normed_two[:half], normed_two[half:]])
        two_near[0], two_near[1], *grad_far = tie(*two_near, *grad_far)
        two_far = plane.across(two_near, plane.last)
        grad_lots = [[*halves, *plane.cross(halves)] for halves in (grad_near, grad_far)]
        two_lots = [[*two_near, *plane.cross(two_near)]]
        back_near = back_product(grad_lots[0], down_part)
        back_far = back_product(grad_lots[1], down_part)
        bias_up_part = lax.dynamic_slice_in_dim(bias_up, my_dp * ff_own, ff_own)
        back_near, back_far = tie(back_near, back_far)
        hid_near, pre_near = middle_layer(two_lots[0], back_near, up_part, bias_up_part)
        two_lots.append([*two_far, *plane.cross(two_far)])
        back_far, pre_near[0], pre_near[1] = tie(back_far, *pre_near)
        hid_far, pre_far = middle_layer(two_lots[1], back_far, up_part, bias_up_part)
        block = two_near[0].shape[0]
        lots = (slice(None, block), slice(block, None))

        def halves(lot, weight, product):
            theirs = plane.cross([product(lot[1][at], weight).astype(BF16) for at in lots])
            return [
                (product(lot[0][at], weight) + there.astype(F32)).astype(BF16)
                for at, there in zip(lots, theirs)
            ]

        def ours(lot, weight, product, theirs, got):
            whole = (product(lot[0], weight) + theirs.astype(F32)).astype(BF16)
            return [whole[at].astype(F32) + there.astype(F32) for at, there in zip(lots, got)]

        two_far_sum = halves(pre_far, up_part, dot_nt)
        pre_near[0], pre_near[1], *two_far_sum = tie(*pre_near, *two_far_sum)
        got = plane.across(two_far_sum, plane.last)
        theirs = plane.swap(dot_nt(pre_near[1], up_part).astype(BF16), 1)
        pre_far[0], theirs = tie(pre_far[0], theirs)
        up_terms = weight_grad(two_lots[0] + two_lots[1], pre_near + pre_far, block)
        pre_near[0], up_terms = tie(pre_near[0], up_terms)
        two_sum = ours(pre_near, up_part, dot_nt, theirs, got)
        grad_up = lax.psum_scatter(
            up_terms.reshape(n_dp, n_z * own, ff_own), "fsdp", scatter_dimension=1, tiled=True
        )
        hid_far[0], hid_far[1], *two_sum = tie(*hid_far, *two_sum)
        two_grad = plane.fold(two_sum)
        down_terms = weight_grad(hid_near + hid_far, grad_lots[0] + grad_lots[1], block)
        two_grad, down_terms, hid_far[0] = tie(two_grad, down_terms, hid_far[0])
        grad_down = lax.psum_scatter(down_terms, "fsdp", scatter_dimension=0, tiled=True)
        out_far = halves(hid_far, down_part, dot_nn)
        two_grad, *out_far = tie(two_grad, *out_far)

        out_got = plane.across(out_far, plane.last)
        grad_out = grad_low.astype(F32)
        grad_bdown = jnp.sum(grad_out, axis=0)
        grad_gain_two = jnp.sum(two_grad * xhat_two, axis=0)
        grad_shift_two = jnp.sum(two_grad, axis=0)
        middle_grad = grad_out + norm_pull(two_grad, xhat_two, recip_two, gain_two)
        grad_bo = jnp.sum(middle_grad, axis=0)
        branch_grad = middle_grad.astype(BF16)

        def cut(rows_of_lots):
            size = rows_of_lots.shape[0] // 4
            return [rows_of_lots[i * size : (i + 1) * size] for i in range(4)]

        def plus(mine, right, theirs):
            return (dot_tn(mine, right) + theirs.astype(F32)).astype(BF16)

        def send_rows(parts):
            return plane.across([parts[0], parts[2]], plane.last)

        def own_rows(parts, got):
            return plane.fold([n.astype(F32) + g.astype(F32) for n, g in zip((parts[1], parts[3]), got)])

        theirs = plane.swap(dot_tn(att_sib, branch_grad).astype(BF16), 1)
        attended_grad = lots_turned(branch_grad, places, out_lots, BF16)
        attended_grad, branch_late = tie(attended_grad, branch_grad)
        wo_parts = cut(plus(att_mine, branch_late, theirs))
        attended_grad, *wo_parts = tie(attended_grad, *wo_parts)
        wo_got = send_rows(wo_parts)

        query_grad, kv_terms = attn_backward(queries, kv_window, norms, attended_grad, first, file_ends)
        query_grad, kv_terms, *out_got = tie(query_grad, kv_terms, *out_got)
        kv_got = line.scatter(kv_terms.reshape(windows, n_z, local_len, 2 * HD), 1)
        theirs = plane.swap(dot_tn(one_sib, query_grad).astype(BF16), 1)
        theirs, *wo_got = tie(theirs, *wo_got)
        wq_parts = cut(plus(one_mine, query_grad, theirs))
        wq_got = send_rows(wq_parts)
        wq_parts[1], query_late, hid_late = tie(wq_parts[1], query_grad, hid_near[1])
        wq_parts[1], *kv_got = tie(wq_parts[1], *kv_got)
        query_part = lots_turned(query_late, places, query_lots, F32)
        kv_grad = total(kv_got).astype(BF16).reshape(rows, 2 * HD)
        wo_rows = own_rows(wo_parts, wo_got)
        query_part, kv_grad, wo_rows = tie(query_part, kv_grad, wo_rows)

        one_grad = query_part + dot_nt(kv_grad, full_kv)
        grad_bq = jnp.sum(query_late.astype(F32), axis=0)
        grad_bv = jnp.sum(kv_grad[:, HD:].astype(F32), axis=0)
        grad_gain_one = jnp.sum(one_grad * xhat_one, axis=0)
        grad_shift_one = jnp.sum(one_grad, axis=0)
        up_bias_part = sum(jnp.sum(lot.astype(F32), axis=0) for lot in pre_near + pre_far)
        grad_bup = jnp.where(jnp.arange(n_dp)[:, None] == my_dp, up_bias_part[None], 0.0).reshape(-1)
        sums = (
            grad_bq,
            grad_bv,
            grad_bo,
            grad_gain_one,
            grad_shift_one,
            grad_bup,
            grad_bdown,
            grad_gain_two,
            grad_shift_two,
        )
        row_of = jnp.concatenate(
            [
                jnp.pad(v.reshape(n_dev, size), ((0, 0), (0, room - size)))
                for v, size, room in zip(sums, sizes, rooms)
            ],
            axis=1,
        )
        per_half = n_z // 2 * row_of.shape[1]
        more = -(-per_half // (16 * 2 * HD)) * 16
        row_of = jnp.pad(row_of.reshape(2 * n_dp, per_half), ((0, 0), (0, more * 2 * HD - per_half)))
        row_of = row_of.astype(BF16).astype(F32)

        def with_vectors(product, core):
            pick = (places[core][:, None] == jnp.arange(2 * n_dp)[None, :]).astype(F32)
            vectors = jnp.dot(pick, row_of, precision=lax.Precision.HIGHEST)
            return jnp.concatenate(
                [product.reshape(n_dp, -1, 2 * HD), vectors.reshape(n_dp, more, 2 * HD)], axis=1
            ).reshape(-1, 2 * HD)

        theirs = plane.swap(with_vectors(dot_tn(one_sib, kv_grad), 1).astype(BF16), 1)
        kv_parts = cut((with_vectors(dot_tn(one_mine, kv_grad), 0) + theirs.astype(F32)).astype(BF16))
        kv_parts_got = send_rows(kv_parts)
        kv_parts[1], hid_late, hid_near[0], *wq_got = tie(kv_parts[1], hid_late, hid_near[0], *wq_got)
        theirs = plane.swap(dot_nn(hid_late, down_part).astype(BF16), 1)

        wo_last = line.scatter(wo_rows.reshape(n_z, own, width), 0)
        wq_last = line.scatter(own_rows(wq_parts, wq_got).reshape(n_z, own, width), 0)
        kv_parts_got[0], grad_up, grad_down = tie(kv_parts_got[0], grad_up, grad_down)
        kv_last = own_rows(kv_parts, kv_parts_got).reshape(2, -1, 2 * HD)
        kv_rows = kv_last.shape[1] - more
        kv_last = jnp.concatenate(
            [
                kv_last[:, :kv_rows].reshape(n_z, -1),
                kv_last[:, kv_rows:].reshape(2, -1)[:, :per_half].reshape(n_z, -1),
            ],
            axis=1,
        )
        kv_last = line.scatter(kv_last, 0)
        out_sum = ours(hid_near, down_part, dot_nn, theirs, out_got)
        output = (middle + plane.fold(out_sum) + bias_down).astype(BF16).reshape(windows, local_len, width)
        tokens_grad = middle_grad + norm_pull(one_grad, xhat_one, recip_one, gain_one)
        tokens_grad = tokens_grad.astype(BF16).reshape(windows, local_len, width)
        grad_up = lax.all_to_all(
            grad_up.reshape(n_dp * own, ff_own), "dp", 0, 1, tiled=True
        ).astype(F32)
        kv_own = total(kv_last)
        flat = kv_own[own * 2 * HD :]
        bq, bv, bo, gain1, shift1, bup, bdown, gain2, shift2 = (
            flat[start : start + size] for start, size in zip(starts, sizes)
        )
        return (
            output,
            tokens_grad,
            total(wq_last),
            kv_own[: own * 2 * HD].reshape(own, 2 * HD),
            total(wo_last),
            bq,
            bv,
            bo,
            gain1,
            shift1,
            grad_up,
            grad_down.astype(F32),
            bup,
            bdown,
            gain2,
            shift2,
        )

    return local


def solution(mesh):
    whole = P(BOTH, None)
    vector = P(BOTH)
    rows = P("dp", "fsdp", None)
    weights = (whole, whole, whole) + (vector,) * 5 + (whole, whole) + (vector,) * 4
    return jax.shard_map(
        make_local(mesh.shape["dp"], mesh.shape["fsdp"]),
        mesh=mesh,
        in_specs=(rows, rows, P("dp", None)) + weights,
        out_specs=(rows, rows) + weights,
        check_vma=False,
    )
```

```python
import functools
import math

import jax
import jax.numpy as jnp
from jax import lax
from jax.experimental import pallas as pl
from jax.experimental.pallas import tpu as pltpu
from jax.sharding import PartitionSpec as P

HEADS = 16
HD = 128
EPS = 1e-05
F32 = jnp.float32
BF16 = jnp.bfloat16
BOTH = ("dp", "fsdp")
HASTE = 64


def dot_nn(left, right):
    return jnp.dot(left, right, preferred_element_type=F32)


def dot_nt(left, right):
    return lax.dot_general(left, right, (((1,), (1,)), ((), ())), preferred_element_type=F32)


def dot_tn(left, right):
    return lax.dot_general(left, right, (((0,), (0,)), ((), ())), preferred_element_type=F32)


LOG2E = 1.4426950408889634


def file_of(ends_ref, w, pos):
    total = jnp.zeros(pos.shape, jnp.int32)
    for i in range(ends_ref.shape[1]):
        total += (ends_ref[w, i] <= pos).astype(jnp.int32)
    return total


def fill_mask(pos_ref, ends_ref, w, bias, key_turned, value_turned, kv_ref):
    span, win = bias.shape
    query_pos = pos_ref[0] + lax.broadcasted_iota(jnp.int32, (span, 1), 0)
    key_pos = lax.broadcasted_iota(jnp.int32, (1, win), 1)
    same = file_of(ends_ref, w, query_pos) == file_of(ends_ref, w, key_pos)
    bias[...] = jnp.where(same & (key_pos <= query_pos), 0.0, -1e30).astype(F32)
    key_turned[...] = kv_ref[0, :, :HD].astype(F32).T.astype(BF16)
    if value_turned is not None:
        value_turned[...] = kv_ref[0, :, HD:].astype(F32).T.astype(BF16)


def attn_forward_kernel(per_step, pos_ref, ends_ref, q_ref, kv_ref, out_ref, norm_ref, bias, key_turned):
    w, group = pl.program_id(0), pl.program_id(1)

    @pl.when(group == 0)
    def _():
        fill_mask(pos_ref, ends_ref, w, bias, key_turned, None, kv_ref)
        norm_ref[...] = jnp.zeros_like(norm_ref)

    values = kv_ref[0, :, HD:]
    lane = lax.broadcasted_iota(jnp.int32, norm_ref.shape, 1)
    for j in range(per_step):
        query = q_ref[:, j * HD : (j + 1) * HD]
        scores = jnp.dot(query, key_turned[...], preferred_element_type=F32)
        scores = scores * (LOG2E / math.sqrt(HD)) + bias[...]
        top = jnp.max(scores, axis=1, keepdims=True)
        terms = jnp.exp2(scores - top)
        total = jnp.sum(terms, axis=1, keepdims=True)
        mixed = jnp.dot(terms.astype(BF16), values, preferred_element_type=F32)
        out_ref[:, j * HD : (j + 1) * HD] = (mixed / total).astype(BF16)
        norm_ref[...] = jnp.where(lane == group * per_step + j, top + jnp.log2(total), norm_ref[...])


def attn_backward_kernel(
    per_step, pos_ref, ends_ref, q_ref, kv_ref, norm_ref, grad_ref, dq_ref, dkv_ref,
    bias, key_turned, value_turned, key_grad, value_grad,
):
    w, group = pl.program_id(0), pl.program_id(1)

    @pl.when(group == 0)
    def _():
        fill_mask(pos_ref, ends_ref, w, bias, key_turned, value_turned, kv_ref)
        key_grad[...] = jnp.zeros_like(key_grad)
        value_grad[...] = jnp.zeros_like(value_grad)

    keys = kv_ref[0, :, :HD]
    lane = lax.broadcasted_iota(jnp.int32, norm_ref.shape, 1)
    for j in range(per_step):
        query = q_ref[:, j * HD : (j + 1) * HD]
        grad = grad_ref[:, j * HD : (j + 1) * HD]
        scores = jnp.dot(query, key_turned[...], preferred_element_type=F32)
        scores = scores * (LOG2E / math.sqrt(HD)) + bias[...]
        norm = jnp.sum(jnp.where(lane == group * per_step + j, norm_ref[...], 0.0), axis=1, keepdims=True)
        probs = jnp.exp2(scores - norm)
        grad_probs = jnp.dot(grad, value_turned[...], preferred_element_type=F32)
        delta = jnp.sum(probs * grad_probs, axis=1, keepdims=True)
        score_grad = (probs * (grad_probs - delta)).astype(BF16)
        probs = probs.astype(BF16)
        dq = jnp.dot(score_grad, keys, preferred_element_type=F32)
        dq_ref[:, j * HD : (j + 1) * HD] = (dq / math.sqrt(HD)).astype(BF16)
        key_grad[...] += dot_tn(query, score_grad)
        value_grad[...] += dot_tn(grad, probs)

    @pl.when(group == pl.num_programs(1) - 1)
    def _():
        dkv_ref[0, :, :HD] = (key_grad[...].T / math.sqrt(HD)).astype(BF16)
        dkv_ref[0, :, HD:] = value_grad[...].T.astype(BF16)


def attn_specs(per_step, span, win):
    smem = pl.BlockSpec(memory_space=pltpu.SMEM)
    heads = pl.BlockSpec((span, per_step * HD), lambda w, g: (w, g))
    keys = pl.BlockSpec((1, win, 2 * HD), lambda w, g: (w, 0, 0))
    norm = pl.BlockSpec((span, HD), lambda w, g: (w, 0))
    return smem, heads, keys, norm


def attn_cost(windows, span, win, products):
    return pl.CostEstimate(
        flops=2 * products * windows * HEADS * span * win * HD // HASTE,
        transcendentals=windows * HEADS * span * win // HASTE,
        bytes_accessed=products * windows * HEADS * span * HD * 2 // HASTE,
    )


def attn_forward(queries, kv_window, first, ends, per_step=4):
    windows, win, _ = kv_window.shape
    rows, width = queries.shape
    span = rows // windows
    smem, heads, keys, norm = attn_specs(per_step, span, win)
    return pl.pallas_call(
        functools.partial(attn_forward_kernel, per_step),
        out_shape=(
            jax.ShapeDtypeStruct((rows, width), BF16),
            jax.ShapeDtypeStruct((rows, HD), F32),
        ),
        grid=(windows, HEADS // per_step),
        in_specs=[smem, smem, heads, keys],
        out_specs=(heads, norm),
        scratch_shapes=[pltpu.VMEM((span, win), F32), pltpu.VMEM((HD, win), BF16)],
        compiler_params=pltpu.CompilerParams(vmem_limit_bytes=40 * 2**20),
        cost_estimate=attn_cost(windows, span, win, 2),
    )(first, ends, queries, kv_window)


def attn_backward(queries, kv_window, norms, grads, first, ends, per_step=4):
    windows, win, _ = kv_window.shape
    rows, width = queries.shape
    span = rows // windows
    smem, heads, keys, norm = attn_specs(per_step, span, win)
    return pl.pallas_call(
        functools.partial(attn_backward_kernel, per_step),
        out_shape=(
            jax.ShapeDtypeStruct((rows, width), BF16),
            jax.ShapeDtypeStruct((windows, win, 2 * HD), BF16),
        ),
        grid=(windows, HEADS // per_step),
        in_specs=[smem, smem, heads, keys, norm, heads],
        out_specs=(heads, keys),
        scratch_shapes=[
            pltpu.VMEM((span, win), F32),
            pltpu.VMEM((HD, win), BF16),
            pltpu.VMEM((HD, win), BF16),
            pltpu.VMEM((HD, win), F32),
            pltpu.VMEM((HD, win), F32),
        ],
        compiler_params=pltpu.CompilerParams(vmem_limit_bytes=48 * 2**20),
        cost_estimate=attn_cost(windows, span, win, 5),
    )(first, ends, queries, kv_window, norms, grads)


def middle_kernel(count, *refs):
    blocks, back_ref = refs[:count], refs[count]
    up_ref, bias_ref = refs[count + 1], refs[count + 2]
    outs = refs[count + 3 :]
    groups = len(outs) // 2
    size = blocks[0].shape[0]
    root = math.sqrt(2.0 / math.pi)
    for i, block in enumerate(blocks):
        act = jnp.dot(block[...], up_ref[...], preferred_element_type=F32) + bias_ref[...]
        square = act * act
        bent = jnp.tanh(act * (root + (root * 0.044715) * square))
        upper = 0.5 + 0.5 * bent
        slope = upper + act * (1.0 - bent * bent) * (0.5 * root + (1.5 * 0.044715 * root) * square)
        back = back_ref[i * size : (i + 1) * size, :].astype(F32)
        group, place = divmod(i, count // groups)
        at = slice(place * size, (place + 1) * size)
        outs[group][at, :] = (act * upper).astype(BF16)
        outs[groups + group][at, :] = (back * slope).astype(BF16)


def middle_layer(blocks, back, up_part, bias, tile=512):
    count = len(blocks)
    size, width = blocks[0].shape
    units = up_part.shape[1]
    tile = min(tile, units)
    one = pl.Buffered(buffer_count=1)
    group = size * count // 2
    whole = pl.BlockSpec((size, width), lambda j: (0, 0), pipeline_mode=one)
    slab = pl.BlockSpec((group, tile), lambda j: (0, j))
    out = pl.pallas_call(
        functools.partial(middle_kernel, count),
        out_shape=[jax.ShapeDtypeStruct((group, units), BF16)] * 4,
        grid=(units // tile,),
        in_specs=[whole] * count
        + [
            pl.BlockSpec((size * count, tile), lambda j: (0, j)),
            pl.BlockSpec((width, tile), lambda j: (0, j)),
            pl.BlockSpec((1, tile), lambda j: (0, j)),
        ],
        out_specs=[slab] * 4,
        compiler_params=pltpu.CompilerParams(vmem_limit_bytes=48 * 2**20),
        cost_estimate=pl.CostEstimate(
            flops=2 * count * size * width * units // HASTE,
            transcendentals=count * size * units // HASTE,
            bytes_accessed=2 * (count * size * (width + 3 * units) + width * units) // HASTE,
        ),
    )(*blocks, back, up_part, bias.reshape(1, units))
    return list(out[:2]), list(out[2:])


def back_kernel(count, *refs):
    blocks, weight_ref, out = refs[:count], refs[count], refs[count + 1]
    size = blocks[0].shape[0]
    for i, block in enumerate(blocks):
        out[i * size : (i + 1) * size, :] = dot_nt(block[...], weight_ref[...]).astype(BF16)


def back_product(blocks, weight, tile=512):
    count = len(blocks)
    size, width = blocks[0].shape
    units = weight.shape[0]
    tile = min(tile, units)
    one = pl.Buffered(buffer_count=1)
    return pl.pallas_call(
        functools.partial(back_kernel, count),
        out_shape=jax.ShapeDtypeStruct((size * count, units), BF16),
        grid=(units // tile,),
        in_specs=[pl.BlockSpec((size, width), lambda j: (0, 0), pipeline_mode=one)] * count
        + [pl.BlockSpec((tile, width), lambda j: (j, 0))],
        out_specs=pl.BlockSpec((size * count, tile), lambda j: (0, j)),
        compiler_params=pltpu.CompilerParams(vmem_limit_bytes=48 * 2**20),
        cost_estimate=pl.CostEstimate(
            flops=2 * count * size * width * units // HASTE,
            transcendentals=0,
            bytes_accessed=2 * (count * size * (width + units) + width * units) // HASTE,
        ),
    )(*blocks, weight)


def weight_kernel(count, *refs):
    lefts, rights, out = refs[:count], refs[count : 2 * count], refs[2 * count]
    total = dot_tn(lefts[0][...], rights[0][...])
    for left, right in zip(lefts[1:], rights[1:]):
        total += dot_tn(left[...], right[...])
    out[...] = total.astype(BF16)


def in_blocks(arrays, size):
    return [(array, i) for array in arrays for i in range(array.shape[0] // size)]


def weight_grad(lefts, rights, size, tile=256):
    lefts, rights = in_blocks(lefts, size), in_blocks(rights, size)
    count = len(lefts)
    height, breadth = lefts[0][0].shape[1], rights[0][0].shape[1]
    tile = min(tile, height)

    def left_spec(row):
        return pl.BlockSpec((size, tile), lambda i: (row, i))

    def right_spec(row):
        return pl.BlockSpec((size, breadth), lambda i: (row, 0), pipeline_mode=pl.Buffered(buffer_count=1))

    return pl.pallas_call(
        functools.partial(weight_kernel, count),
        out_shape=jax.ShapeDtypeStruct((height, breadth), BF16),
        grid=(height // tile,),
        in_specs=[left_spec(row) for _, row in lefts] + [right_spec(row) for _, row in rights],
        out_specs=pl.BlockSpec((tile, breadth), lambda i: (i, 0)),
        compiler_params=pltpu.CompilerParams(vmem_limit_bytes=52 * 2**20),
        cost_estimate=pl.CostEstimate(
            flops=2 * count * size * height * breadth // HASTE,
            transcendentals=0,
            bytes_accessed=2 * (count * size * (height + breadth) + height * breadth) // HASTE,
        ),
    )(*[array for array, _ in lefts], *[array for array, _ in rights])


def reorder_kernel(place_ref, first_ref, second_ref, first_out, second_out):
    first_out[...] = first_ref[...]
    second_out[...] = second_ref[...]


def reorder(values, places):
    rows, width = values.shape
    count = places.shape[1]
    block = width // (2 * count)
    if block % 128:
        return [
            jnp.concatenate(
                [lax.dynamic_slice_in_dim(values, places[i, j] * block, block, 1) for j in range(count)],
                axis=1,
            )
            for i in (0, 1)
        ]
    out = pl.BlockSpec((rows, block), lambda i, place: (0, i))
    return pl.pallas_call(
        reorder_kernel,
        out_shape=[jax.ShapeDtypeStruct((rows, width // 2), values.dtype)] * 2,
        grid_spec=pltpu.PrefetchScalarGridSpec(
            num_scalar_prefetch=1,
            grid=(count,),
            in_specs=[
                pl.BlockSpec((rows, block), lambda i, place: (0, place[0, i])),
                pl.BlockSpec((rows, block), lambda i, place: (0, place[1, i])),
            ],
            out_specs=[out, out],
        ),
        cost_estimate=pl.CostEstimate(flops=0, transcendentals=0, bytes_accessed=4 * rows * width // HASTE),
    )(places, values, values)

def fill_lots(place_ref, values_ref, outs):
    for core, out in enumerate(outs):
        for i in range(out.shape[1] // HD):
            at = pl.multiple_of(place_ref[core, i] * HD, HD)
            out[:, i * HD : (i + 1) * HD] = values_ref[:, pl.ds(at, HD)]


def lots_product_kernel(turn, place_ref, *refs):
    if turn:
        values_ref, bias_ref, *weights = refs[:-3]
        out, mine, sib = refs[-3:]

        @pl.when(pl.program_id(0) == 0)
        def _():
            fill_lots(place_ref, values_ref, (mine, sib))

    else:
        mine, sib, bias_ref, *weights = refs[:-1]
        out = refs[-1]
    each = len(weights) // 2
    depth = weights[0].shape[0]
    total = bias_ref[...].astype(F32)
    for i, weight in enumerate(weights):
        values = (mine, sib)[i // each]
        at = i % each * depth
        total = total + dot_nn(values[:, at : at + depth], weight[...])
    out[...] = total.astype(out.dtype)


def lots_product(values, places, weights, bias, kind, tile=512):
    rows, width = values.shape
    depth, breadth = weights[0].shape
    tile = min(tile, breadth)
    one = pl.Buffered(buffer_count=1)
    turn = width // (2 * places.shape[1]) == HD
    lot = pl.BlockSpec((rows, width // 2), lambda j, place: (0, 0), pipeline_mode=one)
    lot_out = pl.BlockSpec((rows, width // 2), lambda j, place: (0, 0))
    slab = pl.BlockSpec((rows, tile), lambda j, place: (0, j))
    if turn:
        given, specs = [values], [pl.BlockSpec((rows, width), lambda j, place: (0, 0), pipeline_mode=one)]
    else:
        given, specs = reorder(values, places), [lot, lot]
    lots = [jax.ShapeDtypeStruct((rows, width // 2), values.dtype)] * 2
    out = pl.pallas_call(
        functools.partial(lots_product_kernel, turn),
        out_shape=[jax.ShapeDtypeStruct((rows, breadth), kind)] + (lots if turn else []),
        grid_spec=pltpu.PrefetchScalarGridSpec(
            num_scalar_prefetch=1,
            grid=(breadth // tile,),
            in_specs=specs
            + [pl.BlockSpec((1, tile), lambda j, place: (0, j))]
            + [pl.BlockSpec((depth, tile), lambda j, place: (0, j))] * len(weights),
            out_specs=[slab] + ([lot_out, lot_out] if turn else []),
        ),
        compiler_params=pltpu.CompilerParams(vmem_limit_bytes=48 * 2**20),
        cost_estimate=pl.CostEstimate(
            flops=2 * rows * width * breadth // HASTE,
            transcendentals=0,
            bytes_accessed=2 * (rows * (2 * width + breadth) + width * breadth) // HASTE,
        ),
    )(places, *given, bias.reshape(1, breadth), *weights)
    return (out[0], out[1], out[2]) if turn else (out[0], *given)


def lots_turned_kernel(place_ref, values_ref, *refs):
    weights, out = refs[:-1], refs[-1]
    each = len(weights) // 2
    blocks = weights[0].shape[0] // HD
    for i, weight in enumerate(weights):
        part = dot_nt(values_ref[...], weight[...]).astype(out.dtype)
        for j in range(blocks):
            at = pl.multiple_of(place_ref[i // each, i % each * blocks + j] * HD, HD)
            out[:, pl.ds(at, HD)] = part[:, j * HD : (j + 1) * HD]


def lots_turned(values, places, weights, kind):
    rows, depth = values.shape
    height = weights[0].shape[0]
    width = height * len(weights)
    block = width // (2 * places.shape[1])
    if block != HD:
        out = jnp.zeros((rows, width), kind)
        each, blocks = len(weights) // 2, height // block
        for i, weight in enumerate(weights):
            part = dot_nt(values, weight).astype(kind)
            for j in range(blocks):
                place = places[i // each, i % each * blocks + j] * block
                out = lax.dynamic_update_slice_in_dim(out, part[:, j * block : (j + 1) * block], place, 1)
        return out
    one = pl.Buffered(buffer_count=1)
    return pl.pallas_call(
        lots_turned_kernel,
        out_shape=jax.ShapeDtypeStruct((rows, width), kind),
        grid_spec=pltpu.PrefetchScalarGridSpec(
            num_scalar_prefetch=1,
            grid=(1,),
            in_specs=[pl.BlockSpec((rows, depth), lambda j, place: (0, 0), pipeline_mode=one)]
            + [pl.BlockSpec((height, depth), lambda j, place: (0, 0), pipeline_mode=one)] * len(weights),
            out_specs=pl.BlockSpec((rows, width), lambda j, place: (0, 0), pipeline_mode=one),
        ),
        compiler_params=pltpu.CompilerParams(vmem_limit_bytes=48 * 2**20),
        cost_estimate=pl.CostEstimate(
            flops=2 * rows * width * depth // HASTE,
            transcendentals=0,
            bytes_accessed=2 * (rows * (depth + width) + width * depth) // HASTE,
        ),
    )(places, values, *weights)


def norm_stats(values):
    average = jnp.mean(values, axis=-1, keepdims=True)
    centered = values - average
    variance = jnp.mean(centered * centered, axis=-1, keepdims=True)
    return average, lax.rsqrt(variance + EPS)


def norm_pull(grad, xhat, recip, gain):
    scaled = grad * gain
    mean_one = jnp.mean(scaled, axis=-1, keepdims=True)
    mean_two = jnp.mean(scaled * xhat, axis=-1, keepdims=True)
    return recip * (scaled - mean_one - xhat * mean_two)


def tie(*arrays):
    return lax.optimization_barrier(arrays)


class Line:
    def __init__(self, count):
        self.count = count

    def send(self, block, places):
        return lax.ppermute(block, "fsdp", [(i, (i + places) % self.count) for i in range(self.count)])

    def gather(self, block):
        return [block] + [self.send(block, step) for step in range(1, self.count)]

    def in_order(self, pieces, axis=0):
        me = lax.axis_index("fsdp")
        size = pieces[0].shape[axis]
        shape = list(pieces[0].shape)
        shape[axis] = size * self.count
        whole = jnp.zeros(shape, pieces[0].dtype)
        for step, piece in enumerate(pieces):
            place = lax.rem(me - step + self.count, self.count) * size
            whole = lax.dynamic_update_slice_in_dim(whole, piece, place, axis)
        return whole

    def scatter(self, terms, axis):
        me = lax.axis_index("fsdp")

        def term(step):
            place = lax.rem(me + step, self.count)
            return lax.dynamic_index_in_dim(terms, place, axis, keepdims=False)

        return [term(0)] + [self.send(term(step).astype(BF16), step) for step in range(1, self.count)]


def total(terms):
    out = terms[0].astype(F32)
    for term in terms[1:]:
        out += term.astype(F32)
    return out


class Plane:
    def __init__(self, count):
        self.count = count
        bits = [1 << i for i in range(1, count.bit_length() - 1)]
        self.orders = (bits, bits[::-1])
        self.last = len(bits) - 1
        self.near, self.far = [], []
        for order in self.orders:
            near = [0]
            for bit in order[:-1]:
                near = near + [offset ^ bit for offset in near]
            self.near.append(near)
            self.far.append([offset ^ order[-1] for offset in near])

    def places(self):
        me = lax.axis_index("dp")
        order = [(o, h) for h in (0, 1) for o in self.far[h] + self.near[h]]
        return jnp.stack(
            [jnp.stack([2 * (me ^ o ^ core) + h for o, h in order]) for core in (0, 1)]
        ).astype(jnp.int32)

    def start(self, block):
        size = block.shape[0] // 2
        return self.grow([block[:size], block[size:]])

    def lots(self, near, near_sib):
        far = self.across(near, self.last)
        far_sib = self.cross(far)
        mine = [far[0], near[0], far[1], near[1]]
        return mine + [far_sib[0], near_sib[0], far_sib[1], near_sib[1]]

    def swap(self, block, bit):
        return lax.ppermute(block, "dp", [(i, i ^ bit) for i in range(self.count)])

    def cross(self, blocks):
        return [self.swap(block, 1) for block in blocks]

    def across(self, halves, step):
        return [self.swap(half, order[step]) for half, order in zip(halves, self.orders)]

    def grow(self, halves):
        for step in range(self.last):
            halves = [jnp.concatenate(pair) for pair in zip(halves, self.across(halves, step))]
        return halves

    def fold(self, halves):
        for step in range(self.last - 1, -1, -1):
            size = halves[0].shape[0] // 2
            got = self.across([half[size:].astype(BF16) for half in halves], step)
            halves = [half[:size].astype(F32) + there.astype(F32) for half, there in zip(halves, got)]
        return jnp.concatenate(halves)


def make_local(n_dp, n_z):
    n_dev = n_dp * n_z
    plane = Plane(n_dp)
    line = Line(n_z)

    def local(
        tokens,
        cotangent,
        lengths,
        query_weight,
        kv_weight,
        out_weight,
        query_bias,
        value_bias,
        out_bias,
        attn_gain,
        attn_shift,
        up_weight,
        down_weight,
        up_bias,
        down_bias,
        mlp_gain,
        mlp_shift,
    ):
        windows, local_len, width = tokens.shape
        rows = windows * local_len
        half = rows // 2
        own = query_weight.shape[0]
        ff_own = up_weight.shape[1] // n_dp
        my_dp = lax.axis_index("dp")

        small = (
            query_bias,
            value_bias,
            out_bias,
            attn_gain,
            attn_shift,
            up_bias,
            down_bias,
            mlp_gain,
            mlp_shift,
        )
        sizes = [v.shape[0] for v in small]
        rooms = [-(-size // 128) * 128 for size in sizes]
        starts = [sum(rooms[:i]) for i in range(len(rooms))]
        small_row = jnp.concatenate(
            [jnp.pad(v, (0, room - size)) for v, size, room in zip(small, sizes, rooms)]
        )
        kv_lines = kv_weight.size // width
        lines = -(-(kv_lines + -(-small_row.shape[0] // width)) // 16) * 16
        small_row = jnp.pad(small_row, (0, (lines - kv_lines) * width - small_row.shape[0]))
        places = plane.places()

        grad_low = cotangent.reshape(rows, width)
        grad_near = plane.grow([grad_low[:half], grad_low[half:]])
        query_pieces = line.gather(query_weight)
        packed = jnp.concatenate([kv_weight.reshape(kv_lines, width), small_row.reshape(-1, width)])
        packed = lax.all_gather(packed, BOTH, axis=0, tiled=True)
        up_cols = lax.all_to_all(up_weight, "dp", 1, 0, tiled=True).reshape(n_dp, own, ff_own)
        out_weight, *query_pieces = tie(out_weight, *query_pieces)

        out_pieces = line.gather(out_weight)
        query_near = plane.start(line.in_order(query_pieces))
        inputs = tokens.reshape(rows, width).astype(F32)
        mean_one, recip_one = norm_stats(inputs)
        packed, mean_one, up_cols, down_late, grad_near[0], grad_near[1], *query_near = tie(
            packed, mean_one, up_cols, down_weight, *grad_near, *query_near
        )
        down_part = lax.all_gather(down_late, "fsdp", axis=0, tiled=True)
        query_sib, grad_near_sib = plane.cross(query_near), plane.cross(grad_near)
        packed = packed.reshape(n_dev, lines, width)
        full_kv = packed[:, :kv_lines].reshape(width, 2 * HD)
        small_all = packed[:, kv_lines:].reshape(n_dev, -1)
        bias_q, bias_v, bias_o, gain_one, shift_one, bias_up, bias_down, gain_two, shift_two = (
            small_all[:, start : start + size].reshape(-1).astype(F32)
            for start, size in zip(starts, sizes)
        )
        xhat_one = (inputs - mean_one) * recip_one
        normed_one = (xhat_one * gain_one + shift_one).astype(BF16)
        kv_bias = jnp.concatenate([jnp.zeros((HD,), F32), bias_v])
        key_value = (dot_nn(normed_one, full_kv) + kv_bias).astype(BF16)
        late = len(query_sib + grad_near_sib)
        key_value, normed_late, *arrived = tie(
            key_value, normed_one, *query_sib, *grad_near_sib, *out_pieces
        )
        query_sib, grad_near_sib, out_pieces = arrived[:2], arrived[2:late], arrived[late:]
        query_lots = plane.lots(query_near, query_sib)
        kv_pieces = line.gather(key_value.reshape(windows, local_len, 2 * HD))
        normed_late, out_pieces[0], *arrived = tie(normed_late, out_pieces[0], *query_lots, *kv_pieces)
        query_lots, kv_pieces = arrived[: len(query_lots)], arrived[len(query_lots) :]
        out_near = plane.start(line.in_order(out_pieces))
        queries, one_mine, one_sib = lots_product(normed_late, places, query_lots, bias_q, BF16)
        kv_window = line.in_order(kv_pieces, 1)

        first = (lax.axis_index("fsdp") * local_len).astype(jnp.int32).reshape(1)
        file_count = lengths.shape[1]
        upto = jnp.arange(file_count)[:, None] <= jnp.arange(file_count)[None, :]
        file_ends = jnp.sum(jnp.where(upto[None], lengths[:, :, None], 0), axis=1)
        out_sib = plane.cross(out_near)
        queries, kv_window, up_cols, *arrived = tie(queries, kv_window, up_cols, *out_near, *out_sib)
        up_part = lax.all_gather(up_cols, "fsdp", axis=1, tiled=True).reshape(width, ff_own)
        out_lots = plane.lots(arrived[:2], arrived[2:])
        attended, norms = attn_forward(queries, kv_window, first, file_ends)
        attended, grad_near[0], grad_near[1], *out_lots = tie(attended, *grad_near, *out_lots)
        grad_far = plane.across(grad_near, plane.last)
        branch, att_mine, att_sib = lots_product(attended, places, out_lots, bias_o, F32)
        branch, *grad_far = tie(branch, *grad_far)
        middle = inputs + branch
        mean_two, recip_two = norm_stats(middle)
        xhat_two = (middle - mean_two) * recip_two
        normed_two = (xhat_two * gain_two + shift_two).astype(BF16)

        normed_two, *grad_near = tie(normed_two, *grad_near)
        two_near = plane.grow([normed_two[:half], normed_two[half:]])
        grad_far_sib = plane.cross(grad_far)
        two_near[0], two_near[1], *grad_far_sib = tie(*two_near, *grad_far_sib)
        two_far = plane.across(two_near, plane.last)
        grad_lots = [[*grad_near, *grad_near_sib], [*grad_far, *grad_far_sib]]
        two_lots = [[*two_near, *plane.cross(two_near)]]
        back_near = back_product(grad_lots[0], down_part)
        back_far = back_product(grad_lots[1], down_part)
        bias_up_part = lax.dynamic_slice_in_dim(bias_up, my_dp * ff_own, ff_own)
        back_near, back_far = tie(back_near, back_far)
        hid_near, pre_near = middle_layer(two_lots[0], back_near, up_part, bias_up_part)
        two_lots.append([*two_far, *plane.cross(two_far)])
        back_far, pre_near[0], pre_near[1] = tie(back_far, *pre_near)
        hid_far, pre_far = middle_layer(two_lots[1], back_far, up_part, bias_up_part)
        block = two_near[0].shape[0]
        lots = (slice(None, block), slice(block, None))

        def halves(lot, weight, product):
            theirs = plane.cross([product(lot[1][at], weight).astype(BF16) for at in lots])
            return [
                (product(lot[0][at], weight) + there.astype(F32)).astype(BF16)
                for at, there in zip(lots, theirs)
            ]

        def ours(lot, weight, product, theirs, got):
            whole = (product(lot[0], weight) + theirs.astype(F32)).astype(BF16)
            return [whole[at].astype(F32) + there.astype(F32) for at, there in zip(lots, got)]

        two_far_sum = halves(pre_far, up_part, dot_nt)
        pre_near[0], pre_near[1], *two_far_sum = tie(*pre_near, *two_far_sum)
        got = plane.across(two_far_sum, plane.last)
        theirs = plane.swap(dot_nt(pre_near[1], up_part).astype(BF16), 1)
        pre_far[0], theirs = tie(pre_far[0], theirs)
        up_terms = weight_grad(two_lots[0] + two_lots[1], pre_near + pre_far, block)
        pre_near[0], up_terms = tie(pre_near[0], up_terms)
        two_sum = ours(pre_near, up_part, dot_nt, theirs, got)
        grad_up = lax.psum_scatter(
            up_terms.reshape(n_dp, n_z * own, ff_own), "fsdp", scatter_dimension=1, tiled=True
        )
        hid_far[0], hid_far[1], *two_sum = tie(*hid_far, *two_sum)
        two_grad = plane.fold(two_sum)
        down_terms = weight_grad(hid_near + hid_far, grad_lots[0] + grad_lots[1], block)
        two_grad, down_terms, hid_far[0] = tie(two_grad, down_terms, hid_far[0])
        grad_down = lax.psum_scatter(down_terms, "fsdp", scatter_dimension=0, tiled=True)
        out_far = halves(hid_far, down_part, dot_nn)
        two_grad, *out_far = tie(two_grad, *out_far)

        out_got = plane.across(out_far, plane.last)
        grad_out = grad_low.astype(F32)
        grad_bdown = jnp.sum(grad_out, axis=0)
        grad_gain_two = jnp.sum(two_grad * xhat_two, axis=0)
        grad_shift_two = jnp.sum(two_grad, axis=0)
        middle_grad = grad_out + norm_pull(two_grad, xhat_two, recip_two, gain_two)
        grad_bo = jnp.sum(middle_grad, axis=0)
        branch_grad = middle_grad.astype(BF16)

        def cut(rows_of_lots):
            size = rows_of_lots.shape[0] // 4
            return [rows_of_lots[i * size : (i + 1) * size] for i in range(4)]

        def plus(mine, right, theirs):
            return (dot_tn(mine, right) + theirs.astype(F32)).astype(BF16)

        def send_rows(parts):
            return plane.across([parts[0], parts[2]], plane.last)

        def own_rows(parts, got):
            return plane.fold([n.astype(F32) + g.astype(F32) for n, g in zip((parts[1], parts[3]), got)])

        theirs = plane.swap(dot_tn(att_sib, branch_grad).astype(BF16), 1)
        attended_grad = lots_turned(branch_grad, places, out_lots, BF16)
        attended_grad, branch_late = tie(attended_grad, branch_grad)
        wo_parts = cut(plus(att_mine, branch_late, theirs))
        attended_grad, *wo_parts = tie(attended_grad, *wo_parts)
        wo_got = send_rows(wo_parts)

        query_grad, kv_terms = attn_backward(queries, kv_window, norms, attended_grad, first, file_ends)
        query_grad, kv_terms, *out_got = tie(query_grad, kv_terms, *out_got)
        kv_got = line.scatter(kv_terms.reshape(windows, n_z, local_len, 2 * HD), 1)
        theirs = plane.swap(dot_tn(one_sib, query_grad).astype(BF16), 1)
        theirs, grad_up, *wo_got = tie(theirs, grad_up, *wo_got)
        wq_parts = cut(plus(one_mine, query_grad, theirs))
        wq_got = send_rows(wq_parts)
        wq_parts[1], query_late, hid_late = tie(wq_parts[1], query_grad, hid_near[1])
        wq_parts[1], *kv_got = tie(wq_parts[1], *kv_got)
        query_part = lots_turned(query_late, places, query_lots, F32)
        kv_grad = total(kv_got).astype(BF16).reshape(rows, 2 * HD)
        wo_rows = own_rows(wo_parts, wo_got)
        query_part, kv_grad, wo_rows, grad_down = tie(query_part, kv_grad, wo_rows, grad_down)

        one_grad = query_part + dot_nt(kv_grad, full_kv)
        grad_bq = jnp.sum(query_late.astype(F32), axis=0)
        grad_bv = jnp.sum(kv_grad[:, HD:].astype(F32), axis=0)
        grad_gain_one = jnp.sum(one_grad * xhat_one, axis=0)
        grad_shift_one = jnp.sum(one_grad, axis=0)
        up_bias_part = sum(jnp.sum(lot.astype(F32), axis=0) for lot in pre_near + pre_far)
        grad_bup = jnp.where(jnp.arange(n_dp)[:, None] == my_dp, up_bias_part[None], 0.0).reshape(-1)
        sums = (
            grad_bq,
            grad_bv,
            grad_bo,
            grad_gain_one,
            grad_shift_one,
            grad_bup,
            grad_bdown,
            grad_gain_two,
            grad_shift_two,
        )
        row_of = jnp.concatenate(
            [
                jnp.pad(v.reshape(n_dev, size), ((0, 0), (0, room - size)))
                for v, size, room in zip(sums, sizes, rooms)
            ],
            axis=1,
        )
        per_half = n_z // 2 * row_of.shape[1]
        more = -(-per_half // (16 * 2 * HD)) * 16
        row_of = jnp.pad(row_of.reshape(2 * n_dp, per_half), ((0, 0), (0, more * 2 * HD - per_half)))
        row_of = row_of.astype(BF16).astype(F32)

        def with_vectors(product, core):
            pick = (places[core][:, None] == jnp.arange(2 * n_dp)[None, :]).astype(F32)
            vectors = jnp.dot(pick, row_of, precision=lax.Precision.HIGHEST)
            return jnp.concatenate(
                [product.reshape(n_dp, -1, 2 * HD), vectors.reshape(n_dp, more, 2 * HD)], axis=1
            ).reshape(-1, 2 * HD)

        theirs = plane.swap(with_vectors(dot_tn(one_sib, kv_grad), 1).astype(BF16), 1)
        kv_parts = cut((with_vectors(dot_tn(one_mine, kv_grad), 0) + theirs.astype(F32)).astype(BF16))
        kv_parts_got = send_rows(kv_parts)
        kv_parts[1], hid_late, hid_near[0], *wq_got = tie(kv_parts[1], hid_late, hid_near[0], *wq_got)
        theirs = plane.swap(dot_nn(hid_late, down_part).astype(BF16), 1)

        grad_wo = lax.psum_scatter(wo_rows.astype(BF16), "fsdp", scatter_dimension=0, tiled=True)
        wq_rows = own_rows(wq_parts, wq_got).astype(BF16)
        grad_wq = lax.psum_scatter(wq_rows, "fsdp", scatter_dimension=0, tiled=True)
        kv_last = own_rows(kv_parts, kv_parts_got).reshape(2, -1, 2 * HD)
        kv_rows = kv_last.shape[1] - more
        kv_last = jnp.concatenate(
            [
                kv_last[:, :kv_rows].reshape(n_z, -1),
                kv_last[:, kv_rows:].reshape(2, -1)[:, :per_half].reshape(n_z, -1),
            ],
            axis=1,
        )
        kv_last = line.scatter(kv_last, 0)
        out_sum = ours(hid_near, down_part, dot_nn, theirs, out_got)
        output = (middle + plane.fold(out_sum) + bias_down).astype(BF16).reshape(windows, local_len, width)
        tokens_grad = middle_grad + norm_pull(one_grad, xhat_one, recip_one, gain_one)
        tokens_grad = tokens_grad.astype(BF16).reshape(windows, local_len, width)
        grad_up = lax.all_to_all(
            grad_up.reshape(n_dp * own, ff_own), "dp", 0, 1, tiled=True
        ).astype(F32)
        kv_own = total(kv_last)
        flat = kv_own[own * 2 * HD :]
        bq, bv, bo, gain1, shift1, bup, bdown, gain2, shift2 = (
            flat[start : start + size] for start, size in zip(starts, sizes)
        )
        return (
            output,
            tokens_grad,
            grad_wq.astype(F32),
            kv_own[: own * 2 * HD].reshape(own, 2 * HD),
            grad_wo.astype(F32),
            bq,
            bv,
            bo,
            gain1,
            shift1,
            grad_up,
            grad_down.astype(F32),
            bup,
            bdown,
            gain2,
            shift2,
        )

    return local


def solution(mesh):
    whole = P(BOTH, None)
    vector = P(BOTH)
    rows = P("dp", "fsdp", None)
    weights = (whole, whole, whole) + (vector,) * 5 + (whole, whole) + (vector,) * 4
    return jax.shard_map(
        make_local(mesh.shape["dp"], mesh.shape["fsdp"]),
        mesh=mesh,
        in_specs=(rows, rows, P("dp", None)) + weights,
        out_specs=(rows, rows) + weights,
        check_vma=False,
    )
```

```python
import functools
import math

import jax
import jax.numpy as jnp
from jax import lax
from jax.experimental import pallas as pl
from jax.experimental.pallas import tpu as pltpu
from jax.sharding import PartitionSpec as P

HEADS = 16
HD = 128
EPS = 1e-05
F32 = jnp.float32
BF16 = jnp.bfloat16
BOTH = ("dp", "fsdp")
HASTE = 64


def dot_nn(left, right):
    return jnp.dot(left, right, preferred_element_type=F32)


def dot_nt(left, right):
    return lax.dot_general(left, right, (((1,), (1,)), ((), ())), preferred_element_type=F32)


def dot_tn(left, right):
    return lax.dot_general(left, right, (((0,), (0,)), ((), ())), preferred_element_type=F32)


LOG2E = 1.4426950408889634


def file_of(ends_ref, w, pos):
    total = jnp.zeros(pos.shape, jnp.int32)
    for i in range(ends_ref.shape[1]):
        total += (ends_ref[w, i] <= pos).astype(jnp.int32)
    return total


def fill_mask(pos_ref, ends_ref, w, bias, key_turned, value_turned, kv_ref):
    span, win = bias.shape
    query_pos = pos_ref[0] + lax.broadcasted_iota(jnp.int32, (span, 1), 0)
    key_pos = lax.broadcasted_iota(jnp.int32, (1, win), 1)
    same = file_of(ends_ref, w, query_pos) == file_of(ends_ref, w, key_pos)
    bias[...] = jnp.where(same & (key_pos <= query_pos), 0.0, -1e30).astype(F32)
    key_turned[...] = kv_ref[0, :, :HD].astype(F32).T.astype(BF16)
    if value_turned is not None:
        value_turned[...] = kv_ref[0, :, HD:].astype(F32).T.astype(BF16)


def attn_forward_kernel(per_step, pos_ref, ends_ref, q_ref, kv_ref, out_ref, norm_ref, bias, key_turned):
    w, group = pl.program_id(0), pl.program_id(1)

    @pl.when(group == 0)
    def _():
        fill_mask(pos_ref, ends_ref, w, bias, key_turned, None, kv_ref)
        norm_ref[...] = jnp.zeros_like(norm_ref)

    values = kv_ref[0, :, HD:]
    lane = lax.broadcasted_iota(jnp.int32, norm_ref.shape, 1)
    for j in range(per_step):
        query = q_ref[:, j * HD : (j + 1) * HD]
        scores = jnp.dot(query, key_turned[...], preferred_element_type=F32)
        scores = scores * (LOG2E / math.sqrt(HD)) + bias[...]
        top = jnp.max(scores, axis=1, keepdims=True)
        terms = jnp.exp2(scores - top)
        total = jnp.sum(terms, axis=1, keepdims=True)
        mixed = jnp.dot(terms.astype(BF16), values, preferred_element_type=F32)
        out_ref[:, j * HD : (j + 1) * HD] = (mixed / total).astype(BF16)
        norm_ref[...] = jnp.where(lane == group * per_step + j, top + jnp.log2(total), norm_ref[...])


def attn_backward_kernel(
    per_step, pos_ref, ends_ref, q_ref, kv_ref, norm_ref, grad_ref, dq_ref, dkv_ref,
    bias, key_turned, value_turned, key_grad, value_grad,
):
    w, group = pl.program_id(0), pl.program_id(1)

    @pl.when(group == 0)
    def _():
        fill_mask(pos_ref, ends_ref, w, bias, key_turned, value_turned, kv_ref)
        key_grad[...] = jnp.zeros_like(key_grad)
        value_grad[...] = jnp.zeros_like(value_grad)

    keys = kv_ref[0, :, :HD]
    lane = lax.broadcasted_iota(jnp.int32, norm_ref.shape, 1)
    for j in range(per_step):
        query = q_ref[:, j * HD : (j + 1) * HD]
        grad = grad_ref[:, j * HD : (j + 1) * HD]
        scores = jnp.dot(query, key_turned[...], preferred_element_type=F32)
        scores = scores * (LOG2E / math.sqrt(HD)) + bias[...]
        norm = jnp.sum(jnp.where(lane == group * per_step + j, norm_ref[...], 0.0), axis=1, keepdims=True)
        probs = jnp.exp2(scores - norm)
        grad_probs = jnp.dot(grad, value_turned[...], preferred_element_type=F32)
        delta = jnp.sum(probs * grad_probs, axis=1, keepdims=True)
        score_grad = (probs * (grad_probs - delta)).astype(BF16)
        probs = probs.astype(BF16)
        dq = jnp.dot(score_grad, keys, preferred_element_type=F32)
        dq_ref[:, j * HD : (j + 1) * HD] = (dq / math.sqrt(HD)).astype(BF16)
        key_grad[...] += dot_tn(query, score_grad)
        value_grad[...] += dot_tn(grad, probs)

    @pl.when(group == pl.num_programs(1) - 1)
    def _():
        dkv_ref[0, :, :HD] = (key_grad[...].T / math.sqrt(HD)).astype(BF16)
        dkv_ref[0, :, HD:] = value_grad[...].T.astype(BF16)


def attn_specs(per_step, span, win):
    smem = pl.BlockSpec(memory_space=pltpu.SMEM)
    heads = pl.BlockSpec((span, per_step * HD), lambda w, g: (w, g))
    keys = pl.BlockSpec((1, win, 2 * HD), lambda w, g: (w, 0, 0))
    norm = pl.BlockSpec((span, HD), lambda w, g: (w, 0))
    return smem, heads, keys, norm


def attn_cost(windows, span, win, products):
    return pl.CostEstimate(
        flops=2 * products * windows * HEADS * span * win * HD // HASTE,
        transcendentals=windows * HEADS * span * win // HASTE,
        bytes_accessed=products * windows * HEADS * span * HD * 2 // HASTE,
    )


def attn_forward(queries, kv_window, first, ends, per_step=4):
    windows, win, _ = kv_window.shape
    rows, width = queries.shape
    span = rows // windows
    smem, heads, keys, norm = attn_specs(per_step, span, win)
    return pl.pallas_call(
        functools.partial(attn_forward_kernel, per_step),
        out_shape=(
            jax.ShapeDtypeStruct((rows, width), BF16),
            jax.ShapeDtypeStruct((rows, HD), F32),
        ),
        grid=(windows, HEADS // per_step),
        in_specs=[smem, smem, heads, keys],
        out_specs=(heads, norm),
        scratch_shapes=[pltpu.VMEM((span, win), F32), pltpu.VMEM((HD, win), BF16)],
        compiler_params=pltpu.CompilerParams(vmem_limit_bytes=40 * 2**20),
        cost_estimate=attn_cost(windows, span, win, 2),
    )(first, ends, queries, kv_window)


def attn_backward(queries, kv_window, norms, grads, first, ends, per_step=4):
    windows, win, _ = kv_window.shape
    rows, width = queries.shape
    span = rows // windows
    smem, heads, keys, norm = attn_specs(per_step, span, win)
    return pl.pallas_call(
        functools.partial(attn_backward_kernel, per_step),
        out_shape=(
            jax.ShapeDtypeStruct((rows, width), BF16),
            jax.ShapeDtypeStruct((windows, win, 2 * HD), BF16),
        ),
        grid=(windows, HEADS // per_step),
        in_specs=[smem, smem, heads, keys, norm, heads],
        out_specs=(heads, keys),
        scratch_shapes=[
            pltpu.VMEM((span, win), F32),
            pltpu.VMEM((HD, win), BF16),
            pltpu.VMEM((HD, win), BF16),
            pltpu.VMEM((HD, win), F32),
            pltpu.VMEM((HD, win), F32),
        ],
        compiler_params=pltpu.CompilerParams(vmem_limit_bytes=48 * 2**20),
        cost_estimate=attn_cost(windows, span, win, 5),
    )(first, ends, queries, kv_window, norms, grads)


def middle_kernel(count, *refs):
    blocks, back_ref = refs[:count], refs[count]
    up_ref, bias_ref = refs[count + 1], refs[count + 2]
    outs = refs[count + 3 :]
    groups = len(outs) // 2
    size = blocks[0].shape[0]
    root = math.sqrt(2.0 / math.pi)
    for i, block in enumerate(blocks):
        act = jnp.dot(block[...], up_ref[...], preferred_element_type=F32) + bias_ref[...]
        square = act * act
        bent = jnp.tanh(act * (root + (root * 0.044715) * square))
        upper = 0.5 + 0.5 * bent
        slope = upper + act * (1.0 - bent * bent) * (0.5 * root + (1.5 * 0.044715 * root) * square)
        back = back_ref[i * size : (i + 1) * size, :].astype(F32)
        group, place = divmod(i, count // groups)
        at = slice(place * size, (place + 1) * size)
        outs[group][at, :] = (act * upper).astype(BF16)
        outs[groups + group][at, :] = (back * slope).astype(BF16)


def middle_layer(blocks, back, up_part, bias, tile=512):
    count = len(blocks)
    size, width = blocks[0].shape
    units = up_part.shape[1]
    tile = min(tile, units)
    one = pl.Buffered(buffer_count=1)
    group = size * count // 2
    whole = pl.BlockSpec((size, width), lambda j: (0, 0), pipeline_mode=one)
    slab = pl.BlockSpec((group, tile), lambda j: (0, j))
    out = pl.pallas_call(
        functools.partial(middle_kernel, count),
        out_shape=[jax.ShapeDtypeStruct((group, units), BF16)] * 4,
        grid=(units // tile,),
        in_specs=[whole] * count
        + [
            pl.BlockSpec((size * count, tile), lambda j: (0, j)),
            pl.BlockSpec((width, tile), lambda j: (0, j)),
            pl.BlockSpec((1, tile), lambda j: (0, j)),
        ],
        out_specs=[slab] * 4,
        compiler_params=pltpu.CompilerParams(vmem_limit_bytes=48 * 2**20),
        cost_estimate=pl.CostEstimate(
            flops=2 * count * size * width * units // HASTE,
            transcendentals=count * size * units // HASTE,
            bytes_accessed=2 * (count * size * (width + 3 * units) + width * units) // HASTE,
        ),
    )(*blocks, back, up_part, bias.reshape(1, units))
    return list(out[:2]), list(out[2:])


def back_kernel(count, *refs):
    blocks, weight_ref, out = refs[:count], refs[count], refs[count + 1]
    size = blocks[0].shape[0]
    for i, block in enumerate(blocks):
        out[i * size : (i + 1) * size, :] = dot_nt(block[...], weight_ref[...]).astype(BF16)


def back_product(blocks, weight, tile=512):
    count = len(blocks)
    size, width = blocks[0].shape
    units = weight.shape[0]
    tile = min(tile, units)
    one = pl.Buffered(buffer_count=1)
    return pl.pallas_call(
        functools.partial(back_kernel, count),
        out_shape=jax.ShapeDtypeStruct((size * count, units), BF16),
        grid=(units // tile,),
        in_specs=[pl.BlockSpec((size, width), lambda j: (0, 0), pipeline_mode=one)] * count
        + [pl.BlockSpec((tile, width), lambda j: (j, 0))],
        out_specs=pl.BlockSpec((size * count, tile), lambda j: (0, j)),
        compiler_params=pltpu.CompilerParams(vmem_limit_bytes=48 * 2**20),
        cost_estimate=pl.CostEstimate(
            flops=2 * count * size * width * units // HASTE,
            transcendentals=0,
            bytes_accessed=2 * (count * size * (width + units) + width * units) // HASTE,
        ),
    )(*blocks, weight)


def weight_kernel(count, *refs):
    lefts, rights, out = refs[:count], refs[count : 2 * count], refs[2 * count]
    total = dot_tn(lefts[0][...], rights[0][...])
    for left, right in zip(lefts[1:], rights[1:]):
        total += dot_tn(left[...], right[...])
    out[...] = total.astype(BF16)


def in_blocks(arrays, size):
    return [(array, i) for array in arrays for i in range(array.shape[0] // size)]


def weight_grad(lefts, rights, size, tile=256):
    lefts, rights = in_blocks(lefts, size), in_blocks(rights, size)
    count = len(lefts)
    height, breadth = lefts[0][0].shape[1], rights[0][0].shape[1]
    tile = min(tile, height)

    def left_spec(row):
        return pl.BlockSpec((size, tile), lambda i: (row, i))

    def right_spec(row):
        return pl.BlockSpec((size, breadth), lambda i: (row, 0), pipeline_mode=pl.Buffered(buffer_count=1))

    return pl.pallas_call(
        functools.partial(weight_kernel, count),
        out_shape=jax.ShapeDtypeStruct((height, breadth), BF16),
        grid=(height // tile,),
        in_specs=[left_spec(row) for _, row in lefts] + [right_spec(row) for _, row in rights],
        out_specs=pl.BlockSpec((tile, breadth), lambda i: (i, 0)),
        compiler_params=pltpu.CompilerParams(vmem_limit_bytes=52 * 2**20),
        cost_estimate=pl.CostEstimate(
            flops=2 * count * size * height * breadth // HASTE,
            transcendentals=0,
            bytes_accessed=2 * (count * size * (height + breadth) + height * breadth) // HASTE,
        ),
    )(*[array for array, _ in lefts], *[array for array, _ in rights])


def reorder_kernel(place_ref, first_ref, second_ref, first_out, second_out):
    first_out[...] = first_ref[...]
    second_out[...] = second_ref[...]


def reorder(values, places):
    rows, width = values.shape
    count = places.shape[1]
    block = width // (2 * count)
    if block % 128:
        return [
            jnp.concatenate(
                [lax.dynamic_slice_in_dim(values, places[i, j] * block, block, 1) for j in range(count)],
                axis=1,
            )
            for i in (0, 1)
        ]
    out = pl.BlockSpec((rows, block), lambda i, place: (0, i))
    return pl.pallas_call(
        reorder_kernel,
        out_shape=[jax.ShapeDtypeStruct((rows, width // 2), values.dtype)] * 2,
        grid_spec=pltpu.PrefetchScalarGridSpec(
            num_scalar_prefetch=1,
            grid=(count,),
            in_specs=[
                pl.BlockSpec((rows, block), lambda i, place: (0, place[0, i])),
                pl.BlockSpec((rows, block), lambda i, place: (0, place[1, i])),
            ],
            out_specs=[out, out],
        ),
        cost_estimate=pl.CostEstimate(flops=0, transcendentals=0, bytes_accessed=4 * rows * width // HASTE),
    )(places, values, values)


def norm_stats(values):
    average = jnp.mean(values, axis=-1, keepdims=True)
    centered = values - average
    variance = jnp.mean(centered * centered, axis=-1, keepdims=True)
    return average, lax.rsqrt(variance + EPS)


def norm_pull(grad, xhat, recip, gain):
    scaled = grad * gain
    mean_one = jnp.mean(scaled, axis=-1, keepdims=True)
    mean_two = jnp.mean(scaled * xhat, axis=-1, keepdims=True)
    return recip * (scaled - mean_one - xhat * mean_two)


def tie(*arrays):
    return lax.optimization_barrier(arrays)


class Line:
    def __init__(self, count):
        self.count = count

    def send(self, block, places):
        return lax.ppermute(block, "fsdp", [(i, (i + places) % self.count) for i in range(self.count)])

    def gather(self, block):
        return [block] + [self.send(block, step) for step in range(1, self.count)]

    def in_order(self, pieces, axis=0):
        me = lax.axis_index("fsdp")
        size = pieces[0].shape[axis]
        shape = list(pieces[0].shape)
        shape[axis] = size * self.count
        whole = jnp.zeros(shape, pieces[0].dtype)
        for step, piece in enumerate(pieces):
            place = lax.rem(me - step + self.count, self.count) * size
            whole = lax.dynamic_update_slice_in_dim(whole, piece, place, axis)
        return whole

    def scatter(self, terms, axis):
        me = lax.axis_index("fsdp")

        def term(step):
            place = lax.rem(me + step, self.count)
            return lax.dynamic_index_in_dim(terms, place, axis, keepdims=False)

        return [term(0)] + [self.send(term(step).astype(BF16), step) for step in range(1, self.count)]


def total(terms):
    out = terms[0].astype(F32)
    for term in terms[1:]:
        out += term.astype(F32)
    return out


class Plane:
    def __init__(self, count):
        self.count = count
        bits = [1 << i for i in range(1, count.bit_length() - 1)]
        self.orders = (bits, bits[::-1])
        self.last = len(bits) - 1
        self.near, self.far = [], []
        for order in self.orders:
            near = [0]
            for bit in order[:-1]:
                near = near + [offset ^ bit for offset in near]
            self.near.append(near)
            self.far.append([offset ^ order[-1] for offset in near])

    def places(self):
        me = lax.axis_index("dp")
        order = [(o, h) for h in (0, 1) for o in self.far[h] + self.near[h]]
        return jnp.stack(
            [jnp.stack([2 * (me ^ o ^ core) + h for o, h in order]) for core in (0, 1)]
        ).astype(jnp.int32)

    def swap(self, block, bit):
        return lax.ppermute(block, "dp", [(i, i ^ bit) for i in range(self.count)])

    def cross(self, blocks):
        return [self.swap(block, 1) for block in blocks]

    def across(self, halves, step):
        return [self.swap(half, order[step]) for half, order in zip(halves, self.orders)]

    def grow(self, halves):
        for step in range(self.last):
            halves = [jnp.concatenate(pair) for pair in zip(halves, self.across(halves, step))]
        return halves

    def fold(self, halves):
        for step in range(self.last - 1, -1, -1):
            size = halves[0].shape[0] // 2
            got = self.across([half[size:].astype(BF16) for half in halves], step)
            halves = [half[:size].astype(F32) + there.astype(F32) for half, there in zip(halves, got)]
        return jnp.concatenate(halves)


def make_local(n_dp, n_z):
    n_dev = n_dp * n_z
    plane = Plane(n_dp)
    line = Line(n_z)

    def local(
        tokens,
        cotangent,
        lengths,
        query_weight,
        kv_weight,
        out_weight,
        query_bias,
        value_bias,
        out_bias,
        attn_gain,
        attn_shift,
        up_weight,
        down_weight,
        up_bias,
        down_bias,
        mlp_gain,
        mlp_shift,
    ):
        windows, local_len, width = tokens.shape
        rows = windows * local_len
        half = rows // 2
        own = query_weight.shape[0]
        ff_own = up_weight.shape[1] // n_dp
        my_dp = lax.axis_index("dp")

        small = (
            query_bias,
            value_bias,
            out_bias,
            attn_gain,
            attn_shift,
            up_bias,
            down_bias,
            mlp_gain,
            mlp_shift,
        )
        sizes = [v.shape[0] for v in small]
        rooms = [-(-size // 128) * 128 for size in sizes]
        starts = [sum(rooms[:i]) for i in range(len(rooms))]
        small_row = jnp.concatenate(
            [jnp.pad(v, (0, room - size)) for v, size, room in zip(small, sizes, rooms)]
        )
        kv_lines = kv_weight.size // width
        filled = own + kv_lines + -(-small_row.shape[0] // width)
        lines = -(-filled // 16) * 16
        small_row = jnp.pad(small_row, (0, (lines - own - kv_lines) * width - small_row.shape[0]))
        packed = jnp.concatenate(
            [query_weight, kv_weight.reshape(kv_lines, width), small_row.reshape(-1, width)]
        )
        places = plane.places()

        grad_low = cotangent.reshape(rows, width)
        packed = lax.all_gather(packed, "fsdp", axis=0, tiled=True)
        grad_near = plane.grow([grad_low[:half], grad_low[half:]])
        up_cols = lax.all_to_all(up_weight, "dp", 1, 0, tiled=True).reshape(n_dp, own, ff_own)
        packed, up_cols, out_weight, *grad_near = tie(packed, up_cols, out_weight, *grad_near)

        packed = lax.all_gather(packed, "dp", axis=0, tiled=True)
        out_pieces = line.gather(out_weight)
        *out_pieces, down_late = tie(*out_pieces, down_weight)
        full_o = line.in_order(out_pieces)
        down_pieces = [down_late]
        while len(down_pieces) < min(3, n_z):
            down_pieces.append(line.send(down_pieces[-1], 1))
        inputs = tokens.reshape(rows, width).astype(F32)
        mean_one, recip_one = norm_stats(inputs)
        grad_near_sib = plane.cross(grad_near)
        packed, full_o, mean_one, down_pieces[-1], *arrived = tie(
            packed, full_o, mean_one, down_pieces[-1], *grad_near, *grad_near_sib
        )
        grad_near, grad_near_sib = arrived[:2], arrived[2:]

        full_o = lax.all_gather(full_o, "dp", axis=0, tiled=True)
        packed = packed.reshape(n_dev, lines, width)
        full_q = packed[:, :own].reshape(width, width)
        full_kv = packed[:, own : own + kv_lines].reshape(width, 2 * HD)
        small_all = packed[:, own + kv_lines :].reshape(n_dev, -1)
        bias_q, bias_v, bias_o, gain_one, shift_one, bias_up, bias_down, gain_two, shift_two = (
            small_all[:, start : start + size].reshape(-1).astype(F32)
            for start, size in zip(starts, sizes)
        )
        xhat_one = (inputs - mean_one) * recip_one
        normed_one = (xhat_one * gain_one + shift_one).astype(BF16)
        kv_bias = jnp.concatenate([jnp.zeros((HD,), F32), bias_v])
        key_value = (dot_nn(normed_one, full_kv) + kv_bias).astype(BF16)
        key_value, normed_late, up_cols = tie(key_value, normed_one, up_cols)
        kv_pieces = line.gather(key_value.reshape(windows, local_len, 2 * HD))
        queries = (dot_nn(normed_late, full_q) + bias_q).astype(BF16)
        queries, *kv_pieces = tie(queries, *kv_pieces)
        kv_window = line.in_order(kv_pieces, 1)

        first = (lax.axis_index("fsdp") * local_len).astype(jnp.int32).reshape(1)
        file_count = lengths.shape[1]
        upto = jnp.arange(file_count)[:, None] <= jnp.arange(file_count)[None, :]
        file_ends = jnp.sum(jnp.where(upto[None], lengths[:, :, None], 0), axis=1)
        grad_far = plane.across(grad_near, plane.last)
        while len(down_pieces) < n_z:
            down_pieces.append(line.send(down_pieces[-1], 1))
        up_part = lax.all_gather(up_cols, "fsdp", axis=1, tiled=True).reshape(width, ff_own)
        attended, norms = attn_forward(queries, kv_window, first, file_ends)
        attended, down_pieces[-1] = tie(attended, down_pieces[-1])
        middle = inputs + dot_nn(attended, full_o) + bias_o
        mean_two, recip_two = norm_stats(middle)
        xhat_two = (middle - mean_two) * recip_two
        normed_two = (xhat_two * gain_two + shift_two).astype(BF16)

        normed_two, normed_late, *arrived = tie(normed_two, normed_late, *grad_far, *down_pieces)
        grad_far, down_pieces = arrived[:2], arrived[2:]
        two_near = plane.grow([normed_two[:half], normed_two[half:]])
        down_part = line.in_order(down_pieces)
        grad_lots = [[*grad_near, *grad_near_sib], [*grad_far, *plane.cross(grad_far)]]
        back_near = back_product(grad_lots[0], down_part)
        two_near[0], two_near[1], back_near = tie(*two_near, back_near)
        two_far = plane.across(two_near, plane.last)
        two_lots = [[*two_near, *plane.cross(two_near)]]
        back_near, down_late, attended_late, normed_late = tie(
            back_near, down_part, attended, normed_late
        )
        back_far = back_product(grad_lots[1], down_late)
        bias_up_part = lax.dynamic_slice_in_dim(bias_up, my_dp * ff_own, ff_own)
        hid_near, pre_near = middle_layer(two_lots[0], back_near, up_part, bias_up_part)
        att_mine, att_sib = reorder(attended_late, places)
        one_mine, one_sib = reorder(normed_late, places)
        back_far, pre_near[0], pre_near[1], *arrived = tie(
            back_far, *pre_near, att_mine, att_sib, one_mine, one_sib
        )
        att_mine, att_sib, one_mine, one_sib = arrived
        two_lots.append([*two_far, *plane.cross(two_far)])
        hid_far, pre_far = middle_layer(two_lots[1], back_far, up_part, bias_up_part)
        block = two_near[0].shape[0]
        lots = (slice(None, block), slice(block, None))

        def halves(lot, weight, product):
            theirs = plane.cross([product(lot[1][at], weight).astype(BF16) for at in lots])
            return [
                (product(lot[0][at], weight) + there.astype(F32)).astype(BF16)
                for at, there in zip(lots, theirs)
            ]

        def ours(lot, weight, product, theirs, got):
            whole = (product(lot[0], weight) + theirs.astype(F32)).astype(BF16)
            return [whole[at].astype(F32) + there.astype(F32) for at, there in zip(lots, got)]

        two_far_sum = halves(pre_far, up_part, dot_nt)
        pre_near[0], pre_near[1], *two_far_sum = tie(*pre_near, *two_far_sum)
        got = plane.across(two_far_sum, plane.last)
        theirs = plane.swap(dot_nt(pre_near[1], up_part).astype(BF16), 1)
        pre_far[0], theirs = tie(pre_far[0], theirs)
        up_terms = weight_grad(two_lots[0] + two_lots[1], pre_near + pre_far, block)
        pre_near[0], up_terms = tie(pre_near[0], up_terms)
        two_sum = ours(pre_near, up_part, dot_nt, theirs, got)
        grad_up = lax.psum_scatter(
            up_terms.reshape(n_dp, n_z * own, ff_own), "fsdp", scatter_dimension=1, tiled=True
        )
        hid_far[0], hid_far[1], *two_sum = tie(*hid_far, *two_sum)
        two_grad = plane.fold(two_sum)
        down_terms = weight_grad(hid_near + hid_far, grad_lots[0] + grad_lots[1], block)
        two_grad, down_terms, hid_far[0] = tie(two_grad, down_terms, hid_far[0])
        grad_down = lax.psum_scatter(down_terms, "fsdp", scatter_dimension=0, tiled=True)
        out_far = halves(hid_far, down_part, dot_nn)
        two_grad, *out_far = tie(two_grad, *out_far)

        out_got = plane.across(out_far, plane.last)
        grad_out = grad_low.astype(F32)
        grad_bdown = jnp.sum(grad_out, axis=0)
        grad_gain_two = jnp.sum(two_grad * xhat_two, axis=0)
        grad_shift_two = jnp.sum(two_grad, axis=0)
        middle_grad = grad_out + norm_pull(two_grad, xhat_two, recip_two, gain_two)
        grad_bo = jnp.sum(middle_grad, axis=0)
        branch_grad = middle_grad.astype(BF16)

        def cut(rows_of_lots):
            size = rows_of_lots.shape[0] // 4
            return [rows_of_lots[i * size : (i + 1) * size] for i in range(4)]

        def plus(mine, right, theirs):
            return (dot_tn(mine, right) + theirs.astype(F32)).astype(BF16)

        def send_rows(parts):
            return plane.across([parts[0], parts[2]], plane.last)

        def own_rows(parts, got):
            return plane.fold([n.astype(F32) + g.astype(F32) for n, g in zip((parts[1], parts[3]), got)])

        theirs = plane.swap(dot_tn(att_sib, branch_grad).astype(BF16), 1)
        attended_grad = dot_nt(branch_grad, full_o).astype(BF16)
        attended_grad, branch_late = tie(attended_grad, branch_grad)
        wo_parts = cut(plus(att_mine, branch_late, theirs))
        attended_grad, *wo_parts = tie(attended_grad, *wo_parts)
        wo_got = send_rows(wo_parts)

        query_grad, kv_terms = attn_backward(queries, kv_window, norms, attended_grad, first, file_ends)
        query_grad, kv_terms, *out_got = tie(query_grad, kv_terms, *out_got)
        kv_got = line.scatter(kv_terms.reshape(windows, n_z, local_len, 2 * HD), 1)
        theirs = plane.swap(dot_tn(one_sib, query_grad).astype(BF16), 1)
        theirs, grad_up, *wo_got = tie(theirs, grad_up, *wo_got)
        wq_parts = cut(plus(one_mine, query_grad, theirs))
        wq_got = send_rows(wq_parts)
        wq_parts[1], query_late, hid_late = tie(wq_parts[1], query_grad, hid_near[1])
        wq_parts[1], *kv_got = tie(wq_parts[1], *kv_got)
        query_part = dot_nt(query_late, full_q)
        kv_grad = total(kv_got).astype(BF16).reshape(rows, 2 * HD)
        wo_rows = own_rows(wo_parts, wo_got)
        query_part, kv_grad, wo_rows, grad_down = tie(query_part, kv_grad, wo_rows, grad_down)

        one_grad = query_part + dot_nt(kv_grad, full_kv)
        grad_bq = jnp.sum(query_late.astype(F32), axis=0)
        grad_bv = jnp.sum(kv_grad[:, HD:].astype(F32), axis=0)
        grad_gain_one = jnp.sum(one_grad * xhat_one, axis=0)
        grad_shift_one = jnp.sum(one_grad, axis=0)
        up_bias_part = sum(jnp.sum(lot.astype(F32), axis=0) for lot in pre_near + pre_far)
        grad_bup = jnp.where(jnp.arange(n_dp)[:, None] == my_dp, up_bias_part[None], 0.0).reshape(-1)
        sums = (
            grad_bq,
            grad_bv,
            grad_bo,
            grad_gain_one,
            grad_shift_one,
            grad_bup,
            grad_bdown,
            grad_gain_two,
            grad_shift_two,
        )
        row_of = jnp.concatenate(
            [
                jnp.pad(v.reshape(n_dev, size), ((0, 0), (0, room - size)))
                for v, size, room in zip(sums, sizes, rooms)
            ],
            axis=1,
        )
        per_half = n_z // 2 * row_of.shape[1]
        more = -(-per_half // (16 * 2 * HD)) * 16
        row_of = jnp.pad(row_of.reshape(2 * n_dp, per_half), ((0, 0), (0, more * 2 * HD - per_half)))
        row_of = row_of.astype(BF16).astype(F32)

        def with_vectors(product, core):
            pick = (places[core][:, None] == jnp.arange(2 * n_dp)[None, :]).astype(F32)
            vectors = jnp.dot(pick, row_of, precision=lax.Precision.HIGHEST)
            return jnp.concatenate(
                [product.reshape(n_dp, -1, 2 * HD), vectors.reshape(n_dp, more, 2 * HD)], axis=1
            ).reshape(-1, 2 * HD)

        theirs = plane.swap(with_vectors(dot_tn(one_sib, kv_grad), 1).astype(BF16), 1)
        kv_parts = cut((with_vectors(dot_tn(one_mine, kv_grad), 0) + theirs.astype(F32)).astype(BF16))
        kv_parts_got = send_rows(kv_parts)
        kv_parts[1], hid_late, hid_near[0], *wq_got = tie(kv_parts[1], hid_late, hid_near[0], *wq_got)
        theirs = plane.swap(dot_nn(hid_late, down_part).astype(BF16), 1)

        grad_wo = lax.psum_scatter(wo_rows.astype(BF16), "fsdp", scatter_dimension=0, tiled=True)
        wq_rows = own_rows(wq_parts, wq_got).astype(BF16)
        grad_wq = lax.psum_scatter(wq_rows, "fsdp", scatter_dimension=0, tiled=True)
        kv_last = own_rows(kv_parts, kv_parts_got).reshape(2, -1, 2 * HD)
        kv_rows = kv_last.shape[1] - more
        kv_last = jnp.concatenate(
            [
                kv_last[:, :kv_rows].reshape(n_z, -1),
                kv_last[:, kv_rows:].reshape(2, -1)[:, :per_half].reshape(n_z, -1),
            ],
            axis=1,
        )
        kv_last = line.scatter(kv_last, 0)
        out_sum = ours(hid_near, down_part, dot_nn, theirs, out_got)
        output = (middle + plane.fold(out_sum) + bias_down).astype(BF16).reshape(windows, local_len, width)
        tokens_grad = middle_grad + norm_pull(one_grad, xhat_one, recip_one, gain_one)
        tokens_grad = tokens_grad.astype(BF16).reshape(windows, local_len, width)
        grad_up = lax.all_to_all(
            grad_up.reshape(n_dp * own, ff_own), "dp", 0, 1, tiled=True
        ).astype(F32)
        kv_own = total(kv_last)
        flat = kv_own[own * 2 * HD :]
        bq, bv, bo, gain1, shift1, bup, bdown, gain2, shift2 = (
            flat[start : start + size] for start, size in zip(starts, sizes)
        )
        return (
            output,
            tokens_grad,
            grad_wq.astype(F32),
            kv_own[: own * 2 * HD].reshape(own, 2 * HD),
            grad_wo.astype(F32),
            bq,
            bv,
            bo,
            gain1,
            shift1,
            grad_up,
            grad_down.astype(F32),
            bup,
            bdown,
            gain2,
            shift2,
        )

    return local


def solution(mesh):
    whole = P(BOTH, None)
    vector = P(BOTH)
    rows = P("dp", "fsdp", None)
    weights = (whole, whole, whole) + (vector,) * 5 + (whole, whole) + (vector,) * 4
    return jax.shard_map(
        make_local(mesh.shape["dp"], mesh.shape["fsdp"]),
        mesh=mesh,
        in_specs=(rows, rows, P("dp", None)) + weights,
        out_specs=(rows, rows) + weights,
        check_vma=False,
    )
```

```python
import functools
import math

import jax
import jax.numpy as jnp
from jax import lax
from jax.experimental import pallas as pl
from jax.experimental.pallas import tpu as pltpu
from jax.sharding import PartitionSpec as P

HEADS = 16
HD = 128
EPS = 1e-05
F32 = jnp.float32
BF16 = jnp.bfloat16
BOTH = ("dp", "fsdp")
HASTE = 64


def dot_nn(left, right):
    return jnp.dot(left, right, preferred_element_type=F32)


def dot_nt(left, right):
    return lax.dot_general(left, right, (((1,), (1,)), ((), ())), preferred_element_type=F32)


def dot_tn(left, right):
    return lax.dot_general(left, right, (((0,), (0,)), ((), ())), preferred_element_type=F32)


LOG2E = 1.4426950408889634


def file_of(ends_ref, w, pos):
    total = jnp.zeros(pos.shape, jnp.int32)
    for i in range(ends_ref.shape[1]):
        total += (ends_ref[w, i] <= pos).astype(jnp.int32)
    return total


def fill_mask(pos_ref, ends_ref, w, bias, key_turned, value_turned, kv_ref):
    span, win = bias.shape
    query_pos = pos_ref[0] + lax.broadcasted_iota(jnp.int32, (span, 1), 0)
    key_pos = lax.broadcasted_iota(jnp.int32, (1, win), 1)
    same = file_of(ends_ref, w, query_pos) == file_of(ends_ref, w, key_pos)
    bias[...] = jnp.where(same & (key_pos <= query_pos), 0.0, -1e30).astype(F32)
    key_turned[...] = kv_ref[0, :, :HD].astype(F32).T.astype(BF16)
    if value_turned is not None:
        value_turned[...] = kv_ref[0, :, HD:].astype(F32).T.astype(BF16)


def attn_forward_kernel(per_step, pos_ref, ends_ref, q_ref, kv_ref, out_ref, norm_ref, bias, key_turned):
    w, group = pl.program_id(0), pl.program_id(1)

    @pl.when(group == 0)
    def _():
        fill_mask(pos_ref, ends_ref, w, bias, key_turned, None, kv_ref)
        norm_ref[...] = jnp.zeros_like(norm_ref)

    values = kv_ref[0, :, HD:]
    lane = lax.broadcasted_iota(jnp.int32, norm_ref.shape, 1)
    for j in range(per_step):
        query = q_ref[:, j * HD : (j + 1) * HD]
        scores = jnp.dot(query, key_turned[...], preferred_element_type=F32)
        scores = scores * (LOG2E / math.sqrt(HD)) + bias[...]
        top = jnp.max(scores, axis=1, keepdims=True)
        terms = jnp.exp2(scores - top)
        total = jnp.sum(terms, axis=1, keepdims=True)
        mixed = jnp.dot(terms.astype(BF16), values, preferred_element_type=F32)
        out_ref[:, j * HD : (j + 1) * HD] = (mixed / total).astype(BF16)
        norm_ref[...] = jnp.where(lane == group * per_step + j, top + jnp.log2(total), norm_ref[...])


def attn_backward_kernel(
    per_step, pos_ref, ends_ref, q_ref, kv_ref, norm_ref, grad_ref, dq_ref, dkv_ref,
    bias, key_turned, value_turned, key_grad, value_grad,
):
    w, group = pl.program_id(0), pl.program_id(1)

    @pl.when(group == 0)
    def _():
        fill_mask(pos_ref, ends_ref, w, bias, key_turned, value_turned, kv_ref)
        key_grad[...] = jnp.zeros_like(key_grad)
        value_grad[...] = jnp.zeros_like(value_grad)

    keys = kv_ref[0, :, :HD]
    lane = lax.broadcasted_iota(jnp.int32, norm_ref.shape, 1)
    for j in range(per_step):
        query = q_ref[:, j * HD : (j + 1) * HD]
        grad = grad_ref[:, j * HD : (j + 1) * HD]
        scores = jnp.dot(query, key_turned[...], preferred_element_type=F32)
        scores = scores * (LOG2E / math.sqrt(HD)) + bias[...]
        norm = jnp.sum(jnp.where(lane == group * per_step + j, norm_ref[...], 0.0), axis=1, keepdims=True)
        probs = jnp.exp2(scores - norm)
        grad_probs = jnp.dot(grad, value_turned[...], preferred_element_type=F32)
        delta = jnp.sum(probs * grad_probs, axis=1, keepdims=True)
        score_grad = (probs * (grad_probs - delta)).astype(BF16)
        probs = probs.astype(BF16)
        dq = jnp.dot(score_grad, keys, preferred_element_type=F32)
        dq_ref[:, j * HD : (j + 1) * HD] = (dq / math.sqrt(HD)).astype(BF16)
        key_grad[...] += dot_tn(query, score_grad)
        value_grad[...] += dot_tn(grad, probs)

    @pl.when(group == pl.num_programs(1) - 1)
    def _():
        dkv_ref[0, :, :HD] = (key_grad[...].T / math.sqrt(HD)).astype(BF16)
        dkv_ref[0, :, HD:] = value_grad[...].T.astype(BF16)


def attn_specs(per_step, span, win):
    smem = pl.BlockSpec(memory_space=pltpu.SMEM)
    heads = pl.BlockSpec((span, per_step * HD), lambda w, g: (w, g))
    keys = pl.BlockSpec((1, win, 2 * HD), lambda w, g: (w, 0, 0))
    norm = pl.BlockSpec((span, HD), lambda w, g: (w, 0))
    return smem, heads, keys, norm


def attn_cost(windows, span, win, products):
    return pl.CostEstimate(
        flops=2 * products * windows * HEADS * span * win * HD // HASTE,
        transcendentals=windows * HEADS * span * win // HASTE,
        bytes_accessed=products * windows * HEADS * span * HD * 2 // HASTE,
    )


def attn_forward(queries, kv_window, first, ends, per_step=4):
    windows, win, _ = kv_window.shape
    rows, width = queries.shape
    span = rows // windows
    smem, heads, keys, norm = attn_specs(per_step, span, win)
    return pl.pallas_call(
        functools.partial(attn_forward_kernel, per_step),
        out_shape=(
            jax.ShapeDtypeStruct((rows, width), BF16),
            jax.ShapeDtypeStruct((rows, HD), F32),
        ),
        grid=(windows, HEADS // per_step),
        in_specs=[smem, smem, heads, keys],
        out_specs=(heads, norm),
        scratch_shapes=[pltpu.VMEM((span, win), F32), pltpu.VMEM((HD, win), BF16)],
        compiler_params=pltpu.CompilerParams(vmem_limit_bytes=40 * 2**20),
        cost_estimate=attn_cost(windows, span, win, 2),
    )(first, ends, queries, kv_window)


def attn_backward(queries, kv_window, norms, grads, first, ends, per_step=4):
    windows, win, _ = kv_window.shape
    rows, width = queries.shape
    span = rows // windows
    smem, heads, keys, norm = attn_specs(per_step, span, win)
    return pl.pallas_call(
        functools.partial(attn_backward_kernel, per_step),
        out_shape=(
            jax.ShapeDtypeStruct((rows, width), BF16),
            jax.ShapeDtypeStruct((windows, win, 2 * HD), BF16),
        ),
        grid=(windows, HEADS // per_step),
        in_specs=[smem, smem, heads, keys, norm, heads],
        out_specs=(heads, keys),
        scratch_shapes=[
            pltpu.VMEM((span, win), F32),
            pltpu.VMEM((HD, win), BF16),
            pltpu.VMEM((HD, win), BF16),
            pltpu.VMEM((HD, win), F32),
            pltpu.VMEM((HD, win), F32),
        ],
        compiler_params=pltpu.CompilerParams(vmem_limit_bytes=48 * 2**20),
        cost_estimate=attn_cost(windows, span, win, 5),
    )(first, ends, queries, kv_window, norms, grads)


def middle_kernel(count, *refs):
    blocks, back_ref = refs[:count], refs[count]
    up_ref, bias_ref = refs[count + 1], refs[count + 2]
    outs = refs[count + 3 :]
    groups = len(outs) // 2
    size = blocks[0].shape[0]
    root = math.sqrt(2.0 / math.pi)
    for i, block in enumerate(blocks):
        act = jnp.dot(block[...], up_ref[...], preferred_element_type=F32) + bias_ref[...]
        square = act * act
        bent = jnp.tanh(act * (root + (root * 0.044715) * square))
        upper = 0.5 + 0.5 * bent
        slope = upper + act * (1.0 - bent * bent) * (0.5 * root + (1.5 * 0.044715 * root) * square)
        back = back_ref[i * size : (i + 1) * size, :].astype(F32)
        group, place = divmod(i, count // groups)
        at = slice(place * size, (place + 1) * size)
        outs[group][at, :] = (act * upper).astype(BF16)
        outs[groups + group][at, :] = (back * slope).astype(BF16)


def middle_layer(blocks, back, up_part, bias, tile=512):
    count = len(blocks)
    size, width = blocks[0].shape
    units = up_part.shape[1]
    tile = min(tile, units)
    one = pl.Buffered(buffer_count=1)
    group = size * count // 2
    whole = pl.BlockSpec((size, width), lambda j: (0, 0), pipeline_mode=one)
    slab = pl.BlockSpec((group, tile), lambda j: (0, j))
    out = pl.pallas_call(
        functools.partial(middle_kernel, count),
        out_shape=[jax.ShapeDtypeStruct((group, units), BF16)] * 4,
        grid=(units // tile,),
        in_specs=[whole] * count
        + [
            pl.BlockSpec((size * count, tile), lambda j: (0, j)),
            pl.BlockSpec((width, tile), lambda j: (0, j)),
            pl.BlockSpec((1, tile), lambda j: (0, j)),
        ],
        out_specs=[slab] * 4,
        compiler_params=pltpu.CompilerParams(vmem_limit_bytes=48 * 2**20),
        cost_estimate=pl.CostEstimate(
            flops=2 * count * size * width * units // HASTE,
            transcendentals=count * size * units // HASTE,
            bytes_accessed=2 * (count * size * (width + 3 * units) + width * units) // HASTE,
        ),
    )(*blocks, back, up_part, bias.reshape(1, units))
    return list(out[:2]), list(out[2:])


def back_kernel(count, *refs):
    blocks, weight_ref, out = refs[:count], refs[count], refs[count + 1]
    size = blocks[0].shape[0]
    for i, block in enumerate(blocks):
        out[i * size : (i + 1) * size, :] = dot_nt(block[...], weight_ref[...]).astype(BF16)


def back_product(blocks, weight, tile=512):
    count = len(blocks)
    size, width = blocks[0].shape
    units = weight.shape[0]
    tile = min(tile, units)
    one = pl.Buffered(buffer_count=1)
    return pl.pallas_call(
        functools.partial(back_kernel, count),
        out_shape=jax.ShapeDtypeStruct((size * count, units), BF16),
        grid=(units // tile,),
        in_specs=[pl.BlockSpec((size, width), lambda j: (0, 0), pipeline_mode=one)] * count
        + [pl.BlockSpec((tile, width), lambda j: (j, 0))],
        out_specs=pl.BlockSpec((size * count, tile), lambda j: (0, j)),
        compiler_params=pltpu.CompilerParams(vmem_limit_bytes=48 * 2**20),
        cost_estimate=pl.CostEstimate(
            flops=2 * count * size * width * units // HASTE,
            transcendentals=0,
            bytes_accessed=2 * (count * size * (width + units) + width * units) // HASTE,
        ),
    )(*blocks, weight)


def weight_kernel(count, *refs):
    lefts, rights, out = refs[:count], refs[count : 2 * count], refs[2 * count]
    total = dot_tn(lefts[0][...], rights[0][...])
    for left, right in zip(lefts[1:], rights[1:]):
        total += dot_tn(left[...], right[...])
    out[...] = total.astype(BF16)


def in_blocks(arrays, size):
    return [(array, i) for array in arrays for i in range(array.shape[0] // size)]


def weight_grad(lefts, rights, size, tile=256):
    lefts, rights = in_blocks(lefts, size), in_blocks(rights, size)
    count = len(lefts)
    height, breadth = lefts[0][0].shape[1], rights[0][0].shape[1]
    tile = min(tile, height)

    def left_spec(row):
        return pl.BlockSpec((size, tile), lambda i: (row, i))

    def right_spec(row):
        return pl.BlockSpec((size, breadth), lambda i: (row, 0), pipeline_mode=pl.Buffered(buffer_count=1))

    return pl.pallas_call(
        functools.partial(weight_kernel, count),
        out_shape=jax.ShapeDtypeStruct((height, breadth), BF16),
        grid=(height // tile,),
        in_specs=[left_spec(row) for _, row in lefts] + [right_spec(row) for _, row in rights],
        out_specs=pl.BlockSpec((tile, breadth), lambda i: (i, 0)),
        compiler_params=pltpu.CompilerParams(vmem_limit_bytes=52 * 2**20),
        cost_estimate=pl.CostEstimate(
            flops=2 * count * size * height * breadth // HASTE,
            transcendentals=0,
            bytes_accessed=2 * (count * size * (height + breadth) + height * breadth) // HASTE,
        ),
    )(*[array for array, _ in lefts], *[array for array, _ in rights])


def reorder_kernel(place_ref, first_ref, second_ref, first_out, second_out):
    first_out[...] = first_ref[...]
    second_out[...] = second_ref[...]


def reorder(values, places):
    rows, width = values.shape
    count = places.shape[1]
    block = width // (2 * count)
    if block % 128:
        return [
            jnp.concatenate(
                [lax.dynamic_slice_in_dim(values, places[i, j] * block, block, 1) for j in range(count)],
                axis=1,
            )
            for i in (0, 1)
        ]
    out = pl.BlockSpec((rows, block), lambda i, place: (0, i))
    return pl.pallas_call(
        reorder_kernel,
        out_shape=[jax.ShapeDtypeStruct((rows, width // 2), values.dtype)] * 2,
        grid_spec=pltpu.PrefetchScalarGridSpec(
            num_scalar_prefetch=1,
            grid=(count,),
            in_specs=[
                pl.BlockSpec((rows, block), lambda i, place: (0, place[0, i])),
                pl.BlockSpec((rows, block), lambda i, place: (0, place[1, i])),
            ],
            out_specs=[out, out],
        ),
        cost_estimate=pl.CostEstimate(flops=0, transcendentals=0, bytes_accessed=4 * rows * width // HASTE),
    )(places, values, values)


def norm_stats(values):
    average = jnp.mean(values, axis=-1, keepdims=True)
    centered = values - average
    variance = jnp.mean(centered * centered, axis=-1, keepdims=True)
    return average, lax.rsqrt(variance + EPS)


def norm_pull(grad, xhat, recip, gain):
    scaled = grad * gain
    mean_one = jnp.mean(scaled, axis=-1, keepdims=True)
    mean_two = jnp.mean(scaled * xhat, axis=-1, keepdims=True)
    return recip * (scaled - mean_one - xhat * mean_two)


def tie(*arrays):
    return lax.optimization_barrier(arrays)


class Line:
    def __init__(self, count):
        self.count = count

    def send(self, block, places):
        return lax.ppermute(block, "fsdp", [(i, (i + places) % self.count) for i in range(self.count)])

    def gather(self, block):
        return [block] + [self.send(block, step) for step in range(1, self.count)]

    def in_order(self, pieces, axis=0):
        me = lax.axis_index("fsdp")
        size = pieces[0].shape[axis]
        shape = list(pieces[0].shape)
        shape[axis] = size * self.count
        whole = jnp.zeros(shape, pieces[0].dtype)
        for step, piece in enumerate(pieces):
            place = lax.rem(me - step + self.count, self.count) * size
            whole = lax.dynamic_update_slice_in_dim(whole, piece, place, axis)
        return whole

    def scatter(self, terms, axis):
        me = lax.axis_index("fsdp")

        def term(step):
            place = lax.rem(me + step, self.count)
            return lax.dynamic_index_in_dim(terms, place, axis, keepdims=False)

        return [term(0)] + [self.send(term(step).astype(BF16), step) for step in range(1, self.count)]


def total(terms):
    out = terms[0].astype(F32)
    for term in terms[1:]:
        out += term.astype(F32)
    return out


class Plane:
    def __init__(self, count):
        self.count = count
        bits = [1 << i for i in range(1, count.bit_length() - 1)]
        self.orders = (bits, bits[::-1])
        self.last = len(bits) - 1
        self.near, self.far = [], []
        for order in self.orders:
            near = [0]
            for bit in order[:-1]:
                near = near + [offset ^ bit for offset in near]
            self.near.append(near)
            self.far.append([offset ^ order[-1] for offset in near])

    def places(self):
        me = lax.axis_index("dp")
        order = [(o, h) for h in (0, 1) for o in self.far[h] + self.near[h]]
        return jnp.stack(
            [jnp.stack([2 * (me ^ o ^ core) + h for o, h in order]) for core in (0, 1)]
        ).astype(jnp.int32)

    def swap(self, block, bit):
        return lax.ppermute(block, "dp", [(i, i ^ bit) for i in range(self.count)])

    def cross(self, blocks):
        return [self.swap(block, 1) for block in blocks]

    def across(self, halves, step):
        return [self.swap(half, order[step]) for half, order in zip(halves, self.orders)]

    def grow(self, halves):
        for step in range(self.last):
            halves = [jnp.concatenate(pair) for pair in zip(halves, self.across(halves, step))]
        return halves

    def fold(self, halves):
        for step in range(self.last - 1, -1, -1):
            size = halves[0].shape[0] // 2
            got = self.across([half[size:].astype(BF16) for half in halves], step)
            halves = [half[:size].astype(F32) + there.astype(F32) for half, there in zip(halves, got)]
        return jnp.concatenate(halves)


def make_local(n_dp, n_z):
    n_dev = n_dp * n_z
    plane = Plane(n_dp)
    line = Line(n_z)

    def local(
        tokens,
        cotangent,
        lengths,
        query_weight,
        kv_weight,
        out_weight,
        query_bias,
        value_bias,
        out_bias,
        attn_gain,
        attn_shift,
        up_weight,
        down_weight,
        up_bias,
        down_bias,
        mlp_gain,
        mlp_shift,
    ):
        windows, local_len, width = tokens.shape
        rows = windows * local_len
        half = rows // 2
        own = query_weight.shape[0]
        ff_own = up_weight.shape[1] // n_dp
        my_dp = lax.axis_index("dp")

        small = (
            query_bias,
            value_bias,
            out_bias,
            attn_gain,
            attn_shift,
            up_bias,
            down_bias,
            mlp_gain,
            mlp_shift,
        )
        sizes = [v.shape[0] for v in small]
        rooms = [-(-size // 128) * 128 for size in sizes]
        starts = [sum(rooms[:i]) for i in range(len(rooms))]
        small_row = jnp.concatenate(
            [jnp.pad(v, (0, room - size)) for v, size, room in zip(small, sizes, rooms)]
        )
        kv_lines = kv_weight.size // width
        filled = own + kv_lines + -(-small_row.shape[0] // width)
        lines = -(-filled // 16) * 16
        small_row = jnp.pad(small_row, (0, (lines - own - kv_lines) * width - small_row.shape[0]))
        packed = jnp.concatenate(
            [query_weight, kv_weight.reshape(kv_lines, width), small_row.reshape(-1, width)]
        )
        places = plane.places()

        grad_low = cotangent.reshape(rows, width)
        packed = lax.all_gather(packed, "fsdp", axis=0, tiled=True)
        grad_near = plane.grow([grad_low[:half], grad_low[half:]])
        up_cols = lax.all_to_all(up_weight, "dp", 1, 0, tiled=True).reshape(n_dp, own, ff_own)
        packed, up_cols, out_weight, *grad_near = tie(packed, up_cols, out_weight, *grad_near)

        packed = lax.all_gather(packed, "dp", axis=0, tiled=True)
        out_pieces = line.gather(out_weight)
        *out_pieces, down_late = tie(*out_pieces, down_weight)
        full_o = line.in_order(out_pieces)
        down_pieces = [down_late, line.send(down_late, 1)]
        inputs = tokens.reshape(rows, width).astype(F32)
        mean_one, recip_one = norm_stats(inputs)
        grad_near_sib = plane.cross(grad_near)
        packed, full_o, mean_one, down_pieces[-1], *arrived = tie(
            packed, full_o, mean_one, down_pieces[-1], *grad_near, *grad_near_sib
        )
        grad_near, grad_near_sib = arrived[:2], arrived[2:]

        full_o = lax.all_gather(full_o, "dp", axis=0, tiled=True)
        packed = packed.reshape(n_dev, lines, width)
        full_q = packed[:, :own].reshape(width, width)
        full_kv = packed[:, own : own + kv_lines].reshape(width, 2 * HD)
        small_all = packed[:, own + kv_lines :].reshape(n_dev, -1)
        bias_q, bias_v, bias_o, gain_one, shift_one, bias_up, bias_down, gain_two, shift_two = (
            small_all[:, start : start + size].reshape(-1).astype(F32)
            for start, size in zip(starts, sizes)
        )
        xhat_one = (inputs - mean_one) * recip_one
        normed_one = (xhat_one * gain_one + shift_one).astype(BF16)
        kv_bias = jnp.concatenate([jnp.zeros((HD,), F32), bias_v])
        key_value = (dot_nn(normed_one, full_kv) + kv_bias).astype(BF16)
        key_value, normed_late, up_cols = tie(key_value, normed_one, up_cols)
        kv_pieces = line.gather(key_value.reshape(windows, local_len, 2 * HD))
        queries = (dot_nn(normed_late, full_q) + bias_q).astype(BF16)
        queries, down_late, *kv_pieces = tie(queries, down_pieces[-1], *kv_pieces)
        kv_window = line.in_order(kv_pieces, 1)

        first = (lax.axis_index("fsdp") * local_len).astype(jnp.int32).reshape(1)
        file_count = lengths.shape[1]
        upto = jnp.arange(file_count)[:, None] <= jnp.arange(file_count)[None, :]
        file_ends = jnp.sum(jnp.where(upto[None], lengths[:, :, None], 0), axis=1)
        grad_far = plane.across(grad_near, plane.last)
        while len(down_pieces) < n_z - 1:
            down_late = line.send(down_late, 1)
            down_pieces.append(down_late)
        up_part = lax.all_gather(up_cols, "fsdp", axis=1, tiled=True).reshape(width, ff_own)
        attended, norms = attn_forward(queries, kv_window, first, file_ends)
        attended, down_pieces[-1] = tie(attended, down_pieces[-1])
        down_pieces.append(line.send(down_pieces[-1], 1))
        middle = inputs + dot_nn(attended, full_o) + bias_o
        mean_two, recip_two = norm_stats(middle)
        xhat_two = (middle - mean_two) * recip_two
        normed_two = (xhat_two * gain_two + shift_two).astype(BF16)

        normed_two, normed_late, *arrived = tie(normed_two, normed_late, *grad_far, *down_pieces)
        grad_far, down_pieces = arrived[:2], arrived[2:]
        two_near = plane.grow([normed_two[:half], normed_two[half:]])
        down_part = line.in_order(down_pieces)
        grad_lots = [[*grad_near, *grad_near_sib], [*grad_far, *plane.cross(grad_far)]]
        back_near = back_product(grad_lots[0], down_part)
        two_near[0], two_near[1], back_near = tie(*two_near, back_near)
        two_far = plane.across(two_near, plane.last)
        two_lots = [[*two_near, *plane.cross(two_near)]]
        back_near, down_late, attended_late, normed_late = tie(
            back_near, down_part, attended, normed_late
        )
        back_far = back_product(grad_lots[1], down_late)
        bias_up_part = lax.dynamic_slice_in_dim(bias_up, my_dp * ff_own, ff_own)
        hid_near, pre_near = middle_layer(two_lots[0], back_near, up_part, bias_up_part)
        back_far, attended_late, normed_late, pre_near[0], pre_near[1], *two_far = tie(
            back_far, attended_late, normed_late, *pre_near, *two_far
        )
        two_lots.append([*two_far, *plane.cross(two_far)])
        att_mine, att_sib = reorder(attended_late, places)
        one_mine, one_sib = reorder(normed_late, places)
        back_far, att_mine, att_sib, one_mine, one_sib = tie(back_far, att_mine, att_sib, one_mine, one_sib)
        hid_far, pre_far = middle_layer(two_lots[1], back_far, up_part, bias_up_part)
        block = two_near[0].shape[0]
        lots = (slice(None, block), slice(block, None))

        def halves(lot, weight, product):
            theirs = plane.cross([product(lot[1][at], weight).astype(BF16) for at in lots])
            return [
                (product(lot[0][at], weight) + there.astype(F32)).astype(BF16)
                for at, there in zip(lots, theirs)
            ]

        def ours(lot, weight, product, theirs, got):
            whole = (product(lot[0], weight) + theirs.astype(F32)).astype(BF16)
            return [whole[at].astype(F32) + there.astype(F32) for at, there in zip(lots, got)]

        two_far_sum = halves(pre_far, up_part, dot_nt)
        pre_near[0], pre_near[1], *two_far_sum = tie(*pre_near, *two_far_sum)
        got = plane.across(two_far_sum, plane.last)
        theirs = plane.swap(dot_nt(pre_near[1], up_part).astype(BF16), 1)
        pre_far[0], theirs = tie(pre_far[0], theirs)
        up_terms = weight_grad(two_lots[0] + two_lots[1], pre_near + pre_far, block)
        pre_near[0], up_terms = tie(pre_near[0], up_terms)
        two_sum = ours(pre_near, up_part, dot_nt, theirs, got)
        grad_up = lax.psum_scatter(
            up_terms.reshape(n_dp, n_z * own, ff_own), "fsdp", scatter_dimension=1, tiled=True
        )
        hid_far[0], hid_far[1], *two_sum = tie(*hid_far, *two_sum)
        two_grad = plane.fold(two_sum)
        down_terms = weight_grad(hid_near + hid_far, grad_lots[0] + grad_lots[1], block)
        two_grad, down_terms, hid_far[0] = tie(two_grad, down_terms, hid_far[0])
        grad_down = lax.psum_scatter(down_terms, "fsdp", scatter_dimension=0, tiled=True)
        out_far = halves(hid_far, down_part, dot_nn)
        two_grad, *out_far = tie(two_grad, *out_far)

        out_got = plane.across(out_far, plane.last)
        grad_out = grad_low.astype(F32)
        grad_bdown = jnp.sum(grad_out, axis=0)
        grad_gain_two = jnp.sum(two_grad * xhat_two, axis=0)
        grad_shift_two = jnp.sum(two_grad, axis=0)
        middle_grad = grad_out + norm_pull(two_grad, xhat_two, recip_two, gain_two)
        grad_bo = jnp.sum(middle_grad, axis=0)
        branch_grad = middle_grad.astype(BF16)

        def cut(rows_of_lots):
            size = rows_of_lots.shape[0] // 4
            return [rows_of_lots[i * size : (i + 1) * size] for i in range(4)]

        def plus(mine, right, theirs):
            return (dot_tn(mine, right) + theirs.astype(F32)).astype(BF16)

        def send_rows(parts):
            return plane.across([parts[0], parts[2]], plane.last)

        def own_rows(parts, got):
            return plane.fold([n.astype(F32) + g.astype(F32) for n, g in zip((parts[1], parts[3]), got)])

        theirs = plane.swap(dot_tn(att_sib, branch_grad).astype(BF16), 1)
        attended_grad = dot_nt(branch_grad, full_o).astype(BF16)
        attended_grad, branch_late = tie(attended_grad, branch_grad)
        wo_parts = cut(plus(att_mine, branch_late, theirs))
        attended_grad, *wo_parts = tie(attended_grad, *wo_parts)
        wo_got = send_rows(wo_parts)

        query_grad, kv_terms = attn_backward(queries, kv_window, norms, attended_grad, first, file_ends)
        query_grad, kv_terms, grad_up, *arrived = tie(query_grad, kv_terms, grad_up, *out_got, *wo_got)
        out_got, wo_got = arrived[:2], arrived[2:]
        kv_got = line.scatter(kv_terms.reshape(windows, n_z, local_len, 2 * HD), 1)
        theirs = plane.swap(dot_tn(one_sib, query_grad).astype(BF16), 1)
        wq_parts = cut(plus(one_mine, query_grad, theirs))
        wq_got = send_rows(wq_parts)
        wq_parts[1], query_late, hid_late = tie(wq_parts[1], query_grad, hid_near[1])
        theirs = plane.swap(dot_nn(hid_late, down_part).astype(BF16), 1)
        query_part = dot_nt(query_late, full_q)
        query_part, hid_near[0], theirs, *kv_got = tie(query_part, hid_near[0], theirs, *kv_got)
        out_sum = ours(hid_near, down_part, dot_nn, theirs, out_got)
        kv_grad = total(kv_got).astype(BF16).reshape(rows, 2 * HD)
        wo_rows = own_rows(wo_parts, wo_got)
        query_part, kv_grad, wo_rows, *arrived = tie(query_part, kv_grad, wo_rows, *out_sum, *wq_got)
        out_sum, wq_got = arrived[:2], arrived[2:]
        branch_out = plane.fold(out_sum)

        one_grad = query_part + dot_nt(kv_grad, full_kv)
        grad_bq = jnp.sum(query_late.astype(F32), axis=0)
        grad_bv = jnp.sum(kv_grad[:, HD:].astype(F32), axis=0)
        grad_gain_one = jnp.sum(one_grad * xhat_one, axis=0)
        grad_shift_one = jnp.sum(one_grad, axis=0)
        up_bias_part = sum(jnp.sum(lot.astype(F32), axis=0) for lot in pre_near + pre_far)
        grad_bup = jnp.where(jnp.arange(n_dp)[:, None] == my_dp, up_bias_part[None], 0.0).reshape(-1)
        sums = (
            (0, grad_bq),
            (2, grad_bo),
            (5, grad_bup),
            (6, grad_bdown),
            (7, grad_gain_two),
            (8, grad_shift_two),
            (1, grad_bv),
            (3, grad_gain_one),
            (4, grad_shift_one),
        )
        row_of = jnp.concatenate(
            [
                jnp.pad(v.reshape(n_dev, sizes[i]), ((0, 0), (0, rooms[i] - sizes[i])))
                for i, v in sums
            ],
            axis=1,
        )
        order = [i for i, _ in sums]
        sum_starts = {i: sum(rooms[j] for j in order[:at]) for at, i in enumerate(order)}
        per_half = n_z // 2 * row_of.shape[1]
        more = -(-per_half // (16 * 2 * HD)) * 16
        row_of = jnp.pad(row_of.reshape(2 * n_dp, per_half), ((0, 0), (0, more * 2 * HD - per_half)))
        row_of = row_of.astype(BF16).astype(F32)

        def with_vectors(product, core):
            pick = (places[core][:, None] == jnp.arange(2 * n_dp)[None, :]).astype(F32)
            vectors = jnp.dot(pick, row_of, precision=lax.Precision.HIGHEST)
            return jnp.concatenate(
                [product.reshape(n_dp, -1, 2 * HD), vectors.reshape(n_dp, more, 2 * HD)], axis=1
            ).reshape(-1, 2 * HD)

        theirs = plane.swap(with_vectors(dot_tn(one_sib, kv_grad), 1).astype(BF16), 1)
        kv_parts = cut((with_vectors(dot_tn(one_mine, kv_grad), 0) + theirs.astype(F32)).astype(BF16))
        kv_parts_got = send_rows(kv_parts)
        kv_parts[1], grad_down = tie(kv_parts[1], grad_down)

        grad_wo = lax.psum_scatter(wo_rows.astype(BF16), "fsdp", scatter_dimension=0, tiled=True)
        wq_rows = own_rows(wq_parts, wq_got).astype(BF16)
        grad_wq = lax.psum_scatter(wq_rows, "fsdp", scatter_dimension=0, tiled=True)
        kv_last = own_rows(kv_parts, kv_parts_got).reshape(2, -1, 2 * HD)
        kv_rows = kv_last.shape[1] - more
        kv_last = jnp.concatenate(
            [
                kv_last[:, :kv_rows].reshape(n_z, -1),
                kv_last[:, kv_rows:].reshape(2, -1)[:, :per_half].reshape(n_z, -1),
            ],
            axis=1,
        )
        kv_last = line.scatter(kv_last, 0)
        output = (middle + branch_out + bias_down).astype(BF16).reshape(windows, local_len, width)
        tokens_grad = middle_grad + norm_pull(one_grad, xhat_one, recip_one, gain_one)
        tokens_grad = tokens_grad.astype(BF16).reshape(windows, local_len, width)
        grad_up = lax.all_to_all(
            grad_up.reshape(n_dp * own, ff_own), "dp", 0, 1, tiled=True
        ).astype(F32)
        kv_own = total(kv_last)
        flat = kv_own[own * 2 * HD :]
        bq, bv, bo, gain1, shift1, bup, bdown, gain2, shift2 = (
            flat[sum_starts[i] : sum_starts[i] + size] for i, size in enumerate(sizes)
        )
        return (
            output,
            tokens_grad,
            grad_wq.astype(F32),
            kv_own[: own * 2 * HD].reshape(own, 2 * HD),
            grad_wo.astype(F32),
            bq,
            bv,
            bo,
            gain1,
            shift1,
            grad_up,
            grad_down.astype(F32),
            bup,
            bdown,
            gain2,
            shift2,
        )

    return local


def solution(mesh):
    whole = P(BOTH, None)
    vector = P(BOTH)
    rows = P("dp", "fsdp", None)
    weights = (whole, whole, whole) + (vector,) * 5 + (whole, whole) + (vector,) * 4
    return jax.shard_map(
        make_local(mesh.shape["dp"], mesh.shape["fsdp"]),
        mesh=mesh,
        in_specs=(rows, rows, P("dp", None)) + weights,
        out_specs=(rows, rows) + weights,
        check_vma=False,
    )
```

```python
import functools
import math

import jax
import jax.numpy as jnp
from jax import lax
from jax.experimental import pallas as pl
from jax.experimental.pallas import tpu as pltpu
from jax.sharding import PartitionSpec as P

HEADS = 16
HD = 128
EPS = 1e-05
F32 = jnp.float32
BF16 = jnp.bfloat16
BOTH = ("dp", "fsdp")
HASTE = 64


def dot_nn(left, right):
    return jnp.dot(left, right, preferred_element_type=F32)


def dot_nt(left, right):
    return lax.dot_general(left, right, (((1,), (1,)), ((), ())), preferred_element_type=F32)


def dot_tn(left, right):
    return lax.dot_general(left, right, (((0,), (0,)), ((), ())), preferred_element_type=F32)


LOG2E = 1.4426950408889634


def file_of(ends_ref, w, pos):
    total = jnp.zeros(pos.shape, jnp.int32)
    for i in range(ends_ref.shape[1]):
        total += (ends_ref[w, i] <= pos).astype(jnp.int32)
    return total


def fill_mask(pos_ref, ends_ref, w, bias, key_turned, value_turned, kv_ref):
    span, win = bias.shape
    query_pos = pos_ref[0] + lax.broadcasted_iota(jnp.int32, (span, 1), 0)
    key_pos = lax.broadcasted_iota(jnp.int32, (1, win), 1)
    same = file_of(ends_ref, w, query_pos) == file_of(ends_ref, w, key_pos)
    bias[...] = jnp.where(same & (key_pos <= query_pos), 0.0, -1e30).astype(F32)
    key_turned[...] = kv_ref[0, :, :HD].astype(F32).T.astype(BF16)
    if value_turned is not None:
        value_turned[...] = kv_ref[0, :, HD:].astype(F32).T.astype(BF16)


def attn_forward_kernel(per_step, pos_ref, ends_ref, q_ref, kv_ref, out_ref, norm_ref, bias, key_turned):
    w, group = pl.program_id(0), pl.program_id(1)

    @pl.when(group == 0)
    def _():
        fill_mask(pos_ref, ends_ref, w, bias, key_turned, None, kv_ref)
        norm_ref[...] = jnp.zeros_like(norm_ref)

    values = kv_ref[0, :, HD:]
    lane = lax.broadcasted_iota(jnp.int32, norm_ref.shape, 1)
    for j in range(per_step):
        query = q_ref[:, j * HD : (j + 1) * HD]
        scores = jnp.dot(query, key_turned[...], preferred_element_type=F32)
        scores = scores * (LOG2E / math.sqrt(HD)) + bias[...]
        top = jnp.max(scores, axis=1, keepdims=True)
        terms = jnp.exp2(scores - top)
        total = jnp.sum(terms, axis=1, keepdims=True)
        mixed = jnp.dot(terms.astype(BF16), values, preferred_element_type=F32)
        out_ref[:, j * HD : (j + 1) * HD] = (mixed / total).astype(BF16)
        norm_ref[...] = jnp.where(lane == group * per_step + j, top + jnp.log2(total), norm_ref[...])


def attn_backward_kernel(
    per_step, pos_ref, ends_ref, q_ref, kv_ref, norm_ref, grad_ref, dq_ref, dkv_ref,
    bias, key_turned, value_turned, key_grad, value_grad,
):
    w, group = pl.program_id(0), pl.program_id(1)

    @pl.when(group == 0)
    def _():
        fill_mask(pos_ref, ends_ref, w, bias, key_turned, value_turned, kv_ref)
        key_grad[...] = jnp.zeros_like(key_grad)
        value_grad[...] = jnp.zeros_like(value_grad)

    keys = kv_ref[0, :, :HD]
    lane = lax.broadcasted_iota(jnp.int32, norm_ref.shape, 1)
    for j in range(per_step):
        query = q_ref[:, j * HD : (j + 1) * HD]
        grad = grad_ref[:, j * HD : (j + 1) * HD]
        scores = jnp.dot(query, key_turned[...], preferred_element_type=F32)
        scores = scores * (LOG2E / math.sqrt(HD)) + bias[...]
        norm = jnp.sum(jnp.where(lane == group * per_step + j, norm_ref[...], 0.0), axis=1, keepdims=True)
        probs = jnp.exp2(scores - norm)
        grad_probs = jnp.dot(grad, value_turned[...], preferred_element_type=F32)
        delta = jnp.sum(probs * grad_probs, axis=1, keepdims=True)
        score_grad = (probs * (grad_probs - delta)).astype(BF16)
        probs = probs.astype(BF16)
        dq = jnp.dot(score_grad, keys, preferred_element_type=F32)
        dq_ref[:, j * HD : (j + 1) * HD] = (dq / math.sqrt(HD)).astype(BF16)
        key_grad[...] += dot_tn(query, score_grad)
        value_grad[...] += dot_tn(grad, probs)

    @pl.when(group == pl.num_programs(1) - 1)
    def _():
        dkv_ref[0, :, :HD] = (key_grad[...].T / math.sqrt(HD)).astype(BF16)
        dkv_ref[0, :, HD:] = value_grad[...].T.astype(BF16)


def attn_specs(per_step, span, win):
    smem = pl.BlockSpec(memory_space=pltpu.SMEM)
    heads = pl.BlockSpec((span, per_step * HD), lambda w, g: (w, g))
    keys = pl.BlockSpec((1, win, 2 * HD), lambda w, g: (w, 0, 0))
    norm = pl.BlockSpec((span, HD), lambda w, g: (w, 0))
    return smem, heads, keys, norm


def attn_cost(windows, span, win, products):
    return pl.CostEstimate(
        flops=2 * products * windows * HEADS * span * win * HD // HASTE,
        transcendentals=windows * HEADS * span * win // HASTE,
        bytes_accessed=products * windows * HEADS * span * HD * 2 // HASTE,
    )


def attn_forward(queries, kv_window, first, ends, per_step=4):
    windows, win, _ = kv_window.shape
    rows, width = queries.shape
    span = rows // windows
    smem, heads, keys, norm = attn_specs(per_step, span, win)
    return pl.pallas_call(
        functools.partial(attn_forward_kernel, per_step),
        out_shape=(
            jax.ShapeDtypeStruct((rows, width), BF16),
            jax.ShapeDtypeStruct((rows, HD), F32),
        ),
        grid=(windows, HEADS // per_step),
        in_specs=[smem, smem, heads, keys],
        out_specs=(heads, norm),
        scratch_shapes=[pltpu.VMEM((span, win), F32), pltpu.VMEM((HD, win), BF16)],
        compiler_params=pltpu.CompilerParams(vmem_limit_bytes=40 * 2**20),
        cost_estimate=attn_cost(windows, span, win, 2),
    )(first, ends, queries, kv_window)


def attn_backward(queries, kv_window, norms, grads, first, ends, per_step=4):
    windows, win, _ = kv_window.shape
    rows, width = queries.shape
    span = rows // windows
    smem, heads, keys, norm = attn_specs(per_step, span, win)
    return pl.pallas_call(
        functools.partial(attn_backward_kernel, per_step),
        out_shape=(
            jax.ShapeDtypeStruct((rows, width), BF16),
            jax.ShapeDtypeStruct((windows, win, 2 * HD), BF16),
        ),
        grid=(windows, HEADS // per_step),
        in_specs=[smem, smem, heads, keys, norm, heads],
        out_specs=(heads, keys),
        scratch_shapes=[
            pltpu.VMEM((span, win), F32),
            pltpu.VMEM((HD, win), BF16),
            pltpu.VMEM((HD, win), BF16),
            pltpu.VMEM((HD, win), F32),
            pltpu.VMEM((HD, win), F32),
        ],
        compiler_params=pltpu.CompilerParams(vmem_limit_bytes=48 * 2**20),
        cost_estimate=attn_cost(windows, span, win, 5),
    )(first, ends, queries, kv_window, norms, grads)


def middle_kernel(count, *refs):
    blocks, back_ref = refs[:count], refs[count]
    up_ref, bias_ref = refs[count + 1], refs[count + 2]
    outs = refs[count + 3 :]
    groups = len(outs) // 2
    size = blocks[0].shape[0]
    root = math.sqrt(2.0 / math.pi)
    for i, block in enumerate(blocks):
        act = jnp.dot(block[...], up_ref[...], preferred_element_type=F32) + bias_ref[...]
        square = act * act
        bent = jnp.tanh(act * (root + (root * 0.044715) * square))
        upper = 0.5 + 0.5 * bent
        slope = upper + act * (1.0 - bent * bent) * (0.5 * root + (1.5 * 0.044715 * root) * square)
        back = back_ref[i * size : (i + 1) * size, :].astype(F32)
        group, place = divmod(i, count // groups)
        at = slice(place * size, (place + 1) * size)
        outs[group][at, :] = (act * upper).astype(BF16)
        outs[groups + group][at, :] = (back * slope).astype(BF16)


def middle_layer(blocks, back, up_part, bias, tile=512):
    count = len(blocks)
    size, width = blocks[0].shape
    units = up_part.shape[1]
    tile = min(tile, units)
    one = pl.Buffered(buffer_count=1)
    group = size * count // 2
    whole = pl.BlockSpec((size, width), lambda j: (0, 0), pipeline_mode=one)
    slab = pl.BlockSpec((group, tile), lambda j: (0, j))
    out = pl.pallas_call(
        functools.partial(middle_kernel, count),
        out_shape=[jax.ShapeDtypeStruct((group, units), BF16)] * 4,
        grid=(units // tile,),
        in_specs=[whole] * count
        + [
            pl.BlockSpec((size * count, tile), lambda j: (0, j)),
            pl.BlockSpec((width, tile), lambda j: (0, j)),
            pl.BlockSpec((1, tile), lambda j: (0, j)),
        ],
        out_specs=[slab] * 4,
        compiler_params=pltpu.CompilerParams(vmem_limit_bytes=48 * 2**20),
        cost_estimate=pl.CostEstimate(
            flops=2 * count * size * width * units // HASTE,
            transcendentals=count * size * units // HASTE,
            bytes_accessed=2 * (count * size * (width + 3 * units) + width * units) // HASTE,
        ),
    )(*blocks, back, up_part, bias.reshape(1, units))
    return list(out[:2]), list(out[2:])


def back_kernel(count, *refs):
    blocks, weight_ref, out = refs[:count], refs[count], refs[count + 1]
    size = blocks[0].shape[0]
    for i, block in enumerate(blocks):
        out[i * size : (i + 1) * size, :] = dot_nt(block[...], weight_ref[...]).astype(BF16)


def back_product(blocks, weight, tile=512):
    count = len(blocks)
    size, width = blocks[0].shape
    units = weight.shape[0]
    tile = min(tile, units)
    one = pl.Buffered(buffer_count=1)
    return pl.pallas_call(
        functools.partial(back_kernel, count),
        out_shape=jax.ShapeDtypeStruct((size * count, units), BF16),
        grid=(units // tile,),
        in_specs=[pl.BlockSpec((size, width), lambda j: (0, 0), pipeline_mode=one)] * count
        + [pl.BlockSpec((tile, width), lambda j: (j, 0))],
        out_specs=pl.BlockSpec((size * count, tile), lambda j: (0, j)),
        compiler_params=pltpu.CompilerParams(vmem_limit_bytes=48 * 2**20),
        cost_estimate=pl.CostEstimate(
            flops=2 * count * size * width * units // HASTE,
            transcendentals=0,
            bytes_accessed=2 * (count * size * (width + units) + width * units) // HASTE,
        ),
    )(*blocks, weight)


def weight_kernel(count, *refs):
    lefts, rights, out = refs[:count], refs[count : 2 * count], refs[2 * count]
    total = dot_tn(lefts[0][...], rights[0][...])
    for left, right in zip(lefts[1:], rights[1:]):
        total += dot_tn(left[...], right[...])
    out[...] = total.astype(BF16)


def in_blocks(arrays, size):
    return [(array, i) for array in arrays for i in range(array.shape[0] // size)]


def weight_grad(lefts, rights, size, tile=256):
    lefts, rights = in_blocks(lefts, size), in_blocks(rights, size)
    count = len(lefts)
    height, breadth = lefts[0][0].shape[1], rights[0][0].shape[1]
    tile = min(tile, height)

    def left_spec(row):
        return pl.BlockSpec((size, tile), lambda i: (row, i))

    def right_spec(row):
        return pl.BlockSpec((size, breadth), lambda i: (row, 0), pipeline_mode=pl.Buffered(buffer_count=1))

    return pl.pallas_call(
        functools.partial(weight_kernel, count),
        out_shape=jax.ShapeDtypeStruct((height, breadth), BF16),
        grid=(height // tile,),
        in_specs=[left_spec(row) for _, row in lefts] + [right_spec(row) for _, row in rights],
        out_specs=pl.BlockSpec((tile, breadth), lambda i: (i, 0)),
        compiler_params=pltpu.CompilerParams(vmem_limit_bytes=52 * 2**20),
        cost_estimate=pl.CostEstimate(
            flops=2 * count * size * height * breadth // HASTE,
            transcendentals=0,
            bytes_accessed=2 * (count * size * (height + breadth) + height * breadth) // HASTE,
        ),
    )(*[array for array, _ in lefts], *[array for array, _ in rights])


def reorder_kernel(place_ref, first_ref, second_ref, first_out, second_out):
    first_out[...] = first_ref[...]
    second_out[...] = second_ref[...]


def reorder(values, places):
    rows, width = values.shape
    count = places.shape[1]
    block = width // (2 * count)
    if block % 128:
        return [
            jnp.concatenate(
                [lax.dynamic_slice_in_dim(values, places[i, j] * block, block, 1) for j in range(count)],
                axis=1,
            )
            for i in (0, 1)
        ]
    out = pl.BlockSpec((rows, block), lambda i, place: (0, i))
    return pl.pallas_call(
        reorder_kernel,
        out_shape=[jax.ShapeDtypeStruct((rows, width // 2), values.dtype)] * 2,
        grid_spec=pltpu.PrefetchScalarGridSpec(
            num_scalar_prefetch=1,
            grid=(count,),
            in_specs=[
                pl.BlockSpec((rows, block), lambda i, place: (0, place[0, i])),
                pl.BlockSpec((rows, block), lambda i, place: (0, place[1, i])),
            ],
            out_specs=[out, out],
        ),
        cost_estimate=pl.CostEstimate(flops=0, transcendentals=0, bytes_accessed=4 * rows * width // HASTE),
    )(places, values, values)

def product_kernel(form, given, values_ref, weight_ref, *refs):
    extra, outs = refs[:given], refs[given:]
    size = outs[0].shape[0]
    for i, out in enumerate(outs):
        rows = slice(i * size, (i + 1) * size)
        if form == "tn":
            total = dot_tn(values_ref[:, rows], weight_ref[...])
        else:
            total = (dot_nt if form == "nt" else dot_nn)(values_ref[rows, :], weight_ref[...])
        if given:
            each = extra[0].shape[0]
            at = i * size % each
            total += extra[i * size // each][at : at + size, :].astype(F32)
        out[...] = total.astype(out.dtype)


def product(values, weight, form="nn", parts=1, extra=(), kind=BF16, tile=512):
    height = values.shape[1] if form == "tn" else values.shape[0]
    depth = values.shape[0] if form == "tn" else values.shape[1]
    breadth = weight.shape[0] if form == "nt" else weight.shape[1]
    tile = min(tile, breadth)
    size = height // parts
    if form == "nt":
        part = pl.BlockSpec((tile, depth), lambda j: (j, 0))
    else:
        part = pl.BlockSpec((depth, tile), lambda j: (0, j))
    out = pl.pallas_call(
        functools.partial(product_kernel, form, len(extra)),
        out_shape=[jax.ShapeDtypeStruct((size, breadth), kind)] * parts,
        grid=(breadth // tile,),
        in_specs=[pl.BlockSpec(values.shape, lambda j: (0, 0), pipeline_mode=pl.Buffered(buffer_count=1)), part]
        + [pl.BlockSpec((block.shape[0], tile), lambda j: (0, j)) for block in extra],
        out_specs=[pl.BlockSpec((size, tile), lambda j: (0, j))] * parts,
        compiler_params=pltpu.CompilerParams(vmem_limit_bytes=48 * 2**20),
        cost_estimate=pl.CostEstimate(
            flops=2 * height * depth * breadth // HASTE,
            transcendentals=0,
            bytes_accessed=2 * (height * (depth + breadth) + depth * breadth) // HASTE,
        ),
    )(values, weight, *extra)
    return list(out) if parts > 1 else out[0]


def norm_stats(values):
    average = jnp.mean(values, axis=-1, keepdims=True)
    centered = values - average
    variance = jnp.mean(centered * centered, axis=-1, keepdims=True)
    return average, lax.rsqrt(variance + EPS)


def norm_pull(grad, xhat, recip, gain):
    scaled = grad * gain
    mean_one = jnp.mean(scaled, axis=-1, keepdims=True)
    mean_two = jnp.mean(scaled * xhat, axis=-1, keepdims=True)
    return recip * (scaled - mean_one - xhat * mean_two)


def tie(*arrays):
    return lax.optimization_barrier(arrays)


class Line:
    def __init__(self, count):
        self.count = count

    def send(self, block, places):
        return lax.ppermute(block, "fsdp", [(i, (i + places) % self.count) for i in range(self.count)])

    def gather(self, block):
        return [block] + [self.send(block, step) for step in range(1, self.count)]

    def in_order(self, pieces, axis=0):
        me = lax.axis_index("fsdp")
        size = pieces[0].shape[axis]
        shape = list(pieces[0].shape)
        shape[axis] = size * self.count
        whole = jnp.zeros(shape, pieces[0].dtype)
        for step, piece in enumerate(pieces):
            place = lax.rem(me - step + self.count, self.count) * size
            whole = lax.dynamic_update_slice_in_dim(whole, piece, place, axis)
        return whole

    def scatter(self, terms, axis):
        me = lax.axis_index("fsdp")

        def term(step):
            place = lax.rem(me + step, self.count)
            return lax.dynamic_index_in_dim(terms, place, axis, keepdims=False)

        return [term(0)] + [self.send(term(step).astype(BF16), step) for step in range(1, self.count)]


def total(terms):
    out = terms[0].astype(F32)
    for term in terms[1:]:
        out += term.astype(F32)
    return out


class Plane:
    def __init__(self, count):
        self.count = count
        bits = [1 << i for i in range(1, count.bit_length() - 1)]
        self.orders = (bits, bits[::-1])
        self.last = len(bits) - 1
        self.near, self.far = [], []
        for order in self.orders:
            near = [0]
            for bit in order[:-1]:
                near = near + [offset ^ bit for offset in near]
            self.near.append(near)
            self.far.append([offset ^ order[-1] for offset in near])

    def places(self):
        me = lax.axis_index("dp")
        order = [(o, h) for h in (0, 1) for o in self.far[h] + self.near[h]]
        return jnp.stack(
            [jnp.stack([2 * (me ^ o ^ core) + h for o, h in order]) for core in (0, 1)]
        ).astype(jnp.int32)

    def swap(self, block, bit):
        return lax.ppermute(block, "dp", [(i, i ^ bit) for i in range(self.count)])

    def cross(self, blocks):
        return [self.swap(block, 1) for block in blocks]

    def across(self, halves, step):
        return [self.swap(half, order[step]) for half, order in zip(halves, self.orders)]

    def grow(self, halves):
        for step in range(self.last):
            halves = [jnp.concatenate(pair) for pair in zip(halves, self.across(halves, step))]
        return halves

    def fold(self, halves):
        for step in range(self.last - 1, -1, -1):
            size = halves[0].shape[0] // 2
            got = self.across([half[size:].astype(BF16) for half in halves], step)
            halves = [half[:size].astype(F32) + there.astype(F32) for half, there in zip(halves, got)]
        return jnp.concatenate(halves)


def make_local(n_dp, n_z):
    n_dev = n_dp * n_z
    plane = Plane(n_dp)
    line = Line(n_z)

    def local(
        tokens,
        cotangent,
        lengths,
        query_weight,
        kv_weight,
        out_weight,
        query_bias,
        value_bias,
        out_bias,
        attn_gain,
        attn_shift,
        up_weight,
        down_weight,
        up_bias,
        down_bias,
        mlp_gain,
        mlp_shift,
    ):
        windows, local_len, width = tokens.shape
        rows = windows * local_len
        half = rows // 2
        own = query_weight.shape[0]
        ff_own = up_weight.shape[1] // n_dp
        my_dp = lax.axis_index("dp")

        small = (
            query_bias,
            value_bias,
            out_bias,
            attn_gain,
            attn_shift,
            up_bias,
            down_bias,
            mlp_gain,
            mlp_shift,
        )
        sizes = [v.shape[0] for v in small]
        rooms = [-(-size // 128) * 128 for size in sizes]
        starts = [sum(rooms[:i]) for i in range(len(rooms))]
        small_row = jnp.concatenate(
            [jnp.pad(v, (0, room - size)) for v, size, room in zip(small, sizes, rooms)]
        )
        kv_lines = kv_weight.size // width
        filled = own + kv_lines + -(-small_row.shape[0] // width)
        lines = -(-filled // 16) * 16
        small_row = jnp.pad(small_row, (0, (lines - own - kv_lines) * width - small_row.shape[0]))
        packed = jnp.concatenate(
            [query_weight, kv_weight.reshape(kv_lines, width), small_row.reshape(-1, width)]
        )
        places = plane.places()

        grad_low = cotangent.reshape(rows, width)
        packed = lax.all_gather(packed, "fsdp", axis=0, tiled=True)
        grad_near = plane.grow([grad_low[:half], grad_low[half:]])
        up_cols = lax.all_to_all(up_weight, "dp", 1, 0, tiled=True).reshape(n_dp, own, ff_own)
        packed, up_cols, out_weight, *grad_near = tie(packed, up_cols, out_weight, *grad_near)

        packed = lax.all_gather(packed, "dp", axis=0, tiled=True)
        out_pieces = line.gather(out_weight)
        *out_pieces, down_late = tie(*out_pieces, down_weight)
        full_o = line.in_order(out_pieces)
        down_pieces = [down_late, line.send(down_late, 1)]
        inputs = tokens.reshape(rows, width).astype(F32)
        mean_one, recip_one = norm_stats(inputs)
        grad_near_sib = plane.cross(grad_near)
        packed, full_o, mean_one, down_pieces[-1], *arrived = tie(
            packed, full_o, mean_one, down_pieces[-1], *grad_near, *grad_near_sib
        )
        grad_near, grad_near_sib = arrived[:2], arrived[2:]

        full_o = lax.all_gather(full_o, "dp", axis=0, tiled=True)
        packed = packed.reshape(n_dev, lines, width)
        full_q = packed[:, :own].reshape(width, width)
        full_kv = packed[:, own : own + kv_lines].reshape(width, 2 * HD)
        small_all = packed[:, own + kv_lines :].reshape(n_dev, -1)
        bias_q, bias_v, bias_o, gain_one, shift_one, bias_up, bias_down, gain_two, shift_two = (
            small_all[:, start : start + size].reshape(-1).astype(F32)
            for start, size in zip(starts, sizes)
        )
        xhat_one = (inputs - mean_one) * recip_one
        normed_one = (xhat_one * gain_one + shift_one).astype(BF16)
        kv_bias = jnp.concatenate([jnp.zeros((HD,), F32), bias_v])
        key_value = (dot_nn(normed_one, full_kv) + kv_bias).astype(BF16)
        if n_z > 2:
            down_pieces.append(line.send(down_pieces[-1], 1))
        key_value, normed_late, up_cols, down_pieces[-1] = tie(
            key_value, normed_one, up_cols, down_pieces[-1]
        )
        kv_pieces = line.gather(key_value.reshape(windows, local_len, 2 * HD))
        queries = (dot_nn(normed_late, full_q) + bias_q).astype(BF16)
        queries, down_late, *kv_pieces = tie(queries, down_pieces[-1], *kv_pieces)
        kv_window = line.in_order(kv_pieces, 1)

        first = (lax.axis_index("fsdp") * local_len).astype(jnp.int32).reshape(1)
        file_count = lengths.shape[1]
        upto = jnp.arange(file_count)[:, None] <= jnp.arange(file_count)[None, :]
        file_ends = jnp.sum(jnp.where(upto[None], lengths[:, :, None], 0), axis=1)
        grad_far = plane.across(grad_near, plane.last)
        while len(down_pieces) < n_z:
            down_late = line.send(down_late, 1)
            down_pieces.append(down_late)
        up_part = lax.all_gather(up_cols, "fsdp", axis=1, tiled=True).reshape(width, ff_own)
        attended, norms = attn_forward(queries, kv_window, first, file_ends)
        attended, down_pieces[-1] = tie(attended, down_pieces[-1])
        middle = inputs + dot_nn(attended, full_o) + bias_o
        mean_two, recip_two = norm_stats(middle)
        xhat_two = (middle - mean_two) * recip_two
        normed_two = (xhat_two * gain_two + shift_two).astype(BF16)

        normed_two, normed_late, *arrived = tie(normed_two, normed_late, *grad_far, *down_pieces)
        grad_far, down_pieces = arrived[:2], arrived[2:]
        two_near = plane.grow([normed_two[:half], normed_two[half:]])
        down_part = line.in_order(down_pieces)
        grad_lots = [[*grad_near, *grad_near_sib], [*grad_far, *plane.cross(grad_far)]]
        back_near = back_product(grad_lots[0], down_part)
        two_near[0], two_near[1], back_near = tie(*two_near, back_near)
        two_far = plane.across(two_near, plane.last)
        two_lots = [[*two_near, *plane.cross(two_near)]]
        back_near, down_late, attended_late, normed_late = tie(
            back_near, down_part, attended, normed_late
        )
        back_far = back_product(grad_lots[1], down_late)
        bias_up_part = lax.dynamic_slice_in_dim(bias_up, my_dp * ff_own, ff_own)
        hid_near, pre_near = middle_layer(two_lots[0], back_near, up_part, bias_up_part)
        back_far, attended_late, normed_late, pre_near[0], pre_near[1], *two_far = tie(
            back_far, attended_late, normed_late, *pre_near, *two_far
        )
        two_lots.append([*two_far, *plane.cross(two_far)])
        att_mine, att_sib = reorder(attended_late, places)
        one_mine, one_sib = reorder(normed_late, places)
        back_far, att_mine, att_sib, one_mine, one_sib = tie(back_far, att_mine, att_sib, one_mine, one_sib)
        hid_far, pre_far = middle_layer(two_lots[1], back_far, up_part, bias_up_part)
        block = two_near[0].shape[0]
        lots = (slice(None, block), slice(block, None))

        def halves(lot, weight, times):
            theirs = plane.cross([times(lot[1][at], weight).astype(BF16) for at in lots])
            return [
                (times(lot[0][at], weight) + there.astype(F32)).astype(BF16)
                for at, there in zip(lots, theirs)
            ]

        def merge(near, got):
            return [whole.astype(F32) + there.astype(F32) for whole, there in zip(near, got)]

        two_far_sum = halves(pre_far, up_part, dot_nt)
        pre_near[0], pre_near[1], *two_far_sum = tie(*pre_near, *two_far_sum)
        got = plane.across(two_far_sum, plane.last)
        theirs = plane.swap(product(pre_near[1], up_part, "nt"), 1)
        pre_far[0], theirs = tie(pre_far[0], theirs)
        up_terms = weight_grad(two_lots[0] + two_lots[1], pre_near + pre_far, block)
        pre_near[0], up_terms = tie(pre_near[0], up_terms)
        two_near_sum = product(pre_near[0], up_part, "nt", 2, [theirs])
        two_near_sum[0], *got = tie(two_near_sum[0], *got)
        two_sum = merge(two_near_sum, got)
        grad_up = lax.psum_scatter(
            up_terms.reshape(n_dp, n_z * own, ff_own), "fsdp", scatter_dimension=1, tiled=True
        )
        hid_far[0], hid_far[1], *two_sum = tie(*hid_far, *two_sum)
        two_grad = plane.fold(two_sum)
        down_terms = weight_grad(hid_near + hid_far, grad_lots[0] + grad_lots[1], block)
        two_grad, down_terms, hid_far[0] = tie(two_grad, down_terms, hid_far[0])
        grad_down = lax.psum_scatter(down_terms, "fsdp", scatter_dimension=0, tiled=True)
        out_far = halves(hid_far, down_part, dot_nn)
        two_grad, *out_far = tie(two_grad, *out_far)

        out_got = plane.across(out_far, plane.last)
        grad_out = grad_low.astype(F32)
        grad_bdown = jnp.sum(grad_out, axis=0)
        grad_gain_two = jnp.sum(two_grad * xhat_two, axis=0)
        grad_shift_two = jnp.sum(two_grad, axis=0)
        middle_grad = grad_out + norm_pull(two_grad, xhat_two, recip_two, gain_two)
        grad_bo = jnp.sum(middle_grad, axis=0)
        branch_grad = middle_grad.astype(BF16)

        def cut(rows_of_lots):
            size = rows_of_lots.shape[0] // 4
            return [rows_of_lots[i * size : (i + 1) * size] for i in range(4)]

        def send_rows(parts):
            return plane.across([parts[0], parts[2]], plane.last)

        def own_rows(parts, got):
            return plane.fold([n.astype(F32) + g.astype(F32) for n, g in zip((parts[1], parts[3]), got)])

        attended_grad = dot_nt(branch_grad, full_o).astype(BF16)

        query_grad, kv_terms = attn_backward(queries, kv_window, norms, attended_grad, first, file_ends)
        query_grad, kv_terms, grad_up, *out_got = tie(query_grad, kv_terms, grad_up, *out_got)
        kv_got = line.scatter(kv_terms.reshape(windows, n_z, local_len, 2 * HD), 1)
        theirs = plane.swap(dot_tn(one_sib, query_grad).astype(BF16), 1)
        wq_parts = product(one_mine, query_grad, "tn", 4, [theirs])
        wq_got = send_rows(wq_parts)
        wq_parts[1], query_late = tie(wq_parts[1], query_grad)
        query_part = product(query_late, full_q, "nt", kind=F32)
        query_part, att_sib, branch_late, hid_late, *kv_got = tie(
            query_part, att_sib, branch_grad, hid_near[1], *kv_got
        )
        wo_theirs = plane.swap(product(att_sib, branch_late, "tn"), 1)
        theirs = plane.swap(product(hid_late, down_part), 1)
        wo_theirs, *wq_got = tie(wo_theirs, *wq_got)
        wo_parts = product(att_mine, branch_late, "tn", 4, [wo_theirs])
        wo_got = send_rows(wo_parts)
        query_part, hid_near[0], theirs, wo_parts[1], grad_down = tie(
            query_part, hid_near[0], theirs, wo_parts[1], grad_down
        )
        out_sum = merge(product(hid_near[0], down_part, "nn", 2, [theirs]), out_got)
        kv_grad = total(kv_got).astype(BF16).reshape(rows, 2 * HD)
        query_part, kv_grad, *out_sum = tie(query_part, kv_grad, *out_sum)
        branch_out = plane.fold(out_sum)

        one_grad = query_part + dot_nt(kv_grad, full_kv)
        grad_bq = jnp.sum(query_late.astype(F32), axis=0)
        grad_bv = jnp.sum(kv_grad[:, HD:].astype(F32), axis=0)
        grad_gain_one = jnp.sum(one_grad * xhat_one, axis=0)
        grad_shift_one = jnp.sum(one_grad, axis=0)
        up_bias_part = sum(jnp.sum(lot.astype(F32), axis=0) for lot in pre_near + pre_far)
        grad_bup = jnp.where(jnp.arange(n_dp)[:, None] == my_dp, up_bias_part[None], 0.0).reshape(-1)
        sums = (
            (0, grad_bq),
            (2, grad_bo),
            (5, grad_bup),
            (6, grad_bdown),
            (7, grad_gain_two),
            (8, grad_shift_two),
            (1, grad_bv),
            (3, grad_gain_one),
            (4, grad_shift_one),
        )
        row_of = jnp.concatenate(
            [
                jnp.pad(v.reshape(n_dev, sizes[i]), ((0, 0), (0, rooms[i] - sizes[i])))
                for i, v in sums
            ],
            axis=1,
        )
        order = [i for i, _ in sums]
        sum_starts = {i: sum(rooms[j] for j in order[:at]) for at, i in enumerate(order)}
        per_half = n_z // 2 * row_of.shape[1]
        more = -(-per_half // (16 * 2 * HD)) * 16
        row_of = jnp.pad(row_of.reshape(2 * n_dp, per_half), ((0, 0), (0, more * 2 * HD - per_half)))
        row_of = row_of.astype(BF16).astype(F32)

        def with_vectors(product, core):
            pick = (places[core][:, None] == jnp.arange(2 * n_dp)[None, :]).astype(F32)
            vectors = jnp.dot(pick, row_of, precision=lax.Precision.HIGHEST)
            return jnp.concatenate(
                [product.reshape(n_dp, -1, 2 * HD), vectors.reshape(n_dp, more, 2 * HD)], axis=1
            ).reshape(-1, 2 * HD)

        theirs = plane.swap(with_vectors(dot_tn(one_sib, kv_grad), 1).astype(BF16), 1)
        kv_parts = cut((with_vectors(dot_tn(one_mine, kv_grad), 0) + theirs.astype(F32)).astype(BF16))
        kv_parts_got = send_rows(kv_parts)
        kv_parts[1], *wo_got = tie(kv_parts[1], *wo_got)

        both_rows = jnp.concatenate(
            [
                own_rows(parts, got).astype(BF16).reshape(n_z, own, width)
                for parts, got in ((wq_parts, wq_got), (wo_parts, wo_got))
            ],
            axis=1,
        ).reshape(2 * n_z * own, width)
        both_rows = lax.psum_scatter(both_rows, "fsdp", scatter_dimension=0, tiled=True)
        kv_last = own_rows(kv_parts, kv_parts_got).reshape(2, -1, 2 * HD)
        kv_rows = kv_last.shape[1] - more
        kv_last = jnp.concatenate(
            [
                kv_last[:, :kv_rows].reshape(n_z, -1),
                kv_last[:, kv_rows:].reshape(2, -1)[:, :per_half].reshape(n_z, -1),
            ],
            axis=1,
        )
        kv_last = line.scatter(kv_last, 0)
        output = (middle + branch_out + bias_down).astype(BF16).reshape(windows, local_len, width)
        tokens_grad = middle_grad + norm_pull(one_grad, xhat_one, recip_one, gain_one)
        tokens_grad = tokens_grad.astype(BF16).reshape(windows, local_len, width)
        grad_up = lax.all_to_all(
            grad_up.reshape(n_dp * own, ff_own), "dp", 0, 1, tiled=True
        ).astype(F32)
        kv_own = total(kv_last)
        flat = kv_own[own * 2 * HD :]
        bq, bv, bo, gain1, shift1, bup, bdown, gain2, shift2 = (
            flat[sum_starts[i] : sum_starts[i] + size] for i, size in enumerate(sizes)
        )
        return (
            output,
            tokens_grad,
            both_rows[:own].astype(F32),
            kv_own[: own * 2 * HD].reshape(own, 2 * HD),
            both_rows[own:].astype(F32),
            bq,
            bv,
            bo,
            gain1,
            shift1,
            grad_up,
            grad_down.astype(F32),
            bup,
            bdown,
            gain2,
            shift2,
        )

    return local


def solution(mesh):
    whole = P(BOTH, None)
    vector = P(BOTH)
    rows = P("dp", "fsdp", None)
    weights = (whole, whole, whole) + (vector,) * 5 + (whole, whole) + (vector,) * 4
    return jax.shard_map(
        make_local(mesh.shape["dp"], mesh.shape["fsdp"]),
        mesh=mesh,
        in_specs=(rows, rows, P("dp", None)) + weights,
        out_specs=(rows, rows) + weights,
        check_vma=False,
    )
```

```python
import functools
import math

import jax
import jax.numpy as jnp
from jax import lax
from jax.experimental import pallas as pl
from jax.experimental.pallas import tpu as pltpu
from jax.sharding import PartitionSpec as P

HEADS = 16
HD = 128
EPS = 1e-05
F32 = jnp.float32
BF16 = jnp.bfloat16
BOTH = ("dp", "fsdp")
HASTE = 64


def dot_nn(left, right):
    return jnp.dot(left, right, preferred_element_type=F32)


def dot_nt(left, right):
    return lax.dot_general(left, right, (((1,), (1,)), ((), ())), preferred_element_type=F32)


def dot_tn(left, right):
    return lax.dot_general(left, right, (((0,), (0,)), ((), ())), preferred_element_type=F32)


LOG2E = 1.4426950408889634


def file_of(ends_ref, w, pos):
    total = jnp.zeros(pos.shape, jnp.int32)
    for i in range(ends_ref.shape[1]):
        total += (ends_ref[w, i] <= pos).astype(jnp.int32)
    return total


def fill_mask(pos_ref, ends_ref, w, bias, key_turned, value_turned, kv_ref):
    span, win = bias.shape
    query_pos = pos_ref[0] + lax.broadcasted_iota(jnp.int32, (span, 1), 0)
    key_pos = lax.broadcasted_iota(jnp.int32, (1, win), 1)
    same = file_of(ends_ref, w, query_pos) == file_of(ends_ref, w, key_pos)
    bias[...] = jnp.where(same & (key_pos <= query_pos), 0.0, -1e30).astype(F32)
    key_turned[...] = kv_ref[0, :, :HD].astype(F32).T.astype(BF16)
    if value_turned is not None:
        value_turned[...] = kv_ref[0, :, HD:].astype(F32).T.astype(BF16)


def attn_forward_kernel(per_step, pos_ref, ends_ref, q_ref, kv_ref, out_ref, norm_ref, bias, key_turned):
    w, group = pl.program_id(0), pl.program_id(1)

    @pl.when(group == 0)
    def _():
        fill_mask(pos_ref, ends_ref, w, bias, key_turned, None, kv_ref)
        norm_ref[...] = jnp.zeros_like(norm_ref)

    values = kv_ref[0, :, HD:]
    lane = lax.broadcasted_iota(jnp.int32, norm_ref.shape, 1)
    for j in range(per_step):
        query = q_ref[:, j * HD : (j + 1) * HD]
        scores = jnp.dot(query, key_turned[...], preferred_element_type=F32)
        scores = scores * (LOG2E / math.sqrt(HD)) + bias[...]
        top = jnp.max(scores, axis=1, keepdims=True)
        terms = jnp.exp2(scores - top)
        total = jnp.sum(terms, axis=1, keepdims=True)
        mixed = jnp.dot(terms.astype(BF16), values, preferred_element_type=F32)
        out_ref[:, j * HD : (j + 1) * HD] = (mixed / total).astype(BF16)
        norm_ref[...] = jnp.where(lane == group * per_step + j, top + jnp.log2(total), norm_ref[...])


def attn_backward_kernel(
    per_step, pos_ref, ends_ref, q_ref, kv_ref, norm_ref, grad_ref, dq_ref, dkv_ref,
    bias, key_turned, value_turned, key_grad, value_grad,
):
    w, group = pl.program_id(0), pl.program_id(1)

    @pl.when(group == 0)
    def _():
        fill_mask(pos_ref, ends_ref, w, bias, key_turned, value_turned, kv_ref)
        key_grad[...] = jnp.zeros_like(key_grad)
        value_grad[...] = jnp.zeros_like(value_grad)

    keys = kv_ref[0, :, :HD]
    lane = lax.broadcasted_iota(jnp.int32, norm_ref.shape, 1)
    for j in range(per_step):
        query = q_ref[:, j * HD : (j + 1) * HD]
        grad = grad_ref[:, j * HD : (j + 1) * HD]
        scores = jnp.dot(query, key_turned[...], preferred_element_type=F32)
        scores = scores * (LOG2E / math.sqrt(HD)) + bias[...]
        norm = jnp.sum(jnp.where(lane == group * per_step + j, norm_ref[...], 0.0), axis=1, keepdims=True)
        probs = jnp.exp2(scores - norm)
        grad_probs = jnp.dot(grad, value_turned[...], preferred_element_type=F32)
        delta = jnp.sum(probs * grad_probs, axis=1, keepdims=True)
        score_grad = (probs * (grad_probs - delta)).astype(BF16)
        probs = probs.astype(BF16)
        dq = jnp.dot(score_grad, keys, preferred_element_type=F32)
        dq_ref[:, j * HD : (j + 1) * HD] = (dq / math.sqrt(HD)).astype(BF16)
        key_grad[...] += dot_tn(query, score_grad)
        value_grad[...] += dot_tn(grad, probs)

    @pl.when(group == pl.num_programs(1) - 1)
    def _():
        dkv_ref[0, :, :HD] = (key_grad[...].T / math.sqrt(HD)).astype(BF16)
        dkv_ref[0, :, HD:] = value_grad[...].T.astype(BF16)


def attn_specs(per_step, span, win):
    smem = pl.BlockSpec(memory_space=pltpu.SMEM)
    heads = pl.BlockSpec((span, per_step * HD), lambda w, g: (w, g))
    keys = pl.BlockSpec((1, win, 2 * HD), lambda w, g: (w, 0, 0))
    norm = pl.BlockSpec((span, HD), lambda w, g: (w, 0))
    return smem, heads, keys, norm


def attn_cost(windows, span, win, products, haste=HASTE):
    return pl.CostEstimate(
        flops=2 * products * windows * HEADS * span * win * HD // haste,
        transcendentals=windows * HEADS * span * win // haste,
        bytes_accessed=products * windows * HEADS * span * HD * 2 // haste,
    )


def attn_forward(queries, kv_window, first, ends, per_step=4):
    windows, win, _ = kv_window.shape
    rows, width = queries.shape
    span = rows // windows
    smem, heads, keys, norm = attn_specs(per_step, span, win)
    return pl.pallas_call(
        functools.partial(attn_forward_kernel, per_step),
        out_shape=(
            jax.ShapeDtypeStruct((rows, width), BF16),
            jax.ShapeDtypeStruct((rows, HD), F32),
        ),
        grid=(windows, HEADS // per_step),
        in_specs=[smem, smem, heads, keys],
        out_specs=(heads, norm),
        scratch_shapes=[pltpu.VMEM((span, win), F32), pltpu.VMEM((HD, win), BF16)],
        compiler_params=pltpu.CompilerParams(vmem_limit_bytes=40 * 2**20),
        cost_estimate=attn_cost(windows, span, win, 2),
    )(first, ends, queries, kv_window)


def attn_backward(queries, kv_window, norms, grads, first, ends, per_step=4):
    windows, win, _ = kv_window.shape
    rows, width = queries.shape
    span = rows // windows
    smem, heads, keys, norm = attn_specs(per_step, span, win)
    return pl.pallas_call(
        functools.partial(attn_backward_kernel, per_step),
        out_shape=(
            jax.ShapeDtypeStruct((rows, width), BF16),
            jax.ShapeDtypeStruct((windows, win, 2 * HD), BF16),
        ),
        grid=(windows, HEADS // per_step),
        in_specs=[smem, smem, heads, keys, norm, heads],
        out_specs=(heads, keys),
        scratch_shapes=[
            pltpu.VMEM((span, win), F32),
            pltpu.VMEM((HD, win), BF16),
            pltpu.VMEM((HD, win), BF16),
            pltpu.VMEM((HD, win), F32),
            pltpu.VMEM((HD, win), F32),
        ],
        compiler_params=pltpu.CompilerParams(vmem_limit_bytes=48 * 2**20),
        cost_estimate=attn_cost(windows, span, win, 5),
    )(first, ends, queries, kv_window, norms, grads)


def middle_kernel(count, *refs):
    blocks, back_ref = refs[:count], refs[count]
    up_ref, bias_ref = refs[count + 1], refs[count + 2]
    outs, sum_ref = refs[count + 3 : -1], refs[-1]
    groups = len(outs) // 2
    size = blocks[0].shape[0]
    root = math.sqrt(2.0 / math.pi)
    summed = jnp.zeros(sum_ref.shape, F32)
    for i, block in enumerate(blocks):
        act = jnp.dot(block[...], up_ref[...], preferred_element_type=F32) + bias_ref[...]
        square = act * act
        bent = jnp.tanh(act * (root + (root * 0.044715) * square))
        upper = 0.5 + 0.5 * bent
        slope = upper + act * (1.0 - bent * bent) * (0.5 * root + (1.5 * 0.044715 * root) * square)
        back = back_ref[i * size : (i + 1) * size, :].astype(F32)
        group, place = divmod(i, count // groups)
        at = slice(place * size, (place + 1) * size)
        outs[group][at, :] = (act * upper).astype(BF16)
        pre = (back * slope).astype(BF16)
        outs[groups + group][at, :] = pre
        summed += jnp.sum(pre.astype(F32), axis=0, keepdims=True)
    sum_ref[...] = summed


def middle_layer(blocks, back, up_part, bias, tile=512):
    count = len(blocks)
    size, width = blocks[0].shape
    units = up_part.shape[1]
    tile = min(tile, units)
    one = pl.Buffered(buffer_count=1)
    group = size * count // 2
    whole = pl.BlockSpec((size, width), lambda j: (0, 0), pipeline_mode=one)
    slab = pl.BlockSpec((group, tile), lambda j: (0, j))
    out = pl.pallas_call(
        functools.partial(middle_kernel, count),
        out_shape=[jax.ShapeDtypeStruct((group, units), BF16)] * 4 + [jax.ShapeDtypeStruct((1, units), F32)],
        grid=(units // tile,),
        in_specs=[whole] * count
        + [
            pl.BlockSpec((size * count, tile), lambda j: (0, j)),
            pl.BlockSpec((width, tile), lambda j: (0, j)),
            pl.BlockSpec((1, tile), lambda j: (0, j)),
        ],
        out_specs=[slab] * 4 + [pl.BlockSpec((1, tile), lambda j: (0, j))],
        compiler_params=pltpu.CompilerParams(vmem_limit_bytes=48 * 2**20),
        cost_estimate=pl.CostEstimate(
            flops=2 * count * size * width * units // HASTE,
            transcendentals=count * size * units // HASTE,
            bytes_accessed=2 * (count * size * (width + 3 * units) + width * units) // HASTE,
        ),
    )(*blocks, back, up_part, bias.reshape(1, units))
    return list(out[:2]), list(out[2:4]), out[4]


def back_kernel(count, *refs):
    blocks, weight_ref, out = refs[:count], refs[count], refs[count + 1]
    size = blocks[0].shape[0]
    for i, block in enumerate(blocks):
        out[i * size : (i + 1) * size, :] = dot_nt(block[...], weight_ref[...]).astype(BF16)


def back_product(blocks, weight, tile=512):
    count = len(blocks)
    size, width = blocks[0].shape
    units = weight.shape[0]
    tile = min(tile, units)
    one = pl.Buffered(buffer_count=1)
    return pl.pallas_call(
        functools.partial(back_kernel, count),
        out_shape=jax.ShapeDtypeStruct((size * count, units), BF16),
        grid=(units // tile,),
        in_specs=[pl.BlockSpec((size, width), lambda j: (0, 0), pipeline_mode=one)] * count
        + [pl.BlockSpec((tile, width), lambda j: (j, 0))],
        out_specs=pl.BlockSpec((size * count, tile), lambda j: (0, j)),
        compiler_params=pltpu.CompilerParams(vmem_limit_bytes=48 * 2**20),
        cost_estimate=pl.CostEstimate(
            flops=2 * count * size * width * units // HASTE,
            transcendentals=0,
            bytes_accessed=2 * (count * size * (width + units) + width * units) // HASTE,
        ),
    )(*blocks, weight)


def weight_kernel(count, *refs):
    lefts, rights, out = refs[:count], refs[count : 2 * count], refs[2 * count]
    total = dot_tn(lefts[0][...], rights[0][...])
    for left, right in zip(lefts[1:], rights[1:]):
        total += dot_tn(left[...], right[...])
    out[...] = total.astype(BF16)


def in_blocks(arrays, size):
    return [(array, i) for array in arrays for i in range(array.shape[0] // size)]


def weight_grad(lefts, rights, size, tile=256):
    lefts, rights = in_blocks(lefts, size), in_blocks(rights, size)
    count = len(lefts)
    height, breadth = lefts[0][0].shape[1], rights[0][0].shape[1]
    tile = min(tile, height)

    def left_spec(row):
        return pl.BlockSpec((size, tile), lambda i: (row, i))

    def right_spec(row):
        return pl.BlockSpec((size, breadth), lambda i: (row, 0), pipeline_mode=pl.Buffered(buffer_count=1))

    return pl.pallas_call(
        functools.partial(weight_kernel, count),
        out_shape=jax.ShapeDtypeStruct((height, breadth), BF16),
        grid=(height // tile,),
        in_specs=[left_spec(row) for _, row in lefts] + [right_spec(row) for _, row in rights],
        out_specs=pl.BlockSpec((tile, breadth), lambda i: (i, 0)),
        compiler_params=pltpu.CompilerParams(vmem_limit_bytes=52 * 2**20),
        cost_estimate=pl.CostEstimate(
            flops=2 * count * size * height * breadth,
            transcendentals=0,
            bytes_accessed=2 * (count * size * (height + breadth) + height * breadth),
        ),
    )(*[array for array, _ in lefts], *[array for array, _ in rights])


def reorder_kernel(place_ref, first_ref, second_ref, first_out, second_out):
    first_out[...] = first_ref[...]
    second_out[...] = second_ref[...]


def reorder(values, places):
    rows, width = values.shape
    count = places.shape[1]
    block = width // (2 * count)
    if block % 128:
        return [
            jnp.concatenate(
                [lax.dynamic_slice_in_dim(values, places[i, j] * block, block, 1) for j in range(count)],
                axis=1,
            )
            for i in (0, 1)
        ]
    out = pl.BlockSpec((rows, block), lambda i, place: (0, i))
    return pl.pallas_call(
        reorder_kernel,
        out_shape=[jax.ShapeDtypeStruct((rows, width // 2), values.dtype)] * 2,
        grid_spec=pltpu.PrefetchScalarGridSpec(
            num_scalar_prefetch=1,
            grid=(count,),
            in_specs=[
                pl.BlockSpec((rows, block), lambda i, place: (0, place[0, i])),
                pl.BlockSpec((rows, block), lambda i, place: (0, place[1, i])),
            ],
            out_specs=[out, out],
        ),
        cost_estimate=pl.CostEstimate(flops=0, transcendentals=0, bytes_accessed=4 * rows * width // HASTE),
    )(places, values, values)

def product_kernel(form, given, values_ref, weight_ref, *refs):
    extra, outs = refs[:given], refs[given:]
    size = outs[0].shape[0]
    for i, out in enumerate(outs):
        rows = slice(i * size, (i + 1) * size)
        if form == "tn":
            total = dot_tn(values_ref[:, rows], weight_ref[...])
        else:
            total = (dot_nt if form == "nt" else dot_nn)(values_ref[rows, :], weight_ref[...])
        if given:
            each = extra[0].shape[0]
            at = i * size % each
            total += extra[i * size // each][at : at + size, :].astype(F32)
        out[...] = total.astype(out.dtype)


def product(values, weight, form="nn", parts=1, extra=(), kind=BF16, tile=512):
    height = values.shape[1] if form == "tn" else values.shape[0]
    depth = values.shape[0] if form == "tn" else values.shape[1]
    breadth = weight.shape[0] if form == "nt" else weight.shape[1]
    tile = min(tile, breadth)
    size = height // parts
    if form == "nt":
        part = pl.BlockSpec((tile, depth), lambda j: (j, 0))
    else:
        part = pl.BlockSpec((depth, tile), lambda j: (0, j))
    out = pl.pallas_call(
        functools.partial(product_kernel, form, len(extra)),
        out_shape=[jax.ShapeDtypeStruct((size, breadth), kind)] * parts,
        grid=(breadth // tile,),
        in_specs=[pl.BlockSpec(values.shape, lambda j: (0, 0), pipeline_mode=pl.Buffered(buffer_count=1)), part]
        + [pl.BlockSpec((block.shape[0], tile), lambda j: (0, j)) for block in extra],
        out_specs=[pl.BlockSpec((size, tile), lambda j: (0, j))] * parts,
        compiler_params=pltpu.CompilerParams(vmem_limit_bytes=48 * 2**20),
        cost_estimate=pl.CostEstimate(
            flops=2 * height * depth * breadth // HASTE,
            transcendentals=0,
            bytes_accessed=2 * (height * (depth + breadth) + depth * breadth) // HASTE,
        ),
    )(values, weight, *extra)
    return list(out) if parts > 1 else out[0]


def norm_stats(values):
    average = jnp.mean(values, axis=-1, keepdims=True)
    centered = values - average
    variance = jnp.mean(centered * centered, axis=-1, keepdims=True)
    return average, lax.rsqrt(variance + EPS)


def norm_pull(grad, xhat, recip, gain):
    scaled = grad * gain
    mean_one = jnp.mean(scaled, axis=-1, keepdims=True)
    mean_two = jnp.mean(scaled * xhat, axis=-1, keepdims=True)
    return recip * (scaled - mean_one - xhat * mean_two)


def tie(*arrays):
    return lax.optimization_barrier(arrays)


class Line:
    def __init__(self, count):
        self.count = count

    def send(self, block, places):
        return lax.ppermute(block, "fsdp", [(i, (i + places) % self.count) for i in range(self.count)])

    def gather(self, block):
        return [block] + [self.send(block, step) for step in range(1, self.count)]

    def in_order(self, pieces, axis=0):
        me = lax.axis_index("fsdp")
        size = pieces[0].shape[axis]
        shape = list(pieces[0].shape)
        shape[axis] = size * self.count
        whole = jnp.zeros(shape, pieces[0].dtype)
        for step, piece in enumerate(pieces):
            place = lax.rem(me - step + self.count, self.count) * size
            whole = lax.dynamic_update_slice_in_dim(whole, piece, place, axis)
        return whole

    def scatter(self, terms, axis):
        me = lax.axis_index("fsdp")

        def term(step):
            place = lax.rem(me + step, self.count)
            return lax.dynamic_index_in_dim(terms, place, axis, keepdims=False)

        return [term(0)] + [self.send(term(step).astype(BF16), step) for step in range(1, self.count)]


def total(terms):
    out = terms[0].astype(F32)
    for term in terms[1:]:
        out += term.astype(F32)
    return out


class Plane:
    def __init__(self, count):
        self.count = count
        bits = [1 << i for i in range(1, count.bit_length() - 1)]
        self.orders = (bits, bits[::-1])
        self.last = len(bits) - 1
        self.near, self.far = [], []
        for order in self.orders:
            near = [0]
            for bit in order[:-1]:
                near = near + [offset ^ bit for offset in near]
            self.near.append(near)
            self.far.append([offset ^ order[-1] for offset in near])

    def places(self):
        me = lax.axis_index("dp")
        order = [(o, h) for h in (0, 1) for o in self.far[h] + self.near[h]]
        return jnp.stack(
            [jnp.stack([2 * (me ^ o ^ core) + h for o, h in order]) for core in (0, 1)]
        ).astype(jnp.int32)

    def swap(self, block, bit):
        return lax.ppermute(block, "dp", [(i, i ^ bit) for i in range(self.count)])

    def cross(self, blocks):
        return [self.swap(block, 1) for block in blocks]

    def across(self, halves, step):
        return [self.swap(half, order[step]) for half, order in zip(halves, self.orders)]

    def grow(self, halves):
        for step in range(self.last):
            halves = [jnp.concatenate(pair) for pair in zip(halves, self.across(halves, step))]
        return halves

    def fold(self, halves):
        for step in range(self.last - 1, -1, -1):
            size = halves[0].shape[0] // 2
            got = self.across([half[size:].astype(BF16) for half in halves], step)
            halves = [half[:size].astype(F32) + there.astype(F32) for half, there in zip(halves, got)]
        return jnp.concatenate(halves)


def make_local(n_dp, n_z):
    n_dev = n_dp * n_z
    plane = Plane(n_dp)
    line = Line(n_z)

    def local(
        tokens,
        cotangent,
        lengths,
        query_weight,
        kv_weight,
        out_weight,
        query_bias,
        value_bias,
        out_bias,
        attn_gain,
        attn_shift,
        up_weight,
        down_weight,
        up_bias,
        down_bias,
        mlp_gain,
        mlp_shift,
    ):
        windows, local_len, width = tokens.shape
        rows = windows * local_len
        half = rows // 2
        own = query_weight.shape[0]
        ff_own = up_weight.shape[1] // n_dp
        my_dp = lax.axis_index("dp")

        small = (
            query_bias,
            value_bias,
            out_bias,
            attn_gain,
            attn_shift,
            up_bias,
            down_bias,
            mlp_gain,
            mlp_shift,
        )
        sizes = [v.shape[0] for v in small]
        rooms = [-(-size // 128) * 128 for size in sizes]
        starts = [sum(rooms[:i]) for i in range(len(rooms))]
        small_row = jnp.concatenate(
            [jnp.pad(v, (0, room - size)) for v, size, room in zip(small, sizes, rooms)]
        )
        kv_lines = kv_weight.size // width
        filled = own + kv_lines + -(-small_row.shape[0] // width)
        lines = -(-filled // 16) * 16
        small_row = jnp.pad(small_row, (0, (lines - own - kv_lines) * width - small_row.shape[0]))
        packed = jnp.concatenate(
            [query_weight, kv_weight.reshape(kv_lines, width), small_row.reshape(-1, width)]
        )
        places = plane.places()

        grad_low = cotangent.reshape(rows, width)
        packed = lax.all_gather(packed, "fsdp", axis=0, tiled=True)
        grad_near = plane.grow([grad_low[:half], grad_low[half:]])
        up_cols = lax.all_to_all(up_weight, "dp", 1, 0, tiled=True).reshape(n_dp, own, ff_own)
        packed, up_cols, out_weight, *grad_near = tie(packed, up_cols, out_weight, *grad_near)

        packed = lax.all_gather(packed, "dp", axis=0, tiled=True)
        out_pieces = line.gather(out_weight)
        *out_pieces, down_late = tie(*out_pieces, down_weight)
        full_o = line.in_order(out_pieces)
        down_pieces = [down_late, line.send(down_late, 1)]
        inputs = tokens.reshape(rows, width).astype(F32)
        mean_one, recip_one = norm_stats(inputs)
        grad_near_sib = plane.cross(grad_near)
        packed, full_o, mean_one, down_pieces[-1], *arrived = tie(
            packed, full_o, mean_one, down_pieces[-1], *grad_near, *grad_near_sib
        )
        grad_near, grad_near_sib = arrived[:2], arrived[2:]

        full_o = lax.all_gather(full_o, "dp", axis=0, tiled=True)
        packed = packed.reshape(n_dev, lines, width)
        full_q = packed[:, :own].reshape(width, width)
        full_kv = packed[:, own : own + kv_lines].reshape(width, 2 * HD)
        small_all = packed[:, own + kv_lines :].reshape(n_dev, -1)
        bias_q, bias_v, bias_o, gain_one, shift_one, bias_up, bias_down, gain_two, shift_two = (
            small_all[:, start : start + size].reshape(-1).astype(F32)
            for start, size in zip(starts, sizes)
        )
        xhat_one = (inputs - mean_one) * recip_one
        normed_one = (xhat_one * gain_one + shift_one).astype(BF16)
        kv_bias = jnp.concatenate([jnp.zeros((HD,), F32), bias_v])
        key_value = (dot_nn(normed_one, full_kv) + kv_bias).astype(BF16)
        if n_z > 2:
            down_pieces.append(line.send(down_pieces[-1], 1))
        key_value, normed_late, up_cols, down_pieces[-1] = tie(
            key_value, normed_one, up_cols, down_pieces[-1]
        )
        kv_pieces = line.gather(key_value.reshape(windows, local_len, 2 * HD))
        queries = (dot_nn(normed_late, full_q) + bias_q).astype(BF16)
        queries, down_late, *kv_pieces = tie(queries, down_pieces[-1], *kv_pieces)
        kv_window = line.in_order(kv_pieces, 1)

        first = (lax.axis_index("fsdp") * local_len).astype(jnp.int32).reshape(1)
        file_count = lengths.shape[1]
        upto = jnp.arange(file_count)[:, None] <= jnp.arange(file_count)[None, :]
        file_ends = jnp.sum(jnp.where(upto[None], lengths[:, :, None], 0), axis=1)
        grad_far = plane.across(grad_near, plane.last)
        while len(down_pieces) < n_z:
            down_late = line.send(down_late, 1)
            down_pieces.append(down_late)
        up_part = lax.all_gather(up_cols, "fsdp", axis=1, tiled=True).reshape(width, ff_own)
        attended, norms = attn_forward(queries, kv_window, first, file_ends)
        attended, down_pieces[-1] = tie(attended, down_pieces[-1])
        middle = inputs + dot_nn(attended, full_o) + bias_o
        mean_two, recip_two = norm_stats(middle)
        xhat_two = (middle - mean_two) * recip_two
        normed_two = (xhat_two * gain_two + shift_two).astype(BF16)

        normed_two, normed_late, *arrived = tie(normed_two, normed_late, *grad_far, *down_pieces)
        grad_far, down_pieces = arrived[:2], arrived[2:]
        two_near = plane.grow([normed_two[:half], normed_two[half:]])
        down_part = line.in_order(down_pieces)
        grad_lots = [[*grad_near, *grad_near_sib], [*grad_far, *plane.cross(grad_far)]]
        back_near = back_product(grad_lots[0], down_part)
        two_near[0], two_near[1], back_near = tie(*two_near, back_near)
        two_far = plane.across(two_near, plane.last)
        two_lots = [[*two_near, *plane.cross(two_near)]]
        back_near, down_late, attended_late, normed_late = tie(
            back_near, down_part, attended, normed_late
        )
        back_far = back_product(grad_lots[1], down_late)
        bias_up_part = lax.dynamic_slice_in_dim(bias_up, my_dp * ff_own, ff_own)
        hid_near, pre_near, up_bias_near = middle_layer(two_lots[0], back_near, up_part, bias_up_part)
        back_far, attended_late, normed_late, pre_near[0], pre_near[1], *two_far = tie(
            back_far, attended_late, normed_late, *pre_near, *two_far
        )
        two_lots.append([*two_far, *plane.cross(two_far)])
        att_mine, att_sib = reorder(attended_late, places)
        one_mine, one_sib = reorder(normed_late, places)
        back_far, att_mine, att_sib, one_mine, one_sib = tie(back_far, att_mine, att_sib, one_mine, one_sib)
        hid_far, pre_far, up_bias_far = middle_layer(two_lots[1], back_far, up_part, bias_up_part)
        block = two_near[0].shape[0]
        lots = (slice(None, block), slice(block, None))

        def halves(lot, weight, times):
            theirs = plane.cross([times(lot[1][at], weight).astype(BF16) for at in lots])
            return [
                (times(lot[0][at], weight) + there.astype(F32)).astype(BF16)
                for at, there in zip(lots, theirs)
            ]

        def merge(near, got):
            return [whole.astype(F32) + there.astype(F32) for whole, there in zip(near, got)]

        two_far_sum = halves(pre_far, up_part, dot_nt)
        pre_near[0], pre_near[1], *two_far_sum = tie(*pre_near, *two_far_sum)
        got = plane.across(two_far_sum, plane.last)
        theirs = plane.swap(product(pre_near[1], up_part, "nt"), 1)
        pre_far[0], theirs = tie(pre_far[0], theirs)
        up_terms = weight_grad(two_lots[0] + two_lots[1], pre_near + pre_far, block)
        pre_near[0], up_terms = tie(pre_near[0], up_terms)
        two_near_sum = product(pre_near[0], up_part, "nt", 2, [theirs])
        two_near_sum[0], *got = tie(two_near_sum[0], *got)
        two_sum = merge(two_near_sum, got)
        grad_up = lax.psum_scatter(
            up_terms.reshape(n_dp, n_z * own, ff_own), "fsdp", scatter_dimension=1, tiled=True
        )
        hid_far[0], hid_far[1], *two_sum = tie(*hid_far, *two_sum)
        two_grad = plane.fold(two_sum)
        down_terms = weight_grad(hid_near + hid_far, grad_lots[0] + grad_lots[1], block)
        two_grad, down_terms, hid_far[0] = tie(two_grad, down_terms, hid_far[0])
        grad_down = lax.psum_scatter(down_terms, "fsdp", scatter_dimension=0, tiled=True)
        out_far = halves(hid_far, down_part, dot_nn)
        two_grad, *out_far = tie(two_grad, *out_far)

        out_got = plane.across(out_far, plane.last)
        grad_out = grad_low.astype(F32)
        grad_bdown = jnp.sum(grad_out, axis=0)
        grad_gain_two = jnp.sum(two_grad * xhat_two, axis=0)
        grad_shift_two = jnp.sum(two_grad, axis=0)
        middle_grad = grad_out + norm_pull(two_grad, xhat_two, recip_two, gain_two)
        grad_bo = jnp.sum(middle_grad, axis=0)
        branch_grad = middle_grad.astype(BF16)

        def cut(rows_of_lots):
            size = rows_of_lots.shape[0] // 4
            return [rows_of_lots[i * size : (i + 1) * size] for i in range(4)]

        def send_rows(parts):
            return plane.across([parts[0], parts[2]], plane.last)

        def own_rows(parts, got):
            return plane.fold([n.astype(F32) + g.astype(F32) for n, g in zip((parts[1], parts[3]), got)])

        attended_grad = dot_nt(branch_grad, full_o).astype(BF16)

        query_grad, kv_terms = attn_backward(queries, kv_window, norms, attended_grad, first, file_ends)
        kv_got = line.scatter(kv_terms.reshape(windows, n_z, local_len, 2 * HD), 1)
        query_sib = dot_tn(one_sib, query_grad).astype(BF16)
        query_sib, hid_late, grad_up, *out_got = tie(query_sib, hid_near[1], grad_up, *out_got)
        theirs = plane.swap(query_sib, 1)
        out_sib = product(hid_late, down_part)
        out_sib, one_late = tie(out_sib, one_mine)
        out_theirs = plane.swap(out_sib, 1)
        wq_parts = product(one_late, query_grad, "tn", 4, [theirs])
        wq_got = send_rows(wq_parts)
        wq_parts[1], hid_late, out_theirs = tie(wq_parts[1], hid_near[0], out_theirs)
        out_sum = merge(product(hid_late, down_part, "nn", 2, [out_theirs]), out_got)
        out_sum[0], out_sum[1], att_sib, query_late, *kv_got = tie(*out_sum, att_sib, query_grad, *kv_got)
        branch_out = plane.fold(out_sum)
        wo_sib = product(att_sib, branch_grad, "tn")
        wo_sib, query_late = tie(wo_sib, query_late)
        wo_theirs = plane.swap(wo_sib, 1)
        query_part = product(query_late, full_q, "nt", kind=F32)
        query_part, wo_theirs, *wq_got = tie(query_part, wo_theirs, *wq_got)
        wo_parts = product(att_mine, branch_grad, "tn", 4, [wo_theirs])
        wo_got = send_rows(wo_parts)
        kv_grad = total(kv_got).astype(BF16).reshape(rows, 2 * HD)
        query_part, kv_grad, wo_parts[1], branch_out = tie(query_part, kv_grad, wo_parts[1], branch_out)

        one_grad = query_part + dot_nt(kv_grad, full_kv)
        grad_bq = jnp.sum(query_grad.astype(F32), axis=0)
        grad_bv = jnp.sum(kv_grad[:, HD:].astype(F32), axis=0)
        grad_gain_one = jnp.sum(one_grad * xhat_one, axis=0)
        grad_shift_one = jnp.sum(one_grad, axis=0)
        grad_bup = jnp.where(jnp.arange(n_dp)[:, None] == my_dp, up_bias_near + up_bias_far, 0.0).reshape(-1)
        sums = (
            (0, grad_bq),
            (2, grad_bo),
            (5, grad_bup),
            (6, grad_bdown),
            (7, grad_gain_two),
            (8, grad_shift_two),
            (1, grad_bv),
            (3, grad_gain_one),
            (4, grad_shift_one),
        )
        row_of = jnp.concatenate(
            [
                jnp.pad(v.reshape(n_dev, sizes[i]), ((0, 0), (0, rooms[i] - sizes[i])))
                for i, v in sums
            ],
            axis=1,
        )
        order = [i for i, _ in sums]
        sum_starts = {i: sum(rooms[j] for j in order[:at]) for at, i in enumerate(order)}
        per_half = n_z // 2 * row_of.shape[1]
        more = -(-per_half // (16 * 2 * HD)) * 16
        row_of = jnp.pad(row_of.reshape(2 * n_dp, per_half), ((0, 0), (0, more * 2 * HD - per_half)))
        row_of = row_of.astype(BF16).astype(F32)

        def with_vectors(product, core):
            pick = (places[core][:, None] == jnp.arange(2 * n_dp)[None, :]).astype(F32)
            vectors = jnp.dot(pick, row_of, precision=lax.Precision.HIGHEST)
            return jnp.concatenate(
                [product.reshape(n_dp, -1, 2 * HD), vectors.reshape(n_dp, more, 2 * HD)], axis=1
            ).reshape(-1, 2 * HD)

        theirs = plane.swap(with_vectors(dot_tn(one_sib, kv_grad), 1).astype(BF16), 1)
        kv_parts = cut((with_vectors(dot_tn(one_mine, kv_grad), 0) + theirs.astype(F32)).astype(BF16))
        kv_parts_got = send_rows(kv_parts)
        kv_parts[1], grad_down, *wo_got = tie(kv_parts[1], grad_down, *wo_got)

        both_rows = jnp.concatenate(
            [
                own_rows(parts, got).astype(BF16).reshape(n_z, own, width)
                for parts, got in ((wq_parts, wq_got), (wo_parts, wo_got))
            ],
            axis=1,
        ).reshape(2 * n_z * own, width)
        both_rows = lax.psum_scatter(both_rows, "fsdp", scatter_dimension=0, tiled=True)
        kv_last = own_rows(kv_parts, kv_parts_got).reshape(2, -1, 2 * HD)
        kv_rows = kv_last.shape[1] - more
        kv_last = jnp.concatenate(
            [
                kv_last[:, :kv_rows].reshape(n_z, -1),
                kv_last[:, kv_rows:].reshape(2, -1)[:, :per_half].reshape(n_z, -1),
            ],
            axis=1,
        )
        kv_last = line.scatter(kv_last, 0)
        output = (middle + branch_out + bias_down).astype(BF16).reshape(windows, local_len, width)
        tokens_grad = middle_grad + norm_pull(one_grad, xhat_one, recip_one, gain_one)
        tokens_grad = tokens_grad.astype(BF16).reshape(windows, local_len, width)
        grad_up = lax.all_to_all(
            grad_up.reshape(n_dp * own, ff_own), "dp", 0, 1, tiled=True
        ).astype(F32)
        kv_own = total(kv_last)
        flat = kv_own[own * 2 * HD :]
        bq, bv, bo, gain1, shift1, bup, bdown, gain2, shift2 = (
            flat[sum_starts[i] : sum_starts[i] + size] for i, size in enumerate(sizes)
        )
        return (
            output,
            tokens_grad,
            both_rows[:own].astype(F32),
            kv_own[: own * 2 * HD].reshape(own, 2 * HD),
            both_rows[own:].astype(F32),
            bq,
            bv,
            bo,
            gain1,
            shift1,
            grad_up,
            grad_down.astype(F32),
            bup,
            bdown,
            gain2,
            shift2,
        )

    return local


def solution(mesh):
    whole = P(BOTH, None)
    vector = P(BOTH)
    rows = P("dp", "fsdp", None)
    weights = (whole, whole, whole) + (vector,) * 5 + (whole, whole) + (vector,) * 4
    return jax.shard_map(
        make_local(mesh.shape["dp"], mesh.shape["fsdp"]),
        mesh=mesh,
        in_specs=(rows, rows, P("dp", None)) + weights,
        out_specs=(rows, rows) + weights,
        check_vma=False,
    )
```

```python
import functools
import math

import jax
import jax.numpy as jnp
from jax import lax
from jax.experimental import pallas as pl
from jax.experimental.pallas import tpu as pltpu
from jax.sharding import PartitionSpec as P

HEADS = 16
HD = 128
EPS = 1e-05
F32 = jnp.float32
BF16 = jnp.bfloat16
BOTH = ("dp", "fsdp")
HASTE = 64


def dot_nn(left, right):
    return jnp.dot(left, right, preferred_element_type=F32)


def dot_nt(left, right):
    return lax.dot_general(left, right, (((1,), (1,)), ((), ())), preferred_element_type=F32)


def dot_tn(left, right):
    return lax.dot_general(left, right, (((0,), (0,)), ((), ())), preferred_element_type=F32)


LOG2E = 1.4426950408889634


def file_of(ends_ref, w, pos):
    total = jnp.zeros(pos.shape, jnp.int32)
    for i in range(ends_ref.shape[1]):
        total += (ends_ref[w, i] <= pos).astype(jnp.int32)
    return total


def fill_mask(pos_ref, ends_ref, w, bias, key_turned, value_turned, kv_ref):
    span, win = bias.shape
    query_pos = pos_ref[0] + lax.broadcasted_iota(jnp.int32, (span, 1), 0)
    key_pos = lax.broadcasted_iota(jnp.int32, (1, win), 1)
    same = file_of(ends_ref, w, query_pos) == file_of(ends_ref, w, key_pos)
    bias[...] = jnp.where(same & (key_pos <= query_pos), 0.0, -1e30).astype(F32)
    key_turned[...] = kv_ref[0, :, :HD].astype(F32).T.astype(BF16)
    if value_turned is not None:
        value_turned[...] = kv_ref[0, :, HD:].astype(F32).T.astype(BF16)


def attn_forward_kernel(per_step, pos_ref, ends_ref, q_ref, kv_ref, out_ref, norm_ref, bias, key_turned):
    w, group = pl.program_id(0), pl.program_id(1)

    @pl.when(group == 0)
    def _():
        fill_mask(pos_ref, ends_ref, w, bias, key_turned, None, kv_ref)
        norm_ref[...] = jnp.zeros_like(norm_ref)

    values = kv_ref[0, :, HD:]
    lane = lax.broadcasted_iota(jnp.int32, norm_ref.shape, 1)
    for j in range(per_step):
        query = q_ref[:, j * HD : (j + 1) * HD]
        scores = jnp.dot(query, key_turned[...], preferred_element_type=F32)
        scores = scores * (LOG2E / math.sqrt(HD)) + bias[...]
        top = jnp.max(scores, axis=1, keepdims=True)
        terms = jnp.exp2(scores - top)
        total = jnp.sum(terms, axis=1, keepdims=True)
        mixed = jnp.dot(terms.astype(BF16), values, preferred_element_type=F32)
        out_ref[:, j * HD : (j + 1) * HD] = (mixed / total).astype(BF16)
        norm_ref[...] = jnp.where(lane == group * per_step + j, top + jnp.log2(total), norm_ref[...])


def attn_backward_kernel(
    per_step, pos_ref, ends_ref, q_ref, kv_ref, norm_ref, grad_ref, dq_ref, dkv_ref,
    bias, key_turned, value_turned, key_grad, value_grad,
):
    w, group = pl.program_id(0), pl.program_id(1)

    @pl.when(group == 0)
    def _():
        fill_mask(pos_ref, ends_ref, w, bias, key_turned, value_turned, kv_ref)
        key_grad[...] = jnp.zeros_like(key_grad)
        value_grad[...] = jnp.zeros_like(value_grad)

    keys = kv_ref[0, :, :HD]
    lane = lax.broadcasted_iota(jnp.int32, norm_ref.shape, 1)
    for j in range(per_step):
        query = q_ref[:, j * HD : (j + 1) * HD]
        grad = grad_ref[:, j * HD : (j + 1) * HD]
        scores = jnp.dot(query, key_turned[...], preferred_element_type=F32)
        scores = scores * (LOG2E / math.sqrt(HD)) + bias[...]
        norm = jnp.sum(jnp.where(lane == group * per_step + j, norm_ref[...], 0.0), axis=1, keepdims=True)
        probs = jnp.exp2(scores - norm)
        grad_probs = jnp.dot(grad, value_turned[...], preferred_element_type=F32)
        delta = jnp.sum(probs * grad_probs, axis=1, keepdims=True)
        score_grad = (probs * (grad_probs - delta)).astype(BF16)
        probs = probs.astype(BF16)
        dq = jnp.dot(score_grad, keys, preferred_element_type=F32)
        dq_ref[:, j * HD : (j + 1) * HD] = (dq / math.sqrt(HD)).astype(BF16)
        key_grad[...] += dot_tn(query, score_grad)
        value_grad[...] += dot_tn(grad, probs)

    @pl.when(group == pl.num_programs(1) - 1)
    def _():
        dkv_ref[0, :, :HD] = (key_grad[...].T / math.sqrt(HD)).astype(BF16)
        dkv_ref[0, :, HD:] = value_grad[...].T.astype(BF16)


def attn_specs(per_step, span, win):
    smem = pl.BlockSpec(memory_space=pltpu.SMEM)
    heads = pl.BlockSpec((span, per_step * HD), lambda w, g: (w, g))
    keys = pl.BlockSpec((1, win, 2 * HD), lambda w, g: (w, 0, 0))
    norm = pl.BlockSpec((span, HD), lambda w, g: (w, 0))
    return smem, heads, keys, norm


def attn_cost(windows, span, win, products, haste=HASTE):
    return pl.CostEstimate(
        flops=2 * products * windows * HEADS * span * win * HD // haste,
        transcendentals=windows * HEADS * span * win // haste,
        bytes_accessed=products * windows * HEADS * span * HD * 2 // haste,
    )


def attn_forward(queries, kv_window, first, ends, per_step=4):
    windows, win, _ = kv_window.shape
    rows, width = queries.shape
    span = rows // windows
    smem, heads, keys, norm = attn_specs(per_step, span, win)
    return pl.pallas_call(
        functools.partial(attn_forward_kernel, per_step),
        out_shape=(
            jax.ShapeDtypeStruct((rows, width), BF16),
            jax.ShapeDtypeStruct((rows, HD), F32),
        ),
        grid=(windows, HEADS // per_step),
        in_specs=[smem, smem, heads, keys],
        out_specs=(heads, norm),
        scratch_shapes=[pltpu.VMEM((span, win), F32), pltpu.VMEM((HD, win), BF16)],
        compiler_params=pltpu.CompilerParams(vmem_limit_bytes=40 * 2**20),
        cost_estimate=attn_cost(windows, span, win, 2),
    )(first, ends, queries, kv_window)


def attn_backward(queries, kv_window, norms, grads, first, ends, per_step=4):
    windows, win, _ = kv_window.shape
    rows, width = queries.shape
    span = rows // windows
    smem, heads, keys, norm = attn_specs(per_step, span, win)
    return pl.pallas_call(
        functools.partial(attn_backward_kernel, per_step),
        out_shape=(
            jax.ShapeDtypeStruct((rows, width), BF16),
            jax.ShapeDtypeStruct((windows, win, 2 * HD), BF16),
        ),
        grid=(windows, HEADS // per_step),
        in_specs=[smem, smem, heads, keys, norm, heads],
        out_specs=(heads, keys),
        scratch_shapes=[
            pltpu.VMEM((span, win), F32),
            pltpu.VMEM((HD, win), BF16),
            pltpu.VMEM((HD, win), BF16),
            pltpu.VMEM((HD, win), F32),
            pltpu.VMEM((HD, win), F32),
        ],
        compiler_params=pltpu.CompilerParams(vmem_limit_bytes=48 * 2**20),
        cost_estimate=attn_cost(windows, span, win, 5),
    )(first, ends, queries, kv_window, norms, grads)


def middle_kernel(count, *refs):
    blocks, back_ref = refs[:count], refs[count]
    up_ref, bias_ref = refs[count + 1], refs[count + 2]
    outs, sum_ref = refs[count + 3 : -1], refs[-1]
    groups = len(outs) // 2
    size = blocks[0].shape[0]
    root = math.sqrt(2.0 / math.pi)
    summed = jnp.zeros(sum_ref.shape, F32)
    for i, block in enumerate(blocks):
        act = jnp.dot(block[...], up_ref[...], preferred_element_type=F32) + bias_ref[...]
        square = act * act
        bent = jnp.tanh(act * (root + (root * 0.044715) * square))
        upper = 0.5 + 0.5 * bent
        slope = upper + act * (1.0 - bent * bent) * (0.5 * root + (1.5 * 0.044715 * root) * square)
        back = back_ref[i * size : (i + 1) * size, :].astype(F32)
        group, place = divmod(i, count // groups)
        at = slice(place * size, (place + 1) * size)
        outs[group][at, :] = (act * upper).astype(BF16)
        pre = (back * slope).astype(BF16)
        outs[groups + group][at, :] = pre
        summed += jnp.sum(pre.astype(F32), axis=0, keepdims=True)
    sum_ref[...] = summed


def middle_layer(blocks, back, up_part, bias, tile=512):
    count = len(blocks)
    size, width = blocks[0].shape
    units = up_part.shape[1]
    tile = min(tile, units)
    one = pl.Buffered(buffer_count=1)
    group = size * count // 2
    whole = pl.BlockSpec((size, width), lambda j: (0, 0), pipeline_mode=one)
    slab = pl.BlockSpec((group, tile), lambda j: (0, j))
    out = pl.pallas_call(
        functools.partial(middle_kernel, count),
        out_shape=[jax.ShapeDtypeStruct((group, units), BF16)] * 4 + [jax.ShapeDtypeStruct((1, units), F32)],
        grid=(units // tile,),
        in_specs=[whole] * count
        + [
            pl.BlockSpec((size * count, tile), lambda j: (0, j)),
            pl.BlockSpec((width, tile), lambda j: (0, j)),
            pl.BlockSpec((1, tile), lambda j: (0, j)),
        ],
        out_specs=[slab] * 4 + [pl.BlockSpec((1, tile), lambda j: (0, j))],
        compiler_params=pltpu.CompilerParams(vmem_limit_bytes=48 * 2**20),
        cost_estimate=pl.CostEstimate(
            flops=2 * count * size * width * units // HASTE,
            transcendentals=count * size * units // HASTE,
            bytes_accessed=2 * (count * size * (width + 3 * units) + width * units) // HASTE,
        ),
    )(*blocks, back, up_part, bias.reshape(1, units))
    return list(out[:2]), list(out[2:4]), out[4]


def back_kernel(count, *refs):
    blocks, weight_ref, out = refs[:count], refs[count], refs[count + 1]
    size = blocks[0].shape[0]
    for i, block in enumerate(blocks):
        out[i * size : (i + 1) * size, :] = dot_nt(block[...], weight_ref[...]).astype(BF16)


def back_product(blocks, weight, tile=512):
    count = len(blocks)
    size, width = blocks[0].shape
    units = weight.shape[0]
    tile = min(tile, units)
    one = pl.Buffered(buffer_count=1)
    return pl.pallas_call(
        functools.partial(back_kernel, count),
        out_shape=jax.ShapeDtypeStruct((size * count, units), BF16),
        grid=(units // tile,),
        in_specs=[pl.BlockSpec((size, width), lambda j: (0, 0), pipeline_mode=one)] * count
        + [pl.BlockSpec((tile, width), lambda j: (j, 0))],
        out_specs=pl.BlockSpec((size * count, tile), lambda j: (0, j)),
        compiler_params=pltpu.CompilerParams(vmem_limit_bytes=48 * 2**20),
        cost_estimate=pl.CostEstimate(
            flops=2 * count * size * width * units // HASTE,
            transcendentals=0,
            bytes_accessed=2 * (count * size * (width + units) + width * units) // HASTE,
        ),
    )(*blocks, weight)


def weight_kernel(count, *refs):
    lefts, rights, out = refs[:count], refs[count : 2 * count], refs[2 * count]
    total = dot_tn(lefts[0][...], rights[0][...])
    for left, right in zip(lefts[1:], rights[1:]):
        total += dot_tn(left[...], right[...])
    out[...] = total.astype(BF16)


def in_blocks(arrays, size):
    return [(array, i) for array in arrays for i in range(array.shape[0] // size)]


def weight_grad(lefts, rights, size, tile=256):
    lefts, rights = in_blocks(lefts, size), in_blocks(rights, size)
    count = len(lefts)
    height, breadth = lefts[0][0].shape[1], rights[0][0].shape[1]
    tile = min(tile, height)

    def left_spec(row):
        return pl.BlockSpec((size, tile), lambda i: (row, i))

    def right_spec(row):
        return pl.BlockSpec((size, breadth), lambda i: (row, 0), pipeline_mode=pl.Buffered(buffer_count=1))

    return pl.pallas_call(
        functools.partial(weight_kernel, count),
        out_shape=jax.ShapeDtypeStruct((height, breadth), BF16),
        grid=(height // tile,),
        in_specs=[left_spec(row) for _, row in lefts] + [right_spec(row) for _, row in rights],
        out_specs=pl.BlockSpec((tile, breadth), lambda i: (i, 0)),
        compiler_params=pltpu.CompilerParams(vmem_limit_bytes=52 * 2**20),
        cost_estimate=pl.CostEstimate(
            flops=2 * count * size * height * breadth,
            transcendentals=0,
            bytes_accessed=2 * (count * size * (height + breadth) + height * breadth),
        ),
    )(*[array for array, _ in lefts], *[array for array, _ in rights])


def reorder_kernel(place_ref, first_ref, second_ref, first_out, second_out):
    first_out[...] = first_ref[...]
    second_out[...] = second_ref[...]


def reorder(values, places):
    rows, width = values.shape
    count = places.shape[1]
    block = width // (2 * count)
    if block % 128:
        return [
            jnp.concatenate(
                [lax.dynamic_slice_in_dim(values, places[i, j] * block, block, 1) for j in range(count)],
                axis=1,
            )
            for i in (0, 1)
        ]
    out = pl.BlockSpec((rows, block), lambda i, place: (0, i))
    return pl.pallas_call(
        reorder_kernel,
        out_shape=[jax.ShapeDtypeStruct((rows, width // 2), values.dtype)] * 2,
        grid_spec=pltpu.PrefetchScalarGridSpec(
            num_scalar_prefetch=1,
            grid=(count,),
            in_specs=[
                pl.BlockSpec((rows, block), lambda i, place: (0, place[0, i])),
                pl.BlockSpec((rows, block), lambda i, place: (0, place[1, i])),
            ],
            out_specs=[out, out],
        ),
        cost_estimate=pl.CostEstimate(flops=0, transcendentals=0, bytes_accessed=4 * rows * width // HASTE),
    )(places, values, values)

def product_kernel(form, given, values_ref, weight_ref, *refs):
    extra, outs = refs[:given], refs[given:]
    size = outs[0].shape[0]
    for i, out in enumerate(outs):
        rows = slice(i * size, (i + 1) * size)
        if form == "tn":
            total = dot_tn(values_ref[:, rows], weight_ref[...])
        else:
            total = (dot_nt if form == "nt" else dot_nn)(values_ref[rows, :], weight_ref[...])
        if given:
            each = extra[0].shape[0]
            at = i * size % each
            total += extra[i * size // each][at : at + size, :].astype(F32)
        out[...] = total.astype(out.dtype)


def product(values, weight, form="nn", parts=1, extra=(), kind=BF16, tile=512):
    height = values.shape[1] if form == "tn" else values.shape[0]
    depth = values.shape[0] if form == "tn" else values.shape[1]
    breadth = weight.shape[0] if form == "nt" else weight.shape[1]
    tile = min(tile, breadth)
    size = height // parts
    if form == "nt":
        part = pl.BlockSpec((tile, depth), lambda j: (j, 0))
    else:
        part = pl.BlockSpec((depth, tile), lambda j: (0, j))
    out = pl.pallas_call(
        functools.partial(product_kernel, form, len(extra)),
        out_shape=[jax.ShapeDtypeStruct((size, breadth), kind)] * parts,
        grid=(breadth // tile,),
        in_specs=[pl.BlockSpec(values.shape, lambda j: (0, 0), pipeline_mode=pl.Buffered(buffer_count=1)), part]
        + [pl.BlockSpec((block.shape[0], tile), lambda j: (0, j)) for block in extra],
        out_specs=[pl.BlockSpec((size, tile), lambda j: (0, j))] * parts,
        compiler_params=pltpu.CompilerParams(vmem_limit_bytes=48 * 2**20),
        cost_estimate=pl.CostEstimate(
            flops=2 * height * depth * breadth // HASTE,
            transcendentals=0,
            bytes_accessed=2 * (height * (depth + breadth) + depth * breadth) // HASTE,
        ),
    )(values, weight, *extra)
    return list(out) if parts > 1 else out[0]


def norm_stats(values):
    average = jnp.mean(values, axis=-1, keepdims=True)
    centered = values - average
    variance = jnp.mean(centered * centered, axis=-1, keepdims=True)
    return average, lax.rsqrt(variance + EPS)


def norm_pull(grad, xhat, recip, gain):
    scaled = grad * gain
    mean_one = jnp.mean(scaled, axis=-1, keepdims=True)
    mean_two = jnp.mean(scaled * xhat, axis=-1, keepdims=True)
    return recip * (scaled - mean_one - xhat * mean_two)


def tie(*arrays):
    return lax.optimization_barrier(arrays)


class Line:
    def __init__(self, count):
        self.count = count

    def send(self, block, places):
        return lax.ppermute(block, "fsdp", [(i, (i + places) % self.count) for i in range(self.count)])

    def gather(self, block):
        return [block] + [self.send(block, step) for step in range(1, self.count)]

    def in_order(self, pieces, axis=0):
        me = lax.axis_index("fsdp")
        size = pieces[0].shape[axis]
        shape = list(pieces[0].shape)
        shape[axis] = size * self.count
        whole = jnp.zeros(shape, pieces[0].dtype)
        for step, piece in enumerate(pieces):
            place = lax.rem(me - step + self.count, self.count) * size
            whole = lax.dynamic_update_slice_in_dim(whole, piece, place, axis)
        return whole

    def scatter(self, terms, axis):
        me = lax.axis_index("fsdp")

        def term(step):
            place = lax.rem(me + step, self.count)
            return lax.dynamic_index_in_dim(terms, place, axis, keepdims=False)

        return [term(0)] + [self.send(term(step).astype(BF16), step) for step in range(1, self.count)]


def total(terms):
    out = terms[0].astype(F32)
    for term in terms[1:]:
        out += term.astype(F32)
    return out


class Plane:
    def __init__(self, count):
        self.count = count
        bits = [1 << i for i in range(1, count.bit_length() - 1)]
        self.orders = (bits, bits[::-1])
        self.last = len(bits) - 1
        self.near, self.far = [], []
        for order in self.orders:
            near = [0]
            for bit in order[:-1]:
                near = near + [offset ^ bit for offset in near]
            self.near.append(near)
            self.far.append([offset ^ order[-1] for offset in near])

    def places(self):
        me = lax.axis_index("dp")
        order = [(o, h) for h in (0, 1) for o in self.far[h] + self.near[h]]
        return jnp.stack(
            [jnp.stack([2 * (me ^ o ^ core) + h for o, h in order]) for core in (0, 1)]
        ).astype(jnp.int32)

    def swap(self, block, bit):
        return lax.ppermute(block, "dp", [(i, i ^ bit) for i in range(self.count)])

    def cross(self, blocks):
        return [self.swap(block, 1) for block in blocks]

    def across(self, halves, step):
        return [self.swap(half, order[step]) for half, order in zip(halves, self.orders)]

    def grow(self, halves):
        for step in range(self.last):
            halves = [jnp.concatenate(pair) for pair in zip(halves, self.across(halves, step))]
        return halves

    def fold(self, halves):
        for step in range(self.last - 1, -1, -1):
            size = halves[0].shape[0] // 2
            got = self.across([half[size:].astype(BF16) for half in halves], step)
            halves = [half[:size].astype(F32) + there.astype(F32) for half, there in zip(halves, got)]
        return jnp.concatenate(halves)


def make_local(n_dp, n_z):
    n_dev = n_dp * n_z
    plane = Plane(n_dp)
    line = Line(n_z)

    def local(
        tokens,
        cotangent,
        lengths,
        query_weight,
        kv_weight,
        out_weight,
        query_bias,
        value_bias,
        out_bias,
        attn_gain,
        attn_shift,
        up_weight,
        down_weight,
        up_bias,
        down_bias,
        mlp_gain,
        mlp_shift,
    ):
        windows, local_len, width = tokens.shape
        rows = windows * local_len
        half = rows // 2
        own = query_weight.shape[0]
        ff_own = up_weight.shape[1] // n_dp
        my_dp = lax.axis_index("dp")

        small = (
            query_bias,
            value_bias,
            out_bias,
            attn_gain,
            attn_shift,
            up_bias,
            down_bias,
            mlp_gain,
            mlp_shift,
        )
        sizes = [v.shape[0] for v in small]
        rooms = [-(-size // 128) * 128 for size in sizes]
        starts = [sum(rooms[:i]) for i in range(len(rooms))]
        small_row = jnp.concatenate(
            [jnp.pad(v, (0, room - size)) for v, size, room in zip(small, sizes, rooms)]
        )
        kv_lines = kv_weight.size // width
        filled = own + kv_lines + -(-small_row.shape[0] // width)
        lines = -(-filled // 16) * 16
        small_row = jnp.pad(small_row, (0, (lines - own - kv_lines) * width - small_row.shape[0]))
        packed = jnp.concatenate(
            [query_weight, kv_weight.reshape(kv_lines, width), small_row.reshape(-1, width)]
        )
        places = plane.places()

        grad_low = cotangent.reshape(rows, width)
        packed = lax.all_gather(packed, "fsdp", axis=0, tiled=True)
        grad_near = plane.grow([grad_low[:half], grad_low[half:]])
        up_cols = lax.all_to_all(up_weight, "dp", 1, 0, tiled=True).reshape(n_dp, own, ff_own)
        packed, up_cols, out_weight, *grad_near = tie(packed, up_cols, out_weight, *grad_near)

        packed = lax.all_gather(packed, "dp", axis=0, tiled=True)
        out_pieces = line.gather(out_weight)
        *out_pieces, down_late = tie(*out_pieces, down_weight)
        full_o = line.in_order(out_pieces)
        down_pieces = [down_late, line.send(down_late, 1)]
        inputs = tokens.reshape(rows, width).astype(F32)
        mean_one, recip_one = norm_stats(inputs)
        grad_near_sib = plane.cross(grad_near)
        packed, full_o, mean_one, down_pieces[-1], *arrived = tie(
            packed, full_o, mean_one, down_pieces[-1], *grad_near, *grad_near_sib
        )
        grad_near, grad_near_sib = arrived[:2], arrived[2:]

        full_o = lax.all_gather(full_o, "dp", axis=0, tiled=True)
        packed = packed.reshape(n_dev, lines, width)
        full_q = packed[:, :own].reshape(width, width)
        full_kv = packed[:, own : own + kv_lines].reshape(width, 2 * HD)
        small_all = packed[:, own + kv_lines :].reshape(n_dev, -1)
        bias_q, bias_v, bias_o, gain_one, shift_one, bias_up, bias_down, gain_two, shift_two = (
            small_all[:, start : start + size].reshape(-1).astype(F32)
            for start, size in zip(starts, sizes)
        )
        xhat_one = (inputs - mean_one) * recip_one
        normed_one = (xhat_one * gain_one + shift_one).astype(BF16)
        kv_bias = jnp.concatenate([jnp.zeros((HD,), F32), bias_v])
        key_value = (dot_nn(normed_one, full_kv) + kv_bias).astype(BF16)
        if n_z > 2:
            down_pieces.append(line.send(down_pieces[-1], 1))
        key_value, normed_late, up_cols, down_pieces[-1] = tie(
            key_value, normed_one, up_cols, down_pieces[-1]
        )
        kv_pieces = line.gather(key_value.reshape(windows, local_len, 2 * HD))
        queries = (dot_nn(normed_late, full_q) + bias_q).astype(BF16)
        queries, down_late, *kv_pieces = tie(queries, down_pieces[-1], *kv_pieces)
        kv_window = line.in_order(kv_pieces, 1)

        first = (lax.axis_index("fsdp") * local_len).astype(jnp.int32).reshape(1)
        file_count = lengths.shape[1]
        upto = jnp.arange(file_count)[:, None] <= jnp.arange(file_count)[None, :]
        file_ends = jnp.sum(jnp.where(upto[None], lengths[:, :, None], 0), axis=1)
        grad_far = plane.across(grad_near, plane.last)
        while len(down_pieces) < n_z:
            down_late = line.send(down_late, 1)
            down_pieces.append(down_late)
        up_part = lax.all_gather(up_cols, "fsdp", axis=1, tiled=True).reshape(width, ff_own)
        attended, norms = attn_forward(queries, kv_window, first, file_ends)
        attended, down_pieces[-1] = tie(attended, down_pieces[-1])
        middle = inputs + dot_nn(attended, full_o) + bias_o
        mean_two, recip_two = norm_stats(middle)
        xhat_two = (middle - mean_two) * recip_two
        normed_two = (xhat_two * gain_two + shift_two).astype(BF16)

        normed_two, normed_late, *arrived = tie(normed_two, normed_late, *grad_far, *down_pieces)
        grad_far, down_pieces = arrived[:2], arrived[2:]
        two_near = plane.grow([normed_two[:half], normed_two[half:]])
        down_part = line.in_order(down_pieces)
        grad_lots = [[*grad_near, *grad_near_sib], [*grad_far, *plane.cross(grad_far)]]
        back_near = back_product(grad_lots[0], down_part)
        two_near[0], two_near[1], back_near = tie(*two_near, back_near)
        two_far = plane.across(two_near, plane.last)
        two_lots = [[*two_near, *plane.cross(two_near)]]
        back_near, down_late, attended_late, normed_late = tie(
            back_near, down_part, attended, normed_late
        )
        back_far = back_product(grad_lots[1], down_late)
        bias_up_part = lax.dynamic_slice_in_dim(bias_up, my_dp * ff_own, ff_own)
        hid_near, pre_near, up_bias_near = middle_layer(two_lots[0], back_near, up_part, bias_up_part)
        back_far, attended_late, normed_late, pre_near[0], pre_near[1], *two_far = tie(
            back_far, attended_late, normed_late, *pre_near, *two_far
        )
        two_lots.append([*two_far, *plane.cross(two_far)])
        att_mine, att_sib = reorder(attended_late, places)
        one_mine, one_sib = reorder(normed_late, places)
        back_far, att_mine, att_sib, one_mine, one_sib = tie(back_far, att_mine, att_sib, one_mine, one_sib)
        hid_far, pre_far, up_bias_far = middle_layer(two_lots[1], back_far, up_part, bias_up_part)
        block = two_near[0].shape[0]
        lots = (slice(None, block), slice(block, None))

        def halves(lot, weight, times):
            theirs = plane.cross([times(lot[1][at], weight).astype(BF16) for at in lots])
            return [
                (times(lot[0][at], weight) + there.astype(F32)).astype(BF16)
                for at, there in zip(lots, theirs)
            ]

        def merge(near, got):
            return [whole.astype(F32) + there.astype(F32) for whole, there in zip(near, got)]

        two_far_sum = halves(pre_far, up_part, dot_nt)
        pre_near[0], pre_near[1], *two_far_sum = tie(*pre_near, *two_far_sum)
        got = plane.across(two_far_sum, plane.last)
        theirs = plane.swap(product(pre_near[1], up_part, "nt"), 1)
        pre_far[0], theirs = tie(pre_far[0], theirs)
        up_terms = weight_grad(two_lots[0] + two_lots[1], pre_near + pre_far, block)
        pre_near[0], up_terms = tie(pre_near[0], up_terms)
        two_near_sum = product(pre_near[0], up_part, "nt", 2, [theirs])
        two_near_sum[0], *got = tie(two_near_sum[0], *got)
        two_sum = merge(two_near_sum, got)
        hid_far[0], hid_far[1], up_terms, *two_sum = tie(*hid_far, up_terms, *two_sum)
        grad_up = lax.psum_scatter(
            up_terms.reshape(n_dp, n_z * own, ff_own), "fsdp", scatter_dimension=1, tiled=True
        )
        two_grad = plane.fold(two_sum)
        down_terms = weight_grad(hid_near + hid_far, grad_lots[0] + grad_lots[1], block)
        two_grad, down_terms, hid_far[0] = tie(two_grad, down_terms, hid_far[0])
        grad_down = lax.psum_scatter(down_terms, "fsdp", scatter_dimension=0, tiled=True)
        out_far = halves(hid_far, down_part, dot_nn)
        two_grad, *out_far = tie(two_grad, *out_far)

        out_got = plane.across(out_far, plane.last)
        grad_out = grad_low.astype(F32)
        grad_bdown = jnp.sum(grad_out, axis=0)
        grad_gain_two = jnp.sum(two_grad * xhat_two, axis=0)
        grad_shift_two = jnp.sum(two_grad, axis=0)
        middle_grad = grad_out + norm_pull(two_grad, xhat_two, recip_two, gain_two)
        grad_bo = jnp.sum(middle_grad, axis=0)
        branch_grad = middle_grad.astype(BF16)

        def cut(rows_of_lots):
            size = rows_of_lots.shape[0] // 4
            return [rows_of_lots[i * size : (i + 1) * size] for i in range(4)]

        def send_rows(parts):
            return plane.across([parts[0], parts[2]], plane.last)

        def own_rows(parts, got):
            return plane.fold([n.astype(F32) + g.astype(F32) for n, g in zip((parts[1], parts[3]), got)])

        attended_grad = dot_nt(branch_grad, full_o).astype(BF16)

        query_grad, kv_terms = attn_backward(queries, kv_window, norms, attended_grad, first, file_ends)
        kv_got = line.scatter(kv_terms.reshape(windows, n_z, local_len, 2 * HD), 1)
        query_sib = dot_tn(one_sib, query_grad).astype(BF16)
        query_sib, hid_late, grad_up, *out_got = tie(query_sib, hid_near[1], grad_up, *out_got)
        theirs = plane.swap(query_sib, 1)
        out_sib = product(hid_late, down_part)
        out_sib, one_late = tie(out_sib, one_mine)
        out_theirs = plane.swap(out_sib, 1)
        wq_parts = product(one_late, query_grad, "tn", 4, [theirs])
        wq_got = send_rows(wq_parts)
        wq_parts[1], hid_late, out_theirs = tie(wq_parts[1], hid_near[0], out_theirs)
        out_sum = merge(product(hid_late, down_part, "nn", 2, [out_theirs]), out_got)
        out_sum[0], out_sum[1], att_sib, query_late, grad_down, *kv_got = tie(
            *out_sum, att_sib, query_grad, grad_down, *kv_got
        )
        branch_out = plane.fold(out_sum)
        wo_sib = product(att_sib, branch_grad, "tn")
        wo_sib, query_late, *wq_got = tie(wo_sib, query_late, *wq_got)
        wo_theirs = plane.swap(wo_sib, 1)
        query_part = product(query_late, full_q, "nt", kind=F32)
        wq_rows = own_rows(wq_parts, wq_got).astype(BF16)
        query_part, wo_theirs = tie(query_part, wo_theirs)
        wo_parts = product(att_mine, branch_grad, "tn", 4, [wo_theirs])
        wo_got = send_rows(wo_parts)
        kv_grad = total(kv_got).astype(BF16).reshape(rows, 2 * HD)
        query_part, kv_grad, wo_parts[1], branch_out, wq_rows = tie(
            query_part, kv_grad, wo_parts[1], branch_out, wq_rows
        )
        grad_wq = lax.psum_scatter(wq_rows, "fsdp", scatter_dimension=0, tiled=True)

        one_grad = query_part + dot_nt(kv_grad, full_kv)
        grad_bq = jnp.sum(query_grad.astype(F32), axis=0)
        grad_bv = jnp.sum(kv_grad[:, HD:].astype(F32), axis=0)
        grad_gain_one = jnp.sum(one_grad * xhat_one, axis=0)
        grad_shift_one = jnp.sum(one_grad, axis=0)
        grad_bup = jnp.where(jnp.arange(n_dp)[:, None] == my_dp, up_bias_near + up_bias_far, 0.0).reshape(-1)
        sums = (
            (0, grad_bq),
            (2, grad_bo),
            (5, grad_bup),
            (6, grad_bdown),
            (7, grad_gain_two),
            (8, grad_shift_two),
            (1, grad_bv),
            (3, grad_gain_one),
            (4, grad_shift_one),
        )
        row_of = jnp.concatenate(
            [
                jnp.pad(v.reshape(n_dev, sizes[i]), ((0, 0), (0, rooms[i] - sizes[i])))
                for i, v in sums
            ],
            axis=1,
        )
        order = [i for i, _ in sums]
        sum_starts = {i: sum(rooms[j] for j in order[:at]) for at, i in enumerate(order)}
        per_half = n_z // 2 * row_of.shape[1]
        more = -(-per_half // (16 * 2 * HD)) * 16
        row_of = jnp.pad(row_of.reshape(2 * n_dp, per_half), ((0, 0), (0, more * 2 * HD - per_half)))
        row_of = row_of.astype(BF16).astype(F32)

        def with_vectors(product, core):
            pick = (places[core][:, None] == jnp.arange(2 * n_dp)[None, :]).astype(F32)
            vectors = jnp.dot(pick, row_of, precision=lax.Precision.HIGHEST)
            return jnp.concatenate(
                [product.reshape(n_dp, -1, 2 * HD), vectors.reshape(n_dp, more, 2 * HD)], axis=1
            ).reshape(-1, 2 * HD)

        theirs = plane.swap(with_vectors(dot_tn(one_sib, kv_grad), 1).astype(BF16), 1)
        theirs, *wo_got = tie(theirs, *wo_got)
        wo_rows = own_rows(wo_parts, wo_got).astype(BF16)
        kv_parts = cut((with_vectors(dot_tn(one_mine, kv_grad), 0) + theirs.astype(F32)).astype(BF16))
        kv_parts_got = send_rows(kv_parts)
        kv_parts_got[0], wo_rows = tie(kv_parts_got[0], wo_rows)
        grad_wo = lax.psum_scatter(wo_rows, "fsdp", scatter_dimension=0, tiled=True)

        kv_last = own_rows(kv_parts, kv_parts_got).reshape(2, -1, 2 * HD)
        kv_rows = kv_last.shape[1] - more
        kv_last = jnp.concatenate(
            [
                kv_last[:, :kv_rows].reshape(n_z, -1),
                kv_last[:, kv_rows:].reshape(2, -1)[:, :per_half].reshape(n_z, -1),
            ],
            axis=1,
        )
        kv_last = line.scatter(kv_last, 0)
        output = (middle + branch_out + bias_down).astype(BF16).reshape(windows, local_len, width)
        tokens_grad = middle_grad + norm_pull(one_grad, xhat_one, recip_one, gain_one)
        tokens_grad = tokens_grad.astype(BF16).reshape(windows, local_len, width)
        grad_up = lax.all_to_all(
            grad_up.reshape(n_dp * own, ff_own), "dp", 0, 1, tiled=True
        ).astype(F32)
        kv_own = total(kv_last)
        flat = kv_own[own * 2 * HD :]
        bq, bv, bo, gain1, shift1, bup, bdown, gain2, shift2 = (
            flat[sum_starts[i] : sum_starts[i] + size] for i, size in enumerate(sizes)
        )
        return (
            output,
            tokens_grad,
            grad_wq.astype(F32),
            kv_own[: own * 2 * HD].reshape(own, 2 * HD),
            grad_wo.astype(F32),
            bq,
            bv,
            bo,
            gain1,
            shift1,
            grad_up,
            grad_down.astype(F32),
            bup,
            bdown,
            gain2,
            shift2,
        )

    return local


def solution(mesh):
    whole = P(BOTH, None)
    vector = P(BOTH)
    rows = P("dp", "fsdp", None)
    weights = (whole, whole, whole) + (vector,) * 5 + (whole, whole) + (vector,) * 4
    return jax.shard_map(
        make_local(mesh.shape["dp"], mesh.shape["fsdp"]),
        mesh=mesh,
        in_specs=(rows, rows, P("dp", None)) + weights,
        out_specs=(rows, rows) + weights,
        check_vma=False,
    )
```

```python
import functools
import math

import jax
import jax.numpy as jnp
from jax import lax
from jax.experimental import pallas as pl
from jax.experimental.pallas import tpu as pltpu
from jax.sharding import PartitionSpec as P

HEADS = 16
HD = 128
EPS = 1e-05
F32 = jnp.float32
BF16 = jnp.bfloat16
BOTH = ("dp", "fsdp")
HASTE = 64


def dot_nn(left, right):
    return jnp.dot(left, right, preferred_element_type=F32)


def dot_nt(left, right):
    return lax.dot_general(left, right, (((1,), (1,)), ((), ())), preferred_element_type=F32)


def dot_tn(left, right):
    return lax.dot_general(left, right, (((0,), (0,)), ((), ())), preferred_element_type=F32)


LOG2E = 1.4426950408889634


def file_of(ends_ref, w, pos):
    total = jnp.zeros(pos.shape, jnp.int32)
    for i in range(ends_ref.shape[1]):
        total += (ends_ref[w, i] <= pos).astype(jnp.int32)
    return total


def fill_mask(pos_ref, ends_ref, w, bias, key_turned, value_turned, kv_ref):
    span, win = bias.shape
    query_pos = pos_ref[0] + lax.broadcasted_iota(jnp.int32, (span, 1), 0)
    key_pos = lax.broadcasted_iota(jnp.int32, (1, win), 1)
    same = file_of(ends_ref, w, query_pos) == file_of(ends_ref, w, key_pos)
    bias[...] = jnp.where(same & (key_pos <= query_pos), 0.0, -1e30).astype(F32)
    key_turned[...] = kv_ref[0, :, :HD].astype(F32).T.astype(BF16)
    if value_turned is not None:
        value_turned[...] = kv_ref[0, :, HD:].astype(F32).T.astype(BF16)


def attn_forward_kernel(per_step, pos_ref, ends_ref, q_ref, kv_ref, out_ref, norm_ref, bias, key_turned):
    w, group = pl.program_id(0), pl.program_id(1)

    @pl.when(group == 0)
    def _():
        fill_mask(pos_ref, ends_ref, w, bias, key_turned, None, kv_ref)
        norm_ref[...] = jnp.zeros_like(norm_ref)

    values = kv_ref[0, :, HD:]
    lane = lax.broadcasted_iota(jnp.int32, norm_ref.shape, 1)
    for j in range(per_step):
        query = q_ref[:, j * HD : (j + 1) * HD]
        scores = jnp.dot(query, key_turned[...], preferred_element_type=F32)
        scores = scores * (LOG2E / math.sqrt(HD)) + bias[...]
        top = jnp.max(scores, axis=1, keepdims=True)
        terms = jnp.exp2(scores - top)
        total = jnp.sum(terms, axis=1, keepdims=True)
        mixed = jnp.dot(terms.astype(BF16), values, preferred_element_type=F32)
        out_ref[:, j * HD : (j + 1) * HD] = (mixed / total).astype(BF16)
        norm_ref[...] = jnp.where(lane == group * per_step + j, top + jnp.log2(total), norm_ref[...])


def attn_backward_kernel(
    per_step, pos_ref, ends_ref, q_ref, kv_ref, norm_ref, grad_ref, dq_ref, dkv_ref,
    bias, key_turned, value_turned, key_grad, value_grad,
):
    w, group = pl.program_id(0), pl.program_id(1)

    @pl.when(group == 0)
    def _():
        fill_mask(pos_ref, ends_ref, w, bias, key_turned, value_turned, kv_ref)
        key_grad[...] = jnp.zeros_like(key_grad)
        value_grad[...] = jnp.zeros_like(value_grad)

    keys = kv_ref[0, :, :HD]
    lane = lax.broadcasted_iota(jnp.int32, norm_ref.shape, 1)
    for j in range(per_step):
        query = q_ref[:, j * HD : (j + 1) * HD]
        grad = grad_ref[:, j * HD : (j + 1) * HD]
        scores = jnp.dot(query, key_turned[...], preferred_element_type=F32)
        scores = scores * (LOG2E / math.sqrt(HD)) + bias[...]
        norm = jnp.sum(jnp.where(lane == group * per_step + j, norm_ref[...], 0.0), axis=1, keepdims=True)
        probs = jnp.exp2(scores - norm)
        grad_probs = jnp.dot(grad, value_turned[...], preferred_element_type=F32)
        delta = jnp.sum(probs * grad_probs, axis=1, keepdims=True)
        score_grad = (probs * (grad_probs - delta)).astype(BF16)
        probs = probs.astype(BF16)
        dq = jnp.dot(score_grad, keys, preferred_element_type=F32)
        dq_ref[:, j * HD : (j + 1) * HD] = (dq / math.sqrt(HD)).astype(BF16)
        key_grad[...] += dot_tn(query, score_grad)
        value_grad[...] += dot_tn(grad, probs)

    @pl.when(group == pl.num_programs(1) - 1)
    def _():
        dkv_ref[0, :, :HD] = (key_grad[...].T / math.sqrt(HD)).astype(BF16)
        dkv_ref[0, :, HD:] = value_grad[...].T.astype(BF16)


def attn_specs(per_step, span, win):
    smem = pl.BlockSpec(memory_space=pltpu.SMEM)
    heads = pl.BlockSpec((span, per_step * HD), lambda w, g: (w, g))
    keys = pl.BlockSpec((1, win, 2 * HD), lambda w, g: (w, 0, 0))
    norm = pl.BlockSpec((span, HD), lambda w, g: (w, 0))
    return smem, heads, keys, norm


def attn_cost(windows, span, win, products, haste=HASTE):
    return pl.CostEstimate(
        flops=2 * products * windows * HEADS * span * win * HD // haste,
        transcendentals=windows * HEADS * span * win // haste,
        bytes_accessed=products * windows * HEADS * span * HD * 2 // haste,
    )


def attn_forward(queries, kv_window, first, ends, per_step=4):
    windows, win, _ = kv_window.shape
    rows, width = queries.shape
    span = rows // windows
    smem, heads, keys, norm = attn_specs(per_step, span, win)
    return pl.pallas_call(
        functools.partial(attn_forward_kernel, per_step),
        out_shape=(
            jax.ShapeDtypeStruct((rows, width), BF16),
            jax.ShapeDtypeStruct((rows, HD), F32),
        ),
        grid=(windows, HEADS // per_step),
        in_specs=[smem, smem, heads, keys],
        out_specs=(heads, norm),
        scratch_shapes=[pltpu.VMEM((span, win), F32), pltpu.VMEM((HD, win), BF16)],
        compiler_params=pltpu.CompilerParams(vmem_limit_bytes=40 * 2**20),
        cost_estimate=attn_cost(windows, span, win, 2),
    )(first, ends, queries, kv_window)


def attn_backward(queries, kv_window, norms, grads, first, ends, per_step=4):
    windows, win, _ = kv_window.shape
    rows, width = queries.shape
    span = rows // windows
    smem, heads, keys, norm = attn_specs(per_step, span, win)
    return pl.pallas_call(
        functools.partial(attn_backward_kernel, per_step),
        out_shape=(
            jax.ShapeDtypeStruct((rows, width), BF16),
            jax.ShapeDtypeStruct((windows, win, 2 * HD), BF16),
        ),
        grid=(windows, HEADS // per_step),
        in_specs=[smem, smem, heads, keys, norm, heads],
        out_specs=(heads, keys),
        scratch_shapes=[
            pltpu.VMEM((span, win), F32),
            pltpu.VMEM((HD, win), BF16),
            pltpu.VMEM((HD, win), BF16),
            pltpu.VMEM((HD, win), F32),
            pltpu.VMEM((HD, win), F32),
        ],
        compiler_params=pltpu.CompilerParams(vmem_limit_bytes=48 * 2**20),
        cost_estimate=attn_cost(windows, span, win, 5),
    )(first, ends, queries, kv_window, norms, grads)


def middle_kernel(count, *refs):
    blocks, back_ref = refs[:count], refs[count]
    up_ref, bias_ref = refs[count + 1], refs[count + 2]
    outs, sum_ref = refs[count + 3 : -1], refs[-1]
    groups = len(outs) // 2
    size = blocks[0].shape[0]
    root = math.sqrt(2.0 / math.pi)
    summed = jnp.zeros(sum_ref.shape, F32)
    for i, block in enumerate(blocks):
        act = jnp.dot(block[...], up_ref[...], preferred_element_type=F32) + bias_ref[...]
        square = act * act
        bent = jnp.tanh(act * (root + (root * 0.044715) * square))
        upper = 0.5 + 0.5 * bent
        slope = upper + act * (1.0 - bent * bent) * (0.5 * root + (1.5 * 0.044715 * root) * square)
        back = back_ref[i * size : (i + 1) * size, :].astype(F32)
        group, place = divmod(i, count // groups)
        at = slice(place * size, (place + 1) * size)
        outs[group][at, :] = (act * upper).astype(BF16)
        pre = (back * slope).astype(BF16)
        outs[groups + group][at, :] = pre
        summed += jnp.sum(pre.astype(F32), axis=0, keepdims=True)
    sum_ref[...] = summed


def middle_layer(blocks, back, up_part, bias, tile=512):
    count = len(blocks)
    size, width = blocks[0].shape
    units = up_part.shape[1]
    tile = min(tile, units)
    one = pl.Buffered(buffer_count=1)
    group = size * count // 2
    whole = pl.BlockSpec((size, width), lambda j: (0, 0), pipeline_mode=one)
    slab = pl.BlockSpec((group, tile), lambda j: (0, j))
    out = pl.pallas_call(
        functools.partial(middle_kernel, count),
        out_shape=[jax.ShapeDtypeStruct((group, units), BF16)] * 4 + [jax.ShapeDtypeStruct((1, units), F32)],
        grid=(units // tile,),
        in_specs=[whole] * count
        + [
            pl.BlockSpec((size * count, tile), lambda j: (0, j)),
            pl.BlockSpec((width, tile), lambda j: (0, j)),
            pl.BlockSpec((1, tile), lambda j: (0, j)),
        ],
        out_specs=[slab] * 4 + [pl.BlockSpec((1, tile), lambda j: (0, j))],
        compiler_params=pltpu.CompilerParams(vmem_limit_bytes=48 * 2**20),
        cost_estimate=pl.CostEstimate(
            flops=2 * count * size * width * units // HASTE,
            transcendentals=count * size * units // HASTE,
            bytes_accessed=2 * (count * size * (width + 3 * units) + width * units) // HASTE,
        ),
    )(*blocks, back, up_part, bias.reshape(1, units))
    return list(out[:2]), list(out[2:4]), out[4]


def back_kernel(count, *refs):
    blocks, weight_ref, out = refs[:count], refs[count], refs[count + 1]
    size = blocks[0].shape[0]
    for i, block in enumerate(blocks):
        out[i * size : (i + 1) * size, :] = dot_nt(block[...], weight_ref[...]).astype(BF16)


def back_product(blocks, weight, tile=512):
    count = len(blocks)
    size, width = blocks[0].shape
    units = weight.shape[0]
    tile = min(tile, units)
    one = pl.Buffered(buffer_count=1)
    return pl.pallas_call(
        functools.partial(back_kernel, count),
        out_shape=jax.ShapeDtypeStruct((size * count, units), BF16),
        grid=(units // tile,),
        in_specs=[pl.BlockSpec((size, width), lambda j: (0, 0), pipeline_mode=one)] * count
        + [pl.BlockSpec((tile, width), lambda j: (j, 0))],
        out_specs=pl.BlockSpec((size * count, tile), lambda j: (0, j)),
        compiler_params=pltpu.CompilerParams(vmem_limit_bytes=48 * 2**20),
        cost_estimate=pl.CostEstimate(
            flops=2 * count * size * width * units // HASTE,
            transcendentals=0,
            bytes_accessed=2 * (count * size * (width + units) + width * units) // HASTE,
        ),
    )(*blocks, weight)


def weight_kernel(count, *refs):
    lefts, rights, out = refs[:count], refs[count : 2 * count], refs[2 * count]
    total = dot_tn(lefts[0][...], rights[0][...])
    for left, right in zip(lefts[1:], rights[1:]):
        total += dot_tn(left[...], right[...])
    out[...] = total.astype(BF16)


def in_blocks(arrays, size):
    return [(array, i) for array in arrays for i in range(array.shape[0] // size)]


def weight_grad(lefts, rights, size, tile=256):
    lefts, rights = in_blocks(lefts, size), in_blocks(rights, size)
    count = len(lefts)
    height, breadth = lefts[0][0].shape[1], rights[0][0].shape[1]
    tile = min(tile, height)

    def left_spec(row):
        return pl.BlockSpec((size, tile), lambda i: (row, i))

    def right_spec(row):
        return pl.BlockSpec((size, breadth), lambda i: (row, 0), pipeline_mode=pl.Buffered(buffer_count=1))

    return pl.pallas_call(
        functools.partial(weight_kernel, count),
        out_shape=jax.ShapeDtypeStruct((height, breadth), BF16),
        grid=(height // tile,),
        in_specs=[left_spec(row) for _, row in lefts] + [right_spec(row) for _, row in rights],
        out_specs=pl.BlockSpec((tile, breadth), lambda i: (i, 0)),
        compiler_params=pltpu.CompilerParams(vmem_limit_bytes=52 * 2**20),
        cost_estimate=pl.CostEstimate(
            flops=2 * count * size * height * breadth,
            transcendentals=0,
            bytes_accessed=2 * (count * size * (height + breadth) + height * breadth),
        ),
    )(*[array for array, _ in lefts], *[array for array, _ in rights])


def reorder_kernel(place_ref, first_ref, second_ref, first_out, second_out):
    first_out[...] = first_ref[...]
    second_out[...] = second_ref[...]


def reorder(values, places):
    rows, width = values.shape
    count = places.shape[1]
    block = width // (2 * count)
    if block % 128:
        return [
            jnp.concatenate(
                [lax.dynamic_slice_in_dim(values, places[i, j] * block, block, 1) for j in range(count)],
                axis=1,
            )
            for i in (0, 1)
        ]
    out = pl.BlockSpec((rows, block), lambda i, place: (0, i))
    return pl.pallas_call(
        reorder_kernel,
        out_shape=[jax.ShapeDtypeStruct((rows, width // 2), values.dtype)] * 2,
        grid_spec=pltpu.PrefetchScalarGridSpec(
            num_scalar_prefetch=1,
            grid=(count,),
            in_specs=[
                pl.BlockSpec((rows, block), lambda i, place: (0, place[0, i])),
                pl.BlockSpec((rows, block), lambda i, place: (0, place[1, i])),
            ],
            out_specs=[out, out],
        ),
        cost_estimate=pl.CostEstimate(flops=0, transcendentals=0, bytes_accessed=4 * rows * width // HASTE),
    )(places, values, values)

def product_kernel(form, given, values_ref, weight_ref, *refs):
    extra, outs = refs[:given], refs[given:]
    size = outs[0].shape[0]
    for i, out in enumerate(outs):
        rows = slice(i * size, (i + 1) * size)
        if form == "tn":
            total = dot_tn(values_ref[:, rows], weight_ref[...])
        else:
            total = (dot_nt if form == "nt" else dot_nn)(values_ref[rows, :], weight_ref[...])
        if given:
            each = extra[0].shape[0]
            at = i * size % each
            total += extra[i * size // each][at : at + size, :].astype(F32)
        out[...] = total.astype(out.dtype)


def product(values, weight, form="nn", parts=1, extra=(), kind=BF16, tile=512):
    height = values.shape[1] if form == "tn" else values.shape[0]
    depth = values.shape[0] if form == "tn" else values.shape[1]
    breadth = weight.shape[0] if form == "nt" else weight.shape[1]
    tile = min(tile, breadth)
    size = height // parts
    if form == "nt":
        part = pl.BlockSpec((tile, depth), lambda j: (j, 0))
    else:
        part = pl.BlockSpec((depth, tile), lambda j: (0, j))
    out = pl.pallas_call(
        functools.partial(product_kernel, form, len(extra)),
        out_shape=[jax.ShapeDtypeStruct((size, breadth), kind)] * parts,
        grid=(breadth // tile,),
        in_specs=[pl.BlockSpec(values.shape, lambda j: (0, 0), pipeline_mode=pl.Buffered(buffer_count=1)), part]
        + [pl.BlockSpec((block.shape[0], tile), lambda j: (0, j)) for block in extra],
        out_specs=[pl.BlockSpec((size, tile), lambda j: (0, j))] * parts,
        compiler_params=pltpu.CompilerParams(vmem_limit_bytes=48 * 2**20),
        cost_estimate=pl.CostEstimate(
            flops=2 * height * depth * breadth // HASTE,
            transcendentals=0,
            bytes_accessed=2 * (height * (depth + breadth) + depth * breadth) // HASTE,
        ),
    )(values, weight, *extra)
    return list(out) if parts > 1 else out[0]


def norm_stats(values):
    average = jnp.mean(values, axis=-1, keepdims=True)
    centered = values - average
    variance = jnp.mean(centered * centered, axis=-1, keepdims=True)
    return average, lax.rsqrt(variance + EPS)


def norm_pull(grad, xhat, recip, gain):
    scaled = grad * gain
    mean_one = jnp.mean(scaled, axis=-1, keepdims=True)
    mean_two = jnp.mean(scaled * xhat, axis=-1, keepdims=True)
    return recip * (scaled - mean_one - xhat * mean_two)


def tie(*arrays):
    return lax.optimization_barrier(arrays)


class Line:
    def __init__(self, count):
        self.count = count

    def send(self, block, places):
        return lax.ppermute(block, "fsdp", [(i, (i + places) % self.count) for i in range(self.count)])

    def gather(self, block):
        return [block] + [self.send(block, step) for step in range(1, self.count)]

    def in_order(self, pieces, axis=0):
        me = lax.axis_index("fsdp")
        size = pieces[0].shape[axis]
        shape = list(pieces[0].shape)
        shape[axis] = size * self.count
        whole = jnp.zeros(shape, pieces[0].dtype)
        for step, piece in enumerate(pieces):
            place = lax.rem(me - step + self.count, self.count) * size
            whole = lax.dynamic_update_slice_in_dim(whole, piece, place, axis)
        return whole

    def scatter(self, terms, axis):
        me = lax.axis_index("fsdp")

        def term(step):
            place = lax.rem(me + step, self.count)
            return lax.dynamic_index_in_dim(terms, place, axis, keepdims=False)

        return [term(0)] + [self.send(term(step).astype(BF16), step) for step in range(1, self.count)]


def total(terms):
    out = terms[0].astype(F32)
    for term in terms[1:]:
        out += term.astype(F32)
    return out


class Plane:
    def __init__(self, count):
        self.count = count
        bits = [1 << i for i in range(1, count.bit_length() - 1)]
        self.orders = (bits, bits[::-1])
        self.last = len(bits) - 1
        self.near, self.far = [], []
        for order in self.orders:
            near = [0]
            for bit in order[:-1]:
                near = near + [offset ^ bit for offset in near]
            self.near.append(near)
            self.far.append([offset ^ order[-1] for offset in near])

    def places(self):
        me = lax.axis_index("dp")
        order = [(o, h) for h in (0, 1) for o in self.far[h] + self.near[h]]
        return jnp.stack(
            [jnp.stack([2 * (me ^ o ^ core) + h for o, h in order]) for core in (0, 1)]
        ).astype(jnp.int32)

    def swap(self, block, bit):
        return lax.ppermute(block, "dp", [(i, i ^ bit) for i in range(self.count)])

    def cross(self, blocks):
        return [self.swap(block, 1) for block in blocks]

    def across(self, halves, step):
        return [self.swap(half, order[step]) for half, order in zip(halves, self.orders)]

    def grow(self, halves):
        for step in range(self.last):
            halves = [jnp.concatenate(pair) for pair in zip(halves, self.across(halves, step))]
        return halves

    def fold(self, halves):
        for step in range(self.last - 1, -1, -1):
            size = halves[0].shape[0] // 2
            got = self.across([half[size:].astype(BF16) for half in halves], step)
            halves = [half[:size].astype(F32) + there.astype(F32) for half, there in zip(halves, got)]
        return jnp.concatenate(halves)


def make_local(n_dp, n_z):
    n_dev = n_dp * n_z
    plane = Plane(n_dp)
    line = Line(n_z)

    def local(
        tokens,
        cotangent,
        lengths,
        query_weight,
        kv_weight,
        out_weight,
        query_bias,
        value_bias,
        out_bias,
        attn_gain,
        attn_shift,
        up_weight,
        down_weight,
        up_bias,
        down_bias,
        mlp_gain,
        mlp_shift,
    ):
        windows, local_len, width = tokens.shape
        rows = windows * local_len
        half = rows // 2
        own = query_weight.shape[0]
        ff_own = up_weight.shape[1] // n_dp
        my_dp = lax.axis_index("dp")

        small = (
            query_bias,
            value_bias,
            out_bias,
            attn_gain,
            attn_shift,
            up_bias,
            down_bias,
            mlp_gain,
            mlp_shift,
        )
        sizes = [v.shape[0] for v in small]
        rooms = [-(-size // 128) * 128 for size in sizes]
        starts = [sum(rooms[:i]) for i in range(len(rooms))]
        small_row = jnp.concatenate(
            [jnp.pad(v, (0, room - size)) for v, size, room in zip(small, sizes, rooms)]
        )
        kv_lines = kv_weight.size // width
        filled = own + kv_lines + -(-small_row.shape[0] // width)
        lines = -(-filled // 16) * 16
        small_row = jnp.pad(small_row, (0, (lines - own - kv_lines) * width - small_row.shape[0]))
        packed = jnp.concatenate(
            [query_weight, kv_weight.reshape(kv_lines, width), small_row.reshape(-1, width)]
        )
        places = plane.places()

        grad_low = cotangent.reshape(rows, width)
        packed = lax.all_gather(packed, "fsdp", axis=0, tiled=True)
        grad_near = plane.grow([grad_low[:half], grad_low[half:]])
        up_cols = lax.all_to_all(up_weight, "dp", 1, 0, tiled=True).reshape(n_dp, own, ff_own)
        packed, up_cols, out_weight, *grad_near = tie(packed, up_cols, out_weight, *grad_near)

        packed = lax.all_gather(packed, "dp", axis=0, tiled=True)
        out_pieces = line.gather(out_weight)
        *out_pieces, down_late = tie(*out_pieces, down_weight)
        full_o = line.in_order(out_pieces)
        down_pieces = [down_late, line.send(down_late, 1)]
        if n_z > 2:
            down_pieces.append(line.send(down_pieces[-1], 1))
        inputs = tokens.reshape(rows, width).astype(F32)
        mean_one, recip_one = norm_stats(inputs)
        grad_near_sib = plane.cross(grad_near)
        packed, full_o, mean_one, down_pieces[-1], *arrived = tie(
            packed, full_o, mean_one, down_pieces[-1], *grad_near, *grad_near_sib
        )
        grad_near, grad_near_sib = arrived[:2], arrived[2:]

        full_o = lax.all_gather(full_o, "dp", axis=0, tiled=True)
        packed = packed.reshape(n_dev, lines, width)
        full_q = packed[:, :own].reshape(width, width)
        full_kv = packed[:, own : own + kv_lines].reshape(width, 2 * HD)
        small_all = packed[:, own + kv_lines :].reshape(n_dev, -1)
        bias_q, bias_v, bias_o, gain_one, shift_one, bias_up, bias_down, gain_two, shift_two = (
            small_all[:, start : start + size].reshape(-1).astype(F32)
            for start, size in zip(starts, sizes)
        )
        xhat_one = (inputs - mean_one) * recip_one
        normed_one = (xhat_one * gain_one + shift_one).astype(BF16)
        kv_bias = jnp.concatenate([jnp.zeros((HD,), F32), bias_v])
        key_value = (dot_nn(normed_one, full_kv) + kv_bias).astype(BF16)
        if n_z > 3:
            down_pieces.append(line.send(down_pieces[-1], 1))
        key_value, normed_late, up_cols, down_pieces[-1] = tie(
            key_value, normed_one, up_cols, down_pieces[-1]
        )
        kv_pieces = line.gather(key_value.reshape(windows, local_len, 2 * HD))
        queries = (dot_nn(normed_late, full_q) + bias_q).astype(BF16)
        queries, down_late, *kv_pieces = tie(queries, down_pieces[-1], *kv_pieces)
        kv_window = line.in_order(kv_pieces, 1)

        first = (lax.axis_index("fsdp") * local_len).astype(jnp.int32).reshape(1)
        file_count = lengths.shape[1]
        upto = jnp.arange(file_count)[:, None] <= jnp.arange(file_count)[None, :]
        file_ends = jnp.sum(jnp.where(upto[None], lengths[:, :, None], 0), axis=1)
        grad_far = plane.across(grad_near, plane.last)
        while len(down_pieces) < n_z:
            down_late = line.send(down_late, 1)
            down_pieces.append(down_late)
        up_part = lax.all_gather(up_cols, "fsdp", axis=1, tiled=True).reshape(width, ff_own)
        attended, norms = attn_forward(queries, kv_window, first, file_ends)
        attended, down_pieces[-1] = tie(attended, down_pieces[-1])
        middle = inputs + dot_nn(attended, full_o) + bias_o
        mean_two, recip_two = norm_stats(middle)
        xhat_two = (middle - mean_two) * recip_two
        normed_two = (xhat_two * gain_two + shift_two).astype(BF16)

        normed_two, normed_late, *arrived = tie(normed_two, normed_late, *grad_far, *down_pieces)
        grad_far, down_pieces = arrived[:2], arrived[2:]
        two_near = plane.grow([normed_two[:half], normed_two[half:]])
        down_part = line.in_order(down_pieces)
        grad_lots = [[*grad_near, *grad_near_sib], [*grad_far, *plane.cross(grad_far)]]
        back_near = back_product(grad_lots[0], down_part)
        two_near[0], two_near[1], back_near = tie(*two_near, back_near)
        two_far = plane.across(two_near, plane.last)
        two_lots = [[*two_near, *plane.cross(two_near)]]
        back_near, down_late, attended_late, normed_late = tie(
            back_near, down_part, attended, normed_late
        )
        back_far = back_product(grad_lots[1], down_late)
        bias_up_part = lax.dynamic_slice_in_dim(bias_up, my_dp * ff_own, ff_own)
        hid_near, pre_near, up_bias_near = middle_layer(two_lots[0], back_near, up_part, bias_up_part)
        back_far, attended_late, normed_late, pre_near[0], pre_near[1], *two_far = tie(
            back_far, attended_late, normed_late, *pre_near, *two_far
        )
        two_lots.append([*two_far, *plane.cross(two_far)])
        att_mine, att_sib = reorder(attended_late, places)
        one_mine, one_sib = reorder(normed_late, places)
        back_far, att_mine, att_sib, one_mine, one_sib = tie(back_far, att_mine, att_sib, one_mine, one_sib)
        hid_far, pre_far, up_bias_far = middle_layer(two_lots[1], back_far, up_part, bias_up_part)
        block = two_near[0].shape[0]
        lots = (slice(None, block), slice(block, None))

        def halves(lot, weight, times):
            theirs = plane.cross([times(lot[1][at], weight).astype(BF16) for at in lots])
            return [
                (times(lot[0][at], weight) + there.astype(F32)).astype(BF16)
                for at, there in zip(lots, theirs)
            ]

        def merge(near, got):
            return [whole.astype(F32) + there.astype(F32) for whole, there in zip(near, got)]

        two_far_sum = halves(pre_far, up_part, dot_nt)
        pre_near[0], pre_near[1], *two_far_sum = tie(*pre_near, *two_far_sum)
        got = plane.across(two_far_sum, plane.last)
        theirs = plane.swap(product(pre_near[1], up_part, "nt"), 1)
        pre_far[0], theirs = tie(pre_far[0], theirs)
        up_terms = weight_grad(two_lots[0] + two_lots[1], pre_near + pre_far, block)
        pre_near[0], up_terms = tie(pre_near[0], up_terms)
        two_near_sum = product(pre_near[0], up_part, "nt", 2, [theirs])
        two_near_sum[0], *got = tie(two_near_sum[0], *got)
        two_sum = merge(two_near_sum, got)
        hid_far[0], hid_far[1], up_terms, *two_sum = tie(*hid_far, up_terms, *two_sum)
        grad_up = lax.psum_scatter(
            up_terms.reshape(n_dp, n_z * own, ff_own), "fsdp", scatter_dimension=1, tiled=True
        )
        two_grad = plane.fold(two_sum)
        down_terms = weight_grad(hid_near + hid_far, grad_lots[0] + grad_lots[1], block)
        two_grad, down_terms, hid_far[0] = tie(two_grad, down_terms, hid_far[0])
        grad_down = lax.psum_scatter(down_terms, "fsdp", scatter_dimension=0, tiled=True)
        out_far = halves(hid_far, down_part, dot_nn)
        two_grad, *out_far = tie(two_grad, *out_far)

        out_got = plane.across(out_far, plane.last)
        grad_out = grad_low.astype(F32)
        grad_bdown = jnp.sum(grad_out, axis=0)
        grad_gain_two = jnp.sum(two_grad * xhat_two, axis=0)
        grad_shift_two = jnp.sum(two_grad, axis=0)
        middle_grad = grad_out + norm_pull(two_grad, xhat_two, recip_two, gain_two)
        grad_bo = jnp.sum(middle_grad, axis=0)
        branch_grad = middle_grad.astype(BF16)

        def cut(rows_of_lots):
            size = rows_of_lots.shape[0] // 4
            return [rows_of_lots[i * size : (i + 1) * size] for i in range(4)]

        def send_rows(parts):
            return plane.across([parts[0], parts[2]], plane.last)

        def own_rows(parts, got):
            return plane.fold([n.astype(F32) + g.astype(F32) for n, g in zip((parts[1], parts[3]), got)])

        attended_grad = dot_nt(branch_grad, full_o).astype(BF16)

        query_grad, kv_terms = attn_backward(queries, kv_window, norms, attended_grad, first, file_ends)
        kv_got = line.scatter(kv_terms.reshape(windows, n_z, local_len, 2 * HD), 1)
        query_sib = dot_tn(one_sib, query_grad).astype(BF16)
        query_sib, hid_late, grad_up, *out_got = tie(query_sib, hid_near[1], grad_up, *out_got)
        theirs = plane.swap(query_sib, 1)
        out_sib = product(hid_late, down_part)
        out_sib, one_late = tie(out_sib, one_mine)
        out_theirs = plane.swap(out_sib, 1)
        wq_parts = product(one_late, query_grad, "tn", 4, [theirs])
        wq_got = send_rows(wq_parts)
        wq_parts[1], hid_late, out_theirs = tie(wq_parts[1], hid_near[0], out_theirs)
        out_sum = merge(product(hid_late, down_part, "nn", 2, [out_theirs]), out_got)
        out_sum[0], out_sum[1], att_sib, query_late, grad_down, grad_up, *kv_got = tie(
            *out_sum, att_sib, query_grad, grad_down, grad_up, *kv_got
        )
        branch_out = plane.fold(out_sum)
        wo_sib, *wq_got = tie(product(att_sib, branch_grad, "tn"), *wq_got)
        wo_theirs = plane.swap(wo_sib, 1)
        wq_rows = own_rows(wq_parts, wq_got).astype(BF16)
        wo_parts = product(att_mine, branch_grad, "tn", 4, [wo_theirs])
        wo_got = send_rows(wo_parts)
        wo_parts[1], query_late = tie(wo_parts[1], query_late)
        query_part = product(query_late, full_q, "nt", kind=F32)
        kv_grad = total(kv_got).astype(BF16).reshape(rows, 2 * HD)
        query_part, kv_grad, wo_parts[1], branch_out, wq_rows = tie(
            query_part, kv_grad, wo_parts[1], branch_out, wq_rows
        )
        grad_wq = lax.psum_scatter(wq_rows, "fsdp", scatter_dimension=0, tiled=True)

        one_grad = query_part + dot_nt(kv_grad, full_kv)
        grad_bq = jnp.sum(query_late.astype(F32), axis=0)
        grad_bv = jnp.sum(kv_grad[:, HD:].astype(F32), axis=0)
        grad_gain_one = jnp.sum(one_grad * xhat_one, axis=0)
        grad_shift_one = jnp.sum(one_grad, axis=0)
        grad_bup = jnp.where(jnp.arange(n_dp)[:, None] == my_dp, up_bias_near + up_bias_far, 0.0).reshape(-1)
        sums = (
            (0, grad_bq),
            (2, grad_bo),
            (5, grad_bup),
            (6, grad_bdown),
            (7, grad_gain_two),
            (8, grad_shift_two),
            (1, grad_bv),
            (3, grad_gain_one),
            (4, grad_shift_one),
        )
        row_of = jnp.concatenate(
            [
                jnp.pad(v.reshape(n_dev, sizes[i]), ((0, 0), (0, rooms[i] - sizes[i])))
                for i, v in sums
            ],
            axis=1,
        )
        order = [i for i, _ in sums]
        sum_starts = {i: sum(rooms[j] for j in order[:at]) for at, i in enumerate(order)}
        per_half = n_z // 2 * row_of.shape[1]
        more = -(-per_half // (16 * 2 * HD)) * 16
        row_of = jnp.pad(row_of.reshape(2 * n_dp, per_half), ((0, 0), (0, more * 2 * HD - per_half)))
        row_of = row_of.astype(BF16).astype(F32)

        def with_vectors(product, core):
            pick = (places[core][:, None] == jnp.arange(2 * n_dp)[None, :]).astype(F32)
            vectors = jnp.dot(pick, row_of, precision=lax.Precision.HIGHEST)
            return jnp.concatenate(
                [product.reshape(n_dp, -1, 2 * HD), vectors.reshape(n_dp, more, 2 * HD)], axis=1
            ).reshape(-1, 2 * HD)

        theirs = plane.swap(with_vectors(dot_tn(one_sib, kv_grad), 1).astype(BF16), 1)
        theirs, *wo_got = tie(theirs, *wo_got)
        wo_rows = own_rows(wo_parts, wo_got).astype(BF16)
        kv_parts = cut((with_vectors(dot_tn(one_mine, kv_grad), 0) + theirs.astype(F32)).astype(BF16))
        kv_parts_got = send_rows(kv_parts)
        kv_parts_got[0], wo_rows = tie(kv_parts_got[0], wo_rows)
        grad_wo = lax.psum_scatter(wo_rows, "fsdp", scatter_dimension=0, tiled=True)

        kv_last = own_rows(kv_parts, kv_parts_got).reshape(2, -1, 2 * HD)
        kv_rows = kv_last.shape[1] - more
        kv_last = jnp.concatenate(
            [
                kv_last[:, :kv_rows].reshape(n_z, -1),
                kv_last[:, kv_rows:].reshape(2, -1)[:, :per_half].reshape(n_z, -1),
            ],
            axis=1,
        )
        kv_last = line.scatter(kv_last, 0)
        output = (middle + branch_out + bias_down).astype(BF16).reshape(windows, local_len, width)
        tokens_grad = middle_grad + norm_pull(one_grad, xhat_one, recip_one, gain_one)
        tokens_grad = tokens_grad.astype(BF16).reshape(windows, local_len, width)
        grad_up = lax.all_to_all(
            grad_up.reshape(n_dp * own, ff_own), "dp", 0, 1, tiled=True
        ).astype(F32)
        kv_own = total(kv_last)
        flat = kv_own[own * 2 * HD :]
        bq, bv, bo, gain1, shift1, bup, bdown, gain2, shift2 = (
            flat[sum_starts[i] : sum_starts[i] + size] for i, size in enumerate(sizes)
        )
        return (
            output,
            tokens_grad,
            grad_wq.astype(F32),
            kv_own[: own * 2 * HD].reshape(own, 2 * HD),
            grad_wo.astype(F32),
            bq,
            bv,
            bo,
            gain1,
            shift1,
            grad_up,
            grad_down.astype(F32),
            bup,
            bdown,
            gain2,
            shift2,
        )

    return local


def solution(mesh):
    whole = P(BOTH, None)
    vector = P(BOTH)
    rows = P("dp", "fsdp", None)
    weights = (whole, whole, whole) + (vector,) * 5 + (whole, whole) + (vector,) * 4
    return jax.shard_map(
        make_local(mesh.shape["dp"], mesh.shape["fsdp"]),
        mesh=mesh,
        in_specs=(rows, rows, P("dp", None)) + weights,
        out_specs=(rows, rows) + weights,
        check_vma=False,
    )
```

```python
import functools
import math

import jax
import jax.numpy as jnp
from jax import lax
from jax.experimental import pallas as pl
from jax.experimental.pallas import tpu as pltpu
from jax.sharding import PartitionSpec as P

HEADS = 16
HD = 128
EPS = 1e-05
F32 = jnp.float32
BF16 = jnp.bfloat16
BOTH = ("dp", "fsdp")
HASTE = 64


def dot_nn(left, right):
    return jnp.dot(left, right, preferred_element_type=F32)


def dot_nt(left, right):
    return lax.dot_general(left, right, (((1,), (1,)), ((), ())), preferred_element_type=F32)


def dot_tn(left, right):
    return lax.dot_general(left, right, (((0,), (0,)), ((), ())), preferred_element_type=F32)


LOG2E = 1.4426950408889634


def file_of(ends_ref, w, pos):
    total = jnp.zeros(pos.shape, jnp.int32)
    for i in range(ends_ref.shape[1]):
        total += (ends_ref[w, i] <= pos).astype(jnp.int32)
    return total


def fill_mask(pos_ref, ends_ref, w, bias, key_turned, value_turned, kv_ref):
    span, win = bias.shape
    query_pos = pos_ref[0] + lax.broadcasted_iota(jnp.int32, (span, 1), 0)
    key_pos = lax.broadcasted_iota(jnp.int32, (1, win), 1)
    same = file_of(ends_ref, w, query_pos) == file_of(ends_ref, w, key_pos)
    bias[...] = jnp.where(same & (key_pos <= query_pos), 0.0, -1e30).astype(F32)
    key_turned[...] = kv_ref[0, :, :HD].astype(F32).T.astype(BF16)
    if value_turned is not None:
        value_turned[...] = kv_ref[0, :, HD:].astype(F32).T.astype(BF16)


def attn_forward_kernel(per_step, pos_ref, ends_ref, q_ref, kv_ref, out_ref, norm_ref, bias, key_turned):
    w, group = pl.program_id(0), pl.program_id(1)

    @pl.when(group == 0)
    def _():
        fill_mask(pos_ref, ends_ref, w, bias, key_turned, None, kv_ref)
        norm_ref[...] = jnp.zeros_like(norm_ref)

    values = kv_ref[0, :, HD:]
    lane = lax.broadcasted_iota(jnp.int32, norm_ref.shape, 1)
    for j in range(per_step):
        query = q_ref[:, j * HD : (j + 1) * HD]
        scores = jnp.dot(query, key_turned[...], preferred_element_type=F32)
        scores = scores * (LOG2E / math.sqrt(HD)) + bias[...]
        top = jnp.max(scores, axis=1, keepdims=True)
        terms = jnp.exp2(scores - top)
        total = jnp.sum(terms, axis=1, keepdims=True)
        mixed = jnp.dot(terms.astype(BF16), values, preferred_element_type=F32)
        out_ref[:, j * HD : (j + 1) * HD] = (mixed / total).astype(BF16)
        norm_ref[...] = jnp.where(lane == group * per_step + j, top + jnp.log2(total), norm_ref[...])


def attn_backward_kernel(
    per_step, pos_ref, ends_ref, q_ref, kv_ref, norm_ref, grad_ref, dq_ref, dkv_ref,
    bias, key_turned, value_turned, key_grad, value_grad,
):
    w, group = pl.program_id(0), pl.program_id(1)

    @pl.when(group == 0)
    def _():
        fill_mask(pos_ref, ends_ref, w, bias, key_turned, value_turned, kv_ref)
        key_grad[...] = jnp.zeros_like(key_grad)
        value_grad[...] = jnp.zeros_like(value_grad)

    keys = kv_ref[0, :, :HD]
    lane = lax.broadcasted_iota(jnp.int32, norm_ref.shape, 1)
    for j in range(per_step):
        query = q_ref[:, j * HD : (j + 1) * HD]
        grad = grad_ref[:, j * HD : (j + 1) * HD]
        scores = jnp.dot(query, key_turned[...], preferred_element_type=F32)
        scores = scores * (LOG2E / math.sqrt(HD)) + bias[...]
        norm = jnp.sum(jnp.where(lane == group * per_step + j, norm_ref[...], 0.0), axis=1, keepdims=True)
        probs = jnp.exp2(scores - norm)
        grad_probs = jnp.dot(grad, value_turned[...], preferred_element_type=F32)
        delta = jnp.sum(probs * grad_probs, axis=1, keepdims=True)
        score_grad = (probs * (grad_probs - delta)).astype(BF16)
        probs = probs.astype(BF16)
        dq = jnp.dot(score_grad, keys, preferred_element_type=F32)
        dq_ref[:, j * HD : (j + 1) * HD] = (dq / math.sqrt(HD)).astype(BF16)
        key_grad[...] += dot_tn(query, score_grad)
        value_grad[...] += dot_tn(grad, probs)

    @pl.when(group == pl.num_programs(1) - 1)
    def _():
        dkv_ref[0, :, :HD] = (key_grad[...].T / math.sqrt(HD)).astype(BF16)
        dkv_ref[0, :, HD:] = value_grad[...].T.astype(BF16)


def attn_specs(per_step, span, win):
    smem = pl.BlockSpec(memory_space=pltpu.SMEM)
    heads = pl.BlockSpec((span, per_step * HD), lambda w, g: (w, g))
    keys = pl.BlockSpec((1, win, 2 * HD), lambda w, g: (w, 0, 0))
    norm = pl.BlockSpec((span, HD), lambda w, g: (w, 0))
    return smem, heads, keys, norm


def attn_cost(windows, span, win, products, haste=HASTE):
    return pl.CostEstimate(
        flops=2 * products * windows * HEADS * span * win * HD // haste,
        transcendentals=windows * HEADS * span * win // haste,
        bytes_accessed=products * windows * HEADS * span * HD * 2 // haste,
    )


def attn_forward(queries, kv_window, first, ends, per_step=4):
    windows, win, _ = kv_window.shape
    rows, width = queries.shape
    span = rows // windows
    smem, heads, keys, norm = attn_specs(per_step, span, win)
    return pl.pallas_call(
        functools.partial(attn_forward_kernel, per_step),
        out_shape=(
            jax.ShapeDtypeStruct((rows, width), BF16),
            jax.ShapeDtypeStruct((rows, HD), F32),
        ),
        grid=(windows, HEADS // per_step),
        in_specs=[smem, smem, heads, keys],
        out_specs=(heads, norm),
        scratch_shapes=[pltpu.VMEM((span, win), F32), pltpu.VMEM((HD, win), BF16)],
        compiler_params=pltpu.CompilerParams(vmem_limit_bytes=40 * 2**20),
        cost_estimate=attn_cost(windows, span, win, 2),
    )(first, ends, queries, kv_window)


def attn_backward(queries, kv_window, norms, grads, first, ends, per_step=4):
    windows, win, _ = kv_window.shape
    rows, width = queries.shape
    span = rows // windows
    smem, heads, keys, norm = attn_specs(per_step, span, win)
    return pl.pallas_call(
        functools.partial(attn_backward_kernel, per_step),
        out_shape=(
            jax.ShapeDtypeStruct((rows, width), BF16),
            jax.ShapeDtypeStruct((windows, win, 2 * HD), BF16),
        ),
        grid=(windows, HEADS // per_step),
        in_specs=[smem, smem, heads, keys, norm, heads],
        out_specs=(heads, keys),
        scratch_shapes=[
            pltpu.VMEM((span, win), F32),
            pltpu.VMEM((HD, win), BF16),
            pltpu.VMEM((HD, win), BF16),
            pltpu.VMEM((HD, win), F32),
            pltpu.VMEM((HD, win), F32),
        ],
        compiler_params=pltpu.CompilerParams(vmem_limit_bytes=48 * 2**20),
        cost_estimate=attn_cost(windows, span, win, 5),
    )(first, ends, queries, kv_window, norms, grads)


def middle_kernel(count, *refs):
    blocks, back_ref = refs[:count], refs[count]
    up_ref, bias_ref = refs[count + 1], refs[count + 2]
    outs, sum_ref = refs[count + 3 : -1], refs[-1]
    groups = len(outs) // 2
    size = blocks[0].shape[0]
    root = math.sqrt(2.0 / math.pi)
    summed = jnp.zeros(sum_ref.shape, F32)
    for i, block in enumerate(blocks):
        act = jnp.dot(block[...], up_ref[...], preferred_element_type=F32) + bias_ref[...]
        square = act * act
        bent = jnp.tanh(act * (root + (root * 0.044715) * square))
        upper = 0.5 + 0.5 * bent
        slope = upper + act * (1.0 - bent * bent) * (0.5 * root + (1.5 * 0.044715 * root) * square)
        back = back_ref[i * size : (i + 1) * size, :].astype(F32)
        group, place = divmod(i, count // groups)
        at = slice(place * size, (place + 1) * size)
        outs[group][at, :] = (act * upper).astype(BF16)
        pre = (back * slope).astype(BF16)
        outs[groups + group][at, :] = pre
        summed += jnp.sum(pre.astype(F32), axis=0, keepdims=True)
    sum_ref[...] = summed


def middle_layer(blocks, back, up_part, bias, tile=512):
    count = len(blocks)
    size, width = blocks[0].shape
    units = up_part.shape[1]
    tile = min(tile, units)
    one = pl.Buffered(buffer_count=1)
    group = size * count // 2
    whole = pl.BlockSpec((size, width), lambda j: (0, 0), pipeline_mode=one)
    slab = pl.BlockSpec((group, tile), lambda j: (0, j))
    out = pl.pallas_call(
        functools.partial(middle_kernel, count),
        out_shape=[jax.ShapeDtypeStruct((group, units), BF16)] * 4 + [jax.ShapeDtypeStruct((1, units), F32)],
        grid=(units // tile,),
        in_specs=[whole] * count
        + [
            pl.BlockSpec((size * count, tile), lambda j: (0, j)),
            pl.BlockSpec((width, tile), lambda j: (0, j)),
            pl.BlockSpec((1, tile), lambda j: (0, j)),
        ],
        out_specs=[slab] * 4 + [pl.BlockSpec((1, tile), lambda j: (0, j))],
        compiler_params=pltpu.CompilerParams(vmem_limit_bytes=48 * 2**20),
        cost_estimate=pl.CostEstimate(
            flops=2 * count * size * width * units // HASTE,
            transcendentals=count * size * units // HASTE,
            bytes_accessed=2 * (count * size * (width + 3 * units) + width * units) // HASTE,
        ),
    )(*blocks, back, up_part, bias.reshape(1, units))
    return list(out[:2]), list(out[2:4]), out[4]


def back_kernel(count, *refs):
    blocks, weight_ref, out = refs[:count], refs[count], refs[count + 1]
    size = blocks[0].shape[0]
    for i, block in enumerate(blocks):
        out[i * size : (i + 1) * size, :] = dot_nt(block[...], weight_ref[...]).astype(BF16)


def back_product(blocks, weight, tile=512):
    count = len(blocks)
    size, width = blocks[0].shape
    units = weight.shape[0]
    tile = min(tile, units)
    one = pl.Buffered(buffer_count=1)
    return pl.pallas_call(
        functools.partial(back_kernel, count),
        out_shape=jax.ShapeDtypeStruct((size * count, units), BF16),
        grid=(units // tile,),
        in_specs=[pl.BlockSpec((size, width), lambda j: (0, 0), pipeline_mode=one)] * count
        + [pl.BlockSpec((tile, width), lambda j: (j, 0))],
        out_specs=pl.BlockSpec((size * count, tile), lambda j: (0, j)),
        compiler_params=pltpu.CompilerParams(vmem_limit_bytes=48 * 2**20),
        cost_estimate=pl.CostEstimate(
            flops=2 * count * size * width * units // HASTE,
            transcendentals=0,
            bytes_accessed=2 * (count * size * (width + units) + width * units) // HASTE,
        ),
    )(*blocks, weight)


def weight_kernel(count, *refs):
    lefts, rights, out = refs[:count], refs[count : 2 * count], refs[2 * count]
    total = dot_tn(lefts[0][...], rights[0][...])
    for left, right in zip(lefts[1:], rights[1:]):
        total += dot_tn(left[...], right[...])
    out[...] = total.astype(BF16)


def in_blocks(arrays, size):
    return [(array, i) for array in arrays for i in range(array.shape[0] // size)]


def weight_grad(lefts, rights, size, tile=256):
    lefts, rights = in_blocks(lefts, size), in_blocks(rights, size)
    count = len(lefts)
    height, breadth = lefts[0][0].shape[1], rights[0][0].shape[1]
    tile = min(tile, height)

    def left_spec(row):
        return pl.BlockSpec((size, tile), lambda i: (row, i))

    def right_spec(row):
        return pl.BlockSpec((size, breadth), lambda i: (row, 0), pipeline_mode=pl.Buffered(buffer_count=1))

    return pl.pallas_call(
        functools.partial(weight_kernel, count),
        out_shape=jax.ShapeDtypeStruct((height, breadth), BF16),
        grid=(height // tile,),
        in_specs=[left_spec(row) for _, row in lefts] + [right_spec(row) for _, row in rights],
        out_specs=pl.BlockSpec((tile, breadth), lambda i: (i, 0)),
        compiler_params=pltpu.CompilerParams(vmem_limit_bytes=52 * 2**20),
        cost_estimate=pl.CostEstimate(
            flops=2 * count * size * height * breadth,
            transcendentals=0,
            bytes_accessed=2 * (count * size * (height + breadth) + height * breadth),
        ),
    )(*[array for array, _ in lefts], *[array for array, _ in rights])


def reorder_kernel(place_ref, first_ref, second_ref, first_out, second_out):
    first_out[...] = first_ref[...]
    second_out[...] = second_ref[...]


def reorder(values, places):
    rows, width = values.shape
    count = places.shape[1]
    block = width // (2 * count)
    if block % 128:
        return [
            jnp.concatenate(
                [lax.dynamic_slice_in_dim(values, places[i, j] * block, block, 1) for j in range(count)],
                axis=1,
            )
            for i in (0, 1)
        ]
    out = pl.BlockSpec((rows, block), lambda i, place: (0, i))
    return pl.pallas_call(
        reorder_kernel,
        out_shape=[jax.ShapeDtypeStruct((rows, width // 2), values.dtype)] * 2,
        grid_spec=pltpu.PrefetchScalarGridSpec(
            num_scalar_prefetch=1,
            grid=(count,),
            in_specs=[
                pl.BlockSpec((rows, block), lambda i, place: (0, place[0, i])),
                pl.BlockSpec((rows, block), lambda i, place: (0, place[1, i])),
            ],
            out_specs=[out, out],
        ),
        cost_estimate=pl.CostEstimate(flops=0, transcendentals=0, bytes_accessed=4 * rows * width // HASTE),
    )(places, values, values)

def product_kernel(form, given, values_ref, weight_ref, *refs):
    extra, outs = refs[:given], refs[given:]
    size = outs[0].shape[0]
    for i, out in enumerate(outs):
        rows = slice(i * size, (i + 1) * size)
        if form == "tn":
            total = dot_tn(values_ref[:, rows], weight_ref[...])
        else:
            total = (dot_nt if form == "nt" else dot_nn)(values_ref[rows, :], weight_ref[...])
        if given:
            each = extra[0].shape[0]
            at = i * size % each
            total += extra[i * size // each][at : at + size, :].astype(F32)
        out[...] = total.astype(out.dtype)


def product(values, weight, form="nn", parts=1, extra=(), kind=BF16, tile=512):
    height = values.shape[1] if form == "tn" else values.shape[0]
    depth = values.shape[0] if form == "tn" else values.shape[1]
    breadth = weight.shape[0] if form == "nt" else weight.shape[1]
    tile = min(tile, breadth)
    size = height // parts
    if form == "nt":
        part = pl.BlockSpec((tile, depth), lambda j: (j, 0))
    else:
        part = pl.BlockSpec((depth, tile), lambda j: (0, j))
    out = pl.pallas_call(
        functools.partial(product_kernel, form, len(extra)),
        out_shape=[jax.ShapeDtypeStruct((size, breadth), kind)] * parts,
        grid=(breadth // tile,),
        in_specs=[pl.BlockSpec(values.shape, lambda j: (0, 0), pipeline_mode=pl.Buffered(buffer_count=1)), part]
        + [pl.BlockSpec((block.shape[0], tile), lambda j: (0, j)) for block in extra],
        out_specs=[pl.BlockSpec((size, tile), lambda j: (0, j))] * parts,
        compiler_params=pltpu.CompilerParams(vmem_limit_bytes=48 * 2**20),
        cost_estimate=pl.CostEstimate(
            flops=2 * height * depth * breadth // HASTE,
            transcendentals=0,
            bytes_accessed=2 * (height * (depth + breadth) + depth * breadth) // HASTE,
        ),
    )(values, weight, *extra)
    return list(out) if parts > 1 else out[0]


def norm_stats(values):
    average = jnp.mean(values, axis=-1, keepdims=True)
    centered = values - average
    variance = jnp.mean(centered * centered, axis=-1, keepdims=True)
    return average, lax.rsqrt(variance + EPS)


def norm_pull(grad, xhat, recip, gain):
    scaled = grad * gain
    mean_one = jnp.mean(scaled, axis=-1, keepdims=True)
    mean_two = jnp.mean(scaled * xhat, axis=-1, keepdims=True)
    return recip * (scaled - mean_one - xhat * mean_two)


def tie(*arrays):
    return lax.optimization_barrier(arrays)


class Line:
    def __init__(self, count):
        self.count = count

    def send(self, block, places):
        return lax.ppermute(block, "fsdp", [(i, (i + places) % self.count) for i in range(self.count)])

    def gather(self, block):
        return [block] + [self.send(block, step) for step in range(1, self.count)]

    def in_order(self, pieces, axis=0):
        me = lax.axis_index("fsdp")
        size = pieces[0].shape[axis]
        shape = list(pieces[0].shape)
        shape[axis] = size * self.count
        whole = jnp.zeros(shape, pieces[0].dtype)
        for step, piece in enumerate(pieces):
            place = lax.rem(me - step + self.count, self.count) * size
            whole = lax.dynamic_update_slice_in_dim(whole, piece, place, axis)
        return whole

    def scatter(self, terms, axis):
        me = lax.axis_index("fsdp")

        def term(step):
            place = lax.rem(me + step, self.count)
            return lax.dynamic_index_in_dim(terms, place, axis, keepdims=False)

        return [term(0)] + [self.send(term(step).astype(BF16), step) for step in range(1, self.count)]


def total(terms):
    out = terms[0].astype(F32)
    for term in terms[1:]:
        out += term.astype(F32)
    return out


class Plane:
    def __init__(self, count):
        self.count = count
        bits = [1 << i for i in range(1, count.bit_length() - 1)]
        self.orders = (bits, bits[::-1])
        self.last = len(bits) - 1
        self.near, self.far = [], []
        for order in self.orders:
            near = [0]
            for bit in order[:-1]:
                near = near + [offset ^ bit for offset in near]
            self.near.append(near)
            self.far.append([offset ^ order[-1] for offset in near])

    def places(self):
        me = lax.axis_index("dp")
        order = [(o, h) for h in (0, 1) for o in self.far[h] + self.near[h]]
        return jnp.stack(
            [jnp.stack([2 * (me ^ o ^ core) + h for o, h in order]) for core in (0, 1)]
        ).astype(jnp.int32)

    def swap(self, block, bit):
        return lax.ppermute(block, "dp", [(i, i ^ bit) for i in range(self.count)])

    def cross(self, blocks):
        return [self.swap(block, 1) for block in blocks]

    def across(self, halves, step):
        return [self.swap(half, order[step]) for half, order in zip(halves, self.orders)]

    def grow(self, halves):
        for step in range(self.last):
            halves = [jnp.concatenate(pair) for pair in zip(halves, self.across(halves, step))]
        return halves

    def fold(self, halves):
        for step in range(self.last - 1, -1, -1):
            size = halves[0].shape[0] // 2
            got = self.across([half[size:].astype(BF16) for half in halves], step)
            halves = [half[:size].astype(F32) + there.astype(F32) for half, there in zip(halves, got)]
        return jnp.concatenate(halves)


def make_local(n_dp, n_z):
    n_dev = n_dp * n_z
    plane = Plane(n_dp)
    line = Line(n_z)

    def local(
        tokens,
        cotangent,
        lengths,
        query_weight,
        kv_weight,
        out_weight,
        query_bias,
        value_bias,
        out_bias,
        attn_gain,
        attn_shift,
        up_weight,
        down_weight,
        up_bias,
        down_bias,
        mlp_gain,
        mlp_shift,
    ):
        windows, local_len, width = tokens.shape
        rows = windows * local_len
        half = rows // 2
        own = query_weight.shape[0]
        ff_own = up_weight.shape[1] // n_dp
        my_dp = lax.axis_index("dp")

        small = (
            query_bias,
            value_bias,
            out_bias,
            attn_gain,
            attn_shift,
            up_bias,
            down_bias,
            mlp_gain,
            mlp_shift,
        )
        sizes = [v.shape[0] for v in small]
        rooms = [-(-size // 128) * 128 for size in sizes]
        starts = [sum(rooms[:i]) for i in range(len(rooms))]
        small_row = jnp.concatenate(
            [jnp.pad(v, (0, room - size)) for v, size, room in zip(small, sizes, rooms)]
        )
        kv_lines = kv_weight.size // width
        filled = own + kv_lines + -(-small_row.shape[0] // width)
        lines = -(-filled // 16) * 16
        small_row = jnp.pad(small_row, (0, (lines - own - kv_lines) * width - small_row.shape[0]))
        packed = jnp.concatenate(
            [query_weight, kv_weight.reshape(kv_lines, width), small_row.reshape(-1, width)]
        )
        places = plane.places()

        grad_low = cotangent.reshape(rows, width)
        packed = lax.all_gather(packed, "fsdp", axis=0, tiled=True)
        grad_near = plane.grow([grad_low[:half], grad_low[half:]])
        up_cols = lax.all_to_all(up_weight, "dp", 1, 0, tiled=True).reshape(n_dp, own, ff_own)
        packed, up_cols, out_weight, *grad_near = tie(packed, up_cols, out_weight, *grad_near)

        packed = lax.all_gather(packed, "dp", axis=0, tiled=True)
        out_pieces = line.gather(out_weight)
        *out_pieces, down_late = tie(*out_pieces, down_weight)
        full_o = line.in_order(out_pieces)
        down_pieces = [down_late, line.send(down_late, 1)]
        inputs = tokens.reshape(rows, width).astype(F32)
        mean_one, recip_one = norm_stats(inputs)
        grad_near_sib = plane.cross(grad_near)
        packed, full_o, mean_one, down_pieces[-1], *arrived = tie(
            packed, full_o, mean_one, down_pieces[-1], *grad_near, *grad_near_sib
        )
        grad_near, grad_near_sib = arrived[:2], arrived[2:]

        full_o = lax.all_gather(full_o, "dp", axis=0, tiled=True)
        packed = packed.reshape(n_dev, lines, width)
        full_q = packed[:, :own].reshape(width, width)
        full_kv = packed[:, own : own + kv_lines].reshape(width, 2 * HD)
        small_all = packed[:, own + kv_lines :].reshape(n_dev, -1)
        bias_q, bias_v, bias_o, gain_one, shift_one, bias_up, bias_down, gain_two, shift_two = (
            small_all[:, start : start + size].reshape(-1).astype(F32)
            for start, size in zip(starts, sizes)
        )
        xhat_one = (inputs - mean_one) * recip_one
        normed_one = (xhat_one * gain_one + shift_one).astype(BF16)
        kv_bias = jnp.concatenate([jnp.zeros((HD,), F32), bias_v])
        key_value = (dot_nn(normed_one, full_kv) + kv_bias).astype(BF16)
        if n_z > 2:
            down_pieces.append(line.send(down_pieces[-1], 1))
        key_value, normed_late, up_cols, down_pieces[-1] = tie(
            key_value, normed_one, up_cols, down_pieces[-1]
        )
        kv_pieces = line.gather(key_value.reshape(windows, local_len, 2 * HD))
        queries = (dot_nn(normed_late, full_q) + bias_q).astype(BF16)
        queries, down_late, *kv_pieces = tie(queries, down_pieces[-1], *kv_pieces)
        kv_window = line.in_order(kv_pieces, 1)

        first = (lax.axis_index("fsdp") * local_len).astype(jnp.int32).reshape(1)
        file_count = lengths.shape[1]
        upto = jnp.arange(file_count)[:, None] <= jnp.arange(file_count)[None, :]
        file_ends = jnp.sum(jnp.where(upto[None], lengths[:, :, None], 0), axis=1)
        grad_far = plane.across(grad_near, plane.last)
        while len(down_pieces) < n_z:
            down_late = line.send(down_late, 1)
            down_pieces.append(down_late)
        up_part = lax.all_gather(up_cols, "fsdp", axis=1, tiled=True).reshape(width, ff_own)
        attended, norms = attn_forward(queries, kv_window, first, file_ends)
        attended, down_pieces[-1] = tie(attended, down_pieces[-1])
        middle = inputs + dot_nn(attended, full_o) + bias_o
        mean_two, recip_two = norm_stats(middle)
        xhat_two = (middle - mean_two) * recip_two
        normed_two = (xhat_two * gain_two + shift_two).astype(BF16)

        normed_two, normed_late, *arrived = tie(normed_two, normed_late, *grad_far, *down_pieces)
        grad_far, down_pieces = arrived[:2], arrived[2:]
        two_near = plane.grow([normed_two[:half], normed_two[half:]])
        down_part = line.in_order(down_pieces)
        grad_lots = [[*grad_near, *grad_near_sib], [*grad_far, *plane.cross(grad_far)]]
        back_near = back_product(grad_lots[0], down_part)
        two_near[0], two_near[1], back_near = tie(*two_near, back_near)
        two_far = plane.across(two_near, plane.last)
        two_lots = [[*two_near, *plane.cross(two_near)]]
        back_near, down_late, attended_late, normed_late = tie(
            back_near, down_part, attended, normed_late
        )
        back_far = back_product(grad_lots[1], down_late)
        bias_up_part = lax.dynamic_slice_in_dim(bias_up, my_dp * ff_own, ff_own)
        hid_near, pre_near, up_bias_near = middle_layer(two_lots[0], back_near, up_part, bias_up_part)
        back_far, attended_late, normed_late, pre_near[0], pre_near[1], *two_far = tie(
            back_far, attended_late, normed_late, *pre_near, *two_far
        )
        two_lots.append([*two_far, *plane.cross(two_far)])
        att_mine, att_sib = reorder(attended_late, places)
        one_mine, one_sib = reorder(normed_late, places)
        back_far, att_mine, att_sib, one_mine, one_sib = tie(back_far, att_mine, att_sib, one_mine, one_sib)
        hid_far, pre_far, up_bias_far = middle_layer(two_lots[1], back_far, up_part, bias_up_part)
        block = two_near[0].shape[0]
        lots = (slice(None, block), slice(block, None))

        def halves(lot, weight, times):
            theirs = plane.cross([times(lot[1][at], weight).astype(BF16) for at in lots])
            return [
                (times(lot[0][at], weight) + there.astype(F32)).astype(BF16)
                for at, there in zip(lots, theirs)
            ]

        def merge(near, got):
            return [whole.astype(F32) + there.astype(F32) for whole, there in zip(near, got)]

        two_far_sum = halves(pre_far, up_part, dot_nt)
        pre_near[0], pre_near[1], *two_far_sum = tie(*pre_near, *two_far_sum)
        got = plane.across(two_far_sum, plane.last)
        theirs = plane.swap(product(pre_near[1], up_part, "nt"), 1)
        pre_far[0], theirs = tie(pre_far[0], theirs)
        up_terms = weight_grad(two_lots[0] + two_lots[1], pre_near + pre_far, block)
        pre_near[0], up_terms = tie(pre_near[0], up_terms)
        two_near_sum = product(pre_near[0], up_part, "nt", 2, [theirs])
        two_near_sum[0], *got = tie(two_near_sum[0], *got)
        two_sum = merge(two_near_sum, got)
        hid_far[0], hid_far[1], up_terms, *two_sum = tie(*hid_far, up_terms, *two_sum)
        grad_up = lax.psum_scatter(
            up_terms.reshape(n_dp, n_z * own, ff_own), "fsdp", scatter_dimension=1, tiled=True
        )
        two_grad = plane.fold(two_sum)
        down_terms = weight_grad(hid_near + hid_far, grad_lots[0] + grad_lots[1], block)
        two_grad, down_terms, hid_far[0] = tie(two_grad, down_terms, hid_far[0])
        out_far = halves(hid_far, down_part, dot_nn)
        two_grad, *out_far = tie(two_grad, *out_far)

        out_got = plane.across(out_far, plane.last)
        grad_out = grad_low.astype(F32)
        grad_bdown = jnp.sum(grad_out, axis=0)
        grad_gain_two = jnp.sum(two_grad * xhat_two, axis=0)
        grad_shift_two = jnp.sum(two_grad, axis=0)
        middle_grad = grad_out + norm_pull(two_grad, xhat_two, recip_two, gain_two)
        grad_bo = jnp.sum(middle_grad, axis=0)
        branch_grad = middle_grad.astype(BF16)

        def cut(rows_of_lots):
            size = rows_of_lots.shape[0] // 4
            return [rows_of_lots[i * size : (i + 1) * size] for i in range(4)]

        def send_rows(parts):
            return plane.across([parts[0], parts[2]], plane.last)

        def own_rows(parts, got):
            return plane.fold([n.astype(F32) + g.astype(F32) for n, g in zip((parts[1], parts[3]), got)])

        attended_grad = dot_nt(branch_grad, full_o).astype(BF16)

        query_grad, kv_terms = attn_backward(queries, kv_window, norms, attended_grad, first, file_ends)
        kv_got = line.scatter(kv_terms.reshape(windows, n_z, local_len, 2 * HD), 1)
        query_sib = dot_tn(one_sib, query_grad).astype(BF16)
        query_sib, hid_late, grad_up, *out_got = tie(query_sib, hid_near[1], grad_up, *out_got)
        theirs = plane.swap(query_sib, 1)
        out_sib = product(hid_late, down_part)
        out_sib, one_late = tie(out_sib, one_mine)
        out_theirs = plane.swap(out_sib, 1)
        wq_parts = product(one_late, query_grad, "tn", 4, [theirs])
        wq_got = send_rows(wq_parts)
        wq_parts[1], hid_late, out_theirs = tie(wq_parts[1], hid_near[0], out_theirs)
        out_sum = merge(product(hid_late, down_part, "nn", 2, [out_theirs]), out_got)
        out_sum[0], out_sum[1], att_sib, query_late, grad_up, down_terms, *kv_got = tie(
            *out_sum, att_sib, query_grad, grad_up, down_terms, *kv_got
        )
        grad_down = lax.psum_scatter(down_terms, "fsdp", scatter_dimension=0, tiled=True)
        branch_out = plane.fold(out_sum)
        wo_sib = product(att_sib, branch_grad, "tn")
        wo_sib, query_late, *wq_got = tie(wo_sib, query_late, *wq_got)
        wo_theirs = plane.swap(wo_sib, 1)
        query_part = product(query_late, full_q, "nt", kind=F32)
        wq_rows = own_rows(wq_parts, wq_got).astype(BF16)
        query_part, wo_theirs = tie(query_part, wo_theirs)
        wo_parts = product(att_mine, branch_grad, "tn", 4, [wo_theirs])
        wo_got = send_rows(wo_parts)
        kv_grad = total(kv_got).astype(BF16).reshape(rows, 2 * HD)
        query_part, kv_grad, wo_parts[1], branch_out, wq_rows = tie(
            query_part, kv_grad, wo_parts[1], branch_out, wq_rows
        )
        grad_wq = lax.psum_scatter(wq_rows, "fsdp", scatter_dimension=0, tiled=True)

        one_grad = query_part + dot_nt(kv_grad, full_kv)
        grad_bq = jnp.sum(query_late.astype(F32), axis=0)
        grad_bv = jnp.sum(kv_grad[:, HD:].astype(F32), axis=0)
        grad_gain_one = jnp.sum(one_grad * xhat_one, axis=0)
        grad_shift_one = jnp.sum(one_grad, axis=0)
        grad_bup = jnp.where(jnp.arange(n_dp)[:, None] == my_dp, up_bias_near + up_bias_far, 0.0).reshape(-1)
        sums = (
            (0, grad_bq),
            (2, grad_bo),
            (5, grad_bup),
            (6, grad_bdown),
            (7, grad_gain_two),
            (8, grad_shift_two),
            (1, grad_bv),
            (3, grad_gain_one),
            (4, grad_shift_one),
        )
        row_of = jnp.concatenate(
            [
                jnp.pad(v.reshape(n_dev, sizes[i]), ((0, 0), (0, rooms[i] - sizes[i])))
                for i, v in sums
            ],
            axis=1,
        )
        order = [i for i, _ in sums]
        sum_starts = {i: sum(rooms[j] for j in order[:at]) for at, i in enumerate(order)}
        per_half = n_z // 2 * row_of.shape[1]
        more = -(-per_half // (16 * 2 * HD)) * 16
        row_of = jnp.pad(row_of.reshape(2 * n_dp, per_half), ((0, 0), (0, more * 2 * HD - per_half)))
        row_of = row_of.astype(BF16).astype(F32)

        def with_vectors(product, core):
            pick = (places[core][:, None] == jnp.arange(2 * n_dp)[None, :]).astype(F32)
            vectors = jnp.dot(pick, row_of, precision=lax.Precision.HIGHEST)
            return jnp.concatenate(
                [product.reshape(n_dp, -1, 2 * HD), vectors.reshape(n_dp, more, 2 * HD)], axis=1
            ).reshape(-1, 2 * HD)

        theirs = plane.swap(with_vectors(dot_tn(one_sib, kv_grad), 1).astype(BF16), 1)
        theirs, *wo_got = tie(theirs, *wo_got)
        wo_rows = own_rows(wo_parts, wo_got).astype(BF16)
        kv_parts = cut((with_vectors(dot_tn(one_mine, kv_grad), 0) + theirs.astype(F32)).astype(BF16))
        kv_parts_got = send_rows(kv_parts)
        kv_parts_got[0], wo_rows, grad_down = tie(kv_parts_got[0], wo_rows, grad_down)
        grad_wo = lax.psum_scatter(wo_rows, "fsdp", scatter_dimension=0, tiled=True)

        kv_last = own_rows(kv_parts, kv_parts_got).reshape(2, -1, 2 * HD)
        kv_rows = kv_last.shape[1] - more
        kv_last = jnp.concatenate(
            [
                kv_last[:, :kv_rows].reshape(n_z, -1),
                kv_last[:, kv_rows:].reshape(2, -1)[:, :per_half].reshape(n_z, -1),
            ],
            axis=1,
        )
        kv_last = line.scatter(kv_last, 0)
        output = (middle + branch_out + bias_down).astype(BF16).reshape(windows, local_len, width)
        tokens_grad = middle_grad + norm_pull(one_grad, xhat_one, recip_one, gain_one)
        tokens_grad = tokens_grad.astype(BF16).reshape(windows, local_len, width)
        grad_up = lax.all_to_all(
            grad_up.reshape(n_dp * own, ff_own), "dp", 0, 1, tiled=True
        ).astype(F32)
        kv_own = total(kv_last)
        flat = kv_own[own * 2 * HD :]
        bq, bv, bo, gain1, shift1, bup, bdown, gain2, shift2 = (
            flat[sum_starts[i] : sum_starts[i] + size] for i, size in enumerate(sizes)
        )
        return (
            output,
            tokens_grad,
            grad_wq.astype(F32),
            kv_own[: own * 2 * HD].reshape(own, 2 * HD),
            grad_wo.astype(F32),
            bq,
            bv,
            bo,
            gain1,
            shift1,
            grad_up,
            grad_down.astype(F32),
            bup,
            bdown,
            gain2,
            shift2,
        )

    return local


def solution(mesh):
    whole = P(BOTH, None)
    vector = P(BOTH)
    rows = P("dp", "fsdp", None)
    weights = (whole, whole, whole) + (vector,) * 5 + (whole, whole) + (vector,) * 4
    return jax.shard_map(
        make_local(mesh.shape["dp"], mesh.shape["fsdp"]),
        mesh=mesh,
        in_specs=(rows, rows, P("dp", None)) + weights,
        out_specs=(rows, rows) + weights,
        check_vma=False,
    )
```

```python
import functools
import math

import jax
import jax.numpy as jnp
from jax import lax
from jax.experimental import pallas as pl
from jax.experimental.pallas import tpu as pltpu
from jax.sharding import PartitionSpec as P

HEADS = 16
HD = 128
EPS = 1e-05
F32 = jnp.float32
BF16 = jnp.bfloat16
BOTH = ("dp", "fsdp")
HASTE = 64


def dot_nn(left, right):
    return jnp.dot(left, right, preferred_element_type=F32)


def dot_nt(left, right):
    return lax.dot_general(left, right, (((1,), (1,)), ((), ())), preferred_element_type=F32)


def dot_tn(left, right):
    return lax.dot_general(left, right, (((0,), (0,)), ((), ())), preferred_element_type=F32)


LOG2E = 1.4426950408889634


def file_of(ends_ref, w, pos):
    total = jnp.zeros(pos.shape, jnp.int32)
    for i in range(ends_ref.shape[1]):
        total += (ends_ref[w, i] <= pos).astype(jnp.int32)
    return total


def fill_mask(pos_ref, ends_ref, w, bias, key_turned, value_turned, kv_ref):
    span, win = bias.shape
    query_pos = pos_ref[0] + lax.broadcasted_iota(jnp.int32, (span, 1), 0)
    key_pos = lax.broadcasted_iota(jnp.int32, (1, win), 1)
    same = file_of(ends_ref, w, query_pos) == file_of(ends_ref, w, key_pos)
    bias[...] = jnp.where(same & (key_pos <= query_pos), 0.0, -1e30).astype(F32)
    key_turned[...] = kv_ref[0, :, :HD].astype(F32).T.astype(BF16)
    if value_turned is not None:
        value_turned[...] = kv_ref[0, :, HD:].astype(F32).T.astype(BF16)


def attn_forward_kernel(per_step, pos_ref, ends_ref, q_ref, kv_ref, out_ref, norm_ref, bias, key_turned):
    w, group = pl.program_id(0), pl.program_id(1)

    @pl.when(group == 0)
    def _():
        fill_mask(pos_ref, ends_ref, w, bias, key_turned, None, kv_ref)
        norm_ref[...] = jnp.zeros_like(norm_ref)

    values = kv_ref[0, :, HD:]
    lane = lax.broadcasted_iota(jnp.int32, norm_ref.shape, 1)
    for j in range(per_step):
        query = q_ref[:, j * HD : (j + 1) * HD]
        scores = jnp.dot(query, key_turned[...], preferred_element_type=F32)
        scores = scores * (LOG2E / math.sqrt(HD)) + bias[...]
        top = jnp.max(scores, axis=1, keepdims=True)
        terms = jnp.exp2(scores - top)
        total = jnp.sum(terms, axis=1, keepdims=True)
        mixed = jnp.dot(terms.astype(BF16), values, preferred_element_type=F32)
        out_ref[:, j * HD : (j + 1) * HD] = (mixed / total).astype(BF16)
        norm_ref[...] = jnp.where(lane == group * per_step + j, top + jnp.log2(total), norm_ref[...])


def attn_backward_kernel(
    per_step, pos_ref, ends_ref, q_ref, kv_ref, norm_ref, grad_ref, dq_ref, dkv_ref,
    bias, key_turned, value_turned, key_grad, value_grad,
):
    w, group = pl.program_id(0), pl.program_id(1)

    @pl.when(group == 0)
    def _():
        fill_mask(pos_ref, ends_ref, w, bias, key_turned, value_turned, kv_ref)
        key_grad[...] = jnp.zeros_like(key_grad)
        value_grad[...] = jnp.zeros_like(value_grad)

    keys = kv_ref[0, :, :HD]
    lane = lax.broadcasted_iota(jnp.int32, norm_ref.shape, 1)
    for j in range(per_step):
        query = q_ref[:, j * HD : (j + 1) * HD]
        grad = grad_ref[:, j * HD : (j + 1) * HD]
        scores = jnp.dot(query, key_turned[...], preferred_element_type=F32)
        scores = scores * (LOG2E / math.sqrt(HD)) + bias[...]
        norm = jnp.sum(jnp.where(lane == group * per_step + j, norm_ref[...], 0.0), axis=1, keepdims=True)
        probs = jnp.exp2(scores - norm)
        grad_probs = jnp.dot(grad, value_turned[...], preferred_element_type=F32)
        delta = jnp.sum(probs * grad_probs, axis=1, keepdims=True)
        score_grad = (probs * (grad_probs - delta)).astype(BF16)
        probs = probs.astype(BF16)
        dq = jnp.dot(score_grad, keys, preferred_element_type=F32)
        dq_ref[:, j * HD : (j + 1) * HD] = (dq / math.sqrt(HD)).astype(BF16)
        key_grad[...] += dot_tn(query, score_grad)
        value_grad[...] += dot_tn(grad, probs)

    @pl.when(group == pl.num_programs(1) - 1)
    def _():
        dkv_ref[0, :, :HD] = (key_grad[...].T / math.sqrt(HD)).astype(BF16)
        dkv_ref[0, :, HD:] = value_grad[...].T.astype(BF16)


def attn_specs(per_step, span, win):
    smem = pl.BlockSpec(memory_space=pltpu.SMEM)
    heads = pl.BlockSpec((span, per_step * HD), lambda w, g: (w, g))
    keys = pl.BlockSpec((1, win, 2 * HD), lambda w, g: (w, 0, 0))
    norm = pl.BlockSpec((span, HD), lambda w, g: (w, 0))
    return smem, heads, keys, norm


def attn_cost(windows, span, win, products, haste=HASTE):
    return pl.CostEstimate(
        flops=2 * products * windows * HEADS * span * win * HD // haste,
        transcendentals=windows * HEADS * span * win // haste,
        bytes_accessed=products * windows * HEADS * span * HD * 2 // haste,
    )


def attn_forward(queries, kv_window, first, ends, per_step=4):
    windows, win, _ = kv_window.shape
    rows, width = queries.shape
    span = rows // windows
    smem, heads, keys, norm = attn_specs(per_step, span, win)
    return pl.pallas_call(
        functools.partial(attn_forward_kernel, per_step),
        out_shape=(
            jax.ShapeDtypeStruct((rows, width), BF16),
            jax.ShapeDtypeStruct((rows, HD), F32),
        ),
        grid=(windows, HEADS // per_step),
        in_specs=[smem, smem, heads, keys],
        out_specs=(heads, norm),
        scratch_shapes=[pltpu.VMEM((span, win), F32), pltpu.VMEM((HD, win), BF16)],
        compiler_params=pltpu.CompilerParams(vmem_limit_bytes=40 * 2**20),
        cost_estimate=attn_cost(windows, span, win, 2),
    )(first, ends, queries, kv_window)


def attn_backward(queries, kv_window, norms, grads, first, ends, per_step=4):
    windows, win, _ = kv_window.shape
    rows, width = queries.shape
    span = rows // windows
    smem, heads, keys, norm = attn_specs(per_step, span, win)
    return pl.pallas_call(
        functools.partial(attn_backward_kernel, per_step),
        out_shape=(
            jax.ShapeDtypeStruct((rows, width), BF16),
            jax.ShapeDtypeStruct((windows, win, 2 * HD), BF16),
        ),
        grid=(windows, HEADS // per_step),
        in_specs=[smem, smem, heads, keys, norm, heads],
        out_specs=(heads, keys),
        scratch_shapes=[
            pltpu.VMEM((span, win), F32),
            pltpu.VMEM((HD, win), BF16),
            pltpu.VMEM((HD, win), BF16),
            pltpu.VMEM((HD, win), F32),
            pltpu.VMEM((HD, win), F32),
        ],
        compiler_params=pltpu.CompilerParams(vmem_limit_bytes=48 * 2**20),
        cost_estimate=attn_cost(windows, span, win, 5),
    )(first, ends, queries, kv_window, norms, grads)


def middle_kernel(count, *refs):
    blocks, back_ref = refs[:count], refs[count]
    up_ref, bias_ref = refs[count + 1], refs[count + 2]
    outs, sum_ref = refs[count + 3 : -1], refs[-1]
    groups = len(outs) // 2
    size = blocks[0].shape[0]
    root = math.sqrt(2.0 / math.pi)
    summed = jnp.zeros(sum_ref.shape, F32)
    for i, block in enumerate(blocks):
        act = jnp.dot(block[...], up_ref[...], preferred_element_type=F32) + bias_ref[...]
        square = act * act
        bent = jnp.tanh(act * (root + (root * 0.044715) * square))
        upper = 0.5 + 0.5 * bent
        slope = upper + act * (1.0 - bent * bent) * (0.5 * root + (1.5 * 0.044715 * root) * square)
        back = back_ref[i * size : (i + 1) * size, :].astype(F32)
        group, place = divmod(i, count // groups)
        at = slice(place * size, (place + 1) * size)
        outs[group][at, :] = (act * upper).astype(BF16)
        pre = (back * slope).astype(BF16)
        outs[groups + group][at, :] = pre
        summed += jnp.sum(pre.astype(F32), axis=0, keepdims=True)
    sum_ref[...] = summed


def middle_layer(blocks, back, up_part, bias, tile=512):
    count = len(blocks)
    size, width = blocks[0].shape
    units = up_part.shape[1]
    tile = min(tile, units)
    one = pl.Buffered(buffer_count=1)
    group = size * count // 2
    whole = pl.BlockSpec((size, width), lambda j: (0, 0), pipeline_mode=one)
    slab = pl.BlockSpec((group, tile), lambda j: (0, j))
    out = pl.pallas_call(
        functools.partial(middle_kernel, count),
        out_shape=[jax.ShapeDtypeStruct((group, units), BF16)] * 4 + [jax.ShapeDtypeStruct((1, units), F32)],
        grid=(units // tile,),
        in_specs=[whole] * count
        + [
            pl.BlockSpec((size * count, tile), lambda j: (0, j)),
            pl.BlockSpec((width, tile), lambda j: (0, j)),
            pl.BlockSpec((1, tile), lambda j: (0, j)),
        ],
        out_specs=[slab] * 4 + [pl.BlockSpec((1, tile), lambda j: (0, j))],
        compiler_params=pltpu.CompilerParams(vmem_limit_bytes=48 * 2**20),
        cost_estimate=pl.CostEstimate(
            flops=2 * count * size * width * units // HASTE,
            transcendentals=count * size * units // HASTE,
            bytes_accessed=2 * (count * size * (width + 3 * units) + width * units) // HASTE,
        ),
    )(*blocks, back, up_part, bias.reshape(1, units))
    return list(out[:2]), list(out[2:4]), out[4]


def back_kernel(count, *refs):
    blocks, weight_ref, out = refs[:count], refs[count], refs[count + 1]
    size = blocks[0].shape[0]
    for i, block in enumerate(blocks):
        out[i * size : (i + 1) * size, :] = dot_nt(block[...], weight_ref[...]).astype(BF16)


def back_product(blocks, weight, tile=512):
    count = len(blocks)
    size, width = blocks[0].shape
    units = weight.shape[0]
    tile = min(tile, units)
    one = pl.Buffered(buffer_count=1)
    return pl.pallas_call(
        functools.partial(back_kernel, count),
        out_shape=jax.ShapeDtypeStruct((size * count, units), BF16),
        grid=(units // tile,),
        in_specs=[pl.BlockSpec((size, width), lambda j: (0, 0), pipeline_mode=one)] * count
        + [pl.BlockSpec((tile, width), lambda j: (j, 0))],
        out_specs=pl.BlockSpec((size * count, tile), lambda j: (0, j)),
        compiler_params=pltpu.CompilerParams(vmem_limit_bytes=48 * 2**20),
        cost_estimate=pl.CostEstimate(
            flops=2 * count * size * width * units // HASTE,
            transcendentals=0,
            bytes_accessed=2 * (count * size * (width + units) + width * units) // HASTE,
        ),
    )(*blocks, weight)


def weight_kernel(count, *refs):
    lefts, rights, out = refs[:count], refs[count : 2 * count], refs[2 * count]
    total = dot_tn(lefts[0][...], rights[0][...])
    for left, right in zip(lefts[1:], rights[1:]):
        total += dot_tn(left[...], right[...])
    out[...] = total.astype(BF16)


def in_blocks(arrays, size):
    return [(array, i) for array in arrays for i in range(array.shape[0] // size)]


def weight_grad(lefts, rights, size, tile=256):
    lefts, rights = in_blocks(lefts, size), in_blocks(rights, size)
    count = len(lefts)
    height, breadth = lefts[0][0].shape[1], rights[0][0].shape[1]
    tile = min(tile, height)

    def left_spec(row):
        return pl.BlockSpec((size, tile), lambda i: (row, i))

    def right_spec(row):
        return pl.BlockSpec((size, breadth), lambda i: (row, 0), pipeline_mode=pl.Buffered(buffer_count=1))

    return pl.pallas_call(
        functools.partial(weight_kernel, count),
        out_shape=jax.ShapeDtypeStruct((height, breadth), BF16),
        grid=(height // tile,),
        in_specs=[left_spec(row) for _, row in lefts] + [right_spec(row) for _, row in rights],
        out_specs=pl.BlockSpec((tile, breadth), lambda i: (i, 0)),
        compiler_params=pltpu.CompilerParams(vmem_limit_bytes=52 * 2**20),
        cost_estimate=pl.CostEstimate(
            flops=2 * count * size * height * breadth,
            transcendentals=0,
            bytes_accessed=2 * (count * size * (height + breadth) + height * breadth),
        ),
    )(*[array for array, _ in lefts], *[array for array, _ in rights])


def reorder_kernel(place_ref, first_ref, second_ref, first_out, second_out):
    first_out[...] = first_ref[...]
    second_out[...] = second_ref[...]


def reorder(values, places):
    rows, width = values.shape
    count = places.shape[1]
    block = width // (2 * count)
    if block % 128:
        return [
            jnp.concatenate(
                [lax.dynamic_slice_in_dim(values, places[i, j] * block, block, 1) for j in range(count)],
                axis=1,
            )
            for i in (0, 1)
        ]
    out = pl.BlockSpec((rows, block), lambda i, place: (0, i))
    return pl.pallas_call(
        reorder_kernel,
        out_shape=[jax.ShapeDtypeStruct((rows, width // 2), values.dtype)] * 2,
        grid_spec=pltpu.PrefetchScalarGridSpec(
            num_scalar_prefetch=1,
            grid=(count,),
            in_specs=[
                pl.BlockSpec((rows, block), lambda i, place: (0, place[0, i])),
                pl.BlockSpec((rows, block), lambda i, place: (0, place[1, i])),
            ],
            out_specs=[out, out],
        ),
        cost_estimate=pl.CostEstimate(flops=0, transcendentals=0, bytes_accessed=4 * rows * width // HASTE),
    )(places, values, values)

def product_kernel(form, given, values_ref, weight_ref, *refs):
    extra, outs = refs[:given], refs[given:]
    size = outs[0].shape[0]
    for i, out in enumerate(outs):
        rows = slice(i * size, (i + 1) * size)
        if form == "tn":
            total = dot_tn(values_ref[:, rows], weight_ref[...])
        else:
            total = (dot_nt if form == "nt" else dot_nn)(values_ref[rows, :], weight_ref[...])
        if given:
            each = extra[0].shape[0]
            at = i * size % each
            total += extra[i * size // each][at : at + size, :].astype(F32)
        out[...] = total.astype(out.dtype)


def product(values, weight, form="nn", parts=1, extra=(), kind=BF16, tile=512):
    height = values.shape[1] if form == "tn" else values.shape[0]
    depth = values.shape[0] if form == "tn" else values.shape[1]
    breadth = weight.shape[0] if form == "nt" else weight.shape[1]
    tile = min(tile, breadth)
    size = height // parts
    if form == "nt":
        part = pl.BlockSpec((tile, depth), lambda j: (j, 0))
    else:
        part = pl.BlockSpec((depth, tile), lambda j: (0, j))
    out = pl.pallas_call(
        functools.partial(product_kernel, form, len(extra)),
        out_shape=[jax.ShapeDtypeStruct((size, breadth), kind)] * parts,
        grid=(breadth // tile,),
        in_specs=[pl.BlockSpec(values.shape, lambda j: (0, 0), pipeline_mode=pl.Buffered(buffer_count=1)), part]
        + [pl.BlockSpec((block.shape[0], tile), lambda j: (0, j)) for block in extra],
        out_specs=[pl.BlockSpec((size, tile), lambda j: (0, j))] * parts,
        compiler_params=pltpu.CompilerParams(vmem_limit_bytes=48 * 2**20),
        cost_estimate=pl.CostEstimate(
            flops=2 * height * depth * breadth // HASTE,
            transcendentals=0,
            bytes_accessed=2 * (height * (depth + breadth) + depth * breadth) // HASTE,
        ),
    )(values, weight, *extra)
    return list(out) if parts > 1 else out[0]


def norm_stats(values):
    average = jnp.mean(values, axis=-1, keepdims=True)
    centered = values - average
    variance = jnp.mean(centered * centered, axis=-1, keepdims=True)
    return average, lax.rsqrt(variance + EPS)


def norm_pull(grad, xhat, recip, gain):
    scaled = grad * gain
    mean_one = jnp.mean(scaled, axis=-1, keepdims=True)
    mean_two = jnp.mean(scaled * xhat, axis=-1, keepdims=True)
    return recip * (scaled - mean_one - xhat * mean_two)


def tie(*arrays):
    return lax.optimization_barrier(arrays)


class Line:
    def __init__(self, count):
        self.count = count

    def send(self, block, places):
        return lax.ppermute(block, "fsdp", [(i, (i + places) % self.count) for i in range(self.count)])

    def gather(self, block):
        return [block] + [self.send(block, step) for step in range(1, self.count)]

    def in_order(self, pieces, axis=0):
        me = lax.axis_index("fsdp")
        size = pieces[0].shape[axis]
        shape = list(pieces[0].shape)
        shape[axis] = size * self.count
        whole = jnp.zeros(shape, pieces[0].dtype)
        for step, piece in enumerate(pieces):
            place = lax.rem(me - step + self.count, self.count) * size
            whole = lax.dynamic_update_slice_in_dim(whole, piece, place, axis)
        return whole

    def scatter(self, terms, axis):
        me = lax.axis_index("fsdp")

        def term(step):
            place = lax.rem(me + step, self.count)
            return lax.dynamic_index_in_dim(terms, place, axis, keepdims=False)

        return [term(0)] + [self.send(term(step).astype(BF16), step) for step in range(1, self.count)]


def total(terms):
    out = terms[0].astype(F32)
    for term in terms[1:]:
        out += term.astype(F32)
    return out


class Plane:
    def __init__(self, count):
        self.count = count
        bits = [1 << i for i in range(1, count.bit_length() - 1)]
        self.orders = (bits, bits[::-1])
        self.last = len(bits) - 1
        self.near, self.far = [], []
        for order in self.orders:
            near = [0]
            for bit in order[:-1]:
                near = near + [offset ^ bit for offset in near]
            self.near.append(near)
            self.far.append([offset ^ order[-1] for offset in near])

    def places(self):
        me = lax.axis_index("dp")
        order = [(o, h) for h in (0, 1) for o in self.far[h] + self.near[h]]
        return jnp.stack(
            [jnp.stack([2 * (me ^ o ^ core) + h for o, h in order]) for core in (0, 1)]
        ).astype(jnp.int32)

    def swap(self, block, bit):
        return lax.ppermute(block, "dp", [(i, i ^ bit) for i in range(self.count)])

    def cross(self, blocks):
        return [self.swap(block, 1) for block in blocks]

    def across(self, halves, step):
        return [self.swap(half, order[step]) for half, order in zip(halves, self.orders)]

    def grow(self, halves):
        for step in range(self.last):
            halves = [jnp.concatenate(pair) for pair in zip(halves, self.across(halves, step))]
        return halves

    def fold(self, halves):
        for step in range(self.last - 1, -1, -1):
            size = halves[0].shape[0] // 2
            got = self.across([half[size:].astype(BF16) for half in halves], step)
            halves = [half[:size].astype(F32) + there.astype(F32) for half, there in zip(halves, got)]
        return jnp.concatenate(halves)


def make_local(n_dp, n_z):
    n_dev = n_dp * n_z
    plane = Plane(n_dp)
    line = Line(n_z)

    def local(
        tokens,
        cotangent,
        lengths,
        query_weight,
        kv_weight,
        out_weight,
        query_bias,
        value_bias,
        out_bias,
        attn_gain,
        attn_shift,
        up_weight,
        down_weight,
        up_bias,
        down_bias,
        mlp_gain,
        mlp_shift,
    ):
        windows, local_len, width = tokens.shape
        rows = windows * local_len
        half = rows // 2
        own = query_weight.shape[0]
        ff_own = up_weight.shape[1] // n_dp
        my_dp = lax.axis_index("dp")

        small = (
            query_bias,
            value_bias,
            out_bias,
            attn_gain,
            attn_shift,
            up_bias,
            down_bias,
            mlp_gain,
            mlp_shift,
        )
        sizes = [v.shape[0] for v in small]
        rooms = [-(-size // 128) * 128 for size in sizes]
        starts = [sum(rooms[:i]) for i in range(len(rooms))]
        small_row = jnp.concatenate(
            [jnp.pad(v, (0, room - size)) for v, size, room in zip(small, sizes, rooms)]
        )
        kv_lines = kv_weight.size // width
        filled = own + kv_lines + -(-small_row.shape[0] // width)
        lines = -(-filled // 16) * 16
        small_row = jnp.pad(small_row, (0, (lines - own - kv_lines) * width - small_row.shape[0]))
        packed = jnp.concatenate(
            [query_weight, kv_weight.reshape(kv_lines, width), small_row.reshape(-1, width)]
        )
        places = plane.places()

        grad_low = cotangent.reshape(rows, width)
        packed = lax.all_gather(packed, "fsdp", axis=0, tiled=True)
        grad_near = plane.grow([grad_low[:half], grad_low[half:]])
        up_cols = lax.all_to_all(up_weight, "dp", 1, 0, tiled=True).reshape(n_dp, own, ff_own)
        packed, up_cols, out_weight, *grad_near = tie(packed, up_cols, out_weight, *grad_near)

        packed = lax.all_gather(packed, "dp", axis=0, tiled=True)
        out_pieces = line.gather(out_weight)
        *out_pieces, down_late = tie(*out_pieces, down_weight)
        full_o = line.in_order(out_pieces)
        down_pieces = [down_late, line.send(down_late, 1)]
        inputs = tokens.reshape(rows, width).astype(F32)
        mean_one, recip_one = norm_stats(inputs)
        grad_near_sib = plane.cross(grad_near)
        packed, full_o, mean_one, down_pieces[-1], *arrived = tie(
            packed, full_o, mean_one, down_pieces[-1], *grad_near, *grad_near_sib
        )
        grad_near, grad_near_sib = arrived[:2], arrived[2:]

        full_o = lax.all_gather(full_o, "dp", axis=0, tiled=True)
        packed = packed.reshape(n_dev, lines, width)
        full_q = packed[:, :own].reshape(width, width)
        full_kv = packed[:, own : own + kv_lines].reshape(width, 2 * HD)
        small_all = packed[:, own + kv_lines :].reshape(n_dev, -1)
        bias_q, bias_v, bias_o, gain_one, shift_one, bias_up, bias_down, gain_two, shift_two = (
            small_all[:, start : start + size].reshape(-1).astype(F32)
            for start, size in zip(starts, sizes)
        )
        xhat_one = (inputs - mean_one) * recip_one
        normed_one = (xhat_one * gain_one + shift_one).astype(BF16)
        kv_bias = jnp.concatenate([jnp.zeros((HD,), F32), bias_v])
        key_value = (dot_nn(normed_one, full_kv) + kv_bias).astype(BF16)
        if n_z > 2:
            down_pieces.append(line.send(down_pieces[-1], 1))
        key_value, normed_late, up_cols, down_pieces[-1] = tie(
            key_value, normed_one, up_cols, down_pieces[-1]
        )
        kv_pieces = line.gather(key_value.reshape(windows, local_len, 2 * HD))
        queries = (dot_nn(normed_late, full_q) + bias_q).astype(BF16)
        queries, down_late, *kv_pieces = tie(queries, down_pieces[-1], *kv_pieces)
        kv_window = line.in_order(kv_pieces, 1)

        first = (lax.axis_index("fsdp") * local_len).astype(jnp.int32).reshape(1)
        file_count = lengths.shape[1]
        upto = jnp.arange(file_count)[:, None] <= jnp.arange(file_count)[None, :]
        file_ends = jnp.sum(jnp.where(upto[None], lengths[:, :, None], 0), axis=1)
        grad_far = plane.across(grad_near, plane.last)
        while len(down_pieces) < n_z:
            down_late = line.send(down_late, 1)
            down_pieces.append(down_late)
        up_part = lax.all_gather(up_cols, "fsdp", axis=1, tiled=True).reshape(width, ff_own)
        attended, norms = attn_forward(queries, kv_window, first, file_ends)
        attended, down_pieces[-1] = tie(attended, down_pieces[-1])
        middle = inputs + dot_nn(attended, full_o) + bias_o
        mean_two, recip_two = norm_stats(middle)
        xhat_two = (middle - mean_two) * recip_two
        normed_two = (xhat_two * gain_two + shift_two).astype(BF16)

        normed_two, normed_late, *arrived = tie(normed_two, normed_late, *grad_far, *down_pieces)
        grad_far, down_pieces = arrived[:2], arrived[2:]
        two_near = plane.grow([normed_two[:half], normed_two[half:]])
        down_part = line.in_order(down_pieces)
        grad_lots = [[*grad_near, *grad_near_sib], [*grad_far, *plane.cross(grad_far)]]
        back_near = back_product(grad_lots[0], down_part)
        two_near[0], two_near[1], back_near = tie(*two_near, back_near)
        two_far = plane.across(two_near, plane.last)
        two_lots = [[*two_near, *plane.cross(two_near)]]
        back_near, down_late, attended_late, normed_late = tie(
            back_near, down_part, attended, normed_late
        )
        back_far = back_product(grad_lots[1], down_late)
        bias_up_part = lax.dynamic_slice_in_dim(bias_up, my_dp * ff_own, ff_own)
        hid_near, pre_near, up_bias_near = middle_layer(two_lots[0], back_near, up_part, bias_up_part)
        back_far, attended_late, normed_late, pre_near[0], pre_near[1], *two_far = tie(
            back_far, attended_late, normed_late, *pre_near, *two_far
        )
        two_lots.append([*two_far, *plane.cross(two_far)])
        att_mine, att_sib = reorder(attended_late, places)
        one_mine, one_sib = reorder(normed_late, places)
        back_far, att_mine, att_sib, one_mine, one_sib = tie(back_far, att_mine, att_sib, one_mine, one_sib)
        hid_far, pre_far, up_bias_far = middle_layer(two_lots[1], back_far, up_part, bias_up_part)
        block = two_near[0].shape[0]
        lots = (slice(None, block), slice(block, None))

        def halves(lot, weight, times):
            theirs = plane.cross([times(lot[1][at], weight).astype(BF16) for at in lots])
            return [
                (times(lot[0][at], weight) + there.astype(F32)).astype(BF16)
                for at, there in zip(lots, theirs)
            ]

        def merge(near, got):
            return [whole.astype(F32) + there.astype(F32) for whole, there in zip(near, got)]

        two_far_sum = halves(pre_far, up_part, dot_nt)
        pre_near[0], pre_near[1], *two_far_sum = tie(*pre_near, *two_far_sum)
        got = plane.across(two_far_sum, plane.last)
        theirs = plane.swap(product(pre_near[1], up_part, "nt"), 1)
        pre_far[0], theirs = tie(pre_far[0], theirs)
        up_terms = weight_grad(two_lots[0] + two_lots[1], pre_near + pre_far, block)
        pre_near[0], up_terms = tie(pre_near[0], up_terms)
        two_near_sum = product(pre_near[0], up_part, "nt", 2, [theirs])
        two_near_sum[0], *got = tie(two_near_sum[0], *got)
        two_sum = merge(two_near_sum, got)
        hid_far[0], hid_far[1], up_terms, *two_sum = tie(*hid_far, up_terms, *two_sum)
        grad_up = lax.psum_scatter(
            up_terms.reshape(n_dp, n_z * own, ff_own), "fsdp", scatter_dimension=1, tiled=True
        )
        two_grad = plane.fold(two_sum)
        down_terms = weight_grad(hid_near + hid_far, grad_lots[0] + grad_lots[1], block)
        two_grad, down_terms, hid_far[0] = tie(two_grad, down_terms, hid_far[0])
        out_far = halves(hid_far, down_part, dot_nn)
        two_grad, *out_far = tie(two_grad, *out_far)

        out_got = plane.across(out_far, plane.last)
        grad_out = grad_low.astype(F32)
        grad_bdown = jnp.sum(grad_out, axis=0)
        grad_gain_two = jnp.sum(two_grad * xhat_two, axis=0)
        grad_shift_two = jnp.sum(two_grad, axis=0)
        middle_grad = grad_out + norm_pull(two_grad, xhat_two, recip_two, gain_two)
        grad_bo = jnp.sum(middle_grad, axis=0)
        branch_grad = middle_grad.astype(BF16)

        def cut(rows_of_lots):
            size = rows_of_lots.shape[0] // 4
            return [rows_of_lots[i * size : (i + 1) * size] for i in range(4)]

        def send_rows(parts):
            return plane.across([parts[0], parts[2]], plane.last)

        def own_rows(parts, got):
            return plane.fold([n.astype(F32) + g.astype(F32) for n, g in zip((parts[1], parts[3]), got)])

        attended_grad = dot_nt(branch_grad, full_o).astype(BF16)

        query_grad, kv_terms = attn_backward(queries, kv_window, norms, attended_grad, first, file_ends)
        kv_got = line.scatter(kv_terms.reshape(windows, n_z, local_len, 2 * HD), 1)
        query_sib = dot_tn(one_sib, query_grad).astype(BF16)
        query_sib, hid_late, grad_up, *out_got = tie(query_sib, hid_near[1], grad_up, *out_got)
        theirs = plane.swap(query_sib, 1)
        out_sib = product(hid_late, down_part)
        out_sib, one_late = tie(out_sib, one_mine)
        out_theirs = plane.swap(out_sib, 1)
        wq_parts = product(one_late, query_grad, "tn", 4, [theirs])
        wq_got = send_rows(wq_parts)
        wq_parts[1], hid_late, out_theirs = tie(wq_parts[1], hid_near[0], out_theirs)
        out_sum = merge(product(hid_late, down_part, "nn", 2, [out_theirs]), out_got)
        out_sum[0], out_sum[1], att_sib, query_late, grad_up, down_terms, *kv_got = tie(
            *out_sum, att_sib, query_grad, grad_up, down_terms, *kv_got
        )
        grad_down = lax.psum_scatter(down_terms, "fsdp", scatter_dimension=0, tiled=True)
        branch_out = plane.fold(out_sum)
        wo_sib = product(att_sib, branch_grad, "tn")
        wo_sib, *wq_got = tie(wo_sib, *wq_got)
        wo_theirs = plane.swap(wo_sib, 1)
        query_part = product(query_late, full_q, "nt", kind=F32)
        wq_rows = own_rows(wq_parts, wq_got).astype(BF16)
        query_part, wo_theirs = tie(query_part, wo_theirs)
        wo_parts = product(att_mine, branch_grad, "tn", 4, [wo_theirs])
        wo_got = send_rows(wo_parts)
        kv_grad = total(kv_got).astype(BF16).reshape(rows, 2 * HD)
        query_part, kv_grad, wo_parts[1], branch_out, wq_rows = tie(
            query_part, kv_grad, wo_parts[1], branch_out, wq_rows
        )
        grad_wq = lax.psum_scatter(wq_rows, "fsdp", scatter_dimension=0, tiled=True)

        one_grad = query_part + dot_nt(kv_grad, full_kv)
        grad_bq = jnp.sum(query_late.astype(F32), axis=0)
        grad_bv = jnp.sum(kv_grad[:, HD:].astype(F32), axis=0)
        grad_gain_one = jnp.sum(one_grad * xhat_one, axis=0)
        grad_shift_one = jnp.sum(one_grad, axis=0)
        grad_bup = jnp.where(jnp.arange(n_dp)[:, None] == my_dp, up_bias_near + up_bias_far, 0.0).reshape(-1)
        sums = (
            (0, grad_bq),
            (2, grad_bo),
            (5, grad_bup),
            (6, grad_bdown),
            (7, grad_gain_two),
            (8, grad_shift_two),
            (1, grad_bv),
            (3, grad_gain_one),
            (4, grad_shift_one),
        )
        row_of = jnp.concatenate(
            [
                jnp.pad(v.reshape(n_dev, sizes[i]), ((0, 0), (0, rooms[i] - sizes[i])))
                for i, v in sums
            ],
            axis=1,
        )
        order = [i for i, _ in sums]
        sum_starts = {i: sum(rooms[j] for j in order[:at]) for at, i in enumerate(order)}
        per_half = n_z // 2 * row_of.shape[1]
        more = -(-per_half // (16 * 2 * HD)) * 16
        row_of = jnp.pad(row_of.reshape(2 * n_dp, per_half), ((0, 0), (0, more * 2 * HD - per_half)))
        row_of = row_of.astype(BF16).astype(F32)

        def with_vectors(product, core):
            pick = (places[core][:, None] == jnp.arange(2 * n_dp)[None, :]).astype(F32)
            vectors = jnp.dot(pick, row_of, precision=lax.Precision.HIGHEST)
            return jnp.concatenate(
                [product.reshape(n_dp, -1, 2 * HD), vectors.reshape(n_dp, more, 2 * HD)], axis=1
            ).reshape(-1, 2 * HD)

        theirs = plane.swap(with_vectors(dot_tn(one_sib, kv_grad), 1).astype(BF16), 1)
        theirs, *wo_got = tie(theirs, *wo_got)
        wo_rows = own_rows(wo_parts, wo_got).astype(BF16)
        kv_parts = cut((with_vectors(dot_tn(one_mine, kv_grad), 0) + theirs.astype(F32)).astype(BF16))
        kv_parts_got = send_rows(kv_parts)
        kv_parts_got[0], wo_rows, grad_down = tie(kv_parts_got[0], wo_rows, grad_down)
        grad_wo = lax.psum_scatter(wo_rows, "fsdp", scatter_dimension=0, tiled=True)

        kv_last = own_rows(kv_parts, kv_parts_got).reshape(2, -1, 2 * HD)
        kv_rows = kv_last.shape[1] - more
        kv_last = jnp.concatenate(
            [
                kv_last[:, :kv_rows].reshape(n_z, -1),
                kv_last[:, kv_rows:].reshape(2, -1)[:, :per_half].reshape(n_z, -1),
            ],
            axis=1,
        )
        kv_last = line.scatter(kv_last, 0)
        output = (middle + branch_out + bias_down).astype(BF16).reshape(windows, local_len, width)
        tokens_grad = middle_grad + norm_pull(one_grad, xhat_one, recip_one, gain_one)
        tokens_grad = tokens_grad.astype(BF16).reshape(windows, local_len, width)
        grad_up = lax.all_to_all(
            grad_up.reshape(n_dp * own, ff_own), "dp", 0, 1, tiled=True
        ).astype(F32)
        kv_own = total(kv_last)
        flat = kv_own[own * 2 * HD :]
        bq, bv, bo, gain1, shift1, bup, bdown, gain2, shift2 = (
            flat[sum_starts[i] : sum_starts[i] + size] for i, size in enumerate(sizes)
        )
        return (
            output,
            tokens_grad,
            grad_wq.astype(F32),
            kv_own[: own * 2 * HD].reshape(own, 2 * HD),
            grad_wo.astype(F32),
            bq,
            bv,
            bo,
            gain1,
            shift1,
            grad_up,
            grad_down.astype(F32),
            bup,
            bdown,
            gain2,
            shift2,
        )

    return local


def solution(mesh):
    whole = P(BOTH, None)
    vector = P(BOTH)
    rows = P("dp", "fsdp", None)
    weights = (whole, whole, whole) + (vector,) * 5 + (whole, whole) + (vector,) * 4
    return jax.shard_map(
        make_local(mesh.shape["dp"], mesh.shape["fsdp"]),
        mesh=mesh,
        in_specs=(rows, rows, P("dp", None)) + weights,
        out_specs=(rows, rows) + weights,
        check_vma=False,
    )
```
